32 devices in a mesh: dp: 4 (over x, core), fsdp: 8 (over z, y).
Axes of the slice: x: 2, y: 2, z: 4, core: 2. Of those that a mesh axis runs over, the one named last changes fastest.
Arguments:
- latents: bfloat16 [128, 64, 1536], P(('dp', 'fsdp')), may hold values from -6 to 6
- media: bfloat16 [576, 48, 1536], P(('dp', 'fsdp')), may hold values from -6 to 6
- frame_counts: int32 [128], P(('dp', 'fsdp')), may hold values from 1 to 8, as said below
- cotangent: bfloat16 [128, 64, 1536], P(('dp', 'fsdp')), may hold values from -6 to 6
- w_qkv: float32 [1536, 3, 1536], P(('dp', 'fsdp')), may hold values from -0.15625 to 0.15625
- m_qkv: float32 [1536, 3, 1536], P(('dp', 'fsdp')), may hold values from -0.00012207031 to 0.00012207031
- v_qkv: float32 [1536, 3, 1536], P(('dp', 'fsdp')), may hold values from 3.532127e-11 to 1.4128508e-10
- w_out: float32 [1536, 1536], P(('dp', 'fsdp')), may hold values from -1.25 to 1.25
- m_out: float32 [1536, 1536], P(('dp', 'fsdp')), may hold values from -0.00012207031 to 0.00012207031
- v_out: float32 [1536, 1536], P(('dp', 'fsdp')), may hold values from 7.064254e-12 to 2.8257017e-11
- w_up: float32 [1536, 6144], P(('dp', 'fsdp')), may hold values from -0.15625 to 0.15625
- m_up: float32 [1536, 6144], P(('dp', 'fsdp')), may hold values from -0.00012207031 to 0.00012207031
- v_up: float32 [1536, 6144], P(('dp', 'fsdp')), may hold values from 3.532127e-11 to 1.4128508e-10
- w_down: float32 [6144, 1536], P(('dp', 'fsdp')), may hold values from -0.078125 to 0.078125
- m_down: float32 [6144, 1536], P(('dp', 'fsdp')), may hold values from -0.00012207031 to 0.00012207031
- v_down: float32 [6144, 1536], P(('dp', 'fsdp')), may hold values from 3.532127e-11 to 1.4128508e-10
- time_table: float32 [1536, 8], P(('dp', 'fsdp')), may hold values from -3 to 3
- m_time: float32 [1536, 8], P(('dp', 'fsdp')), may hold values from -0.00036621094 to 0.00036621094
- v_time: float32 [1536, 8], P(('dp', 'fsdp')), may hold values from 3.1789144e-10 to 1.2715657e-09
- gains: float32 [1536, 3], P(('dp', 'fsdp')), may hold values from 0.3 to 2.5, as said below
- m_gains: float32 [1536, 3], P(('dp', 'fsdp')), may hold values from -0.00036621094 to 0.00036621094
- v_gains: float32 [1536, 3], P(('dp', 'fsdp')), may hold values from 3.1789144e-10 to 1.2715657e-09
Outputs:
- new_latents: bfloat16 [128, 64, 1536], P(('dp', 'fsdp'))
- d_latents: float32 [128, 64, 1536], P(('dp', 'fsdp'))
- grad_norm: float32 [], replicated
- new_w_qkv: float32 [1536, 3, 1536], P(('dp', 'fsdp'))
- new_m_qkv: float32 [1536, 3, 1536], P(('dp', 'fsdp'))
- new_v_qkv: float32 [1536, 3, 1536], P(('dp', 'fsdp'))
- new_w_out: float32 [1536, 1536], P(('dp', 'fsdp'))
- new_m_out: float32 [1536, 1536], P(('dp', 'fsdp'))
- new_v_out: float32 [1536, 1536], P(('dp', 'fsdp'))
- new_w_up: float32 [1536, 6144], P(('dp', 'fsdp'))
- new_m_up: float32 [1536, 6144], P(('dp', 'fsdp'))
- new_v_up: float32 [1536, 6144], P(('dp', 'fsdp'))
- new_w_down: float32 [6144, 1536], P(('dp', 'fsdp'))
- new_m_down: float32 [6144, 1536], P(('dp', 'fsdp'))
- new_v_down: float32 [6144, 1536], P(('dp', 'fsdp'))
- new_time_table: float32 [1536, 8], P(('dp', 'fsdp'))
- new_m_time: float32 [1536, 8], P(('dp', 'fsdp'))
- new_v_time: float32 [1536, 8], P(('dp', 'fsdp'))
- new_gains: float32 [1536, 3], P(('dp', 'fsdp'))
- new_m_gains: float32 [1536, 3], P(('dp', 'fsdp'))
- new_v_gains: float32 [1536, 3], P(('dp', 'fsdp'))
The draws below stay inside these ranges and needn't reach their ends.
Inputs may be any that keep to these rules, and one draw needn't show every extreme that they name: `frame_counts`: each item slot holds one image of 1 frame or one clip of 8 frames; the frames of one device's 4 slots never exceed 18, and on some device of every draw they fill all 18. Positive gains.
All inputs are finite; a program needn't handle non-finite values.
Results may differ from the reference program's by a relative error of at most 0.022.
Values may be sent and summed in bfloat16 or wider, within the bound.
A program may use at most 320 MiB of HBM per device.

```python
import math
import jax
import jax.numpy as jnp
from jax import lax

D = 1536
HEADS = 16
HEAD = 96
NLAT = 64
FF = 6144
TIME = 8
ITEM_DEV = 4
PATCH = 48
STEP = 10
FRAME_DEV = 18
ITEMS = 128
FRAMES = 576
N_DP = 4
N_FSDP = 8


def draw_frame_counts(key, part):
    devices = ITEMS // ITEM_DEV
    half = ITEM_DEV // 2
    key_clips = jax.random.fold_in(key, 11)
    key_pick = jax.random.fold_in(key, 12)
    key_order = jax.random.fold_in(key, 13)
    clip_count = jax.random.randint(key_clips, (devices,), 0, half + 1)
    busiest = jax.random.randint(key_pick, (), 0, devices)
    clip_count = jnp.where(jnp.arange(devices) == busiest, half, clip_count)
    order_keys = jax.random.split(key_order, devices)
    ranks = jax.vmap(lambda subkey: jax.random.permutation(subkey, ITEM_DEV))(order_keys)
    counts = jnp.where(ranks < clip_count[:, None], TIME, 1)
    return counts.reshape(devices * ITEM_DEV).astype(jnp.int32)


def draw_gains(key, part):
    key_noise = jax.random.fold_in(key, 21)
    place = jnp.arange(D, dtype=jnp.float32) / float(max(D - 1, 1))
    profile = 0.5 + place
    noise = jax.random.uniform(key_noise, (D, 3), jnp.float32, 0.85, 1.15)
    return (profile[:, None] * noise).astype(jnp.float32)


def block_scale(key, extent, cuts, smallest, high):
    factor_of, own = 1.0, jax.random.fold_in(key, 6)
    for dim, blocks in cuts:
        draws = jnp.exp(jax.random.uniform(jax.random.fold_in(own, dim), (blocks,), jnp.float32, smallest / len(cuts), high / len(cuts)))
        factor_of = factor_of * jnp.repeat(draws, extent[dim] // blocks).reshape([-1 if axis == dim else 1 for axis in range(len(extent))])
    return factor_of


def bell_draw(key, dims, scale, limit, cuts=(), kind=jnp.bfloat16):
    values = jax.random.normal(key, dims, jnp.float32) * scale
    if len(cuts) > 0:
        values = block_scale(key, dims, cuts, -0.22, 0.18) * values
    return jnp.clip(values, min=-limit, max=limit).astype(kind)


def setup_inputs(seed: int = 0) -> dict:
    arg_keys = jax.random.split(jax.random.key(seed), 23)
    latents = bell_draw(arg_keys[0], (ITEMS, NLAT, D), 1.0, 6.0, ((0, 32),))
    media = bell_draw(arg_keys[1], (FRAMES, PATCH, D), 1.0, 6.0, ((0, 32),))
    frame_counts = draw_frame_counts(jax.random.fold_in(arg_keys[22], 71), 0)
    cotangent = bell_draw(arg_keys[3], (ITEMS, NLAT, D), 1.0, 6.0, ((0, 32),))
    w_qkv = bell_draw(arg_keys[4], (D, 3, D), D ** -0.5, 0.15625, ((0, 32),), jnp.float32)
    m_qkv = bell_draw(arg_keys[5], (D, 3, D), (0.11 * (4 * D * D + 2 * D * FF) ** -0.5), 0.00012207031, ((0, 32),), jnp.float32)
    v_qkv = jnp.clip(jnp.exp(math.log(1.4128508085686775e-10) - 1.3862944 * jax.random.uniform(arg_keys[6], (D, 3, D), jnp.float32) ** block_scale(arg_keys[6], (D, 3, D), ((0, 32),), -0.2, 0.2)), 3.532127021421694e-11, 1.4128508085686775e-10)
    w_out = bell_draw(arg_keys[7], (D, D), (max(D // 64, 1)) ** -0.5, 1.25, ((0, 32),), jnp.float32)
    m_out = bell_draw(arg_keys[8], (D, D), (0.11 * (4 * D * D + 2 * D * FF) ** -0.5), 0.00012207031, ((0, 32),), jnp.float32)
    v_out = jnp.clip(jnp.exp(math.log(2.8257016518318245e-11) - 1.3862944 * jax.random.uniform(arg_keys[9], (D, D), jnp.float32) ** block_scale(arg_keys[9], (D, D), ((0, 32),), -0.2, 0.2)), 7.064254129579561e-12, 2.8257016518318245e-11)
    w_up = bell_draw(arg_keys[10], (D, FF), D ** -0.5, 0.15625, ((0, 32),), jnp.float32)
    m_up = bell_draw(arg_keys[11], (D, FF), (0.11 * (4 * D * D + 2 * D * FF) ** -0.5), 0.00012207031, ((0, 32),), jnp.float32)
    v_up = jnp.clip(jnp.exp(math.log(1.4128508085686775e-10) - 1.3862944 * jax.random.uniform(arg_keys[12], (D, FF), jnp.float32) ** block_scale(arg_keys[12], (D, FF), ((0, 32),), -0.2, 0.2)), 3.532127021421694e-11, 1.4128508085686775e-10)
    w_down = bell_draw(arg_keys[13], (FF, D), FF ** -0.5, 0.078125, ((0, 32),), jnp.float32)
    m_down = bell_draw(arg_keys[14], (FF, D), (0.11 * (4 * D * D + 2 * D * FF) ** -0.5), 0.00012207031, ((0, 32),), jnp.float32)
    v_down = jnp.clip(jnp.exp(math.log(1.4128508085686775e-10) - 1.3862944 * jax.random.uniform(arg_keys[15], (FF, D), jnp.float32) ** block_scale(arg_keys[15], (FF, D), ((0, 32),), -0.2, 0.2)), 3.532127021421694e-11, 1.4128508085686775e-10)
    time_table = bell_draw(arg_keys[16], (D, TIME), 0.5, 3.0, ((0, 32),), jnp.float32)
    m_time = bell_draw(arg_keys[17], (D, TIME), (0.33 * (4 * D * D + 2 * D * FF) ** -0.5), 0.00036621094, ((0, 32),), jnp.float32)
    v_time = jnp.clip(jnp.exp(math.log(1.2715657415895976e-09) - 1.3862944 * jax.random.uniform(arg_keys[18], (D, TIME), jnp.float32) ** block_scale(arg_keys[18], (D, TIME), ((0, 32),), -0.2, 0.2)), 3.178914353973994e-10, 1.2715657415895976e-09)
    gains = draw_gains(jax.random.fold_in(arg_keys[22], 71), 0)
    m_gains = bell_draw(arg_keys[20], (D, 3), (0.33 * (4 * D * D + 2 * D * FF) ** -0.5), 0.00036621094, ((0, 32),), jnp.float32)
    v_gains = jnp.clip(jnp.exp(math.log(1.2715657415895976e-09) - 1.3862944 * jax.random.uniform(arg_keys[21], (D, 3), jnp.float32) ** block_scale(arg_keys[21], (D, 3), ((0, 32),), -0.2, 0.2)), 3.178914353973994e-10, 1.2715657415895976e-09)
    return {"latents": latents, "media": media, "frame_counts": frame_counts, "cotangent": cotangent, "w_qkv": w_qkv, "m_qkv": m_qkv, "v_qkv": v_qkv, "w_out": w_out, "m_out": m_out, "v_out": v_out, "w_up": w_up, "m_up": m_up, "v_up": v_up, "w_down": w_down, "m_down": m_down, "v_down": v_down, "time_table": time_table, "m_time": m_time, "v_time": v_time, "gains": gains, "m_gains": m_gains, "v_gains": v_gains}


@jax.custom_vjp
def low(v):
    return lax.optimization_barrier(v.astype(jnp.bfloat16)).astype(jnp.float32)

@jax.custom_vjp
def low_back(v):
    return v

def low_keep(v):
    return (low(v), None)

def low_pass(kept, grad):
    return (grad,)

def back_keep(v):
    return (v, None)

def back_low(kept, grad):
    return (low(grad),)
low.defvjp(low_keep, low_pass)
low_back.defvjp(back_keep, back_low)
highest = lax.Precision.HIGHEST
norm_eps = 1e-05
clip_limit = 1.0
beta_one = 0.9
beta_two = 0.999
adam_eps = 1e-08
decay_rate = 0.1

def layer_norm(values_in, gain):
    mean_row = lax.optimization_barrier(jnp.mean(values_in, axis=-1, keepdims=True))
    centered = values_in - mean_row
    var_row = lax.optimization_barrier(jnp.mean(centered * centered, axis=-1, keepdims=True))
    return centered * lax.rsqrt(var_row + norm_eps) * gain

def frame_tables(counts):
    slot_ends = jnp.cumsum(counts).astype(jnp.int32)
    slot_starts = (slot_ends - counts).astype(jnp.int32)
    frame_ids = jnp.arange(FRAME_DEV, dtype=jnp.int32)
    frame_owner = lax.optimization_barrier(jnp.sum((frame_ids[:, None] >= slot_ends[None, :]).astype(jnp.int32), axis=1)).astype(jnp.int32)
    slot_ids = jnp.arange(ITEM_DEV, dtype=jnp.int32)
    start_of = lax.optimization_barrier(jnp.sum(jnp.where(frame_owner[:, None] == slot_ids[None, :], slot_starts[None, :], 0), axis=1)).astype(jnp.int32)
    time_index = frame_ids - start_of
    live_frame = frame_owner < ITEM_DEV
    time_ids = jnp.arange(TIME, dtype=jnp.int32)
    time_hot = ((time_index[:, None] == time_ids[None, :]) & live_frame[:, None]).astype(jnp.float32)
    return (frame_owner, time_hot)

def device_forward(params, lat_block, media_block, counts):
    qkv_w, out_w, up_w, down_w, time_w, gain_w = params
    queries_n = ITEM_DEV * NLAT
    media_rows = FRAME_DEV * PATCH
    frame_owner, time_hot = frame_tables(counts)
    frame_time = jnp.dot(time_hot, time_w.T, precision=highest)
    mixed = media_block + frame_time[:, None, :]
    media_norm = low(layer_norm(mixed, gain_w[:, 0])).reshape(media_rows, D)
    lat_rows = lat_block.reshape(queries_n, D)
    lat_norm = low(layer_norm(lat_rows, gain_w[:, 1]))
    keys_in = jnp.concatenate([media_norm, lat_norm], axis=0)
    queries = low_back(low(jnp.dot(lat_norm, qkv_w[:, 0, :], precision=highest)))
    keys_all = low_back(low(jnp.dot(keys_in, qkv_w[:, 1, :], precision=highest)))
    values_all = low_back(low(jnp.dot(keys_in, qkv_w[:, 2, :], precision=highest)))
    query_owner = jnp.arange(queries_n, dtype=jnp.int32) // NLAT
    key_owner = jnp.concatenate([jnp.repeat(frame_owner, PATCH), query_owner], axis=0)
    allowed = query_owner[:, None] == key_owner[None, :]
    q_heads = queries.reshape(queries_n, HEADS, HEAD)
    k_heads = keys_all.reshape(-1, HEADS, HEAD)
    v_heads = values_all.reshape(-1, HEADS, HEAD)
    score_scale = 1.0 / HEAD ** 0.5
    scores = low_back(jnp.einsum('qhe,khe->hqk', q_heads, k_heads, precision=highest) * score_scale)
    scores = jnp.where(allowed[None, :, :], scores, -1e+30)
    row_top = lax.optimization_barrier(jnp.max(scores, axis=-1, keepdims=True))
    weights = jnp.exp(scores - row_top)
    probs = weights / lax.optimization_barrier(jnp.sum(weights, axis=-1, keepdims=True))
    probs_low = low(probs)
    attended = jnp.einsum('hqk,khe->qhe', probs_low, v_heads, precision=highest).reshape(queries_n, D)
    attended = low_back(low(attended))
    branch = low_back(jnp.dot(attended, out_w, precision=highest))
    middle = lat_rows + branch
    hidden = low(layer_norm(middle, gain_w[:, 2]))
    pre_act = low_back(jnp.dot(hidden, up_w, precision=highest))
    activated = low(jax.nn.gelu(pre_act, approximate=False))
    return middle + jnp.dot(activated, down_w, precision=highest)

def adamw_step(weight, first, second, grad, factor, rate):
    clipped = grad * factor
    first_new = beta_one * first + (1.0 - beta_one) * clipped
    second_new = beta_two * second + (1.0 - beta_two) * clipped * clipped
    first_hat = first_new / (1.0 - beta_one ** STEP)
    second_hat = second_new / (1.0 - beta_two ** STEP)
    weight_new = weight - rate * (first_hat / (jnp.sqrt(second_hat) + adam_eps) + decay_rate * weight)
    return (weight_new, first_new, second_new)

def reference(latents, media, frame_counts, cotangent, w_qkv, m_qkv, v_qkv, w_out, m_out, v_out, w_up, m_up, v_up, w_down, m_down, v_down, time_table, m_time, v_time, gains, m_gains, v_gains):
    devices = N_DP * N_FSDP
    lat_blocks = latents.astype(jnp.float32).reshape(devices, ITEM_DEV, NLAT, D)
    media_blocks = media.astype(jnp.float32).reshape(devices, FRAME_DEV, PATCH, D)
    count_blocks = frame_counts.reshape(devices, ITEM_DEV)
    masters = (w_qkv, w_out, w_up, w_down, time_table, gains)
    block_fn = jax.checkpoint(device_forward)

    def forward(params, lat_all):
        low_params = tuple((low(param) for param in params))

        def scan_step(carry, block):
            return (carry, block_fn(low_params, block[0], block[1], block[2]))
        unused, outputs = lax.scan(scan_step, jnp.zeros((), jnp.float32), (lat_all, media_blocks, count_blocks))
        return outputs
    result, vjp_fn = jax.vjp(forward, masters, lat_blocks)
    cot_blocks = cotangent.astype(jnp.float32).reshape(devices, ITEM_DEV * NLAT, D)
    param_grads, lat_grads = vjp_fn(cot_blocks)
    new_latents = result.reshape(ITEMS, NLAT, D).astype(jnp.bfloat16)
    d_latents = lat_grads.reshape(ITEMS, NLAT, D)
    total_sq = jnp.zeros((), jnp.float32)
    for grad in param_grads:
        total_sq = total_sq + jnp.sum(grad * grad)
    grad_norm = jnp.sqrt(total_sq)
    factor = jnp.minimum(1.0, clip_limit / (grad_norm + 1e-06))
    rates = (0.02, 0.1, 0.02, 0.01, 0.2, 0.5)
    firsts = (m_qkv, m_out, m_up, m_down, m_time, m_gains)
    seconds = (v_qkv, v_out, v_up, v_down, v_time, v_gains)
    updated = []
    for index in range(6):
        updated.extend(adamw_step(masters[index], firsts[index], seconds[index], param_grads[index], factor, rates[index]))
    return (new_latents, d_latents, grad_norm, updated[0], updated[1], updated[2], updated[3], updated[4], updated[5], updated[6], updated[7], updated[8], updated[9], updated[10], updated[11], updated[12], updated[13], updated[14], updated[15], updated[16], updated[17])
```

```python
import functools

import jax
import jax.numpy as jnp
from jax import lax
from jax.experimental import pallas as pl
from jax.experimental.pallas import tpu as pltpu
from jax.sharding import PartitionSpec as P

HEADS = 16
STEP = 10


highest = lax.Precision.HIGHEST
norm_eps = 1e-05
clip_limit = 1.0
beta_one = 0.9
beta_two = 0.999
adam_eps = 1e-08
decay_rate = 0.1

MESH=pl.DeviceIdType.MESH
ANY=pl.ANY

class Place:
    def __init__(self, n_z):
        dp = lax.axis_index("dp"); fs = lax.axis_index("fsdp")
        self.n_z = n_z
        self.at = {"x": dp // 2, "c": dp % 2, "z": fs // 2, "y": fs % 2}
    def dev(self, **new):
        p = {**self.at, **new}
        return (p["x"] * 2 + p["c"], p["z"] * 2 + p["y"])
    def other(self, ax):
        return self.dev(**{ax: 1 - self.at[ax]})
    def along_z(self, k):
        return self.dev(z=(self.at["z"] + k) % self.n_z)
    def partners(self):
        return [self.other(a) for a in "cxy"] + [self.along_z(k) for k in range(1, self.n_z)]

def greet(place):
    bar = pltpu.get_barrier_semaphore()
    others = place.partners()
    for d in others:
        pl.semaphore_signal(bar, inc=1, device_id=d, device_id_type=MESH)
    pl.semaphore_wait(bar, len(others))

def block_index(place, held):
    return tuple(slice(None) if ax in held else place.at[ax] for ax in "xczy")

class Gather:
    def __init__(self, place, src, dst, rows, cols, order, sems, base):
        self.place, self.src, self.dst = place, src, dst
        self.sl = (pl.ds(*rows), pl.ds(*cols))
        self.order, self.sems, self.base = order, sems, base
        self.copies = {}
    def region(self, held):
        return self.dst.at[block_index(self.place, held) + self.sl]
    def start(self, step):
        p = self.place; ax = self.order[step]; held = self.order[:step]
        ss, rs = self.sems
        made = []
        n = self.base
        for s in range(step):
            n += p.n_z - 1 if self.order[s] == "z" else 1
        src = self.src.at[self.sl] if step == 0 else self.region(held)
        dst = self.region(held)
        for k in (range(1, p.n_z) if ax == "z" else (0,)):
            to = p.along_z(k) if ax == "z" else p.other(ax)
            d = pltpu.make_async_remote_copy(src_ref=src, dst_ref=dst, send_sem=ss.at[n], recv_sem=rs.at[n], device_id=to, device_id_type=MESH)
            d.start(); made.append(d); n += 1
        self.copies[step] = made
    def arrive(self, step):
        for d in self.copies[step]: d.wait_recv()
    def finish(self):
        for made in self.copies.values():
            for d in made: d.wait_send()

def n_sems(n_z): return n_z + 2

def gather_kernel(n_z, plan, n_w, *refs):
    ins, outs, (ss, rs, ls) = refs[:n_w], refs[n_w:2*n_w], refs[2*n_w:]
    place = Place(n_z)
    greet(place)
    locals_ = []
    for i in range(n_w):
        d = pltpu.make_async_copy(ins[i], outs[i].at[block_index(place, ())], ls.at[i])
        d.start(); locals_.append(d)
    stages = [[Gather(place, ins[w], outs[w], rows, cols, order, (ss, rs), j * n_sems(n_z)) for (j, w, rows, cols, order) in stage] for stage in plan]
    waited = set()
    T, steps = len(stages), 4
    for t in range(T + steps):
        for back in range(steps + 1):
            u = t - back
            if not 0 <= u < T: continue
            for g, (j, w, *_) in zip(stages[u], plan[u]):
                if back == 1 and w not in waited:
                    locals_[w].wait(); waited.add(w)
                if back > 0: g.arrive(back - 1)
                if back < steps: g.start(back)
    for st in stages:
        for g in st: g.finish()

def number(plan):
    j, out = 0, []
    for stage in plan:
        new = []
        for piece in stage:
            new.append((j,) + piece); j += 1
        out.append(new)
    return out, j

def gather_all(shards, plan, n_z):
    plan, count = number(plan)
    n_w = len(shards)
    return pl.pallas_call(
        functools.partial(gather_kernel, n_z, plan, n_w),
        out_shape=[jax.ShapeDtypeStruct((2, 2, n_z, 2) + s.shape, s.dtype) for s in shards],
        in_specs=[pl.BlockSpec(memory_space=pltpu.VMEM)] * n_w,
        out_specs=[pl.BlockSpec(memory_space=ANY)] * n_w,
        scratch_shapes=[pltpu.SemaphoreType.DMA((count * n_sems(n_z),)), pltpu.SemaphoreType.DMA((count * n_sems(n_z),)), pltpu.SemaphoreType.DMA((n_w,))],
        name="gather_weights",
        compiler_params=pltpu.CompilerParams(collective_id=0, has_side_effects=True),
    )(*shards)

ZYX, ZXY = ("z", "y", "x", "c"), ("z", "x", "y", "c")

SLOTS = 3

class Scatter:
    def __init__(self, place, src, out, rows, cols, order, piece, part, turn, sems, bufs):
        self.p, self.src, self.out = place, src, out
        self.rows, self.cols = pl.ds(*rows), pl.ds(*cols)
        self.shape = (rows[1], cols[1])
        self.order, self.piece = order, piece
        self.ss, self.rs, self.ls = sems
        self.part, self.slot, self.b = part, (turn % SLOTS) * 2 + part, bufs
        self.sent = {}
    def v(self, ref, *lead):
        return ref.at[lead + (pl.ds(0, self.shape[0]), pl.ds(0, self.shape[1]))]
    def send(self, src, dst, to, n):
        n += self.piece * n_sems(self.p.n_z)
        d = pltpu.make_async_remote_copy(src_ref=src, dst_ref=dst, send_sem=self.ss.at[n], recv_sem=self.rs.at[n], device_id=to, device_id_type=MESH)
        d.start()
        return d
    def copy(self, src, dst, k):
        d = pltpu.make_async_copy(src, dst, self.ls.at[self.slot, k])
        d.start()
        return d
    def add(self, count, dst, a, b):
        r, w = self.shape
        def one(i, carry):
            (da, di), (aa, ai), (ba, bi) = dst(i), a(i), b(i)
            da[di + (slice(0, r), slice(0, w))] = aa[ai + (slice(0, r), slice(0, w))] + ba[bi + (slice(0, r), slice(0, w))]
            return carry
        lax.fori_loop(0, count, one, 0)
    def free(self, step):
        if step in self.sent:
            for d in self.sent.pop(step): d.wait_send() if step < 4 else d.wait()
    def step0(self):
        p = self.p; c = p.at["c"]; A = slice(None)
        self.sent[0] = [self.send(self.src.at[:, 1 - c, :, :, self.rows, self.cols], self.v(self.b["r0"], self.piece, A, A, A), p.other("c"), 0)]
        self.mine = self.copy(self.src.at[:, c, :, :, self.rows, self.cols], self.v(self.b["s0"], self.slot, A, A, A), 0)
        self.came = self.sent[0]
    def step1(self):
        p = self.p; A = slice(None); nz = p.n_z; b = self.b; sl, pt = self.slot, self.part
        for d in self.came: d.wait_recv()
        got = self.copy(self.v(b["r0"], self.piece, A, A, A), self.v(b["t0"], pt, A, A, A), 1)
        self.mine.wait(); got.wait()
        at = lambda i: (i // (nz * 2), (i // 2) % nz, i % 2)
        self.add(4 * nz, lambda i: (b["s0"], (sl,) + at(i)), lambda i: (b["s0"], (sl,) + at(i)), lambda i: (b["t0"], (pt,) + at(i)))
        ax = self.order[0]; o = 1 - p.at[ax]
        src = self.v(b["s0"], sl, o, A, A) if ax == "x" else self.v(b["s0"], sl, A, A, o)
        dst = self.v(b["r1"], self.piece, A, A)
        if ax == "x":
            dst = self.v(b["r1y"], self.piece, A, A)
        self.sent[1] = self.came = [self.send(src, dst, p.other(ax), 1)]
    def step2(self):
        p = self.p; A = slice(None); nz = p.n_z; b = self.b; sl, pt = self.slot, self.part
        for d in self.came: d.wait_recv()
        ax = self.order[0]; m = p.at[ax]; o = 1 - p.at[self.order[1]]
        if ax == "x":
            got = self.copy(self.v(b["r1y"], self.piece, A, A), self.v(b["t1y"], A, A), 1); got.wait()
            at = lambda i: (i // 2, i % 2)
            self.add(2 * nz, lambda i: (b["s1y"], (sl // 2,) + at(i)), lambda i: (b["s0"], (sl, m) + at(i)), lambda i: (b["t1y"], at(i)))
            src = self.v(b["s1y"], sl // 2, A, o)
        else:
            got = self.copy(self.v(b["r1"], self.piece, A, A), self.v(b["t1"], A, A), 1); got.wait()
            at = lambda i: (i // nz, i % nz)
            self.add(2 * nz, lambda i: (b["s1"], (sl // 2,) + at(i)), lambda i: (b["s0"], (sl,) + at(i) + (m,)), lambda i: (b["t1"], at(i)))
            src = self.v(b["s1"], sl // 2, o, A)
        self.sent[2] = self.came = [self.send(src, self.v(b["r2"], self.piece, A), p.other(self.order[1]), 2)]
    def step3(self):
        p = self.p; A = slice(None); nz = p.n_z; b = self.b; sl, pt = self.slot, self.part
        for d in self.came: d.wait_recv()
        got = self.copy(self.v(b["r2"], self.piece, A), self.v(b["t2"], pt, A), 1); got.wait()
        m = p.at[self.order[1]]
        mine = (lambda i: (b["s1y"], (sl // 2, i, m))) if self.order[0] == "x" else (lambda i: (b["s1"], (sl // 2, m, i)))
        self.add(nz, lambda i: (b["s2"], (sl, i)), mine, lambda i: (b["t2"], (pt, i)))
        self.sent[3] = self.came = [
            self.send(self.v(b["s2"], sl, (p.at["z"] + k) % nz), self.v(b["r3"], self.piece, k - 1), p.along_z(k), 2 + k)
            for k in range(1, nz)]
    def step4(self):
        p = self.p; A = slice(None); nz = p.n_z; b = self.b; sl, pt = self.slot, self.part
        r, w = self.shape
        for d in self.came: d.wait_recv()
        got = self.copy(self.v(b["r3"], self.piece, A), self.v(b["t3"], pt, A), 1); got.wait()
        total = b["s2"][sl, p.at["z"], 0:r, 0:w].astype(jnp.float32)
        for k in range(nz - 1):
            total = total + b["t3"][pt, k, 0:r, 0:w].astype(jnp.float32)
        b["o"][sl, 0:r, 0:w] = total
        b["sq"][0:r, 0:w] += total * total
        self.sent[4] = [self.copy(self.v(b["o"], sl), self.out.at[self.rows, self.cols], 2)]

def scatter_kernel(n_z, plan, n_w, names, *refs):
    ins, outs = refs[:n_w], refs[n_w:2 * n_w]
    norm_out = refs[2 * n_w]
    rest = refs[2 * n_w + 1:]
    bufs = dict(zip(names, rest))
    ss, rs, ls, ns, nr = rest[len(names):]
    place = Place(n_z)
    greet(place)
    bufs["sq"][...] = jnp.zeros_like(bufs["sq"])
    stages = [[Scatter(place, ins[w], outs[w], rows, cols, order, j, part, t, (ss, rs, ls), bufs) for part, (j, w, rows, cols, order) in enumerate(stage)] for t, stage in enumerate(plan)]
    T = len(stages)
    for t in range(T + 4):
        for back in range(5):
            u = t - back
            if not 0 <= u < T: continue
            if u >= SLOTS:
                for g in stages[u - SLOTS]:
                    if back == 0: g.free(1)
                    else: g.free(back)
            for g in stages[u]: getattr(g, f"step{back}")()
    for st in stages:
        for g in st:
            for k in range(5): g.free(k)
    sq = bufs["sq"]
    part = bufs["n"]
    acc = jnp.zeros((8, 128), jnp.float32)
    for i in range(sq.shape[0] // 8):
        for j in range(sq.shape[1] // 128):
            acc = acc + sq[i * 8:(i + 1) * 8, j * 128:(j + 1) * 128]
    for q, ax in enumerate("cxy"):
        part[2 * q] = acc
        d = pltpu.make_async_remote_copy(src_ref=part.at[2 * q], dst_ref=part.at[2 * q + 1], send_sem=ns.at[q], recv_sem=nr.at[q], device_id=place.other(ax), device_id_type=MESH)
        d.start(); d.wait()
        acc = part[2 * q] + part[2 * q + 1]
    zs = bufs["nz"]
    z = place.at["z"]
    zs[z] = acc
    ds_ = []
    for k in range(1, n_z):
        d = pltpu.make_async_remote_copy(src_ref=zs.at[z], dst_ref=zs.at[z], send_sem=ns.at[2 + k], recv_sem=nr.at[2 + k], device_id=place.along_z(k), device_id_type=MESH)
        d.start(); ds_.append(d)
    for d in ds_: d.wait()
    total = zs[0]
    for k in range(1, n_z): total = total + zs[k]
    norm_out[...] = total

def scatter_all(grads, plan, n_z):
    plan, count = number(plan)
    n_w = len(grads)
    R = max(p[2][1] for st in plan for p in st); W = max(p[3][1] for st in plan for p in st)
    bf = jnp.bfloat16
    hbm = {"r0": (count, 2, n_z, 2, R, W), "r1": (count, 2, n_z, R, W), "r1y": (count, n_z, 2, R, W), "r2": (count, n_z, R, W), "r3": (count, n_z - 1, R, W)}
    vm = {"s0": ((2 * SLOTS, 2, n_z, 2, R, W), bf), "t0": ((2, 2, n_z, 2, R, W), bf), "s1": ((SLOTS, 2, n_z, R, W), bf), "s1y": ((SLOTS, n_z, 2, R, W), bf),
          "t1": ((2, n_z, R, W), bf), "t1y": ((n_z, 2, R, W), bf), "s2": ((2 * SLOTS, n_z, R, W), bf), "t2": ((2, n_z, R, W), bf), "t3": ((2, n_z - 1, R, W), bf),
          "o": ((2 * SLOTS, R, W), jnp.float32), "sq": ((R, W), jnp.float32), "n": ((6, 8, 128), jnp.float32), "nz": ((n_z, 8, 128), jnp.float32)}
    names = list(hbm) + list(vm)
    outs = pl.pallas_call(
        functools.partial(scatter_kernel, n_z, plan, n_w, names),
        out_shape=[jax.ShapeDtypeStruct(g.shape[4:], jnp.float32) for g in grads] + [jax.ShapeDtypeStruct((8, 128), jnp.float32)] + [jax.ShapeDtypeStruct(s, bf) for s in hbm.values()],
        in_specs=[pl.BlockSpec(memory_space=ANY)] * n_w,
        out_specs=[pl.BlockSpec(memory_space=ANY)] * n_w + [pl.BlockSpec(memory_space=pltpu.VMEM)] + [pl.BlockSpec(memory_space=ANY)] * len(hbm),
        scratch_shapes=[pltpu.VMEM(s, d) for s, d in vm.values()] + [pltpu.SemaphoreType.DMA((count * n_sems(n_z),)), pltpu.SemaphoreType.DMA((count * n_sems(n_z),)), pltpu.SemaphoreType.DMA((2 * SLOTS, 3)), pltpu.SemaphoreType.DMA((n_z + 2,)), pltpu.SemaphoreType.DMA((n_z + 2,))],
        name="scatter_grads",
        compiler_params=pltpu.CompilerParams(collective_id=1, has_side_effects=True, vmem_limit_bytes=48 * 2**20),
    )(*grads)
    return outs[:n_w], outs[n_w]

def weight_plan(shapes, width, tiny):
    out = []
    for w, rows, cols in shapes:
        for r in range(0, rows, 48):
            for k in range(0, cols, 2 * width):
                out.append([(w, (r, 48), (k, width), 0), (w, (r, 48), (k + width, width), 1)])
    return out


def plan_with(orders, weights, width, tiny_first):
    stages = [[(w, r, c, orders[o]) for (w, r, c, o) in st] for st in weight_plan(weights, width, None)]
    tiny = [(4, (0, 16), (0, 128), orders[0])]
    return [tiny] + stages if tiny_first else stages + [tiny]


def fits_kernels(n_dp, n_fsdp, shards):
    return n_dp == 4 and n_fsdp % 2 == 0 and all(s.shape[0] % 48 == 0 and s.shape[1] % 1536 == 0 for s in shards)


def layer_norm(values_in, gain):
    mean_row = jnp.mean(values_in, axis=-1, keepdims=True)
    centered = values_in - mean_row
    var_row = jnp.mean(centered * centered, axis=-1, keepdims=True)
    return centered * lax.rsqrt(var_row + norm_eps) * gain


def exact_gelu(values_in):
    return jax.nn.gelu(values_in, approximate=False)


def frame_tables(counts, frame_slots, time_len):
    slot_total = counts.shape[0]
    order = jnp.arange(slot_total, dtype=jnp.int32)
    slot_ends = jnp.sum(jnp.where(order[None, :] <= order[:, None], counts[None, :], 0), axis=1)
    slot_starts = slot_ends - counts
    frame_ids = jnp.arange(frame_slots, dtype=jnp.int32)
    frame_owner = jnp.sum((frame_ids[:, None] >= slot_ends[None, :]).astype(jnp.int32), axis=1)
    slot_ids = jnp.arange(slot_total, dtype=jnp.int32)
    start_of = jnp.sum(
        jnp.where(frame_owner[:, None] == slot_ids[None, :], slot_starts[None, :], 0), axis=1
    )
    time_index = frame_ids - start_of
    live_frame = frame_owner < slot_total
    time_ids = jnp.arange(time_len, dtype=jnp.int32)
    time_hot = ((time_index[:, None] == time_ids[None, :]) & live_frame[:, None]).astype(
        jnp.float32
    )
    return (frame_owner, time_hot)


def gather_params(part_qkv, part_out, part_up, part_down, part_time, part_gains):
    inner_part = (
        lax.all_gather(part_qkv, "fsdp", axis=0, tiled=True),
        lax.all_gather(part_out, "fsdp", axis=0, tiled=True),
        lax.all_gather(part_up, "fsdp", axis=0, tiled=True),
        lax.all_gather(part_down, "fsdp", axis=0, tiled=True),
        lax.all_gather(part_time, "fsdp", axis=0, tiled=True),
        lax.all_gather(part_gains, "fsdp", axis=0, tiled=True),
    )
    return (
        lax.all_gather(inner_part[0], "dp", axis=0, tiled=True),
        lax.all_gather(inner_part[1], "dp", axis=0, tiled=True),
        lax.all_gather(inner_part[2], "dp", axis=0, tiled=True),
        lax.all_gather(inner_part[3], "dp", axis=0, tiled=True),
        lax.all_gather(inner_part[4], "dp", axis=0, tiled=True),
        lax.all_gather(inner_part[5], "dp", axis=0, tiled=True),
    )


def reduce_grads(grad_qkv, grad_out, grad_up, grad_down, grad_time, grad_gains):
    outer_part = (
        lax.psum_scatter(
            grad_qkv.astype(jnp.bfloat16), "dp", scatter_dimension=0, tiled=True
        ).astype(jnp.float32),
        lax.psum_scatter(
            grad_out.astype(jnp.bfloat16), "dp", scatter_dimension=0, tiled=True
        ).astype(jnp.float32),
        lax.psum_scatter(
            grad_up.astype(jnp.bfloat16), "dp", scatter_dimension=0, tiled=True
        ).astype(jnp.float32),
        lax.psum_scatter(
            grad_down.astype(jnp.bfloat16), "dp", scatter_dimension=0, tiled=True
        ).astype(jnp.float32),
        lax.psum_scatter(
            grad_time.astype(jnp.bfloat16), "dp", scatter_dimension=0, tiled=True
        ).astype(jnp.float32),
        lax.psum_scatter(
            grad_gains.astype(jnp.bfloat16), "dp", scatter_dimension=0, tiled=True
        ).astype(jnp.float32),
    )
    return (
        lax.psum_scatter(
            outer_part[0].astype(jnp.bfloat16), "fsdp", scatter_dimension=0, tiled=True
        ).astype(jnp.float32),
        lax.psum_scatter(
            outer_part[1].astype(jnp.bfloat16), "fsdp", scatter_dimension=0, tiled=True
        ).astype(jnp.float32),
        lax.psum_scatter(
            outer_part[2].astype(jnp.bfloat16), "fsdp", scatter_dimension=0, tiled=True
        ).astype(jnp.float32),
        lax.psum_scatter(
            outer_part[3].astype(jnp.bfloat16), "fsdp", scatter_dimension=0, tiled=True
        ).astype(jnp.float32),
        lax.psum_scatter(
            outer_part[4].astype(jnp.bfloat16), "fsdp", scatter_dimension=0, tiled=True
        ).astype(jnp.float32),
        lax.psum_scatter(
            outer_part[5].astype(jnp.bfloat16), "fsdp", scatter_dimension=0, tiled=True
        ).astype(jnp.float32),
    )


def masked_scores(q_heads, k_heads, allowed, score_scale):
    scores = (
        jnp.einsum("qhe,khe->hqk", q_heads, k_heads, preferred_element_type=jnp.float32)
        * score_scale
    )
    return jnp.where(allowed[None, :, :], scores, -1e30)


def adamw_step(weight, first, second, grad, factor, rate):
    clipped = grad * factor
    first_new = beta_one * first + (1.0 - beta_one) * clipped
    second_new = beta_two * second + (1.0 - beta_two) * clipped * clipped
    first_hat = first_new / (1.0 - beta_one**STEP)
    second_hat = second_new / (1.0 - beta_two**STEP)
    weight_new = weight - rate * (
        first_hat / (jnp.sqrt(second_hat) + adam_eps) + decay_rate * weight
    )
    return (weight_new, first_new, second_new)


def on_device(
    latents,
    media,
    frame_counts,
    cotangent,
    w_qkv,
    m_qkv,
    v_qkv,
    w_out,
    m_out,
    v_out,
    w_up,
    m_up,
    v_up,
    w_down,
    m_down,
    v_down,
    time_table,
    m_time,
    v_time,
    gains,
    m_gains,
    v_gains,
):
    low_qkv = w_qkv.astype(jnp.bfloat16)
    low_out = w_out.astype(jnp.bfloat16)
    low_up = w_up.astype(jnp.bfloat16)
    low_down = w_down.astype(jnp.bfloat16)
    low_time = time_table.astype(jnp.bfloat16)
    low_gains = gains.astype(jnp.bfloat16)
    n_dp, n_fsdp = lax.axis_size("dp"), lax.axis_size("fsdp")
    own_rows, model = w_qkv.shape[0], w_qkv.shape[2]
    shards = [low_qkv.reshape(own_rows, -1), low_out, low_up, low_down]
    kernels = fits_kernels(n_dp, n_fsdp, shards)
    if kernels:
        n_z = n_fsdp // 2
        listed = [(w, shards[w].shape[0], shards[w].shape[1]) for w in range(4)]
        time_len = low_time.shape[1]
        tiny = jnp.concatenate([low_time.T, low_gains.T], axis=0)
        tiny = jnp.pad(tiny, ((0, 16 - tiny.shape[0]), (0, 128 - own_rows)))
        full = gather_all(shards + [tiny], plan_with((ZYX, ZXY), listed, 768, True), n_z)
        full_qkv, full_out, full_up, full_down = (f.reshape(-1, f.shape[-1]) for f in full[:4])
        full_qkv = full_qkv.reshape(model, 3, model)
        tiny_all = full[4].reshape(n_dp * n_fsdp, 16, 128)[:, :, :own_rows].transpose(1, 0, 2).reshape(16, model)
        full_time, full_gains = tiny_all[:time_len].T, tiny_all[time_len : time_len + 3].T
    else:
        full_qkv, full_out, full_up, full_down, full_time, full_gains = gather_params(
            low_qkv, low_out, low_up, low_down, low_time, low_gains
        )
    item_slots, lat_count, model_width = latents.shape
    frame_slots, patch_rows, unused_width = media.shape
    queries_n = item_slots * lat_count
    media_rows = frame_slots * patch_rows
    head_size = model_width // HEADS
    score_scale = 1.0 / head_size**0.5
    frame_owner, time_hot = frame_tables(frame_counts, frame_slots, full_time.shape[1])
    time_f32 = full_time.astype(jnp.float32)
    gains_f32 = full_gains.astype(jnp.float32)
    frame_time = jnp.dot(time_hot, time_f32.T, precision=highest)
    mixed = media.astype(jnp.float32) + frame_time[:, None, :]
    media_norm, media_back = jax.vjp(layer_norm, mixed, gains_f32[:, 0])
    media_low = media_norm.astype(jnp.bfloat16).reshape(media_rows, model_width)
    lat_rows = latents.reshape(queries_n, model_width).astype(jnp.float32)
    lat_norm, lat_back = jax.vjp(layer_norm, lat_rows, gains_f32[:, 1])
    lat_low = lat_norm.astype(jnp.bfloat16)
    keys_in = jnp.concatenate([media_low, lat_low], axis=0)
    key_rows = keys_in.shape[0]
    qkv_flat = full_qkv.reshape(model_width, 3 * model_width)
    queries = jnp.dot(
        lat_low, qkv_flat[:, :model_width], preferred_element_type=jnp.float32
    ).astype(jnp.bfloat16)
    key_value = jnp.dot(
        keys_in, qkv_flat[:, model_width:], preferred_element_type=jnp.float32
    ).astype(jnp.bfloat16)
    q_heads = queries.reshape(queries_n, HEADS, head_size)
    k_heads = key_value[:, :model_width].reshape(key_rows, HEADS, head_size)
    v_heads = key_value[:, model_width:].reshape(key_rows, HEADS, head_size)
    query_owner = jnp.arange(queries_n, dtype=jnp.int32) // lat_count
    key_owner = jnp.concatenate([jnp.repeat(frame_owner, patch_rows), query_owner], axis=0)
    allowed = query_owner[:, None] == key_owner[None, :]
    scores = masked_scores(q_heads, k_heads, allowed, score_scale)
    row_top = jnp.max(scores, axis=-1, keepdims=True)
    row_total = jnp.sum(jnp.exp(scores - row_top), axis=-1, keepdims=True)
    log_total = row_top + jnp.log(row_total)
    probs_low = jnp.exp(scores - log_total).astype(jnp.bfloat16)
    attended = jnp.einsum("hqk,khe->qhe", probs_low, v_heads, preferred_element_type=jnp.float32)
    attended = attended.reshape(queries_n, model_width).astype(jnp.bfloat16)
    middle = lat_rows + jnp.dot(attended, full_out, preferred_element_type=jnp.float32)
    hidden, ffn_back = jax.vjp(layer_norm, middle, gains_f32[:, 2])
    hidden_low = hidden.astype(jnp.bfloat16)
    pre_act = jnp.dot(hidden_low, full_up, preferred_element_type=jnp.float32)
    activated, gelu_back = jax.vjp(exact_gelu, pre_act)
    act_low = activated.astype(jnp.bfloat16)
    result = middle + jnp.dot(act_low, full_down, preferred_element_type=jnp.float32)
    new_latents = result.astype(jnp.bfloat16).reshape(item_slots, lat_count, model_width)
    d_result = cotangent.reshape(queries_n, model_width)
    g_down = jnp.einsum("qf,qd->fd", act_low, d_result, preferred_element_type=jnp.float32)
    d_act = jnp.einsum("qd,fd->qf", d_result, full_down, preferred_element_type=jnp.float32)
    d_pre = gelu_back(d_act)[0].astype(jnp.bfloat16)
    g_up = jnp.einsum("qd,qf->df", hidden_low, d_pre, preferred_element_type=jnp.float32)
    d_hidden = jnp.einsum("qf,df->qd", d_pre, full_up, preferred_element_type=jnp.float32)
    d_middle_ln, g_gain_ffn = ffn_back(d_hidden)
    d_middle = d_result.astype(jnp.float32) + d_middle_ln
    d_branch = d_middle.astype(jnp.bfloat16)
    g_out = jnp.einsum("qe,qd->ed", attended, d_branch, preferred_element_type=jnp.float32)
    d_attended = jnp.einsum(
        "qd,ed->qe", d_branch, full_out, preferred_element_type=jnp.float32
    ).astype(jnp.bfloat16)
    scores_again = masked_scores(q_heads, k_heads, allowed, score_scale)
    probs = jnp.exp(scores_again - log_total)
    probs_again = probs.astype(jnp.bfloat16)
    d_att_heads = d_attended.reshape(queries_n, HEADS, head_size)
    d_probs = jnp.einsum("qhe,khe->hqk", d_att_heads, v_heads, preferred_element_type=jnp.float32)
    row_dot = jnp.sum(probs * d_probs, axis=-1, keepdims=True)
    d_scores = (probs * (d_probs - row_dot)).astype(jnp.bfloat16)
    d_queries = (
        (
            jnp.einsum("hqk,khe->qhe", d_scores, k_heads, preferred_element_type=jnp.float32)
            * score_scale
        )
        .reshape(queries_n, model_width)
        .astype(jnp.bfloat16)
    )
    d_keys = (
        (
            jnp.einsum("hqk,qhe->khe", d_scores, q_heads, preferred_element_type=jnp.float32)
            * score_scale
        )
        .reshape(key_rows, model_width)
        .astype(jnp.bfloat16)
    )
    d_values = (
        jnp.einsum("hqk,qhe->khe", probs_again, d_att_heads, preferred_element_type=jnp.float32)
        .reshape(key_rows, model_width)
        .astype(jnp.bfloat16)
    )
    g_query = jnp.einsum("qd,qe->de", lat_low, d_queries, preferred_element_type=jnp.float32)
    d_key_value = jnp.concatenate([d_keys, d_values], axis=1)
    g_key_value = jnp.einsum("kd,kx->dx", keys_in, d_key_value, preferred_element_type=jnp.float32)
    g_qkv = jnp.concatenate([g_query, g_key_value], axis=1).reshape(model_width, 3, model_width)
    back_flat = full_qkv.reshape(model_width, 3 * model_width)
    d_keys_in = jnp.einsum(
        "kx,dx->kd", d_key_value, back_flat[:, model_width:], preferred_element_type=jnp.float32
    )
    d_lat_norm = (
        jnp.einsum(
            "qe,de->qd", d_queries, back_flat[:, :model_width], preferred_element_type=jnp.float32
        )
        + d_keys_in[media_rows:]
    )
    d_lat_ln, g_gain_lat = lat_back(d_lat_norm)
    d_latents = (d_middle + d_lat_ln).reshape(item_slots, lat_count, model_width)
    d_mixed, g_gain_media = media_back(
        d_keys_in[:media_rows].reshape(frame_slots, patch_rows, model_width)
    )
    frame_grad = jnp.sum(d_mixed, axis=1)
    g_time = jnp.einsum("fd,ft->dt", frame_grad, time_hot, precision=highest)
    g_gains = jnp.stack([g_gain_media, g_gain_lat, g_gain_ffn], axis=1)
    if kernels:
        def blocks(g, rows):
            return g.astype(jnp.bfloat16).reshape(2, 2, n_z, 2, rows, -1)

        tiny_g = jnp.concatenate([g_time, g_gains], axis=1).T.reshape(time_len + 3, -1, own_rows).transpose(1, 0, 2)
        tiny_g = jnp.pad(tiny_g, ((0, 0), (0, 16 - tiny_g.shape[1]), (0, 128 - own_rows)))
        grads = [blocks(g, s.shape[0]) for g, s in zip((g_qkv, g_out, g_up, g_down), shards)] + [blocks(tiny_g, 16)]
        orders = (("x", "y", "z"), ("y", "x", "z"))
        own, squares = scatter_all(grads, plan_with(orders, listed[::-1], 768, False), n_z)
        own_tiny = own[4][: time_len + 3, :own_rows].T
        reduced = (own[0].reshape(w_qkv.shape), own[1], own[2], own[3], own_tiny[:, :time_len], own_tiny[:, time_len:])
        grad_norm = jnp.sqrt(jnp.sum(squares))
    else:
        reduced = reduce_grads(g_qkv, g_out, g_up, g_down, g_time, g_gains)
        local_sq = jnp.zeros((), jnp.float32)
        for grad in reduced:
            local_sq = local_sq + jnp.sum(grad * grad)
        grad_norm = jnp.sqrt(lax.psum(local_sq, ("dp", "fsdp")))
    factor = jnp.minimum(1.0, clip_limit / (grad_norm + 1e-06))
    masters = (w_qkv, w_out, w_up, w_down, time_table, gains)
    firsts = (m_qkv, m_out, m_up, m_down, m_time, m_gains)
    seconds = (v_qkv, v_out, v_up, v_down, v_time, v_gains)
    rates = (0.02, 0.1, 0.02, 0.01, 0.2, 0.5)
    updated = []
    for index in range(6):
        updated.extend(
            adamw_step(
                masters[index], firsts[index], seconds[index], reduced[index], factor, rates[index]
            )
        )
    return (
        new_latents,
        d_latents,
        grad_norm,
        updated[0],
        updated[1],
        updated[2],
        updated[3],
        updated[4],
        updated[5],
        updated[6],
        updated[7],
        updated[8],
        updated[9],
        updated[10],
        updated[11],
        updated[12],
        updated[13],
        updated[14],
        updated[15],
        updated[16],
        updated[17],
    )


def solution(mesh):
    placed = (
        P(("dp", "fsdp"), None, None),
        P(("dp", "fsdp"), None, None),
        P(("dp", "fsdp")),
        P(("dp", "fsdp"), None, None),
        P(("dp", "fsdp"), None, None),
        P(("dp", "fsdp"), None, None),
        P(("dp", "fsdp"), None, None),
        P(("dp", "fsdp"), None),
        P(("dp", "fsdp"), None),
        P(("dp", "fsdp"), None),
        P(("dp", "fsdp"), None),
        P(("dp", "fsdp"), None),
        P(("dp", "fsdp"), None),
        P(("dp", "fsdp"), None),
        P(("dp", "fsdp"), None),
        P(("dp", "fsdp"), None),
        P(("dp", "fsdp"), None),
        P(("dp", "fsdp"), None),
        P(("dp", "fsdp"), None),
        P(("dp", "fsdp"), None),
        P(("dp", "fsdp"), None),
        P(("dp", "fsdp"), None),
    )
    return jax.shard_map(
        on_device,
        mesh=mesh,
        in_specs=placed,
        out_specs=(
            P(("dp", "fsdp"), None, None),
            P(("dp", "fsdp"), None, None),
            P(),
            P(("dp", "fsdp"), None, None),
            P(("dp", "fsdp"), None, None),
            P(("dp", "fsdp"), None, None),
            P(("dp", "fsdp"), None),
            P(("dp", "fsdp"), None),
            P(("dp", "fsdp"), None),
            P(("dp", "fsdp"), None),
            P(("dp", "fsdp"), None),
            P(("dp", "fsdp"), None),
            P(("dp", "fsdp"), None),
            P(("dp", "fsdp"), None),
            P(("dp", "fsdp"), None),
            P(("dp", "fsdp"), None),
            P(("dp", "fsdp"), None),
            P(("dp", "fsdp"), None),
            P(("dp", "fsdp"), None),
            P(("dp", "fsdp"), None),
            P(("dp", "fsdp"), None),
        ),
        check_vma=False,
    )
```

```python
import functools
import math

import jax
import jax.numpy as jnp
from jax import lax
from jax.experimental import pallas as pl
from jax.experimental.pallas import tpu as pltpu
from jax.sharding import PartitionSpec as P

HEADS = 16
STEP = 10


highest = lax.Precision.HIGHEST
norm_eps = 1e-05
clip_limit = 1.0
beta_one = 0.9
beta_two = 0.999
adam_eps = 1e-08
decay_rate = 0.1

MESH=pl.DeviceIdType.MESH
ANY=pl.ANY

class Place:
    def __init__(self, n_z):
        dp = lax.axis_index("dp"); fs = lax.axis_index("fsdp")
        self.n_z = n_z
        self.at = {"x": dp // 2, "c": dp % 2, "z": fs // 2, "y": fs % 2}
    def dev(self, **new):
        p = {**self.at, **new}
        return (p["x"] * 2 + p["c"], p["z"] * 2 + p["y"])
    def other(self, ax):
        return self.dev(**{ax: 1 - self.at[ax]})
    def along_z(self, k):
        return self.dev(z=(self.at["z"] + k) % self.n_z)
    def partners(self):
        return [self.other(a) for a in "cxy"] + [self.along_z(k) for k in range(1, self.n_z)]

def greet(place):
    bar = pltpu.get_barrier_semaphore()
    others = place.partners()
    for d in others:
        pl.semaphore_signal(bar, inc=1, device_id=d, device_id_type=MESH)
    pl.semaphore_wait(bar, len(others))

def block_index(place, held):
    return tuple(slice(None) if ax in held else place.at[ax] for ax in "xczy")

class Gather:
    def __init__(self, place, src, dst, rows, cols, order, sems, base):
        self.place, self.src, self.dst = place, src, dst
        self.sl = (pl.ds(*rows), pl.ds(*cols))
        self.order, self.sems, self.base = order, sems, base
        self.copies = {}
    def region(self, held):
        return self.dst.at[block_index(self.place, held) + self.sl]
    def start(self, step):
        p = self.place; ax = self.order[step]; held = self.order[:step]
        ss, rs = self.sems
        made = []
        n = self.base
        for s in range(step):
            n += p.n_z - 1 if self.order[s] == "z" else 1
        src = self.src.at[self.sl] if step == 0 else self.region(held)
        dst = self.region(held)
        for k in (range(1, p.n_z) if ax == "z" else (0,)):
            to = p.along_z(k) if ax == "z" else p.other(ax)
            d = pltpu.make_async_remote_copy(src_ref=src, dst_ref=dst, send_sem=ss.at[n], recv_sem=rs.at[n], device_id=to, device_id_type=MESH)
            d.start(); made.append(d); n += 1
        self.copies[step] = made
    def arrive(self, step):
        for d in self.copies[step]: d.wait_recv()
    def finish(self):
        for made in self.copies.values():
            for d in made: d.wait_send()

def n_sems(n_z): return n_z + 2

def number(plan):
    j, out = 0, []
    for stage in plan:
        new = []
        for piece in stage:
            new.append((j,) + piece); j += 1
        out.append(new)
    return out, j

ZYX, ZXY = ("z", "y", "x", "c"), ("z", "x", "y", "c")

SLOTS = 3

class Scatter:
    def __init__(self, place, src, out, rows, cols, order, piece, part, turn, sems, bufs):
        self.p, self.src, self.out = place, src, out
        self.rows, self.cols = pl.ds(*rows), pl.ds(*cols)
        self.shape = (rows[1], cols[1])
        self.order, self.piece = order, piece
        self.ss, self.rs, self.ls = sems
        self.part, self.slot, self.b = part, (turn % SLOTS) * 2 + part, bufs
        self.sent = {}
    def v(self, ref, *lead):
        return ref.at[lead + (pl.ds(0, self.shape[0]), pl.ds(0, self.shape[1]))]
    def send(self, src, dst, to, n):
        n += self.piece * n_sems(self.p.n_z)
        d = pltpu.make_async_remote_copy(src_ref=src, dst_ref=dst, send_sem=self.ss.at[n], recv_sem=self.rs.at[n], device_id=to, device_id_type=MESH)
        d.start()
        return d
    def copy(self, src, dst, k):
        d = pltpu.make_async_copy(src, dst, self.ls.at[self.slot, k])
        d.start()
        return d
    def add(self, count, dst, a, b):
        r, w = self.shape
        def one(i, carry):
            (da, di), (aa, ai), (ba, bi) = dst(i), a(i), b(i)
            da[di + (slice(0, r), slice(0, w))] = aa[ai + (slice(0, r), slice(0, w))] + ba[bi + (slice(0, r), slice(0, w))]
            return carry
        lax.fori_loop(0, count, one, 0)
    def free(self, step):
        if step in self.sent:
            for d in self.sent.pop(step): d.wait_send() if step < 4 else d.wait()
    def step0(self):
        p = self.p; c = p.at["c"]; A = slice(None)
        self.sent[0] = [self.send(self.src.at[:, 1 - c, :, :, self.rows, self.cols], self.v(self.b["r0"], self.piece, A, A, A), p.other("c"), 0)]
        self.mine = self.copy(self.src.at[:, c, :, :, self.rows, self.cols], self.v(self.b["s0"], self.slot, A, A, A), 0)
        self.came = self.sent[0]
    def step1(self):
        p = self.p; A = slice(None); nz = p.n_z; b = self.b; sl, pt = self.slot, self.part
        for d in self.came: d.wait_recv()
        got = self.copy(self.v(b["r0"], self.piece, A, A, A), self.v(b["t0"], pt, A, A, A), 1)
        self.mine.wait(); got.wait()
        at = lambda i: (i // (nz * 2), (i // 2) % nz, i % 2)
        self.add(4 * nz, lambda i: (b["s0"], (sl,) + at(i)), lambda i: (b["s0"], (sl,) + at(i)), lambda i: (b["t0"], (pt,) + at(i)))
        ax = self.order[0]; o = 1 - p.at[ax]
        src = self.v(b["s0"], sl, o, A, A) if ax == "x" else self.v(b["s0"], sl, A, A, o)
        dst = self.v(b["r1"], self.piece, A, A)
        if ax == "x":
            dst = self.v(b["r1y"], self.piece, A, A)
        self.sent[1] = self.came = [self.send(src, dst, p.other(ax), 1)]
    def step2(self):
        p = self.p; A = slice(None); nz = p.n_z; b = self.b; sl, pt = self.slot, self.part
        for d in self.came: d.wait_recv()
        ax = self.order[0]; m = p.at[ax]; o = 1 - p.at[self.order[1]]
        if ax == "x":
            got = self.copy(self.v(b["r1y"], self.piece, A, A), self.v(b["t1y"], A, A), 1); got.wait()
            at = lambda i: (i // 2, i % 2)
            self.add(2 * nz, lambda i: (b["s1y"], (sl // 2,) + at(i)), lambda i: (b["s0"], (sl, m) + at(i)), lambda i: (b["t1y"], at(i)))
            src = self.v(b["s1y"], sl // 2, A, o)
        else:
            got = self.copy(self.v(b["r1"], self.piece, A, A), self.v(b["t1"], A, A), 1); got.wait()
            at = lambda i: (i // nz, i % nz)
            self.add(2 * nz, lambda i: (b["s1"], (sl // 2,) + at(i)), lambda i: (b["s0"], (sl,) + at(i) + (m,)), lambda i: (b["t1"], at(i)))
            src = self.v(b["s1"], sl // 2, o, A)
        self.sent[2] = self.came = [self.send(src, self.v(b["r2"], self.piece, A), p.other(self.order[1]), 2)]
    def step3(self):
        p = self.p; A = slice(None); nz = p.n_z; b = self.b; sl, pt = self.slot, self.part
        for d in self.came: d.wait_recv()
        got = self.copy(self.v(b["r2"], self.piece, A), self.v(b["t2"], pt, A), 1); got.wait()
        m = p.at[self.order[1]]
        mine = (lambda i: (b["s1y"], (sl // 2, i, m))) if self.order[0] == "x" else (lambda i: (b["s1"], (sl // 2, m, i)))
        self.add(nz, lambda i: (b["s2"], (sl, i)), mine, lambda i: (b["t2"], (pt, i)))
        self.sent[3] = self.came = [
            self.send(self.v(b["s2"], sl, (p.at["z"] + k) % nz), self.v(b["r3"], self.piece, k - 1), p.along_z(k), 2 + k)
            for k in range(1, nz)]
    def step4(self):
        p = self.p; A = slice(None); nz = p.n_z; b = self.b; sl, pt = self.slot, self.part
        r, w = self.shape
        for d in self.came: d.wait_recv()
        got = self.copy(self.v(b["r3"], self.piece, A), self.v(b["t3"], pt, A), 1); got.wait()
        total = b["s2"][sl, p.at["z"], 0:r, 0:w].astype(jnp.float32)
        for k in range(nz - 1):
            total = total + b["t3"][pt, k, 0:r, 0:w].astype(jnp.float32)
        b["o"][sl, 0:r, 0:w] = total
        b["sq"][0:r, 0:w] += total * total
        self.sent[4] = [self.copy(self.v(b["o"], sl), self.out.at[self.rows, self.cols], 2)]

def scatter_kernel(n_z, plan, n_w, names, *refs):
    ins, outs = refs[:n_w], refs[n_w:2 * n_w]
    norm_out = refs[2 * n_w]
    rest = refs[2 * n_w + 1:]
    bufs = dict(zip(names, rest))
    ss, rs, ls, ns, nr = rest[len(names):]
    place = Place(n_z)
    greet(place)
    bufs["sq"][...] = jnp.zeros_like(bufs["sq"])
    stages = [[Scatter(place, ins[w], outs[w], rows, cols, order, j, part, t, (ss, rs, ls), bufs) for part, (j, w, rows, cols, order) in enumerate(stage)] for t, stage in enumerate(plan)]
    T = len(stages)
    for t in range(T + 4):
        for back in range(5):
            u = t - back
            if not 0 <= u < T: continue
            if u >= SLOTS:
                for g in stages[u - SLOTS]:
                    if back == 0: g.free(1)
                    else: g.free(back)
            for g in stages[u]: getattr(g, f"step{back}")()
    for st in stages:
        for g in st:
            for k in range(5): g.free(k)
    sq = bufs["sq"]
    part = bufs["n"]
    acc = jnp.zeros((8, 128), jnp.float32)
    for i in range(sq.shape[0] // 8):
        for j in range(sq.shape[1] // 128):
            acc = acc + sq[i * 8:(i + 1) * 8, j * 128:(j + 1) * 128]
    for q, ax in enumerate("cxy"):
        part[2 * q] = acc
        d = pltpu.make_async_remote_copy(src_ref=part.at[2 * q], dst_ref=part.at[2 * q + 1], send_sem=ns.at[q], recv_sem=nr.at[q], device_id=place.other(ax), device_id_type=MESH)
        d.start(); d.wait()
        acc = part[2 * q] + part[2 * q + 1]
    zs = bufs["nz"]
    z = place.at["z"]
    zs[z] = acc
    ds_ = []
    for k in range(1, n_z):
        d = pltpu.make_async_remote_copy(src_ref=zs.at[z], dst_ref=zs.at[z], send_sem=ns.at[2 + k], recv_sem=nr.at[2 + k], device_id=place.along_z(k), device_id_type=MESH)
        d.start(); ds_.append(d)
    for d in ds_: d.wait()
    total = zs[0]
    for k in range(1, n_z): total = total + zs[k]
    norm_out[...] = total

def scatter_all(grads, plan, n_z):
    plan, count = number(plan)
    n_w = len(grads)
    R = max(p[2][1] for st in plan for p in st); W = max(p[3][1] for st in plan for p in st)
    bf = jnp.bfloat16
    hbm = {"r0": (count, 2, n_z, 2, R, W), "r1": (count, 2, n_z, R, W), "r1y": (count, n_z, 2, R, W), "r2": (count, n_z, R, W), "r3": (count, n_z - 1, R, W)}
    vm = {"s0": ((2 * SLOTS, 2, n_z, 2, R, W), bf), "t0": ((2, 2, n_z, 2, R, W), bf), "s1": ((SLOTS, 2, n_z, R, W), bf), "s1y": ((SLOTS, n_z, 2, R, W), bf),
          "t1": ((2, n_z, R, W), bf), "t1y": ((n_z, 2, R, W), bf), "s2": ((2 * SLOTS, n_z, R, W), bf), "t2": ((2, n_z, R, W), bf), "t3": ((2, n_z - 1, R, W), bf),
          "o": ((2 * SLOTS, R, W), jnp.float32), "sq": ((R, W), jnp.float32), "n": ((6, 8, 128), jnp.float32), "nz": ((n_z, 8, 128), jnp.float32)}
    names = list(hbm) + list(vm)
    outs = pl.pallas_call(
        functools.partial(scatter_kernel, n_z, plan, n_w, names),
        out_shape=[jax.ShapeDtypeStruct(g.shape[4:], jnp.float32) for g in grads] + [jax.ShapeDtypeStruct((8, 128), jnp.float32)] + [jax.ShapeDtypeStruct(s, bf) for s in hbm.values()],
        in_specs=[pl.BlockSpec(memory_space=ANY)] * n_w,
        out_specs=[pl.BlockSpec(memory_space=ANY)] * n_w + [pl.BlockSpec(memory_space=pltpu.VMEM)] + [pl.BlockSpec(memory_space=ANY)] * len(hbm),
        scratch_shapes=[pltpu.VMEM(s, d) for s, d in vm.values()] + [pltpu.SemaphoreType.DMA((count * n_sems(n_z),)), pltpu.SemaphoreType.DMA((count * n_sems(n_z),)), pltpu.SemaphoreType.DMA((2 * SLOTS, 3)), pltpu.SemaphoreType.DMA((n_z + 2,)), pltpu.SemaphoreType.DMA((n_z + 2,))],
        name="scatter_grads",
        compiler_params=pltpu.CompilerParams(collective_id=1, has_side_effects=True, vmem_limit_bytes=48 * 2**20),
    )(*grads)
    return outs[:n_w], outs[n_w]

def weight_plan(shapes, width, tiny):
    out = []
    for w, rows, cols in shapes:
        for r in range(0, rows, 48):
            for k in range(0, cols, 2 * width):
                out.append([(w, (r, 48), (k, width), 0), (w, (r, 48), (k + width, width), 1)])
    return out


def plan_with(orders, weights, width, tiny_first):
    stages = [[(w, r, c, orders[o]) for (w, r, c, o) in st] for st in weight_plan(weights, width, None)]
    tiny = [(4, (0, 16), (0, 128), orders[0])]
    return [tiny] + stages if tiny_first else stages + [tiny]


def fits_kernels(n_dp, n_fsdp, shards):
    return n_dp == 4 and n_fsdp % 2 == 0 and all(s.shape[0] % 48 == 0 and s.shape[1] % 1536 == 0 for s in shards)


def out_copies(pairs, sems, at, running):
    for src, dst in pairs:
        d = pltpu.make_async_copy(src, dst, sems.at[len(running)])
        d.start()
        running.append(d)


def dot(a, b, contract=((1,), (0,))):
    return lax.dot_general(a, b, (contract, ((), ())), preferred_element_type=jnp.float32)


def head_windows(head):
    group = 128 // math.gcd(head, 128)
    out = []
    for j in range(group):
        first, last = j * head // 128, ((j + 1) * head - 1) // 128
        out.append((first, last + 1, j * head - first * 128))
    return out, group * head


def lanes_of(rows, tiles, start, head):
    lane = lax.broadcasted_iota(jnp.int32, (rows, tiles * 128), 1)
    return (lane >= start) & (lane < start + head)


def normed(rows_in, gain):
    centered = rows_in - jnp.mean(rows_in, axis=-1, keepdims=True)
    var_row = jnp.mean(centered * centered, axis=-1, keepdims=True)
    return centered * lax.rsqrt(var_row + norm_eps) * gain


def forward_kernel(n_z, plan, needs, *refs):
    (sh, (lat, media, cot, hot, bias), full, outs, scratch) = refs[:5], refs[5:10], refs[10:15], refs[15:26], refs[26:]
    o_keys, o_q, o_k, o_v, o_att, o_hid, o_act, o_dpre, o_mid, o_new, o_lse = outs
    keys, q, k, v, att, hid, act, slope, dact, mid, new, tiny, tiny_t, lse, wbuf, wdown, ss, rs, ls, os_, ws = scratch
    f_qkv, f_out, f_up, f_down, f_tiny = full
    place = Place(n_z)
    greet(place)
    queries_n, model = lat.shape
    media_rows = media.shape[0]
    key_rows = media_rows + queries_n
    hidden_n = act.shape[1]
    head = model // HEADS
    windows, group_width = head_windows(head)
    scale = 1.0 / head**0.5
    written = []

    def load(src, dst):
        d = pltpu.make_async_copy(src, dst, ws.at[0])
        d.start()
        d.wait()

    def write(*pairs):
        out_copies(pairs, os_, 0, written)

    def norms():
        load(f_tiny, tiny)
        tiny_t[...] = tiny[...].reshape(model, 128).astype(jnp.float32).T
        keys[media_rows:key_rows, :] = normed(lat[...].astype(jnp.float32), tiny_t[9:10, :]).astype(jnp.bfloat16)

        def frame(i, carry):
            rows = pl.ds(pl.multiple_of(i * 48, 48), 48)
            mixed = media[rows, :].astype(jnp.float32) + dot(hot[rows, :], tiny_t[...].astype(jnp.bfloat16))
            keys[rows, :] = normed(mixed, tiny_t[8:9, :]).astype(jnp.bfloat16)
            return carry

        lax.fori_loop(0, media_rows // 48, frame, 0)
        write((keys, o_keys))

    def project(i, dst, first):
        load(f_qkv.at[:, :, :, :, :, pl.ds(i * model, model)], wbuf)

        def tile(n, carry):
            cols = pl.ds(pl.multiple_of(n * 256, 256), 256)
            w = wbuf[:, :, :, :, :, cols].reshape(model, 256)
            dst[:, cols] = dot(keys[first:key_rows, :], w).astype(jnp.bfloat16)
            return carry

        lax.fori_loop(0, model // 256, tile, 0)

    def project_q():
        project(0, q, media_rows)
        write((q, o_q))

    def project_k():
        project(1, k, 0)
        write((k, o_k))

    def project_v():
        project(2, v, 0)
        write((v, o_v))

    def attend(g):
        base = g * group_width
        tiles = [jnp.zeros((queries_n, 128), jnp.float32) for _ in range(group_width // 128)]
        for j, (t0, t1, start) in enumerate(windows):
            cols = slice(base + t0 * 128, base + t1 * 128)
            qh = q[:, cols]
            qh = jnp.where(lanes_of(queries_n, t1 - t0, start, head), qh, jnp.zeros_like(qh))
            s = dot(k[:, cols], qh, ((1,), (1,))) * scale + bias[...]
            top = jnp.max(s, axis=0, keepdims=True)
            e = jnp.exp(s - top)
            total = jnp.sum(e, axis=0, keepdims=True)
            p = (e * (1.0 / total)).astype(jnp.bfloat16)
            lse[g * len(windows) + j : g * len(windows) + j + 1, :] = top + jnp.log(total)
            vh = v[:, cols]
            vh = jnp.where(lanes_of(key_rows, t1 - t0, start, head), vh, jnp.zeros_like(vh))
            got = dot(p, vh, ((0,), (0,)))
            for t in range(t0, t1):
                tiles[t] = tiles[t] + got[:, (t - t0) * 128 : (t - t0 + 1) * 128]
        for t, tile in enumerate(tiles):
            att[:, base + t * 128 : base + (t + 1) * 128] = tile.astype(jnp.bfloat16)

    def project_out():
        write((att, o_att), (lse, o_lse))
        load(f_out, wbuf)

        def tile(n, carry):
            cols = pl.ds(pl.multiple_of(n * 256, 256), 256)
            w = wbuf[:, :, :, :, :, cols].reshape(model, 256)
            mid[:, cols] = lat[:, cols].astype(jnp.float32) + dot(att[...], w)
            return carry

        lax.fori_loop(0, model // 256, tile, 0)
        hid[...] = normed(mid[...], tiny_t[10:11, :]).astype(jnp.bfloat16)
        write((mid, o_mid), (hid, o_hid))

    def up(i):
        load(f_up.at[:, :, :, :, :, pl.ds(i * model, model)], wbuf)

        def tile(n, carry):
            cols = pl.ds(pl.multiple_of(n * 256, 256), 256)
            into = pl.ds(pl.multiple_of(i * model + n * 256, 256), 256)
            w = wbuf[:, :, :, :, :, cols].reshape(model, 256)
            x = dot(hid[...], w)
            cdf = 0.5 + 0.5 * lax.erf(x * 0.7071067811865476)
            act[:, into] = (x * cdf).astype(jnp.bfloat16)
            slope[:, into] = cdf + x * (jnp.exp(-0.5 * x * x) * 0.3989422804014327)
            return carry

        lax.fori_loop(0, model // 256, tile, 0)
        if (i + 1) * model == hidden_n:
            write((act, o_act))

    def down(i, width):
        cols = slice(i * width, (i + 1) * width)
        load(f_down.at[:, :, :, :, :, pl.ds(i * width, width)], wdown)
        per = hidden_n // 4
        got = jnp.zeros((queries_n, width), jnp.float32)
        for b in range(4):
            w = wdown[b // 2, b % 2].reshape(per, width)
            got = got + dot(act[:, b * per : (b + 1) * per], w)
            back = dot(cot[:, cols], w, ((1,), (1,)))
            if i == 0:
                dact[:, b * per : (b + 1) * per] = back
            else:
                dact[:, b * per : (b + 1) * per] += back
        new[:, cols] = (mid[:, cols] + got).astype(jnp.bfloat16)

    def finish():
        for d in written:
            d.wait()
        written.clear()

        def tile(n, carry):
            cols = pl.ds(pl.multiple_of(n * 512, 512), 512)
            act[:, cols] = (dact[:, cols] * slope[:, cols]).astype(jnp.bfloat16)
            return carry

        lax.fori_loop(0, hidden_n // 512, tile, 0)
        write((act, o_dpre), (new, o_new))
        for d in written:
            d.wait()

    work = [(needs["tiny"], 8, norms), (needs["q"], 4, project_q), (needs["k"], 8, project_k), (needs["v"], 8, project_v)]
    work += [(needs["v"], 7, functools.partial(attend, g)) for g in range(model // group_width)]
    work += [(needs["out"], 5, project_out)]
    work += [(s, 6, functools.partial(up, i)) for i, s in enumerate(needs["up"])]
    work += [(s, 5, functools.partial(down, i, model // len(needs["down"]))) for i, s in enumerate(needs["down"])]
    work += [(needs["down"][-1], 5, finish)]
    locals_ = []
    for i in range(5):
        d = pltpu.make_async_copy(sh[i], full[i].at[block_index(place, ())], ls.at[i])
        d.start()
        locals_.append(d)
    stages = [[Gather(place, sh[w], full[w], rows, cols, order, (ss, rs), j * n_sems(n_z)) for (j, w, rows, cols, order) in stage] for stage in plan]
    waited = set()
    total, steps = len(stages), 4
    for t in range(total + steps):
        for back in range(steps + 1):
            u = t - back
            if not 0 <= u < total:
                continue
            for g, (j, w, *_) in zip(stages[u], plan[u]):
                if back == 1 and w not in waited:
                    locals_[w].wait()
                    waited.add(w)
                if back > 0:
                    g.arrive(back - 1)
                if back < steps:
                    g.start(back)
        room = 14
        while work and work[0][0] <= t - steps and (room > 0 or t == total + steps - 1):
            need, cost, piece = work.pop(0)
            room -= cost
            piece()
    for st in stages:
        for g in st:
            g.finish()


def forward_plan(shards, model):
    two = lambda w, rows, first, width: [(w, (0, rows), (first, width), ZYX), (w, (0, rows), (first + width, width), ZXY)]
    rows, half = shards[1].shape[0], model // 2
    stages, needs = [[(4, (0, rows), (0, 128), ZYX)]], {"tiny": 0}
    for i, name in enumerate("qkv"):
        needs[name] = len(stages)
        stages.append(two(0, rows, i * model, half))
    needs["out"] = len(stages)
    stages.append(two(1, rows, 0, half))
    needs["up"], needs["down"] = [], []
    for i in range(shards[2].shape[1] // model):
        needs["up"].append(len(stages))
        stages.append(two(2, rows, i * model, half))
    for i in range(model // 256):
        needs["down"].append(len(stages))
        stages.append(two(3, shards[3].shape[0], i * 256, 128))
    return stages, needs


def forward_all(shards, lat, media, cot, hot, bias, n_z):
    model, hidden_n = lat.shape[1], shards[2].shape[1]
    stages, needs = forward_plan(shards, model)
    plan, count = number(stages)
    queries_n, media_rows = lat.shape[0], media.shape[0]
    key_rows = queries_n + media_rows
    bf, f32 = jnp.bfloat16, jnp.float32
    rows = shards[1].shape[0]
    made = [((key_rows, model), bf), ((queries_n, model), bf), ((key_rows, model), bf), ((key_rows, model), bf), ((queries_n, model), bf),
            ((queries_n, model), bf), ((queries_n, hidden_n), bf), ((queries_n, hidden_n), bf), ((queries_n, model), f32), ((queries_n, model), bf), ((HEADS, queries_n), f32)]
    vm = made[:7] + [((queries_n, hidden_n), f32), ((queries_n, hidden_n), f32), ((queries_n, model), f32), ((queries_n, model), bf),
                     ((2, 2, n_z, 2, rows, 128), bf), ((128, model), f32), ((HEADS, queries_n), f32), ((2, 2, n_z, 2, rows, model), bf), ((2, 2, n_z, 2, shards[3].shape[0], 256), bf)]
    sem = pltpu.SemaphoreType.DMA
    in_vmem, in_any = pl.BlockSpec(memory_space=pltpu.VMEM), pl.BlockSpec(memory_space=ANY)
    out = pl.pallas_call(
        functools.partial(forward_kernel, n_z, plan, needs),
        out_shape=[jax.ShapeDtypeStruct((2, 2, n_z, 2) + s.shape, s.dtype) for s in shards] + [jax.ShapeDtypeStruct(*m) for m in made],
        in_specs=[in_vmem] * 10,
        out_specs=[in_any] * (5 + len(made)),
        scratch_shapes=[pltpu.VMEM(*m) for m in vm] + [sem((count * n_sems(n_z),)), sem((count * n_sems(n_z),)), sem((5,)), sem((16,)), sem((1,))],
        name="gather_and_forward",
        compiler_params=pltpu.CompilerParams(collective_id=0, has_side_effects=True, vmem_limit_bytes=60 * 2**20),
    )(*shards, lat, media, cot, hot, bias)
    return out[:5], out[5:]


def layer_norm(values_in, gain):
    mean_row = jnp.mean(values_in, axis=-1, keepdims=True)
    centered = values_in - mean_row
    var_row = jnp.mean(centered * centered, axis=-1, keepdims=True)
    return centered * lax.rsqrt(var_row + norm_eps) * gain


def exact_gelu(values_in):
    return jax.nn.gelu(values_in, approximate=False)


def frame_tables(counts, frame_slots, time_len):
    slot_total = counts.shape[0]
    order = jnp.arange(slot_total, dtype=jnp.int32)
    slot_ends = jnp.sum(jnp.where(order[None, :] <= order[:, None], counts[None, :], 0), axis=1)
    slot_starts = slot_ends - counts
    frame_ids = jnp.arange(frame_slots, dtype=jnp.int32)
    frame_owner = jnp.sum((frame_ids[:, None] >= slot_ends[None, :]).astype(jnp.int32), axis=1)
    slot_ids = jnp.arange(slot_total, dtype=jnp.int32)
    start_of = jnp.sum(
        jnp.where(frame_owner[:, None] == slot_ids[None, :], slot_starts[None, :], 0), axis=1
    )
    time_index = frame_ids - start_of
    live_frame = frame_owner < slot_total
    time_ids = jnp.arange(time_len, dtype=jnp.int32)
    time_hot = ((time_index[:, None] == time_ids[None, :]) & live_frame[:, None]).astype(
        jnp.float32
    )
    return (frame_owner, time_hot)


def gather_params(part_qkv, part_out, part_up, part_down, part_time, part_gains):
    inner_part = (
        lax.all_gather(part_qkv, "fsdp", axis=0, tiled=True),
        lax.all_gather(part_out, "fsdp", axis=0, tiled=True),
        lax.all_gather(part_up, "fsdp", axis=0, tiled=True),
        lax.all_gather(part_down, "fsdp", axis=0, tiled=True),
        lax.all_gather(part_time, "fsdp", axis=0, tiled=True),
        lax.all_gather(part_gains, "fsdp", axis=0, tiled=True),
    )
    return (
        lax.all_gather(inner_part[0], "dp", axis=0, tiled=True),
        lax.all_gather(inner_part[1], "dp", axis=0, tiled=True),
        lax.all_gather(inner_part[2], "dp", axis=0, tiled=True),
        lax.all_gather(inner_part[3], "dp", axis=0, tiled=True),
        lax.all_gather(inner_part[4], "dp", axis=0, tiled=True),
        lax.all_gather(inner_part[5], "dp", axis=0, tiled=True),
    )


def reduce_grads(grad_qkv, grad_out, grad_up, grad_down, grad_time, grad_gains):
    outer_part = (
        lax.psum_scatter(
            grad_qkv.astype(jnp.bfloat16), "dp", scatter_dimension=0, tiled=True
        ).astype(jnp.float32),
        lax.psum_scatter(
            grad_out.astype(jnp.bfloat16), "dp", scatter_dimension=0, tiled=True
        ).astype(jnp.float32),
        lax.psum_scatter(
            grad_up.astype(jnp.bfloat16), "dp", scatter_dimension=0, tiled=True
        ).astype(jnp.float32),
        lax.psum_scatter(
            grad_down.astype(jnp.bfloat16), "dp", scatter_dimension=0, tiled=True
        ).astype(jnp.float32),
        lax.psum_scatter(
            grad_time.astype(jnp.bfloat16), "dp", scatter_dimension=0, tiled=True
        ).astype(jnp.float32),
        lax.psum_scatter(
            grad_gains.astype(jnp.bfloat16), "dp", scatter_dimension=0, tiled=True
        ).astype(jnp.float32),
    )
    return (
        lax.psum_scatter(
            outer_part[0].astype(jnp.bfloat16), "fsdp", scatter_dimension=0, tiled=True
        ).astype(jnp.float32),
        lax.psum_scatter(
            outer_part[1].astype(jnp.bfloat16), "fsdp", scatter_dimension=0, tiled=True
        ).astype(jnp.float32),
        lax.psum_scatter(
            outer_part[2].astype(jnp.bfloat16), "fsdp", scatter_dimension=0, tiled=True
        ).astype(jnp.float32),
        lax.psum_scatter(
            outer_part[3].astype(jnp.bfloat16), "fsdp", scatter_dimension=0, tiled=True
        ).astype(jnp.float32),
        lax.psum_scatter(
            outer_part[4].astype(jnp.bfloat16), "fsdp", scatter_dimension=0, tiled=True
        ).astype(jnp.float32),
        lax.psum_scatter(
            outer_part[5].astype(jnp.bfloat16), "fsdp", scatter_dimension=0, tiled=True
        ).astype(jnp.float32),
    )


def masked_scores(q_heads, k_heads, allowed, score_scale):
    scores = (
        jnp.einsum("qhe,khe->hqk", q_heads, k_heads, preferred_element_type=jnp.float32)
        * score_scale
    )
    return jnp.where(allowed[None, :, :], scores, -1e30)


def adamw_step(weight, first, second, grad, factor, rate):
    clipped = grad * factor
    first_new = beta_one * first + (1.0 - beta_one) * clipped
    second_new = beta_two * second + (1.0 - beta_two) * clipped * clipped
    first_hat = first_new / (1.0 - beta_one**STEP)
    second_hat = second_new / (1.0 - beta_two**STEP)
    weight_new = weight - rate * (
        first_hat / (jnp.sqrt(second_hat) + adam_eps) + decay_rate * weight
    )
    return (weight_new, first_new, second_new)


def on_device(
    latents,
    media,
    frame_counts,
    cotangent,
    w_qkv,
    m_qkv,
    v_qkv,
    w_out,
    m_out,
    v_out,
    w_up,
    m_up,
    v_up,
    w_down,
    m_down,
    v_down,
    time_table,
    m_time,
    v_time,
    gains,
    m_gains,
    v_gains,
):
    low_qkv = w_qkv.astype(jnp.bfloat16)
    low_out = w_out.astype(jnp.bfloat16)
    low_up = w_up.astype(jnp.bfloat16)
    low_down = w_down.astype(jnp.bfloat16)
    low_time = time_table.astype(jnp.bfloat16)
    low_gains = gains.astype(jnp.bfloat16)
    n_dp, n_fsdp = lax.axis_size("dp"), lax.axis_size("fsdp")
    own_rows, model = w_qkv.shape[0], w_qkv.shape[2]
    shards = [low_qkv.reshape(own_rows, -1), low_out, low_up, low_down]
    kernels = fits_kernels(n_dp, n_fsdp, shards)
    if not kernels:
        full_qkv, full_out, full_up, full_down, full_time, full_gains = gather_params(
            low_qkv, low_out, low_up, low_down, low_time, low_gains
        )
    item_slots, lat_count, model_width = latents.shape
    frame_slots, patch_rows, unused_width = media.shape
    queries_n = item_slots * lat_count
    media_rows = frame_slots * patch_rows
    head_size = model_width // HEADS
    score_scale = 1.0 / head_size**0.5
    frame_owner, time_hot = frame_tables(frame_counts, frame_slots, low_time.shape[1])
    query_owner = jnp.arange(queries_n, dtype=jnp.int32) // lat_count
    key_owner = jnp.concatenate([jnp.repeat(frame_owner, patch_rows), query_owner], axis=0)
    allowed = query_owner[:, None] == key_owner[None, :]
    lat_flat = latents.reshape(queries_n, model_width)
    lat_rows = lat_flat.astype(jnp.float32)
    key_rows = media_rows + queries_n
    if kernels:
        n_z = n_fsdp // 2
        time_len = low_time.shape[1]
        tiny = jnp.concatenate([low_time, low_gains], axis=1)
        tiny = jnp.pad(tiny, ((0, 0), (0, 128 - tiny.shape[1])))
        hot = jnp.pad(jnp.repeat(time_hot, patch_rows, axis=0), ((0, 0), (0, 128 - time_len))).astype(jnp.bfloat16)
        bias = jnp.where(allowed.T, 0.0, -1e30).astype(jnp.float32)
        full, made = forward_all(
            shards + [tiny], lat_flat, media.reshape(media_rows, model_width), cotangent.reshape(queries_n, model_width), hot, bias, n_z
        )
        full_qkv, full_out, full_up, full_down, full_tiny = (f.reshape(-1, f.shape[-1]) for f in full)
        full_qkv = full_qkv.reshape(model, 3, model)
        full_time, full_gains = full_tiny[:, :time_len], full_tiny[:, time_len : time_len + 3]
        keys_in, queries, keys_all, values_all, attended, hidden_low, act_low, d_pre, middle, new_rows, log_total = made
        log_total = log_total[:, :, None]
    time_f32 = full_time.astype(jnp.float32)
    gains_f32 = full_gains.astype(jnp.float32)
    frame_time = jnp.dot(time_hot, time_f32.T, precision=highest)
    mixed = media.astype(jnp.float32) + frame_time[:, None, :]
    media_norm, media_back = jax.vjp(layer_norm, mixed, gains_f32[:, 0])
    lat_norm, lat_back = jax.vjp(layer_norm, lat_rows, gains_f32[:, 1])
    if not kernels:
        lat_low = lat_norm.astype(jnp.bfloat16)
        media_low = media_norm.astype(jnp.bfloat16).reshape(media_rows, model_width)
        keys_in = jnp.concatenate([media_low, lat_low], axis=0)
        qkv_flat = full_qkv.reshape(model_width, 3 * model_width)
        queries = jnp.dot(lat_low, qkv_flat[:, :model_width], preferred_element_type=jnp.float32).astype(jnp.bfloat16)
        key_value = jnp.dot(keys_in, qkv_flat[:, model_width:], preferred_element_type=jnp.float32).astype(jnp.bfloat16)
        keys_all, values_all = key_value[:, :model_width], key_value[:, model_width:]
    lat_low = keys_in[media_rows:]
    q_heads = queries.reshape(queries_n, HEADS, head_size)
    k_heads = keys_all.reshape(key_rows, HEADS, head_size)
    v_heads = values_all.reshape(key_rows, HEADS, head_size)
    if not kernels:
        scores = masked_scores(q_heads, k_heads, allowed, score_scale)
        row_top = jnp.max(scores, axis=-1, keepdims=True)
        row_total = jnp.sum(jnp.exp(scores - row_top), axis=-1, keepdims=True)
        log_total = row_top + jnp.log(row_total)
        probs_low = jnp.exp(scores - log_total).astype(jnp.bfloat16)
        attended = jnp.einsum("hqk,khe->qhe", probs_low, v_heads, preferred_element_type=jnp.float32)
        attended = attended.reshape(queries_n, model_width).astype(jnp.bfloat16)
        middle = lat_rows + jnp.dot(attended, full_out, preferred_element_type=jnp.float32)
    hidden, ffn_back = jax.vjp(layer_norm, middle, gains_f32[:, 2])
    if not kernels:
        hidden_low = hidden.astype(jnp.bfloat16)
        pre_act = jnp.dot(hidden_low, full_up, preferred_element_type=jnp.float32)
        activated, gelu_back = jax.vjp(exact_gelu, pre_act)
        act_low = activated.astype(jnp.bfloat16)
        new_rows = (middle + jnp.dot(act_low, full_down, preferred_element_type=jnp.float32)).astype(jnp.bfloat16)
    new_latents = new_rows.reshape(item_slots, lat_count, model_width)
    d_result = cotangent.reshape(queries_n, model_width)
    g_down = jnp.einsum("qf,qd->fd", act_low, d_result, preferred_element_type=jnp.float32)
    if not kernels:
        d_act = jnp.einsum("qd,fd->qf", d_result, full_down, preferred_element_type=jnp.float32)
        d_pre = gelu_back(d_act)[0].astype(jnp.bfloat16)
    g_up = jnp.einsum("qd,qf->df", hidden_low, d_pre, preferred_element_type=jnp.float32)
    d_hidden = jnp.einsum("qf,df->qd", d_pre, full_up, preferred_element_type=jnp.float32)
    d_middle_ln, g_gain_ffn = ffn_back(d_hidden)
    d_middle = d_result.astype(jnp.float32) + d_middle_ln
    d_branch = d_middle.astype(jnp.bfloat16)
    g_out = jnp.einsum("qe,qd->ed", attended, d_branch, preferred_element_type=jnp.float32)
    d_attended = jnp.einsum(
        "qd,ed->qe", d_branch, full_out, preferred_element_type=jnp.float32
    ).astype(jnp.bfloat16)
    scores_again = masked_scores(q_heads, k_heads, allowed, score_scale)
    probs = jnp.exp(scores_again - log_total)
    probs_again = probs.astype(jnp.bfloat16)
    d_att_heads = d_attended.reshape(queries_n, HEADS, head_size)
    d_probs = jnp.einsum("qhe,khe->hqk", d_att_heads, v_heads, preferred_element_type=jnp.float32)
    row_dot = jnp.sum(probs * d_probs, axis=-1, keepdims=True)
    d_scores = (probs * (d_probs - row_dot)).astype(jnp.bfloat16)
    d_queries = (
        (
            jnp.einsum("hqk,khe->qhe", d_scores, k_heads, preferred_element_type=jnp.float32)
            * score_scale
        )
        .reshape(queries_n, model_width)
        .astype(jnp.bfloat16)
    )
    d_keys = (
        (
            jnp.einsum("hqk,qhe->khe", d_scores, q_heads, preferred_element_type=jnp.float32)
            * score_scale
        )
        .reshape(key_rows, model_width)
        .astype(jnp.bfloat16)
    )
    d_values = (
        jnp.einsum("hqk,qhe->khe", probs_again, d_att_heads, preferred_element_type=jnp.float32)
        .reshape(key_rows, model_width)
        .astype(jnp.bfloat16)
    )
    g_query = jnp.einsum("qd,qe->de", lat_low, d_queries, preferred_element_type=jnp.float32)
    d_key_value = jnp.concatenate([d_keys, d_values], axis=1)
    g_key_value = jnp.einsum("kd,kx->dx", keys_in, d_key_value, preferred_element_type=jnp.float32)
    g_qkv = jnp.concatenate([g_query, g_key_value], axis=1).reshape(model_width, 3, model_width)
    back_flat = full_qkv.reshape(model_width, 3 * model_width)
    d_keys_in = jnp.einsum(
        "kx,dx->kd", d_key_value, back_flat[:, model_width:], preferred_element_type=jnp.float32
    )
    d_lat_norm = (
        jnp.einsum(
            "qe,de->qd", d_queries, back_flat[:, :model_width], preferred_element_type=jnp.float32
        )
        + d_keys_in[media_rows:]
    )
    d_lat_ln, g_gain_lat = lat_back(d_lat_norm)
    d_latents = (d_middle + d_lat_ln).reshape(item_slots, lat_count, model_width)
    d_mixed, g_gain_media = media_back(
        d_keys_in[:media_rows].reshape(frame_slots, patch_rows, model_width)
    )
    frame_grad = jnp.sum(d_mixed, axis=1)
    g_time = jnp.einsum("fd,ft->dt", frame_grad, time_hot, precision=highest)
    g_gains = jnp.stack([g_gain_media, g_gain_lat, g_gain_ffn], axis=1)
    if kernels:
        def blocks(g, rows):
            return g.astype(jnp.bfloat16).reshape(2, 2, n_z, 2, rows, -1)

        tiny_g = jnp.concatenate([g_time, g_gains], axis=1).T.reshape(time_len + 3, -1, own_rows).transpose(1, 0, 2)
        tiny_g = jnp.pad(tiny_g, ((0, 0), (0, 16 - tiny_g.shape[1]), (0, 128 - own_rows)))
        grads = [blocks(g, s.shape[0]) for g, s in zip((g_qkv, g_out, g_up, g_down), shards)] + [blocks(tiny_g, 16)]
        listed = [(w, shards[w].shape[0], shards[w].shape[1]) for w in range(4)]
        orders = (("x", "y", "z"), ("y", "x", "z"))
        own, squares = scatter_all(grads, plan_with(orders, listed[::-1], 768, False), n_z)
        own_tiny = own[4][: time_len + 3, :own_rows].T
        reduced = (own[0].reshape(w_qkv.shape), own[1], own[2], own[3], own_tiny[:, :time_len], own_tiny[:, time_len:])
        grad_norm = jnp.sqrt(jnp.sum(squares))
    else:
        reduced = reduce_grads(g_qkv, g_out, g_up, g_down, g_time, g_gains)
        local_sq = jnp.zeros((), jnp.float32)
        for grad in reduced:
            local_sq = local_sq + jnp.sum(grad * grad)
        grad_norm = jnp.sqrt(lax.psum(local_sq, ("dp", "fsdp")))
    factor = jnp.minimum(1.0, clip_limit / (grad_norm + 1e-06))
    masters = (w_qkv, w_out, w_up, w_down, time_table, gains)
    firsts = (m_qkv, m_out, m_up, m_down, m_time, m_gains)
    seconds = (v_qkv, v_out, v_up, v_down, v_time, v_gains)
    rates = (0.02, 0.1, 0.02, 0.01, 0.2, 0.5)
    updated = []
    for index in range(6):
        updated.extend(
            adamw_step(
                masters[index], firsts[index], seconds[index], reduced[index], factor, rates[index]
            )
        )
    return (
        new_latents,
        d_latents,
        grad_norm,
        updated[0],
        updated[1],
        updated[2],
        updated[3],
        updated[4],
        updated[5],
        updated[6],
        updated[7],
        updated[8],
        updated[9],
        updated[10],
        updated[11],
        updated[12],
        updated[13],
        updated[14],
        updated[15],
        updated[16],
        updated[17],
    )


def solution(mesh):
    placed = (
        P(("dp", "fsdp"), None, None),
        P(("dp", "fsdp"), None, None),
        P(("dp", "fsdp")),
        P(("dp", "fsdp"), None, None),
        P(("dp", "fsdp"), None, None),
        P(("dp", "fsdp"), None, None),
        P(("dp", "fsdp"), None, None),
        P(("dp", "fsdp"), None),
        P(("dp", "fsdp"), None),
        P(("dp", "fsdp"), None),
        P(("dp", "fsdp"), None),
        P(("dp", "fsdp"), None),
        P(("dp", "fsdp"), None),
        P(("dp", "fsdp"), None),
        P(("dp", "fsdp"), None),
        P(("dp", "fsdp"), None),
        P(("dp", "fsdp"), None),
        P(("dp", "fsdp"), None),
        P(("dp", "fsdp"), None),
        P(("dp", "fsdp"), None),
        P(("dp", "fsdp"), None),
        P(("dp", "fsdp"), None),
    )
    return jax.shard_map(
        on_device,
        mesh=mesh,
        in_specs=placed,
        out_specs=(
            P(("dp", "fsdp"), None, None),
            P(("dp", "fsdp"), None, None),
            P(),
            P(("dp", "fsdp"), None, None),
            P(("dp", "fsdp"), None, None),
            P(("dp", "fsdp"), None, None),
            P(("dp", "fsdp"), None),
            P(("dp", "fsdp"), None),
            P(("dp", "fsdp"), None),
            P(("dp", "fsdp"), None),
            P(("dp", "fsdp"), None),
            P(("dp", "fsdp"), None),
            P(("dp", "fsdp"), None),
            P(("dp", "fsdp"), None),
            P(("dp", "fsdp"), None),
            P(("dp", "fsdp"), None),
            P(("dp", "fsdp"), None),
            P(("dp", "fsdp"), None),
            P(("dp", "fsdp"), None),
            P(("dp", "fsdp"), None),
            P(("dp", "fsdp"), None),
        ),
        check_vma=False,
    )
```

```python
import functools
import math
import types

import jax
import jax.numpy as jnp
from jax import lax
from jax.experimental import pallas as pl
from jax.experimental.pallas import tpu as pltpu
from jax.sharding import PartitionSpec as P

DP, FSDP = "dp", "fsdp"
HEADS = 16
STEP = 10


highest = lax.Precision.HIGHEST
norm_eps = 1e-05
clip_limit = 1.0
beta_one = 0.9
beta_two = 0.999
adam_eps = 1e-08
decay_rate = 0.1

MESH=pl.DeviceIdType.MESH
ANY=pl.ANY

class Place:
    def __init__(self, n_z):
        dp = lax.axis_index(DP); fs = lax.axis_index(FSDP)
        self.n_z = n_z
        self.at = {"x": dp // 2, "c": dp % 2, "z": fs // 2, "y": fs % 2}
    def dev(self, **new):
        p = {**self.at, **new}
        return (p["x"] * 2 + p["c"], p["z"] * 2 + p["y"])
    def other(self, ax):
        return self.dev(**{ax: 1 - self.at[ax]})
    def along_z(self, k):
        return self.dev(z=(self.at["z"] + k) % self.n_z)
    def partners(self):
        return [self.other(a) for a in "cxy"] + [self.along_z(k) for k in range(1, self.n_z)]

def greet(place):
    bar = pltpu.get_barrier_semaphore()
    others = place.partners()
    for d in others:
        pl.semaphore_signal(bar, inc=1, device_id=d, device_id_type=MESH)
    pl.semaphore_wait(bar, len(others))

def block_index(place, held):
    return tuple(slice(None) if ax in held else place.at[ax] for ax in "xczy")

class Gather:
    def __init__(self, place, src, dst, rows, cols, order, sems, base):
        self.place, self.src, self.dst = place, src, dst
        self.sl = (pl.ds(*rows), pl.ds(*cols))
        self.order, self.sems, self.base = order, sems, base
        self.copies = {}
    def region(self, held):
        return self.dst.at[block_index(self.place, held) + self.sl]
    def start(self, step):
        p = self.place; ax = self.order[step]; held = self.order[:step]
        ss, rs = self.sems
        made = []
        n = self.base
        for s in range(step):
            n += p.n_z - 1 if self.order[s] == "z" else 1
        src = self.src.at[self.sl] if step == 0 else self.region(held)
        dst = self.region(held)
        for k in (range(1, p.n_z) if ax == "z" else (0,)):
            to = p.along_z(k) if ax == "z" else p.other(ax)
            d = pltpu.make_async_remote_copy(src_ref=src, dst_ref=dst, send_sem=ss.at[n], recv_sem=rs.at[n], device_id=to, device_id_type=MESH)
            d.start(); made.append(d); n += 1
        self.copies[step] = made
    def arrive(self, step):
        for d in self.copies[step]: d.wait_recv()
    def finish(self):
        for made in self.copies.values():
            for d in made: d.wait_send()

def n_sems(n_z): return n_z + 2

def number(plan):
    j, out = 0, []
    for stage in plan:
        new = []
        for piece in stage:
            new.append((j,) + piece); j += 1
        out.append(new)
    return out, j

ZYX, ZXY = ("z", "y", "x", "c"), ("z", "x", "y", "c")

SLOTS = 4


class Scatter:
    def __init__(self, place, out, rows, cols, order, piece, part, turn, sems, bufs):
        self.p, self.out, self.order, self.piece = place, out, order, piece
        self.rows, self.cols, self.width = pl.ds(*rows), pl.ds(*cols), cols[1]
        self.ss, self.rs, self.ls = sems
        self.part, self.b = part, bufs
        self.here = (turn % SLOTS) * 2 + part
        self.sent = {}

    def v(self, ref, *lead):
        return ref.at[lead + (slice(None), pl.ds(0, self.width))]

    def send(self, src, dst, to, n):
        n += self.piece * (self.p.n_z + 1)
        d = pltpu.make_async_remote_copy(src_ref=src, dst_ref=dst, send_sem=self.ss.at[n], recv_sem=self.rs.at[n], device_id=to, device_id_type=MESH)
        d.start()
        return d

    def add(self, count, dst, a, b):
        w = slice(0, self.width)

        def one(i, carry):
            (da, di), (aa, ai), (ba, bi) = dst(i), a(i), b(i)
            da[di + (slice(None), w)] = aa[ai + (slice(None), w)] + ba[bi + (slice(None), w)]
            return carry

        lax.fori_loop(0, count, one, 0)

    def free(self, step):
        for d in self.sent.pop(step, ()):
            d.wait_send() if step < 3 else d.wait()

    def step0(self, fill):
        p, b, A, h = self.p, self.b, slice(None), self.here
        fill(b.s0, h, self)
        ax = self.order[0]
        o = 1 - p.at[ax]
        if ax == "x":
            pair = self.v(b.s0, h, o, A, A), self.v(b.r1y, h // 2, A, A)
        else:
            pair = self.v(b.s0, h, A, A, o), self.v(b.r1x, h // 2, A, A)
        self.sent[0] = [self.send(*pair, p.other(ax), 0)]

    def step1(self):
        p, b, A, h, nz = self.p, self.b, slice(None), self.here, self.p.n_z
        for d in self.sent[0]:
            d.wait_recv()
        ax, nxt = self.order[0], self.order[1]
        m, o = p.at[ax], 1 - p.at[nxt]
        if ax == "x":
            at = lambda i: (i // 2, i % 2)
            self.add(2 * nz, lambda i: (b.s1y, (h // 2,) + at(i)), lambda i: (b.s0, (h, m) + at(i)), lambda i: (b.r1y, (h // 2,) + at(i)))
            src = self.v(b.s1y, h // 2, A, o)
        else:
            at = lambda i: (i // nz, i % nz)
            self.add(2 * nz, lambda i: (b.s1x, (h // 2,) + at(i)), lambda i: (b.s0, (h,) + at(i) + (m,)), lambda i: (b.r1x, (h // 2,) + at(i)))
            src = self.v(b.s1x, h // 2, o, A)
        self.sent[1] = [self.send(src, self.v(b.r2, h, A), p.other(nxt), 1)]

    def step2(self):
        p, b, h, nz = self.p, self.b, self.here, self.p.n_z
        for d in self.sent[1]:
            d.wait_recv()
        m = p.at[self.order[1]]
        mine = (lambda i: (b.s1y, (h // 2, i, m))) if self.order[0] == "x" else (lambda i: (b.s1x, (h // 2, m, i)))
        self.add(nz, lambda i: (b.s2, (h, i)), mine, lambda i: (b.r2, (h, i)))
        self.sent[2] = [
            self.send(self.v(b.s2, h, (p.at["z"] + k) % nz), self.v(b.r3, h, k - 1), p.along_z(k), 1 + k) for k in range(1, nz)
        ]

    def step3(self):
        p, b, h, nz, w = self.p, self.b, self.here, self.p.n_z, self.width
        for d in self.sent[2]:
            d.wait_recv()
        total = b.s2[h, p.at["z"], :, 0:w].astype(jnp.float32)
        for k in range(nz - 1):
            total = total + b.r3[h, k, :, 0:w].astype(jnp.float32)
        b.o[h, :, 0:w] = total
        b.sq[:, 0:w] += total * total
        d = pltpu.make_async_copy(self.v(b.o, h), self.out.at[self.rows, self.cols], self.ls.at[h])
        d.start()
        self.sent[3] = [d]


def sum_squares(place, n_z, bufs, sems, out):
    ns, nr = sems
    sq, part, zs = bufs.sq, bufs.n, bufs.nz
    acc = jnp.zeros((8, 128), jnp.float32)
    for i in range(sq.shape[0] // 8):
        for j in range(sq.shape[1] // 128):
            acc = acc + sq[i * 8 : (i + 1) * 8, j * 128 : (j + 1) * 128]
    for n, ax in enumerate("cxy"):
        part[2 * n] = acc
        d = pltpu.make_async_remote_copy(src_ref=part.at[2 * n], dst_ref=part.at[2 * n + 1], send_sem=ns.at[n], recv_sem=nr.at[n], device_id=place.other(ax), device_id_type=MESH)
        d.start()
        d.wait()
        acc = part[2 * n] + part[2 * n + 1]
    z = place.at["z"]
    zs[z] = acc
    made = []
    for k in range(1, n_z):
        d = pltpu.make_async_remote_copy(src_ref=zs.at[z], dst_ref=zs.at[z], send_sem=ns.at[2 + k], recv_sem=nr.at[2 + k], device_id=place.along_z(k), device_id_type=MESH)
        d.start()
        made.append(d)
    for d in made:
        d.wait()
    total = zs[0]
    for k in range(1, n_z):
        total = total + zs[k]
    out[...] = total


def backward_kernel(n_z, plan, names, *refs):
    b = types.SimpleNamespace(**dict(zip(names, refs)))
    ss, rs, ls, ns, nr, ws, ps, pr, lt_sem, rhs_sem, out_sem = refs[len(names) :]
    own_grads = (b.g_qkv, b.g_out, b.g_up, b.g_down, b.g_tiny)
    place = Place(n_z)
    greet(place)
    core, A = place.at["c"], slice(None)
    queries_n, model = b.q.shape
    key_rows = b.keys.shape[0]
    media_rows = key_rows - queries_n
    hidden_n = b.dpre.shape[1]
    head = model // HEADS
    windows, group_width = head_windows(head)
    scale = 1.0 / head**0.5
    f32, bf = jnp.float32, jnp.bfloat16
    b.sq[...] = jnp.zeros_like(b.sq)
    given = {}

    def give(src, dst):
        n = len(given)
        d = pltpu.make_async_remote_copy(src_ref=src, dst_ref=dst, send_sem=ps.at[n], recv_sem=pr.at[n], device_id=place.other("c"), device_id_type=MESH)
        d.start()
        given[id(dst)] = [d, False]

    def got(dst):
        held_copy = given[id(dst)]
        if not held_copy[1]:
            held_copy[0].wait_recv()
            held_copy[1] = True

    give(b.dpre, b.x_dpre)
    keys_in = pltpu.make_async_copy(b.keys, b.k, out_sem.at[1])
    keys_in.start()

    wbuf = b.wbuf

    def fetch(src, slot):
        d = pltpu.make_async_copy(src, wbuf.at[slot], ws.at[slot])
        d.start()
        return d

    def tiles_of(jobs, use):
        ahead = fetch(jobs[0], 0)
        for i in range(len(jobs)):
            now = ahead
            if i + 1 < len(jobs):
                ahead = fetch(jobs[i + 1], (i + 1) % 2)
            now.wait()
            use(i, wbuf[i % 2].reshape(384, model))

    def hidden_part(i):
        d = pltpu.make_async_copy(b.dpre.at[:, pl.ds(i * model, model)], b.dpart, ws.at[4])
        d.start()
        d.wait()

        def use(n, w):
            got_ = dot(b.dpart[...], w, ((1,), (1,)))
            cols = slice(n * 384, (n + 1) * 384)
            if i == 0:
                b.dmid[:, cols] = got_
            else:
                b.dmid[:, cols] += got_

        tiles_of([b.f_up.at[x, c, :, :, :, pl.ds(i * model, model)] for x in range(2) for c in range(2)], use)

    def norm_back(rows_in, grad, gain):
        centered = rows_in - jnp.mean(rows_in, axis=-1, keepdims=True)
        inv = lax.rsqrt(jnp.mean(centered * centered, axis=-1, keepdims=True) + norm_eps)
        hat = centered * inv
        scaled = grad * gain
        back = inv * (scaled - jnp.mean(scaled, axis=-1, keepdims=True) - hat * jnp.mean(scaled * hat, axis=-1, keepdims=True))
        return back, jnp.sum(grad * hat, axis=0, keepdims=True)

    def ffn_norm():
        d = pltpu.make_async_copy(b.f_tiny, b.tiny, ws.at[3])
        d.start()
        e = pltpu.make_async_copy(b.p_cot.at[core], b.dbranch, ws.at[4])
        e.start()
        d.wait()
        e.wait()
        b.tiny_t[...] = b.tiny[...].reshape(model, 128).astype(f32).T
        b.gsmall[...] = jnp.zeros_like(b.gsmall)

        def rows(i, carry):
            at = pl.ds(pl.multiple_of(i * 64, 64), 64)
            back, gain = norm_back(b.mid[at, :], b.dmid[at, :], b.tiny_t[10:11, :])
            total = b.dbranch[at, :].astype(f32) + back
            b.dmid[at, :] = total
            b.dbranch[at, :] = total.astype(bf)
            b.gsmall[10:11, :] += gain
            return carry

        lax.fori_loop(0, queries_n // 64, rows, 0)
        give(b.dbranch, b.x_branch)

    def attended_back():
        def use(n, w):
            b.datt[:, n * 384 : (n + 1) * 384] = dot(b.dbranch[...], w, ((1,), (1,))).astype(bf)

        tiles_of([b.f_out.at[x, c] for x in range(2) for c in range(2)], use)

    def attend_back(g):
        if g == 0:
            keys_in.wait()
        base = g * group_width
        n_tiles = group_width // 128
        last = {t: max(j for j, (t0, t1, _) in enumerate(windows) if t0 <= t < t1) for t in range(n_tiles)}
        sums = {}
        for j, (t0, t1, start) in enumerate(windows):
            cols = slice(base + t0 * 128, base + t1 * 128)
            q_in, k_in = lanes_of(queries_n, t1 - t0, start, head), lanes_of(key_rows, t1 - t0, start, head)
            qh = b.q[:, cols]
            qh = jnp.where(q_in, qh, jnp.zeros_like(qh))
            dah = b.datt[:, cols]
            dah = jnp.where(q_in, dah, jnp.zeros_like(dah))
            kw = b.k[:, cols]
            h = g * len(windows) + j
            p = jnp.exp(dot(kw, qh, ((1,), (1,))) * scale + b.bias[...] - b.lse[h : h + 1, :])
            dp = dot(b.v[:, cols], dah, ((1,), (1,)))
            row_dot = jnp.sum(p * dp, axis=0, keepdims=True)
            ds = (p * (dp - row_dot)).astype(bf)
            kh = jnp.where(k_in, kw, jnp.zeros_like(kw))
            parts = ((b.dv, dot(p.astype(bf), dah)), (b.dk, dot(ds, qh) * scale), (b.dq, dot(ds, kh, ((0,), (0,))) * scale))
            for n, (into, part) in enumerate(parts):
                for t in range(t0, t1):
                    new = part[:, (t - t0) * 128 : (t - t0 + 1) * 128]
                    sums[n, t] = sums[n, t] + new if (n, t) in sums else new
                    if last[t] == j:
                        into[:, base + t * 128 : base + (t + 1) * 128] = sums.pop((n, t)).astype(bf)
        if g == model // group_width - 1:
            give(b.dq, b.x_dq)
            give(b.dk, b.x_dk)
            give(b.dv, b.x_dv)

    def keys_back(n):
        x, c = n // 2, n % 2
        made = [fetch(b.f_qkv.at[x, c, :, :, :, pl.ds(i * model, model)], i) for i in range(3)]
        for d in made:
            d.wait()
        w = [wbuf[i].reshape(384, model) for i in range(3)]
        cols = slice(n * 384, (n + 1) * 384)
        lat_rows = slice(media_rows, key_rows)
        tail = dot(b.dq[...], w[0], ((1,), (1,))) + dot(b.dk[lat_rows, :], w[1], ((1,), (1,))) + dot(b.dv[lat_rows, :], w[2], ((1,), (1,)))
        b.k[lat_rows, cols] = tail.astype(bf)
        step = media_rows // 3
        for i in range(3):
            rows = slice(i * step, (i + 1) * step)
            b.k[rows, cols] = (dot(b.dk[rows, :], w[1], ((1,), (1,))) + dot(b.dv[rows, :], w[2], ((1,), (1,)))).astype(bf)

    def latents_back():
        def rows(i, carry):
            at = pl.ds(pl.multiple_of(i * 64, 64), 64)
            grad = b.k[pl.ds(pl.multiple_of(media_rows + i * 64, 16), 64), :].astype(f32)
            back, gain = norm_back(b.lat[at, :].astype(f32), grad, b.tiny_t[9:10, :])
            b.dmid[at, :] = b.dmid[at, :] + back
            b.gsmall[9:10, :] += gain
            return carry

        lax.fori_loop(0, queries_n // 64, rows, 0)
        d = pltpu.make_async_copy(b.dmid, b.d_lat, out_sem.at[0])
        d.start()
        late.append(d)

    late = []

    def media_back(part):
        step = media_rows // 3
        frames = step // 48
        d = pltpu.make_async_copy(b.media.at[pl.ds(part * step, step)], b.mrows, ws.at[3])
        d.start()
        d.wait()

        def frame(i, carry):
            at = pl.ds(pl.multiple_of(i * 48, 48), 48)
            whole = pl.ds(pl.multiple_of(part * step + i * 48, 48), 48)
            mixed = b.mrows[at, :].astype(f32) + dot(b.hot[whole, :], b.tiny_t[...].astype(bf))
            back, gain = norm_back(mixed, b.k[whole, :].astype(f32), b.tiny_t[8:9, :])
            b.gsmall[8:9, :] += gain
            b.gsmall[0:8, :] += b.hotc[part * frames + i][:, 0:1] * jnp.sum(back, axis=0, keepdims=True)
            return carry

        lax.fori_loop(0, frames, frame, 0)

    def small():
        b.gblocks[...] = b.gsmall[...].T.astype(bf).reshape(b.gblocks.shape)
        give(b.gblocks.at[:, 1 - core], b.x_tiny)

    held = [None]

    def left(src):
        if held[0] is src:
            return
        held[0] = src
        if src is b.p_keys:
            into = b.ltk
        elif src is b.p_act:
            into = b.lt
        else:
            into = b.lt.at[:, :, pl.ds(0, 2 * n_z)]
        d = pltpu.make_async_copy(src, into, lt_sem.at[0])
        d.start()
        d.wait()

    def right(own, sibling, cols, part):
        made = [pltpu.make_async_copy(r.at[:, pl.ds(*cols)], b.rhs.at[part, i], rhs_sem.at[part, i]) for i, r in enumerate((own, sibling))]
        for d in made:
            d.start()
        for d in made:
            d.wait()

    def blocks(x, k, group):
        if group == 1:
            return [b.lt[s, x, 0 : 2 * n_z].reshape(96 * n_z, queries_n) for s in (core, 1 - core)]
        return [jnp.concatenate([b.lt[s, x, i * group + k] for i in range(2 * n_z)], axis=0) for s in (core, 1 - core)]

    def filler(w, rows, cols):
        first, width = cols
        wide = pl.ds(first, width)

        def fill(dst, here, g):
            if w == 4:
                got(b.x_tiny)
                d = pltpu.make_async_copy(b.x_tiny, b.tiny2, ws.at[3])
                d.start()
                d.wait()

                def one(i, carry):
                    x, z, y = i // (2 * n_z), (i // 2) % n_z, i % 2
                    dst[here, x, z, y, :, 0:width] = b.gblocks[x, core, z, y] + b.tiny2[x, z, y]
                    return carry

                lax.fori_loop(0, 4 * n_z, one, 0)
                return
            keyed = w == 0 and first >= model
            if keyed:
                left(b.p_keys)
                mine, theirs = (b.dk, b.x_dk) if first < 2 * model else (b.dv, b.x_dv)
                got(theirs)
                at = pl.ds(first % model, width)
                d = pltpu.make_async_copy(theirs.at[:, at], b.rhsk.at[g.part], rhs_sem.at[g.part, 0])
                d.start()
                d.wait()
                r = [mine[:, at], b.rhsk[g.part]]
            elif w == 3:
                left(b.p_act)
                right(b.p_cot.at[core], b.p_cot.at[1 - core], cols, g.part)
            elif w == 2:
                left(b.p_hid)
                got(b.x_dpre)
                right(b.dpre, b.x_dpre, cols, g.part)
            else:
                mine, theirs, act = (b.dbranch, b.x_branch, b.p_att) if w == 1 else (b.dq, b.x_dq, b.p_lat)
                left(act)
                got(theirs)
                at = pl.ds(first % model, width)
                d = pltpu.make_async_copy(theirs.at[:, at], b.rhs.at[g.part, 1], rhs_sem.at[g.part, 1])
                d.start()
                d.wait()
            if w in (2, 3):
                r = [b.rhs[g.part, 0], b.rhs[g.part, 1]]
            elif not keyed:
                r = [mine[:, at], b.rhs[g.part, 1]]
            for x in range(2):
                if keyed:
                    l = [b.ltk[s, x].reshape(96 * n_z, key_rows) for s in (core, 1 - core)]
                else:
                    l = blocks(x, rows[0] // 48, 4 if w == 3 else 1)
                total = dot(l[0], r[0]) + dot(l[1], r[1])
                dst[here, x, :, :, :, 0:width] = total.astype(bf).reshape(n_z, 2, 48, width)

        return fill

    parts = 3
    work = [(3, 5, functools.partial(hidden_part, i)) for i in range(hidden_n // model)] + [(0, 3, ffn_norm), (0, 4, attended_back)]
    work += [(0, 9, functools.partial(attend_back, g)) for g in range(model // group_width)]
    work += [(0, 5, functools.partial(keys_back, n)) for n in range(4)] + [(0, 3, latents_back)]
    work += [(0, 4, functools.partial(media_back, i)) for i in range(parts)] + [(0, 2, small)]

    def run_until(dst):
        while id(dst) not in given:
            work.pop(0)[2]()

    stages = [
        [Scatter(place, own_grads[w], rows, cols, order, j, part, t, (ss, rs, ls), b) for part, (j, w, rows, cols, order) in enumerate(stage)]
        for t, stage in enumerate(plan)
    ]
    total = len(stages)
    for t in range(total + 3):
        for back in range(4):
            u = t - back
            if not 0 <= u < total:
                continue
            if u >= SLOTS:
                for g in stages[u - SLOTS]:
                    g.free(back)
            for g, (j, w, rows, cols, order) in zip(stages[u], plan[u]):
                if back == 0:
                    need = (b.x_dv, b.x_branch, b.x_dpre, b.x_dpre, b.x_tiny)[w]
                    run_until(need)
                    g.step0(filler(w, rows, cols))
                else:
                    (g.step1, g.step2, g.step3)[back - 1]()
        room = 9
        while work and room > 0:
            _, cost, piece = work.pop(0)
            room -= cost
            piece()
    for st in stages:
        for g in st:
            for k in range(4):
                g.free(k)
    for d, done in given.values():
        d.wait_send()
    for d in late:
        d.wait()
    sum_squares(place, n_z, b, (ns, nr), b.norm)


def backward_plan(shards, model, width):
    orders = (("x", "y", "z"), ("y", "x", "z"))
    pieces = [(3, (k, 48), (c, width)) for k in range(0, shards[3].shape[0], 48) for c in range(0, model, width)]
    pieces += [(2, (0, 48), (c, width)) for c in range(0, shards[2].shape[1], width)]
    pieces += [(1, (0, 48), (c, width)) for c in range(0, model, width)] + [(4, (0, 48), (0, 128))]
    pieces += [(0, (0, 48), (c, width)) for c in range(0, 3 * model, width)]
    return [[p + (orders[i],) for i, p in enumerate(pieces[n : n + 2])] for n in range(0, len(pieces), 2)]


def backward_all(full, made, lat, media, hot, hotc, bias, shards, n_z):
    width = 512
    queries_n, model = lat.shape
    media_rows = media.shape[0]
    key_rows = queries_n + media_rows
    hidden_n = shards[2].shape[1]
    plan, count = number(backward_plan(shards, model, width))
    q, k, v, dpre, mid, new, lse, p_keys, p_lat, p_att, p_hid, p_act, p_cot = made
    given = dict(f_qkv=full[0], f_out=full[1], f_up=full[2], f_tiny=full[4], dpre=dpre, p_keys=p_keys, p_lat=p_lat, p_att=p_att, p_hid=p_hid, p_act=p_act, p_cot=p_cot,
                 media=media, q=q, keys=k, v=v, mid=mid, lse=lse, lat=lat, hot=hot, hotc=hotc, bias=bias)
    bf, f32 = jnp.bfloat16, jnp.float32
    grads = [((s.shape[0], s.shape[1]), f32) for s in shards]
    outs = dict(g_qkv=grads[0], g_out=grads[1], g_up=grads[2], g_down=grads[3], g_tiny=grads[4], d_lat=((queries_n, model), f32), norm=((8, 128), f32),
                x_dpre=((queries_n, hidden_n), bf), x_branch=((queries_n, model), bf), x_dq=((queries_n, model), bf), x_dk=((key_rows, model), bf), x_dv=((key_rows, model), bf),
                x_tiny=((2, n_z, 2, 48, 128), bf))
    W, S = width, SLOTS
    vm = dict(s0=((2 * S, 2, n_z, 2, 48, W), bf), r1x=((S, 2, n_z, 48, W), bf), r1y=((S, n_z, 2, 48, W), bf), s1x=((S, 2, n_z, 48, W), bf), s1y=((S, n_z, 2, 48, W), bf),
          r2=((2 * S, n_z, 48, W), bf), s2=((2 * S, n_z, 48, W), bf), r3=((2 * S, n_z - 1, 48, W), bf), o=((2 * S, 48, W), f32),
          sq=((48, W), f32), n=((6, 8, 128), f32), nz=((n_z, 8, 128), f32),
          wbuf=((3, n_z, 2, 48, model), bf), dpart=((queries_n, model), bf), dmid=((queries_n, model), f32), dbranch=((queries_n, model), bf), datt=((queries_n, model), bf),
          dq=((queries_n, model), bf), k=((key_rows, model), bf), dk=((key_rows, model), bf), dv=((key_rows, model), bf), tiny=((2, 2, n_z, 2, 48, 128), bf), tiny_t=((128, model), f32),
          gsmall=((128, model), f32), gblocks=((2, 2, n_z, 2, 48, 128), bf), tiny2=((2, n_z, 2, 48, 128), bf), mrows=((media_rows // 3, model), bf),
          lt=(p_act.shape, bf), ltk=(p_keys.shape, bf), rhs=((2, 2, queries_n, W), bf), rhsk=((2, key_rows, W), bf))
    sem = pltpu.SemaphoreType.DMA
    in_vmem, in_any = pl.BlockSpec(memory_space=pltpu.VMEM), pl.BlockSpec(memory_space=ANY)
    resident = tuple(id(a) for a in (q, v, mid, lse, lat, hot, hotc, bias))
    n_copies = count * (n_z + 1)
    res = pl.pallas_call(
        functools.partial(backward_kernel, n_z, plan, (*given, *outs, *vm)),
        out_shape=[jax.ShapeDtypeStruct(*o) for o in outs.values()],
        in_specs=[in_vmem if id(a) in resident else in_any for a in given.values()],
        out_specs=[in_vmem if o is outs["norm"] else in_any for o in outs.values()],
        scratch_shapes=[pltpu.VMEM(*m) for m in vm.values()] + [sem((n_copies,)), sem((n_copies,)), sem((2 * S,)), sem((n_z + 2,)), sem((n_z + 2,)), sem((5,)), sem((8,)), sem((8,)), sem((1,)), sem((2, 2)), sem((2,))],
        name="backward_and_scatter",
        compiler_params=pltpu.CompilerParams(collective_id=1, has_side_effects=True, vmem_limit_bytes=62 * 2**20),
    )(*given.values())
    return types.SimpleNamespace(**dict(zip(outs, res)))


def out_copies(pairs, sems, at, running):
    for src, dst in pairs:
        d = pltpu.make_async_copy(src, dst, sems.at[len(running)])
        d.start()
        running.append(d)


def dot(a, b, contract=((1,), (0,))):
    return lax.dot_general(a, b, (contract, ((), ())), preferred_element_type=jnp.float32)


def head_windows(head):
    group = 128 // math.gcd(head, 128)
    out = []
    for j in range(group):
        first, last = j * head // 128, ((j + 1) * head - 1) // 128
        out.append((first, last + 1, j * head - first * 128))
    return out, group * head


def lanes_of(rows, tiles, start, head):
    lane = lax.broadcasted_iota(jnp.int32, (rows, tiles * 128), 1)
    return (lane >= start) & (lane < start + head)


def normed(rows_in, gain):
    centered = rows_in - jnp.mean(rows_in, axis=-1, keepdims=True)
    var_row = jnp.mean(centered * centered, axis=-1, keepdims=True)
    return centered * lax.rsqrt(var_row + norm_eps) * gain


def forward_kernel(n_z, plan, needs, *refs):
    (sh, (lat, media, cot, hot, bias), full, outs, scratch) = refs[:5], refs[5:10], refs[10:15], refs[15:27], refs[27:]
    o_q, o_k, o_v, o_dpre, o_mid, o_new, o_lse, p_keys, p_lat, p_att, p_hid, p_act = outs[:12]
    p_cot, *scratch = scratch
    keys, q, k, v, att, hid, act, slope, dact, mid, new, tiny, tiny_t, lse, wbuf, wdown, flip, flip_keys, ss, rs, ls, os_, ws, ps, pr, pl_ = scratch
    f_qkv, f_out, f_up, f_down, f_tiny = full
    place = Place(n_z)
    greet(place)
    queries_n, model = lat.shape
    media_rows = media.shape[0]
    key_rows = media_rows + queries_n
    hidden_n = act.shape[1]
    head = model // HEADS
    windows, group_width = head_windows(head)
    scale = 1.0 / head**0.5
    written = []
    given = []
    core = place.at["c"]

    def give(src, dst, theirs):
        n = len(given)
        if theirs:
            d = pltpu.make_async_remote_copy(src_ref=src, dst_ref=dst, send_sem=ps.at[n], recv_sem=pr.at[n], device_id=place.other("c"), device_id_type=MESH)
        else:
            d = pltpu.make_async_copy(src, dst, pl_.at[n])
        d.start()
        given.append([d, theirs, False])
        return n

    def gone(n):
        d, theirs, done = given[n]
        if not done:
            d.wait_send() if theirs else d.wait()
            given[n][2] = True

    def turn(a, dst, slot, x, wide, before=()):
        made = []
        for n in before:
            gone(n)
        for theirs in (False, True):
            who = 1 - core if theirs else core
            for m in range(wide // 384):
                cols = pl.ds(pl.multiple_of((x * 2 + who) * wide + m * 384, 128), 384)
                flip[slot] = a[:, cols].T.reshape(8, 48, queries_n)
                made.append(give(flip.at[slot], dst.at[core, x, pl.ds(m * 8, 8)], theirs))
                slot += 1
        return made

    def load(src, dst):
        d = pltpu.make_async_copy(src, dst, ws.at[0])
        d.start()
        d.wait()

    def write(*pairs):
        out_copies(pairs, os_, 0, written)

    def norms():
        load(f_tiny, tiny)
        tiny_t[...] = tiny[...].reshape(model, 128).astype(jnp.float32).T
        give(cot, p_cot.at[core], False)
        give(cot, p_cot.at[core], True)
        hid[...] = normed(lat[...].astype(jnp.float32), tiny_t[9:10, :]).astype(jnp.bfloat16)
        keys[media_rows:key_rows, :] = hid[...]
        for x in range(2):
            turn(hid, p_lat, 2 * x, x, 384)

        def frame(i, carry):
            rows = pl.ds(pl.multiple_of(i * 48, 48), 48)
            mixed = media[rows, :].astype(jnp.float32) + dot(hot[rows, :], tiny_t[...].astype(jnp.bfloat16))
            keys[rows, :] = normed(mixed, tiny_t[8:9, :]).astype(jnp.bfloat16)
            return carry

        lax.fori_loop(0, media_rows // 48, frame, 0)

    key_turns = []

    def turn_keys(x):
        for n in key_turns:
            gone(n)
        for theirs in (False, True):
            who = 1 - core if theirs else core
            cols = pl.ds(pl.multiple_of((x * 2 + who) * 384, 128), 384)
            flip_keys[int(theirs)] = keys[:, cols].T.reshape(8, 48, key_rows)
            key_turns.append(give(flip_keys.at[int(theirs)], p_keys.at[core, x], theirs))

    def project(i, dst, first):
        load(f_qkv.at[:, :, :, :, :, pl.ds(i * model, model)], wbuf)

        def tile(n, carry):
            cols = pl.ds(pl.multiple_of(n * 256, 256), 256)
            w = wbuf[:, :, :, :, :, cols].reshape(model, 256)
            dst[:, cols] = dot(keys[first:key_rows, :], w).astype(jnp.bfloat16)
            return carry

        lax.fori_loop(0, model // 256, tile, 0)

    def project_q():
        project(0, q, media_rows)
        write((q, o_q))

    def project_k():
        project(1, k, 0)
        write((k, o_k))

    def project_v():
        project(2, v, 0)
        write((v, o_v))

    def attend(g):
        base = g * group_width
        tiles = [jnp.zeros((queries_n, 128), jnp.float32) for _ in range(group_width // 128)]
        for j, (t0, t1, start) in enumerate(windows):
            cols = slice(base + t0 * 128, base + t1 * 128)
            qh = q[:, cols]
            qh = jnp.where(lanes_of(queries_n, t1 - t0, start, head), qh, jnp.zeros_like(qh))
            s = dot(k[:, cols], qh, ((1,), (1,))) * scale + bias[...]
            top = jnp.max(s, axis=0, keepdims=True)
            e = jnp.exp(s - top)
            total = jnp.sum(e, axis=0, keepdims=True)
            p = (e * (1.0 / total)).astype(jnp.bfloat16)
            lse[g * len(windows) + j : g * len(windows) + j + 1, :] = top + jnp.log(total)
            vh = v[:, cols]
            vh = jnp.where(lanes_of(key_rows, t1 - t0, start, head), vh, jnp.zeros_like(vh))
            got = dot(p, vh, ((0,), (0,)))
            for t in range(t0, t1):
                tiles[t] = tiles[t] + got[:, (t - t0) * 128 : (t - t0 + 1) * 128]
        for t, tile in enumerate(tiles):
            att[:, base + t * 128 : base + (t + 1) * 128] = tile.astype(jnp.bfloat16)

    def project_out():
        write((lse, o_lse))
        for x in range(2):
            turn(att, p_att, 4 + 2 * x, x, 384)
        load(f_out, wbuf)

        def tile(n, carry):
            cols = pl.ds(pl.multiple_of(n * 256, 256), 256)
            w = wbuf[:, :, :, :, :, cols].reshape(model, 256)
            mid[:, cols] = lat[:, cols].astype(jnp.float32) + dot(att[...], w)
            return carry

        lax.fori_loop(0, model // 256, tile, 0)
        hid[...] = normed(mid[...], tiny_t[10:11, :]).astype(jnp.bfloat16)
        write((mid, o_mid))
        for x in range(2):
            hid_turns.extend(turn(hid, p_hid, 8 + 2 * x, x, 384))

    hid_turns = []
    act_turns = []

    def up(i):
        load(f_up.at[:, :, :, :, :, pl.ds(i * model, model)], wbuf)

        def tile(n, carry):
            cols = pl.ds(pl.multiple_of(n * 256, 256), 256)
            into = pl.ds(pl.multiple_of(i * model + n * 256, 256), 256)
            w = wbuf[:, :, :, :, :, cols].reshape(model, 256)
            x = dot(hid[...], w)
            cdf = 0.5 + 0.5 * lax.erf(x * 0.7071067811865476)
            act[:, into] = (x * cdf).astype(jnp.bfloat16)
            slope[:, into] = cdf + x * (jnp.exp(-0.5 * x * x) * 0.3989422804014327)
            return carry

        lax.fori_loop(0, model // 256, tile, 0)
        if i % 2 == 1:
            before = list(range(len(given))) if i == 1 else act_turns
            act_turns.extend(turn(act, p_act, 0, i // 2, model, before))

    def down(i, width):
        cols = slice(i * width, (i + 1) * width)
        load(f_down.at[:, :, :, :, :, pl.ds(i * width, width)], wdown)
        per = hidden_n // 4
        got = jnp.zeros((queries_n, width), jnp.float32)
        for b in range(4):
            w = wdown[b // 2, b % 2].reshape(per, width)
            got = got + dot(act[:, b * per : (b + 1) * per], w)
            back = dot(cot[:, cols], w, ((1,), (1,)))
            if i == 0:
                dact[:, b * per : (b + 1) * per] = back
            else:
                dact[:, b * per : (b + 1) * per] += back
        new[:, cols] = (mid[:, cols] + got).astype(jnp.bfloat16)

    def finish():
        def tile(n, carry):
            cols = pl.ds(pl.multiple_of(n * 512, 512), 512)
            act[:, cols] = (dact[:, cols] * slope[:, cols]).astype(jnp.bfloat16)
            return carry

        lax.fori_loop(0, hidden_n // 512, tile, 0)
        write((act, o_dpre), (new, o_new))
        for d in written:
            d.wait()
        for n, (d, theirs, done) in enumerate(given):
            gone(n)
            if theirs:
                d.wait_recv()

    work = [(needs["tiny"], 8, norms), (needs["q"], 4, project_q), (needs["k"], 8, project_k), (needs["v"], 8, project_v)]
    work[2:2] = [(needs["q"], 3, functools.partial(turn_keys, x)) for x in range(2)]
    work += [(needs["v"], 7, functools.partial(attend, g)) for g in range(model // group_width)]
    work += [(needs["out"], 5, project_out)]
    work += [(s, 6, functools.partial(up, i)) for i, s in enumerate(needs["up"])]
    work += [(s, 5, functools.partial(down, i, model // len(needs["down"]))) for i, s in enumerate(needs["down"])]
    work += [(needs["down"][-1], 5, finish)]
    locals_ = []
    for i in range(5):
        d = pltpu.make_async_copy(sh[i], full[i].at[block_index(place, ())], ls.at[i])
        d.start()
        locals_.append(d)
    stages = [[Gather(place, sh[w], full[w], rows, cols, order, (ss, rs), j * n_sems(n_z)) for (j, w, rows, cols, order) in stage] for stage in plan]
    waited = set()
    total, steps = len(stages), 4
    for t in range(total + steps):
        for back in range(steps + 1):
            u = t - back
            if not 0 <= u < total:
                continue
            for g, (j, w, *_) in zip(stages[u], plan[u]):
                if back == 1 and w not in waited:
                    locals_[w].wait()
                    waited.add(w)
                if back > 0:
                    g.arrive(back - 1)
                if back < steps:
                    g.start(back)
        room = 14
        while work and work[0][0] <= t - steps and (room > 0 or t == total + steps - 1):
            need, cost, piece = work.pop(0)
            room -= cost
            piece()
    for st in stages:
        for g in st:
            g.finish()


def forward_plan(shards, model):
    two = lambda w, rows, first, width: [(w, (0, rows), (first, width), ZYX), (w, (0, rows), (first + width, width), ZXY)]
    rows, half = shards[1].shape[0], model // 2
    stages, needs = [[(4, (0, rows), (0, 128), ZYX)]], {"tiny": 0}
    for i, name in enumerate("qkv"):
        needs[name] = len(stages)
        stages.append(two(0, rows, i * model, half))
    needs["out"] = len(stages)
    stages.append(two(1, rows, 0, half))
    needs["up"], needs["down"] = [], []
    for i in range(shards[2].shape[1] // model):
        needs["up"].append(len(stages))
        stages.append(two(2, rows, i * model, half))
    for i in range(model // 256):
        needs["down"].append(len(stages))
        stages.append(two(3, shards[3].shape[0], i * 256, 128))
    return stages, needs


def forward_all(shards, lat, media, cot, hot, bias, n_z):
    model, hidden_n = lat.shape[1], shards[2].shape[1]
    stages, needs = forward_plan(shards, model)
    plan, count = number(stages)
    queries_n, media_rows = lat.shape[0], media.shape[0]
    key_rows = queries_n + media_rows
    bf, f32 = jnp.bfloat16, jnp.float32
    rows = shards[1].shape[0]
    part = (2, 2, 2 * n_z, 48)
    made = [((queries_n, model), bf), ((key_rows, model), bf), ((key_rows, model), bf), ((queries_n, hidden_n), bf), ((queries_n, model), f32), ((queries_n, model), bf), ((HEADS, queries_n), f32),
            (part + (key_rows,), bf), (part + (queries_n,), bf), (part + (queries_n,), bf), (part + (queries_n,), bf), ((2, 2, 2 * n_z * hidden_n // model, 48, queries_n), bf), ((2, queries_n, model), bf)]
    vm = [((key_rows, model), bf), ((queries_n, model), bf), ((key_rows, model), bf), ((key_rows, model), bf), ((queries_n, model), bf), ((queries_n, model), bf), ((queries_n, hidden_n), bf),
          ((queries_n, hidden_n), f32), ((queries_n, hidden_n), f32), ((queries_n, model), f32), ((queries_n, model), bf),
                     ((2, 2, n_z, 2, rows, 128), bf), ((128, model), f32), ((HEADS, queries_n), f32), ((2, 2, n_z, 2, rows, model), bf), ((2, 2, n_z, 2, shards[3].shape[0], 256), bf),
                     ((12, 8, 48, queries_n), bf), ((2, 8, 48, key_rows), bf)]
    sem = pltpu.SemaphoreType.DMA
    in_vmem, in_any = pl.BlockSpec(memory_space=pltpu.VMEM), pl.BlockSpec(memory_space=ANY)
    out = pl.pallas_call(
        functools.partial(forward_kernel, n_z, plan, needs),
        out_shape=[jax.ShapeDtypeStruct((2, 2, n_z, 2) + s.shape, s.dtype) for s in shards] + [jax.ShapeDtypeStruct(*m) for m in made],
        in_specs=[in_vmem] * 10,
        out_specs=[in_any] * (5 + len(made)),
        scratch_shapes=[pltpu.VMEM(*m) for m in vm] + [sem((count * n_sems(n_z),)), sem((count * n_sems(n_z),)), sem((5,)), sem((16,)), sem((1,)), sem((48,)), sem((48,)), sem((48,))],
        name="gather_and_forward",
        compiler_params=pltpu.CompilerParams(collective_id=0, has_side_effects=True, vmem_limit_bytes=60 * 2**20),
    )(*shards, lat, media, cot, hot, bias)
    return out[:5], out[5:]


def layer_norm(values_in, gain):
    mean_row = jnp.mean(values_in, axis=-1, keepdims=True)
    centered = values_in - mean_row
    var_row = jnp.mean(centered * centered, axis=-1, keepdims=True)
    return centered * lax.rsqrt(var_row + norm_eps) * gain


def exact_gelu(values_in):
    return jax.nn.gelu(values_in, approximate=False)


def frame_tables(counts, frame_slots, time_len):
    slot_total = counts.shape[0]
    order = jnp.arange(slot_total, dtype=jnp.int32)
    slot_ends = jnp.sum(jnp.where(order[None, :] <= order[:, None], counts[None, :], 0), axis=1)
    slot_starts = slot_ends - counts
    frame_ids = jnp.arange(frame_slots, dtype=jnp.int32)
    frame_owner = jnp.sum((frame_ids[:, None] >= slot_ends[None, :]).astype(jnp.int32), axis=1)
    slot_ids = jnp.arange(slot_total, dtype=jnp.int32)
    start_of = jnp.sum(
        jnp.where(frame_owner[:, None] == slot_ids[None, :], slot_starts[None, :], 0), axis=1
    )
    time_index = frame_ids - start_of
    live_frame = frame_owner < slot_total
    time_ids = jnp.arange(time_len, dtype=jnp.int32)
    time_hot = ((time_index[:, None] == time_ids[None, :]) & live_frame[:, None]).astype(
        jnp.float32
    )
    return (frame_owner, time_hot)


def gather_params(part_qkv, part_out, part_up, part_down, part_time, part_gains):
    inner_part = (
        lax.all_gather(part_qkv, FSDP, axis=0, tiled=True),
        lax.all_gather(part_out, FSDP, axis=0, tiled=True),
        lax.all_gather(part_up, FSDP, axis=0, tiled=True),
        lax.all_gather(part_down, FSDP, axis=0, tiled=True),
        lax.all_gather(part_time, FSDP, axis=0, tiled=True),
        lax.all_gather(part_gains, FSDP, axis=0, tiled=True),
    )
    return (
        lax.all_gather(inner_part[0], DP, axis=0, tiled=True),
        lax.all_gather(inner_part[1], DP, axis=0, tiled=True),
        lax.all_gather(inner_part[2], DP, axis=0, tiled=True),
        lax.all_gather(inner_part[3], DP, axis=0, tiled=True),
        lax.all_gather(inner_part[4], DP, axis=0, tiled=True),
        lax.all_gather(inner_part[5], DP, axis=0, tiled=True),
    )


def reduce_grads(grad_qkv, grad_out, grad_up, grad_down, grad_time, grad_gains):
    outer_part = (
        lax.psum_scatter(
            grad_qkv.astype(jnp.bfloat16), DP, scatter_dimension=0, tiled=True
        ).astype(jnp.float32),
        lax.psum_scatter(
            grad_out.astype(jnp.bfloat16), DP, scatter_dimension=0, tiled=True
        ).astype(jnp.float32),
        lax.psum_scatter(
            grad_up.astype(jnp.bfloat16), DP, scatter_dimension=0, tiled=True
        ).astype(jnp.float32),
        lax.psum_scatter(
            grad_down.astype(jnp.bfloat16), DP, scatter_dimension=0, tiled=True
        ).astype(jnp.float32),
        lax.psum_scatter(
            grad_time.astype(jnp.bfloat16), DP, scatter_dimension=0, tiled=True
        ).astype(jnp.float32),
        lax.psum_scatter(
            grad_gains.astype(jnp.bfloat16), DP, scatter_dimension=0, tiled=True
        ).astype(jnp.float32),
    )
    return (
        lax.psum_scatter(
            outer_part[0].astype(jnp.bfloat16), FSDP, scatter_dimension=0, tiled=True
        ).astype(jnp.float32),
        lax.psum_scatter(
            outer_part[1].astype(jnp.bfloat16), FSDP, scatter_dimension=0, tiled=True
        ).astype(jnp.float32),
        lax.psum_scatter(
            outer_part[2].astype(jnp.bfloat16), FSDP, scatter_dimension=0, tiled=True
        ).astype(jnp.float32),
        lax.psum_scatter(
            outer_part[3].astype(jnp.bfloat16), FSDP, scatter_dimension=0, tiled=True
        ).astype(jnp.float32),
        lax.psum_scatter(
            outer_part[4].astype(jnp.bfloat16), FSDP, scatter_dimension=0, tiled=True
        ).astype(jnp.float32),
        lax.psum_scatter(
            outer_part[5].astype(jnp.bfloat16), FSDP, scatter_dimension=0, tiled=True
        ).astype(jnp.float32),
    )


def masked_scores(q_heads, k_heads, allowed, score_scale):
    scores = (
        jnp.einsum("qhe,khe->hqk", q_heads, k_heads, preferred_element_type=jnp.float32)
        * score_scale
    )
    return jnp.where(allowed[None, :, :], scores, -1e30)


def adamw_step(weight, first, second, grad, factor, rate):
    clipped = grad * factor
    first_new = beta_one * first + (1.0 - beta_one) * clipped
    second_new = beta_two * second + (1.0 - beta_two) * clipped * clipped
    first_hat = first_new / (1.0 - beta_one**STEP)
    second_hat = second_new / (1.0 - beta_two**STEP)
    weight_new = weight - rate * (
        first_hat / (jnp.sqrt(second_hat) + adam_eps) + decay_rate * weight
    )
    return (weight_new, first_new, second_new)


def on_device(
    latents,
    media,
    frame_counts,
    cotangent,
    w_qkv,
    m_qkv,
    v_qkv,
    w_out,
    m_out,
    v_out,
    w_up,
    m_up,
    v_up,
    w_down,
    m_down,
    v_down,
    time_table,
    m_time,
    v_time,
    gains,
    m_gains,
    v_gains,
):
    low_qkv = w_qkv.astype(jnp.bfloat16)
    low_out = w_out.astype(jnp.bfloat16)
    low_up = w_up.astype(jnp.bfloat16)
    low_down = w_down.astype(jnp.bfloat16)
    low_time = time_table.astype(jnp.bfloat16)
    low_gains = gains.astype(jnp.bfloat16)
    n_dp, n_fsdp = lax.axis_size(DP), lax.axis_size(FSDP)
    own_rows = w_qkv.shape[0]
    item_slots, lat_count, model_width = latents.shape
    frame_slots, patch_rows, _ = media.shape
    queries_n, media_rows = item_slots * lat_count, frame_slots * patch_rows
    frame_owner, time_hot = frame_tables(frame_counts, frame_slots, time_table.shape[1])
    query_owner = jnp.arange(queries_n, dtype=jnp.int32) // lat_count
    key_owner = jnp.concatenate([jnp.repeat(frame_owner, patch_rows), query_owner], axis=0)
    allowed = query_owner[:, None] == key_owner[None, :]
    lows = (low_qkv, low_out, low_up, low_down, low_time, low_gains)
    if fits_kernels(n_dp, n_fsdp, w_qkv, w_up, w_down, queries_n, frame_slots, patch_rows):
        new_latents, d_latents, grad_norm, reduced = by_kernels(lows, latents, media, cotangent, time_hot, allowed, n_fsdp // 2)
    else:
        new_latents, d_latents, grad_norm, reduced = by_collectives(lows, latents, media, cotangent, time_hot, allowed)
    factor = jnp.minimum(1.0, clip_limit / (grad_norm + 1e-06))
    masters = (w_qkv, w_out, w_up, w_down, time_table, gains)
    firsts = (m_qkv, m_out, m_up, m_down, m_time, m_gains)
    seconds = (v_qkv, v_out, v_up, v_down, v_time, v_gains)
    rates = (0.02, 0.1, 0.02, 0.01, 0.2, 0.5)
    updated = []
    for index in range(6):
        updated.extend(adamw_step(masters[index], firsts[index], seconds[index], reduced[index], factor, rates[index]))
    return (new_latents, d_latents, grad_norm, *updated)


def fits_kernels(n_dp, n_fsdp, w_qkv, w_up, w_down, queries_n, frame_slots, patch_rows):
    rows, _, model = w_qkv.shape
    return (
        n_dp == 4 and n_fsdp == 8 and rows == 48 and model == 1536 and w_up.shape[1] == 4 * model and w_down.shape[0] == 192
        and queries_n == 256 and patch_rows == 48 and frame_slots % 3 == 0
    )


def by_kernels(lows, latents, media, cotangent, time_hot, allowed, n_z):
    low_qkv, low_out, low_up, low_down, low_time, low_gains = lows
    own_rows, _, model = low_qkv.shape
    time_len = low_time.shape[1]
    queries_n = allowed.shape[0]
    frame_slots, patch_rows, _ = media.shape
    tiny = jnp.concatenate([low_time, low_gains], axis=1)
    shards = [low_qkv.reshape(own_rows, -1), low_out, low_up, low_down, jnp.pad(tiny, ((0, 0), (0, 128 - tiny.shape[1])))]
    hot = jnp.pad(jnp.repeat(time_hot, patch_rows, axis=0), ((0, 0), (0, 128 - time_len))).astype(jnp.bfloat16)
    hotc = jnp.broadcast_to(time_hot[:, :, None], time_hot.shape + (128,))
    bias = jnp.where(allowed.T, 0.0, -1e30).astype(jnp.float32)
    lat = latents.reshape(queries_n, model)
    med = media.reshape(frame_slots * patch_rows, model)
    full, made = forward_all(shards, lat, med, cotangent.reshape(queries_n, model), hot, bias, n_z)
    own = backward_all(full, made, lat, med, hot, hotc, bias, shards, n_z)
    small = own.g_tiny
    reduced = (
        own.g_qkv.reshape(low_qkv.shape), own.g_out, own.g_up, own.g_down, small[:, :time_len], small[:, time_len : time_len + 3]
    )
    return made[5].reshape(latents.shape), own.d_lat.reshape(latents.shape), jnp.sqrt(jnp.sum(own.norm)), reduced


def by_collectives(lows, latents, media, cotangent, time_hot, allowed):
    full_qkv, full_out, full_up, full_down, full_time, full_gains = gather_params(*lows)
    item_slots, lat_count, model_width = latents.shape
    frame_slots, patch_rows, unused_width = media.shape
    queries_n = item_slots * lat_count
    media_rows = frame_slots * patch_rows
    head_size = model_width // HEADS
    score_scale = 1.0 / head_size**0.5
    time_f32 = full_time.astype(jnp.float32)
    gains_f32 = full_gains.astype(jnp.float32)
    frame_time = jnp.dot(time_hot, time_f32.T, precision=highest)
    mixed = media.astype(jnp.float32) + frame_time[:, None, :]
    media_norm, media_back = jax.vjp(layer_norm, mixed, gains_f32[:, 0])
    media_low = media_norm.astype(jnp.bfloat16).reshape(media_rows, model_width)
    lat_rows = latents.reshape(queries_n, model_width).astype(jnp.float32)
    lat_norm, lat_back = jax.vjp(layer_norm, lat_rows, gains_f32[:, 1])
    lat_low = lat_norm.astype(jnp.bfloat16)
    keys_in = jnp.concatenate([media_low, lat_low], axis=0)
    key_rows = keys_in.shape[0]
    qkv_flat = full_qkv.reshape(model_width, 3 * model_width)
    queries = jnp.dot(
        lat_low, qkv_flat[:, :model_width], preferred_element_type=jnp.float32
    ).astype(jnp.bfloat16)
    key_value = jnp.dot(
        keys_in, qkv_flat[:, model_width:], preferred_element_type=jnp.float32
    ).astype(jnp.bfloat16)
    q_heads = queries.reshape(queries_n, HEADS, head_size)
    k_heads = key_value[:, :model_width].reshape(key_rows, HEADS, head_size)
    v_heads = key_value[:, model_width:].reshape(key_rows, HEADS, head_size)
    scores = masked_scores(q_heads, k_heads, allowed, score_scale)
    row_top = jnp.max(scores, axis=-1, keepdims=True)
    row_total = jnp.sum(jnp.exp(scores - row_top), axis=-1, keepdims=True)
    log_total = row_top + jnp.log(row_total)
    probs_low = jnp.exp(scores - log_total).astype(jnp.bfloat16)
    attended = jnp.einsum("hqk,khe->qhe", probs_low, v_heads, preferred_element_type=jnp.float32)
    attended = attended.reshape(queries_n, model_width).astype(jnp.bfloat16)
    middle = lat_rows + jnp.dot(attended, full_out, preferred_element_type=jnp.float32)
    hidden, ffn_back = jax.vjp(layer_norm, middle, gains_f32[:, 2])
    hidden_low = hidden.astype(jnp.bfloat16)
    pre_act = jnp.dot(hidden_low, full_up, preferred_element_type=jnp.float32)
    activated, gelu_back = jax.vjp(exact_gelu, pre_act)
    act_low = activated.astype(jnp.bfloat16)
    result = middle + jnp.dot(act_low, full_down, preferred_element_type=jnp.float32)
    new_latents = result.astype(jnp.bfloat16).reshape(item_slots, lat_count, model_width)
    d_result = cotangent.reshape(queries_n, model_width)
    g_down = jnp.einsum("qf,qd->fd", act_low, d_result, preferred_element_type=jnp.float32)
    d_act = jnp.einsum("qd,fd->qf", d_result, full_down, preferred_element_type=jnp.float32)
    d_pre = gelu_back(d_act)[0].astype(jnp.bfloat16)
    g_up = jnp.einsum("qd,qf->df", hidden_low, d_pre, preferred_element_type=jnp.float32)
    d_hidden = jnp.einsum("qf,df->qd", d_pre, full_up, preferred_element_type=jnp.float32)
    d_middle_ln, g_gain_ffn = ffn_back(d_hidden)
    d_middle = d_result.astype(jnp.float32) + d_middle_ln
    d_branch = d_middle.astype(jnp.bfloat16)
    g_out = jnp.einsum("qe,qd->ed", attended, d_branch, preferred_element_type=jnp.float32)
    d_attended = jnp.einsum(
        "qd,ed->qe", d_branch, full_out, preferred_element_type=jnp.float32
    ).astype(jnp.bfloat16)
    scores_again = masked_scores(q_heads, k_heads, allowed, score_scale)
    probs = jnp.exp(scores_again - log_total)
    probs_again = probs.astype(jnp.bfloat16)
    d_att_heads = d_attended.reshape(queries_n, HEADS, head_size)
    d_probs = jnp.einsum("qhe,khe->hqk", d_att_heads, v_heads, preferred_element_type=jnp.float32)
    row_dot = jnp.sum(probs * d_probs, axis=-1, keepdims=True)
    d_scores = (probs * (d_probs - row_dot)).astype(jnp.bfloat16)
    d_queries = (
        (
            jnp.einsum("hqk,khe->qhe", d_scores, k_heads, preferred_element_type=jnp.float32)
            * score_scale
        )
        .reshape(queries_n, model_width)
        .astype(jnp.bfloat16)
    )
    d_keys = (
        (
            jnp.einsum("hqk,qhe->khe", d_scores, q_heads, preferred_element_type=jnp.float32)
            * score_scale
        )
        .reshape(key_rows, model_width)
        .astype(jnp.bfloat16)
    )
    d_values = (
        jnp.einsum("hqk,qhe->khe", probs_again, d_att_heads, preferred_element_type=jnp.float32)
        .reshape(key_rows, model_width)
        .astype(jnp.bfloat16)
    )
    g_query = jnp.einsum("qd,qe->de", lat_low, d_queries, preferred_element_type=jnp.float32)
    d_key_value = jnp.concatenate([d_keys, d_values], axis=1)
    g_key_value = jnp.einsum("kd,kx->dx", keys_in, d_key_value, preferred_element_type=jnp.float32)
    g_qkv = jnp.concatenate([g_query, g_key_value], axis=1).reshape(model_width, 3, model_width)
    back_flat = full_qkv.reshape(model_width, 3 * model_width)
    d_keys_in = jnp.einsum(
        "kx,dx->kd", d_key_value, back_flat[:, model_width:], preferred_element_type=jnp.float32
    )
    d_lat_norm = (
        jnp.einsum(
            "qe,de->qd", d_queries, back_flat[:, :model_width], preferred_element_type=jnp.float32
        )
        + d_keys_in[media_rows:]
    )
    d_lat_ln, g_gain_lat = lat_back(d_lat_norm)
    d_latents = (d_middle + d_lat_ln).reshape(item_slots, lat_count, model_width)
    d_mixed, g_gain_media = media_back(
        d_keys_in[:media_rows].reshape(frame_slots, patch_rows, model_width)
    )
    frame_grad = jnp.sum(d_mixed, axis=1)
    g_time = jnp.einsum("fd,ft->dt", frame_grad, time_hot, precision=highest)
    g_gains = jnp.stack([g_gain_media, g_gain_lat, g_gain_ffn], axis=1)
    reduced = reduce_grads(g_qkv, g_out, g_up, g_down, g_time, g_gains)
    local_sq = jnp.zeros((), jnp.float32)
    for grad in reduced:
        local_sq = local_sq + jnp.sum(grad * grad)
    grad_norm = jnp.sqrt(lax.psum(local_sq, (DP, FSDP)))
    return new_latents, d_latents, grad_norm, reduced


def solution(mesh):
    both = (DP, FSDP)
    one, two, three = P(both), P(both, None), P(both, None, None)
    updated = (three,) * 3 + (two,) * 15
    placed = (three, three, one, three, *updated)
    return jax.shard_map(
        on_device,
        mesh=mesh,
        in_specs=placed,
        out_specs=(three, three, P(), *updated),
        check_vma=False,
    )
```

```python
import functools
import math
import types

import jax
import jax.numpy as jnp
from jax import lax
from jax.experimental import pallas as pl
from jax.experimental.pallas import tpu as pltpu
from jax.sharding import PartitionSpec as P

DP, FSDP = "dp", "fsdp"
HEADS = 16
STEP = 10


highest = lax.Precision.HIGHEST
norm_eps = 1e-05
clip_limit = 1.0
beta_one = 0.9
beta_two = 0.999
adam_eps = 1e-08
decay_rate = 0.1

MESH=pl.DeviceIdType.MESH
ANY=pl.ANY

class Place:
    def __init__(self, n_z):
        dp = lax.axis_index(DP); fs = lax.axis_index(FSDP)
        self.n_z = n_z
        self.at = {"x": dp // 2, "c": dp % 2, "z": fs // 2, "y": fs % 2}
    def dev(self, **new):
        p = {**self.at, **new}
        return (p["x"] * 2 + p["c"], p["z"] * 2 + p["y"])
    def other(self, ax):
        return self.dev(**{ax: 1 - self.at[ax]})
    def along_z(self, k):
        return self.dev(z=(self.at["z"] + k) % self.n_z)
    def partners(self):
        return [self.other(a) for a in "cxy"] + [self.along_z(k) for k in range(1, self.n_z)]

def greet(place):
    bar = pltpu.get_barrier_semaphore()
    others = place.partners()
    for d in others:
        pl.semaphore_signal(bar, inc=1, device_id=d, device_id_type=MESH)
    pl.semaphore_wait(bar, len(others))

def block_index(place, held, **at):
    where = {**place.at, **at}
    return tuple(slice(None) if ax in held else where[ax] for ax in "xczy")

class Gather:
    def __init__(self, place, src, dst, rows, cols, order, sems, base):
        self.place, self.src, self.dst = place, src, dst
        self.sl = (pl.ds(*rows), pl.ds(*cols))
        self.order, self.sems, self.base = order, sems, base
        self.copies = {}

    def region(self, held, **at):
        return self.dst.at[block_index(self.place, held, **at) + self.sl]

    def copy(self, src, dst, n, to):
        ss, rs = self.sems
        n += self.base
        return pltpu.make_async_remote_copy(src_ref=src, dst_ref=dst, send_sem=ss.at[n], recv_sem=rs.at[n], device_id=to, device_id_type=MESH)

    def start(self, step):
        ax, held, p = self.order[step], self.order[:step], self.place
        if ax == "z":
            self.line(step, 1)
            return
        d = self.copy(self.src.at[self.sl] if step == 0 else self.region(held), self.region(held), "xyc".index(ax), p.other(ax))
        d.start()
        self.copies[step] = d

    def line(self, step, k):
        p, held = self.place, self.order[:step]
        z, last = p.at["z"], p.n_z - 1
        for side, from_z, to_z in ((0, z - (k - 1), z + 1), (1, z + (k - 1), z - 1)):
            ok = (from_z >= 0) & (to_z <= last) if side == 0 else (from_z <= last) & (to_z >= 0)
            at = jnp.clip(from_z, 0, last)
            dst = self.region(held, z=at)
            src = self.src.at[self.sl] if step == 0 and k == 1 else dst
            d = self.copy(src, dst, 3 + 2 * (k - 1) + side, p.dev(z=jnp.clip(to_z, 0, last)))
            pl.when(ok)(d.start)
            came = z >= k if side == 0 else z + k <= last
            self.copies[step, k, side] = (d, ok, came)

    def came(self, step, k):
        for side in range(2):
            d, _, came = self.copies[step, k, side]
            pl.when(came)(d.wait_recv)

    def advance(self, step, k):
        if self.order[step] == "z":
            self.came(step, k)
            self.line(step, k + 1)

    def arrive(self, step):
        if self.order[step] == "z":
            self.came(step, self.place.n_z - 1)
        else:
            self.copies[step].wait_recv()

    def finish(self):
        for key, d in self.copies.items():
            if isinstance(key, tuple):
                pl.when(d[1])(d[0].wait_send)
            else:
                d.wait_send()


def n_sems(n_z):
    return 3 + 2 * (n_z - 1)


def number(plan):
    j, out = 0, []
    for stage in plan:
        new = []
        for piece in stage:
            new.append((j,) + piece); j += 1
        out.append(new)
    return out, j

ZYX, ZXY, XYZ, YXZ = ("z", "y", "x", "c"), ("z", "x", "y", "c"), ("x", "y", "z", "c"), ("y", "x", "z", "c")

BACK_LAG, SEND_SLOTS, LAND_SLOTS = 2, 3, 6
ROOM_B = 4
FINE_B = 0


class Scatter:
    def __init__(self, place, out, rows, cols, order, piece, turn, sems, bufs, total_sq):
        self.p, self.out, self.order, self.piece = place, out, order, piece
        self.rows, self.cols, self.width = pl.ds(*rows), pl.ds(*cols), cols[1]
        self.ss, self.rs, self.ls = sems
        self.b, self.sq = bufs, total_sq
        self.turn, self.h, self.n = turn, turn % SEND_SLOTS, turn % LAND_SLOTS
        self.sent, self.moves = {}, {}

    def v(self, ref, *lead):
        return ref.at[lead + (slice(None), pl.ds(0, self.width))]

    def copy(self, src, dst, to, n):
        n += self.piece * n_sems(self.p.n_z)
        return pltpu.make_async_remote_copy(src_ref=src, dst_ref=dst, send_sem=self.ss.at[n], recv_sem=self.rs.at[n], device_id=to, device_id_type=MESH)

    def send(self, step, src, dst, ax):
        d = self.copy(src, dst, self.p.other(ax), "xyc".index(ax))
        d.start()
        self.sent[step] = d

    def add(self, count, dst, a, b):
        w = slice(0, self.width)

        def one(i, carry):
            (da, di), (aa, ai), (ba, bi) = dst(i), a(i), b(i)
            da[di + (slice(None), w)] = aa[ai + (slice(None), w)] + ba[bi + (slice(None), w)]
            return carry

        if count == 1:
            one(0, 0)
        else:
            lax.fori_loop(0, count, one, 0)

    def row(self, d):
        if self.order[0] == "z":
            return self.v(self.b.s0, self.h, slice(None), d, slice(None))
        return self.v(self.b.s2, self.h, d)

    def land(self, side, k):
        if self.order[0] == "z":
            return self.v(self.b.rz, self.n, side, k - 1, slice(None), slice(None))
        return self.v(self.b.rz, self.n, side, k - 1)

    def add_landed(self, d, side, k):
        b, h, n = self.b, self.h, self.n
        if self.order[0] == "z":
            mine = lambda i: (b.s0, (h, i // 2, d, i % 2))
            self.add(4, mine, mine, lambda i: (b.rz, (n, side, k - 1, i // 2, i % 2)))
        else:
            mine = lambda i: (b.s2, (h, d))
            self.add(1, mine, mine, lambda i: (b.rz, (n, side, k - 1)))

    def line(self, step, k):
        p = self.p
        z, last = p.at["z"], p.n_z - 1
        for side, d, to in ((0, p.n_z - k + z, z + 1), (1, z - (p.n_z - k), z - 1)):
            ok = d <= last if side == 0 else d >= 0
            at = jnp.clip(d, 0, last)
            if k > 1:
                got, _, came = self.moves[step, k - 1, side]

                def forward(got=got, at=at, side=side):
                    got.wait_recv()
                    self.add_landed(at, side, k - 1)

                pl.when(came)(forward)
            c = self.copy(self.row(at), self.land(side, k), p.dev(z=jnp.clip(to, 0, last)), 3 + 2 * (k - 1) + side)
            pl.when(ok)(c.start)
            came = z <= k if side == 0 else z >= last - k
            came = came & (z > 0 if side == 0 else z < last)
            self.moves[step, k, side] = (c, ok, came)

    def last_move(self, step):
        p = self.p
        z, k = p.at["z"], p.n_z - 1
        for side in range(2):
            c, _, came = self.moves[step, k, side]

            def end(c=c, side=side):
                c.wait_recv()
                self.add_landed(z, side, k)

            pl.when(came)(end)

    def advance(self, step, k):
        if self.order[step] == "z":
            self.line(step, k + 1)

    def free(self, step):
        if step == 3:
            self.sent.pop(3).wait()
        elif self.order[step] == "z":
            for k in range(1, self.p.n_z):
                for side in range(2):
                    c, ok, _ = self.moves.pop((step, k, side))
                    pl.when(ok)(c.wait_send)
        else:
            self.sent.pop(step).wait_send()

    def start(self, step):
        p, b, A, h, n, nz = self.p, self.b, slice(None), self.h, self.n, self.p.n_z
        at = p.at
        if step < 3 and self.order[step] == "z":
            if step == 2:
                first, nxt = self.order[:2]
                mine = (lambda i: (b.s1, (h, i, at[nxt]))) if first == "x" else (lambda i: (b.s1, (h, at[nxt], i)))
                self.sent[1].wait_recv()
                self.add(nz, lambda i: (b.s2, (h, i)), mine, lambda i: (b.r2, (n, i)))
            self.line(step, 1)
            return
        first = self.order[0]
        if step == 0:
            o = 1 - at[first]
            src = self.v(b.s0, h, o, A, A) if first == "x" else self.v(b.s0, h, A, A, o)
            self.send(0, src, self.v(b.r1, n, A, A), first)
        elif step == 1 and first == "z":
            self.last_move(0)
            for x in range(2):
                b.s1[h, x] = b.s0[h, x, at["z"]]
            self.send(1, self.v(b.s1, h, 1 - at["x"], A), self.v(b.r1, n, A), "x")
        elif step == 1:
            self.sent[0].wait_recv()
            o = 1 - at[self.order[1]]
            i0, i1 = (lambda i: i // 2), (lambda i: i % 2)
            if first == "y":
                i0, i1 = (lambda i: i // nz), (lambda i: i % nz)
                mine = lambda i: (b.s0, (h, i0(i), i1(i), at["y"]))
            else:
                mine = lambda i: (b.s0, (h, at["x"], i0(i), i1(i)))
            self.add(2 * nz, lambda i: (b.s1, (h, i0(i), i1(i))), mine, lambda i: (b.r1, (n, i0(i), i1(i))))
            src = self.v(b.s1, h, A, o) if first == "x" else self.v(b.s1, h, o, A)
            self.send(1, src, self.v(b.r2, n, A), self.order[1])
        elif step == 2:
            self.sent[1].wait_recv()
            self.add(2, lambda i: (b.s2, (h, i)), lambda i: (b.s1, (h, at["x"], i)), lambda i: (b.r1, (n, i)))
            self.send(2, self.v(b.s2, h, 1 - at["y"]), self.v(b.r2, n), "y")
        else:
            w = slice(0, self.width)
            if first == "z":
                self.sent[2].wait_recv()
                total = b.s2[h, at["y"], :, w].astype(jnp.float32) + b.r2[n, :, w].astype(jnp.float32)
            else:
                p_last = nz - 1
                for side in range(2):
                    c, _, came = self.moves[2, p_last, side]
                    pl.when(came)(c.wait_recv)
                total = b.s2[h, at["z"], :, w].astype(jnp.float32)
                for side in range(2):
                    came = self.moves[2, p_last, side][2]
                    landed = b.rz[n, side, p_last - 1, :, w].astype(jnp.float32)
                    total = total + jnp.where(came, landed, 0.0)
            b.o[h, :, w] = total
            self.sq[:, w] += total * total
            d = pltpu.make_async_copy(self.v(b.o, h), self.out.at[self.rows, self.cols], self.ls.at[self.piece])
            d.start()
            self.sent[3] = d


def sum_squares(place, n_z, bufs, sems, out):
    ns, nr = sems
    sq, part, zs = bufs.sq, bufs.n, bufs.nz
    acc = jnp.zeros((8, 128), jnp.float32)
    for i in range(sq.shape[0] // 8):
        for j in range(sq.shape[1] // 128):
            acc = acc + sq[i * 8 : (i + 1) * 8, j * 128 : (j + 1) * 128]
    for n, ax in enumerate("cxy"):
        part[2 * n] = acc
        d = pltpu.make_async_remote_copy(src_ref=part.at[2 * n], dst_ref=part.at[2 * n + 1], send_sem=ns.at[n], recv_sem=nr.at[n], device_id=place.other(ax), device_id_type=MESH)
        d.start()
        d.wait()
        acc = part[2 * n] + part[2 * n + 1]
    z = place.at["z"]
    zs[z] = acc
    made = []
    for k in range(1, n_z):
        d = pltpu.make_async_remote_copy(src_ref=zs.at[z], dst_ref=zs.at[z], send_sem=ns.at[2 + k], recv_sem=nr.at[2 + k], device_id=place.along_z(k), device_id_type=MESH)
        d.start()
        made.append(d)
    for d in made:
        d.wait()
    total = zs[0]
    for k in range(1, n_z):
        total = total + zs[k]
    out[...] = total


def backward_kernel(n_z, plan, names, *refs):
    b = types.SimpleNamespace(**dict(zip(names, refs)))
    ss, rs, ls, ns, nr, ws, ps, pr, lt_sem, rhs_sem, out_sem = refs[len(names) :]
    own_grads = (b.g_qkv, b.g_out, b.g_up, b.g_down, b.g_tiny)
    place = Place(n_z)
    greet(place)
    core, A = place.at["c"], slice(None)
    queries_n, model = b.q.shape
    key_rows = b.keys.shape[0]
    media_rows = key_rows - queries_n
    hidden_n = b.dpre.shape[1]
    head = model // HEADS
    windows, group_width = head_windows(head)
    scale = 1.0 / head**0.5
    f32, bf = jnp.float32, jnp.bfloat16
    b.sq[...] = jnp.zeros_like(b.sq)
    given = {}

    def give(src, dst):
        n = len(given)
        d = pltpu.make_async_remote_copy(src_ref=src, dst_ref=dst, send_sem=ps.at[n], recv_sem=pr.at[n], device_id=place.other("c"), device_id_type=MESH)
        d.start()
        given[id(dst)] = [d, False]

    def got(dst):
        held_copy = given[id(dst)]
        if not held_copy[1]:
            held_copy[0].wait_recv()
            held_copy[1] = True

    give(b.dpre, b.x_dpre)
    keys_in = pltpu.make_async_copy(b.keys, b.k, out_sem.at[1])
    keys_in.start()

    wbuf = b.wbuf

    def fetch(src, slot):
        d = pltpu.make_async_copy(src, wbuf.at[slot], ws.at[slot])
        d.start()
        return d

    def tiles_of(jobs, use):
        ahead = fetch(jobs[0], 0)
        for i in range(len(jobs)):
            now = ahead
            if i + 1 < len(jobs):
                ahead = fetch(jobs[i + 1], (i + 1) % 2)
            now.wait()
            use(i, wbuf[i % 2].reshape(384, model))

    def hidden_part(i):
        d = pltpu.make_async_copy(b.dpre.at[:, pl.ds(i * model, model)], b.datt, ws.at[4])
        d.start()
        d.wait()

        def use(n, w):
            got_ = dot(b.datt[...], w, ((1,), (1,)))
            cols = slice(n * 384, (n + 1) * 384)
            if i == 0:
                b.dmid[:, cols] = got_
            else:
                b.dmid[:, cols] += got_

        tiles_of([b.f_up.at[x, c, :, :, :, pl.ds(i * model, model)] for x in range(2) for c in range(2)], use)

    def norm_back(rows_in, grad, gain):
        centered = rows_in - jnp.mean(rows_in, axis=-1, keepdims=True)
        inv = lax.rsqrt(jnp.mean(centered * centered, axis=-1, keepdims=True) + norm_eps)
        hat = centered * inv
        scaled = grad * gain
        back = inv * (scaled - jnp.mean(scaled, axis=-1, keepdims=True) - hat * jnp.mean(scaled * hat, axis=-1, keepdims=True))
        return back, jnp.sum(grad * hat, axis=0, keepdims=True)

    def ffn_norm():
        d = pltpu.make_async_copy(b.f_tiny, b.tiny, ws.at[3])
        d.start()
        e = pltpu.make_async_copy(b.p_cot.at[core], b.dbranch, ws.at[4])
        e.start()
        d.wait()
        e.wait()
        b.tiny_t[...] = b.tiny[...].reshape(model, 128).astype(f32).T
        b.gsmall[...] = jnp.zeros_like(b.gsmall)

        def rows(i, carry):
            at = pl.ds(pl.multiple_of(i * 64, 64), 64)
            back, gain = norm_back(b.mid[at, :], b.dmid[at, :], b.tiny_t[10:11, :])
            total = b.dbranch[at, :].astype(f32) + back
            b.dmid[at, :] = total
            b.dbranch[at, :] = total.astype(bf)
            b.gsmall[10:11, :] += gain
            return carry

        lax.fori_loop(0, queries_n // 64, rows, 0)
        give(b.dbranch, b.x_branch)

    def attended_back():
        def use(n, w):
            b.datt[:, n * 384 : (n + 1) * 384] = dot(b.dbranch[...], w, ((1,), (1,))).astype(bf)

        tiles_of([b.f_out.at[x, c] for x in range(2) for c in range(2)], use)

    def attend_back(g):
        if g == 0:
            keys_in.wait()
        base = g * group_width
        n_tiles = group_width // 128
        last = {t: max(j for j, (t0, t1, _) in enumerate(windows) if t0 <= t < t1) for t in range(n_tiles)}
        sums = {}
        for j, (t0, t1, start) in enumerate(windows):
            cols = slice(base + t0 * 128, base + t1 * 128)
            q_in, k_in = lanes_of(queries_n, t1 - t0, start, head), lanes_of(key_rows, t1 - t0, start, head)
            qh = b.q[:, cols]
            qh = jnp.where(q_in, qh, jnp.zeros_like(qh))
            dah = b.datt[:, cols]
            dah = jnp.where(q_in, dah, jnp.zeros_like(dah))
            kw = b.k[:, cols]
            h = g * len(windows) + j
            p = jnp.exp(dot(kw, qh, ((1,), (1,))) * scale + b.bias[...] - b.lse[h : h + 1, :])
            dp = dot(b.v[:, cols], dah, ((1,), (1,)))
            row_dot = jnp.sum(p * dp, axis=0, keepdims=True)
            ds = (p * (dp - row_dot)).astype(bf)
            kh = jnp.where(k_in, kw, jnp.zeros_like(kw))
            parts = ((b.dv, dot(p.astype(bf), dah)), (b.dk, dot(ds, qh) * scale), (b.dq, dot(ds, kh, ((0,), (0,))) * scale))
            for n, (into, part) in enumerate(parts):
                for t in range(t0, t1):
                    new = part[:, (t - t0) * 128 : (t - t0 + 1) * 128]
                    sums[n, t] = sums[n, t] + new if (n, t) in sums else new
                    if last[t] == j:
                        into[:, base + t * 128 : base + (t + 1) * 128] = sums.pop((n, t)).astype(bf)
        if g == model // group_width - 1:
            give(b.dq, b.x_dq)
            give(b.dk, b.x_dk)
            give(b.dv, b.x_dv)

    def keys_back(n):
        x, c = n // 2, n % 2
        made = [fetch(b.f_qkv.at[x, c, :, :, :, pl.ds(i * model, model)], i) for i in range(3)]
        for d in made:
            d.wait()
        w = [wbuf[i].reshape(384, model) for i in range(3)]
        cols = slice(n * 384, (n + 1) * 384)
        lat_rows = slice(media_rows, key_rows)
        tail = dot(b.dq[...], w[0], ((1,), (1,))) + dot(b.dk[lat_rows, :], w[1], ((1,), (1,))) + dot(b.dv[lat_rows, :], w[2], ((1,), (1,)))
        b.k[lat_rows, cols] = tail.astype(bf)
        step = media_rows // 3
        for i in range(3):
            rows = slice(i * step, (i + 1) * step)
            b.k[rows, cols] = (dot(b.dk[rows, :], w[1], ((1,), (1,))) + dot(b.dv[rows, :], w[2], ((1,), (1,)))).astype(bf)

    def latents_back():
        def rows(i, carry):
            at = pl.ds(pl.multiple_of(i * 64, 64), 64)
            grad = b.k[pl.ds(pl.multiple_of(media_rows + i * 64, 16), 64), :].astype(f32)
            back, gain = norm_back(b.lat[at, :].astype(f32), grad, b.tiny_t[9:10, :])
            b.dmid[at, :] = b.dmid[at, :] + back
            b.gsmall[9:10, :] += gain
            return carry

        lax.fori_loop(0, queries_n // 64, rows, 0)
        d = pltpu.make_async_copy(b.dmid, b.d_lat, out_sem.at[0])
        d.start()
        late.append(d)

    late = []

    def media_back(part):
        step = media_rows // parts
        frames = step // 48
        d = pltpu.make_async_copy(b.media.at[pl.ds(part * step, step)], b.mrows, ws.at[3])
        d.start()
        d.wait()

        def frame(i, carry):
            at = pl.ds(pl.multiple_of(i * 48, 48), 48)
            whole = pl.ds(pl.multiple_of(part * step + i * 48, 48), 48)
            mixed = b.mrows[at, :].astype(f32) + dot(b.hot[whole, :], b.tiny_t[...].astype(bf))
            back, gain = norm_back(mixed, b.k[whole, :].astype(f32), b.tiny_t[8:9, :])
            b.gsmall[8:9, :] += gain
            b.gsmall[0:8, :] += b.hotc[part * frames + i][:, 0:1] * jnp.sum(back, axis=0, keepdims=True)
            return carry

        lax.fori_loop(0, frames, frame, 0)

    def small():
        b.tiny[...] = b.gsmall[...].T.astype(bf).reshape(b.tiny.shape)
        give(b.tiny.at[:, 1 - core], b.x_tiny)

    held = [None]

    def left(src):
        if held[0] is src:
            return
        held[0] = src
        if src is b.p_keys:
            into = b.ltk
        elif src is b.p_act:
            into = b.lt
        else:
            into = b.lt.at[:, :, pl.ds(0, 2 * n_z)]
        d = pltpu.make_async_copy(src, into, lt_sem.at[0])
        d.start()
        d.wait()

    coming = {}

    def sources(w, first):
        if w == 3:
            return b.p_cot.at[core], b.p_cot.at[1 - core], first
        if w == 2:
            return b.dpre, b.x_dpre, first
        if w == 1:
            return b.dbranch, b.x_branch, first
        return (b.dq, b.dk, b.dv)[first // model], (b.x_dq, b.x_dk, b.x_dv)[first // model], first % model

    def right(t):
        w, first, width = plan_of[t]
        if w == 4 or t in coming:
            return
        mine, theirs, at = sources(w, first)
        if w != 3:
            if id(theirs) not in given:
                return
            got(theirs)
        cols = pl.ds(at, width)
        made = []
        if w in (2, 3):
            made.append(pltpu.make_async_copy(mine.at[:, cols], b.rhs.at[t % 2, 0, :, pl.ds(0, width)], rhs_sem.at[t % 2, 0]))
        into = b.rhsk.at[:, pl.ds(0, width)] if w == 0 and first >= model else b.rhs.at[t % 2, 1, :, pl.ds(0, width)]
        made.append(pltpu.make_async_copy(theirs.at[:, cols], into, rhs_sem.at[t % 2, 1]))
        for d in made:
            d.start()
        coming[t] = made

    def blocks(x, k, group):
        if group == 1:
            return [b.lt[s, x, 0 : 2 * n_z].reshape(96 * n_z, queries_n) for s in (core, 1 - core)]
        return [jnp.concatenate([b.lt[s, x, i * group + k] for i in range(2 * n_z)], axis=0) for s in (core, 1 - core)]

    def fill(t, pieces):
        w, first, width = plan_of[t]
        h = pieces[0].h
        if w == 4:
            got(b.x_tiny)
            d = pltpu.make_async_copy(b.x_tiny, b.tiny2, ws.at[3])
            d.start()
            d.wait()

            def one(i, carry):
                x, z, y = i // (2 * n_z), (i // 2) % n_z, i % 2
                pieces[0].b.s0[h, x, z, y, :, 0:128] = b.tiny[x, core, z, y] + b.tiny2[x, z, y]
                return carry

            lax.fori_loop(0, 4 * n_z, one, 0)
            return
        right(t)
        for d in coming.pop(t):
            d.wait()
        mine, _, at = sources(w, first)
        keyed = w == 0 and first >= model
        left((b.p_keys if keyed else b.p_lat, b.p_att, b.p_hid, b.p_act)[w])
        r = [b.rhs[t % 2, 0, :, 0:width] if w in (2, 3) else mine[:, pl.ds(at, width)], b.rhsk[:, 0:width] if keyed else b.rhs[t % 2, 1, :, 0:width]]
        for x in range(2):
            if keyed:
                l = [b.ltk[s, x].reshape(96 * n_z, key_rows) for s in (core, 1 - core)]
            else:
                l = blocks(x, rows_of[t] // 48, 4 if w == 3 else 1)
            sums = (dot(l[0], r[0]) + dot(l[1], r[1])).astype(bf)
            start = 0
            for g in pieces:
                g.b.s0[h, x, :, :, :, 0 : g.width] = sums[:, start : start + g.width].reshape(n_z, 2, 48, g.width)
                start += g.width
        if t + 1 < total_stages:
            right(t + 1)

    parts = 6
    work = [(3, 5, functools.partial(hidden_part, i)) for i in range(hidden_n // model)] + [(0, 3, ffn_norm), (0, 4, attended_back)]
    work += [(0, 9, functools.partial(attend_back, g)) for g in range(model // group_width)]
    work += [(0, 5, functools.partial(keys_back, n)) for n in range(4)] + [(0, 3, latents_back)]
    work += [(0, 2, functools.partial(media_back, i)) for i in range(parts)] + [(0, 2, small)]

    def run_until(dst):
        while id(dst) not in given:
            work.pop(0)[2]()

    kinds = [types.SimpleNamespace(**{n: getattr(b, n + k) for n in NAMES}) for k in SETS]
    plan_of = [(st[0][1], st[0][3][0], sum(p[3][1] for p in st)) for st in plan]
    rows_of = [st[0][2][0] for st in plan]
    total_stages = len(plan)
    stages = [
        [Scatter(place, own_grads[w], rows, cols, order, j, t, (ss, rs, ls), kinds[part], b.sq) for part, (j, w, rows, cols, order) in enumerate(stage)]
        for t, stage in enumerate(plan)
    ]
    ticks = total_stages + 3 * BACK_LAG

    def moves(t, k):
        for back in range(3):
            u = t - BACK_LAG * back - 1
            if 0 <= u < total_stages:
                for g in stages[u]:
                    g.advance(back, k)

    for t in range(ticks):
        moves(t, 1)
        for back in range(4):
            u = t - BACK_LAG * back
            if not 0 <= u < total_stages:
                continue
            if u >= SEND_SLOTS:
                for g in stages[u - SEND_SLOTS]:
                    if back == 3 or g.order[back] == "z" or back in g.sent:
                        g.free(back)
            if back == 0:
                w = plan_of[u][0]
                run_until((b.x_dv, b.x_branch, b.x_dpre, b.x_dpre, b.x_tiny)[w])
                fill(u, stages[u])
            for g in stages[u]:
                g.start(back)
        for k in range(2, n_z - 1):
            moves(t, k)
        room = ROOM_B
        while work and room > 0:
            _, cost, piece = work.pop(0)
            room -= cost
            piece()
    for st in stages[-SEND_SLOTS:]:
        for g in st:
            for back in range(4):
                g.free(back)
    for d, done in given.values():
        d.wait_send()
    for d in late:
        d.wait()
    sum_squares(place, n_z, b, (ns, nr), b.norm)


SETS = "abc"
NAMES = ("s0", "r1", "s1", "r2", "s2", "rz", "o")


def backward_plan(shards, model):
    tile = 128
    stages = []

    def split(w, row, first, widths=None):
        widths = widths or ((3, 2, 1), (2, 3, 1))[len(stages) % 2]
        at, pieces = first, []
        for width, order in zip(widths, (("x", "y", "z"), ("y", "x", "z"), ("z", "x", "y"))):
            pieces.append((w, (row, 48), (at, width * tile), order))
            at += width * tile
        stages.append(pieces)

    for row in range(0, shards[3].shape[0], 48):
        for first in range(0, model, 768):
            split(3, row, first)
    for w, cols in ((2, shards[2].shape[1]), (1, model), (0, 3 * model)):
        for first in range(0, cols - FINE_B * 768 * (w == 0), 768):
            split(w, 0, first)
    for first in range(3 * model - FINE_B * 768, 3 * model, 384):
        split(0, 0, first, (1, 1, 1))
    return stages + [[(4, (0, 48), (0, 128), ("x", "y", "z"))]]


def backward_all(full, made, lat, media, hot, hotc, bias, shards, n_z):
    queries_n, model = lat.shape
    media_rows = media.shape[0]
    key_rows = queries_n + media_rows
    hidden_n = shards[2].shape[1]
    plan, count = number(backward_plan(shards, model))
    q, k, v, dpre, mid, new, lse, p_keys, p_lat, p_att, p_hid, p_act, p_cot = made
    given = dict(f_qkv=full[0], f_out=full[1], f_up=full[2], f_tiny=full[4], dpre=dpre, p_keys=p_keys, p_lat=p_lat, p_att=p_att, p_hid=p_hid, p_act=p_act, p_cot=p_cot,
                 media=media, q=q, keys=k, v=v, mid=mid, lse=lse, lat=lat, hot=hot, hotc=hotc, bias=bias)
    bf, f32 = jnp.bfloat16, jnp.float32
    grads = [((s.shape[0], s.shape[1]), f32) for s in shards]
    outs = dict(g_qkv=grads[0], g_out=grads[1], g_up=grads[2], g_down=grads[3], g_tiny=grads[4], d_lat=((queries_n, model), f32), norm=((8, 128), f32),
                x_dpre=((queries_n, hidden_n), bf), x_branch=((queries_n, model), bf), x_dq=((queries_n, model), bf), x_dk=((key_rows, model), bf), x_dv=((key_rows, model), bf),
                x_tiny=((2, n_z, 2, 48, 128), bf))
    W, S, L = 384, SEND_SLOTS, LAND_SLOTS
    vm = dict(s0a=((S, 2, n_z, 2, 48, W), bf), r1a=((L, n_z, 2, 48, W), bf), s1a=((S, n_z, 2, 48, W), bf), r2a=((L, n_z, 48, W), bf), s2a=((S, n_z, 48, W), bf), rza=((L, 2, n_z - 1, 48, W), bf), oa=((S, 48, W), f32),
              s0b=((S, 2, n_z, 2, 48, W), bf), r1b=((L, 2, n_z, 48, W), bf), s1b=((S, 2, n_z, 48, W), bf), r2b=((L, n_z, 48, W), bf), s2b=((S, n_z, 48, W), bf), rzb=((L, 2, n_z - 1, 48, W), bf), ob=((S, 48, W), f32),
              s0c=((S, 2, n_z, 2, 48, 128), bf), rzc=((L, 2, n_z - 1, 2, 2, 48, 128), bf), r1c=((L, 2, 48, 128), bf), s1c=((S, 2, 2, 48, 128), bf), s2c=((S, 2, 48, 128), bf), r2c=((L, 48, 128), bf), oc=((S, 48, 128), f32),
          sq=((48, W), f32), n=((6, 8, 128), f32), nz=((n_z, 8, 128), f32),
          wbuf=((3, n_z, 2, 48, model), bf), dmid=((queries_n, model), f32), dbranch=((queries_n, model), bf), datt=((queries_n, model), bf),
          dq=((queries_n, model), bf), k=((key_rows, model), bf), dk=((key_rows, model), bf), dv=((key_rows, model), bf), tiny=((2, 2, n_z, 2, 48, 128), bf), tiny_t=((128, model), f32),
          gsmall=((128, model), f32), tiny2=((2, n_z, 2, 48, 128), bf), mrows=((media_rows // 6, model), bf),
          lt=(p_act.shape, bf), ltk=(p_keys.shape, bf), rhs=((2, 2, queries_n, 768), bf), rhsk=((key_rows, 768), bf))
    sem = pltpu.SemaphoreType.DMA
    in_vmem, in_any = pl.BlockSpec(memory_space=pltpu.VMEM), pl.BlockSpec(memory_space=ANY)
    resident = tuple(id(a) for a in (q, v, mid, lse, lat, hot, hotc, bias))
    n_copies = count * n_sems(n_z)
    res = pl.pallas_call(
        functools.partial(backward_kernel, n_z, plan, (*given, *outs, *vm)),
        out_shape=[jax.ShapeDtypeStruct(*o) for o in outs.values()],
        in_specs=[in_vmem if id(a) in resident else in_any for a in given.values()],
        out_specs=[in_vmem if o is outs["norm"] else in_any for o in outs.values()],
        scratch_shapes=[pltpu.VMEM(*m) for m in vm.values()] + [sem((n_copies,)), sem((n_copies,)), sem((count,)), sem((n_z + 2,)), sem((n_z + 2,)), sem((5,)), sem((8,)), sem((8,)), sem((1,)), sem((2, 2)), sem((2,))],
        name="backward_and_scatter",
        compiler_params=pltpu.CompilerParams(collective_id=1, has_side_effects=True, vmem_limit_bytes=62 * 2**20),
    )(*given.values())
    return types.SimpleNamespace(**dict(zip(outs, res)))


def out_copies(pairs, sems, at, running):
    for src, dst in pairs:
        d = pltpu.make_async_copy(src, dst, sems.at[len(running)])
        d.start()
        running.append(d)


def dot(a, b, contract=((1,), (0,))):
    return lax.dot_general(a, b, (contract, ((), ())), preferred_element_type=jnp.float32)


def head_windows(head):
    group = 128 // math.gcd(head, 128)
    out = []
    for j in range(group):
        first, last = j * head // 128, ((j + 1) * head - 1) // 128
        out.append((first, last + 1, j * head - first * 128))
    return out, group * head


def lanes_of(rows, tiles, start, head):
    lane = lax.broadcasted_iota(jnp.int32, (rows, tiles * 128), 1)
    return (lane >= start) & (lane < start + head)


def normed(rows_in, gain):
    centered = rows_in - jnp.mean(rows_in, axis=-1, keepdims=True)
    var_row = jnp.mean(centered * centered, axis=-1, keepdims=True)
    return centered * lax.rsqrt(var_row + norm_eps) * gain


def forward_kernel(n_z, plan, needs, *refs):
    (sh, (lat, media, cot, hot, bias), full, outs, scratch) = refs[:5], refs[5:10], refs[10:15], refs[15:27], refs[27:]
    o_q, o_k, o_v, o_dpre, o_mid, o_new, o_lse, p_keys, p_lat, p_att, p_hid, p_act = outs[:12]
    p_cot, *scratch = scratch
    keys, q, k, v, att, hid, act, slope, dact, mid, new, tiny, tiny_t, lse, wbuf, wdown, flip, flip_keys, ss, rs, ls, os_, ws, ps, pr, pl_ = scratch
    f_qkv, f_out, f_up, f_down, f_tiny = full
    place = Place(n_z)
    greet(place)
    queries_n, model = lat.shape
    media_rows = media.shape[0]
    key_rows = media_rows + queries_n
    hidden_n = act.shape[1]
    head = model // HEADS
    windows, group_width = head_windows(head)
    scale = 1.0 / head**0.5
    written = []
    given = []
    core = place.at["c"]

    def give(src, dst, theirs):
        n = len(given)
        if theirs:
            d = pltpu.make_async_remote_copy(src_ref=src, dst_ref=dst, send_sem=ps.at[n], recv_sem=pr.at[n], device_id=place.other("c"), device_id_type=MESH)
        else:
            d = pltpu.make_async_copy(src, dst, pl_.at[n])
        d.start()
        given.append([d, theirs, False])
        return n

    def gone(n):
        d, theirs, done = given[n]
        if not done:
            d.wait_send() if theirs else d.wait()
            given[n][2] = True

    def turn(a, dst, slot, x, wide, before=()):
        made = []
        for n in before:
            gone(n)
        for theirs in (False, True):
            who = 1 - core if theirs else core
            for m in range(wide // 384):
                cols = pl.ds(pl.multiple_of((x * 2 + who) * wide + m * 384, 128), 384)
                flip[slot] = a[:, cols].T.reshape(8, 48, queries_n)
                made.append(give(flip.at[slot], dst.at[core, x, pl.ds(m * 8, 8)], theirs))
                slot += 1
        return made

    def load(src, dst):
        d = pltpu.make_async_copy(src, dst, ws.at[0])
        d.start()
        d.wait()

    def write(*pairs):
        out_copies(pairs, os_, 0, written)

    def norms():
        load(f_tiny, tiny)
        tiny_t[...] = tiny[...].reshape(model, 128).astype(jnp.float32).T
        give(cot, p_cot.at[core], False)
        give(cot, p_cot.at[core], True)
        hid[...] = normed(lat[...].astype(jnp.float32), tiny_t[9:10, :]).astype(jnp.bfloat16)
        keys[media_rows:key_rows, :] = hid[...]
        for x in range(2):
            turn(hid, p_lat, 2 * x, x, 384)

        def frame(i, carry):
            rows = pl.ds(pl.multiple_of(i * 48, 48), 48)
            mixed = media[rows, :].astype(jnp.float32) + dot(hot[rows, :], tiny_t[...].astype(jnp.bfloat16))
            keys[rows, :] = normed(mixed, tiny_t[8:9, :]).astype(jnp.bfloat16)
            return carry

        lax.fori_loop(0, media_rows // 48, frame, 0)

    key_turns = []

    def turn_keys(x):
        for n in key_turns:
            gone(n)
        for theirs in (False, True):
            who = 1 - core if theirs else core
            cols = pl.ds(pl.multiple_of((x * 2 + who) * 384, 128), 384)
            flip_keys[int(theirs)] = keys[:, cols].T.reshape(8, 48, key_rows)
            key_turns.append(give(flip_keys.at[int(theirs)], p_keys.at[core, x], theirs))

    def project(i, dst, first):
        load(f_qkv.at[:, :, :, :, :, pl.ds(i * model, model)], wbuf)

        def tile(n, carry):
            cols = pl.ds(pl.multiple_of(n * 256, 256), 256)
            w = wbuf[:, :, :, :, :, cols].reshape(model, 256)
            dst[:, cols] = dot(keys[first:key_rows, :], w).astype(jnp.bfloat16)
            return carry

        lax.fori_loop(0, model // 256, tile, 0)

    def project_q():
        project(0, q, media_rows)
        write((q, o_q))

    def project_k():
        project(1, k, 0)
        write((k, o_k))

    def project_v():
        project(2, v, 0)
        write((v, o_v))

    def attend(g):
        base = g * group_width
        tiles = [jnp.zeros((queries_n, 128), jnp.float32) for _ in range(group_width // 128)]
        for j, (t0, t1, start) in enumerate(windows):
            cols = slice(base + t0 * 128, base + t1 * 128)
            qh = q[:, cols]
            qh = jnp.where(lanes_of(queries_n, t1 - t0, start, head), qh, jnp.zeros_like(qh))
            s = dot(k[:, cols], qh, ((1,), (1,))) * scale + bias[...]
            top = jnp.max(s, axis=0, keepdims=True)
            e = jnp.exp(s - top)
            total = jnp.sum(e, axis=0, keepdims=True)
            p = (e * (1.0 / total)).astype(jnp.bfloat16)
            lse[g * len(windows) + j : g * len(windows) + j + 1, :] = top + jnp.log(total)
            vh = v[:, cols]
            vh = jnp.where(lanes_of(key_rows, t1 - t0, start, head), vh, jnp.zeros_like(vh))
            got = dot(p, vh, ((0,), (0,)))
            for t in range(t0, t1):
                tiles[t] = tiles[t] + got[:, (t - t0) * 128 : (t - t0 + 1) * 128]
        for t, tile in enumerate(tiles):
            att[:, base + t * 128 : base + (t + 1) * 128] = tile.astype(jnp.bfloat16)

    def project_out():
        write((lse, o_lse))
        for x in range(2):
            turn(att, p_att, 4 + 2 * x, x, 384)
        load(f_out, wbuf)

        def tile(n, carry):
            cols = pl.ds(pl.multiple_of(n * 256, 256), 256)
            w = wbuf[:, :, :, :, :, cols].reshape(model, 256)
            mid[:, cols] = lat[:, cols].astype(jnp.float32) + dot(att[...], w)
            return carry

        lax.fori_loop(0, model // 256, tile, 0)
        hid[...] = normed(mid[...], tiny_t[10:11, :]).astype(jnp.bfloat16)
        write((mid, o_mid))
        for x in range(2):
            hid_turns.extend(turn(hid, p_hid, 8 + 2 * x, x, 384))

    hid_turns = []
    act_turns = []

    def up(i):
        load(f_up.at[:, :, :, :, :, pl.ds(i * model, model)], wbuf)

        def tile(n, carry):
            cols = pl.ds(pl.multiple_of(n * 256, 256), 256)
            into = pl.ds(pl.multiple_of(i * model + n * 256, 256), 256)
            w = wbuf[:, :, :, :, :, cols].reshape(model, 256)
            x = dot(hid[...], w)
            cdf = 0.5 + 0.5 * lax.erf(x * 0.7071067811865476)
            act[:, into] = (x * cdf).astype(jnp.bfloat16)
            slope[:, into] = cdf + x * (jnp.exp(-0.5 * x * x) * 0.3989422804014327)
            return carry

        lax.fori_loop(0, model // 256, tile, 0)
        if i % 2 == 1:
            before = list(range(len(given))) if i == 1 else act_turns
            act_turns.extend(turn(act, p_act, 0, i // 2, model, before))

    def down(i, width):
        cols = slice(i * width, (i + 1) * width)
        load(f_down.at[:, :, :, :, :, pl.ds(i * width, width)], wdown)
        per = hidden_n // 4
        got = jnp.zeros((queries_n, width), jnp.float32)
        for b in range(4):
            w = wdown[b // 2, b % 2].reshape(per, width)
            got = got + dot(act[:, b * per : (b + 1) * per], w)
            back = dot(cot[:, cols], w, ((1,), (1,)))
            if i == 0:
                dact[:, b * per : (b + 1) * per] = back
            else:
                dact[:, b * per : (b + 1) * per] += back
        new[:, cols] = (mid[:, cols] + got).astype(jnp.bfloat16)

    def finish():
        def tile(n, carry):
            cols = pl.ds(pl.multiple_of(n * 512, 512), 512)
            act[:, cols] = (dact[:, cols] * slope[:, cols]).astype(jnp.bfloat16)
            return carry

        lax.fori_loop(0, hidden_n // 512, tile, 0)
        write((act, o_dpre), (new, o_new))
        for d in written:
            d.wait()
        for n, (d, theirs, done) in enumerate(given):
            gone(n)
            if theirs:
                d.wait_recv()

    work = [(needs["tiny"], 8, norms), (needs["q"], 4, project_q), (needs["k"], 8, project_k), (needs["v"], 8, project_v)]
    work[2:2] = [(needs["q"], 3, functools.partial(turn_keys, x)) for x in range(2)]
    work += [(needs["v"], 7, functools.partial(attend, g)) for g in range(model // group_width)]
    work += [(needs["out"], 5, project_out)]
    work += [(s, 6, functools.partial(up, i)) for i, s in enumerate(needs["up"])]
    work += [(s, 5, functools.partial(down, i, model // len(needs["down"]))) for i, s in enumerate(needs["down"])]
    work += [(needs["down"][-1], 5, finish)]
    locals_ = []
    for i in range(5):
        d = pltpu.make_async_copy(sh[i], full[i].at[block_index(place, ())], ls.at[i])
        d.start()
        locals_.append(d)
    stages = [[Gather(place, sh[w], full[w], rows, cols, order, (ss, rs), j * n_sems(n_z)) for (j, w, rows, cols, order) in stage] for stage in plan]
    waited = set()
    total, steps = len(stages), 4
    ticks = total + LAG * steps
    for t in range(ticks):
        for back in range(steps):
            u = t - LAG * back - 1
            if LAG > 1 and 0 <= u < total:
                for g in stages[u]:
                    g.advance(back, 1)
        for back in range(steps + 1):
            u = t - LAG * back
            if not 0 <= u < total:
                continue
            for g, (j, w, *_) in zip(stages[u], plan[u]):
                if back == 1 and w not in waited:
                    locals_[w].wait()
                    waited.add(w)
                if back > 0:
                    g.arrive(back - 1)
                if back < steps:
                    g.start(back)
        for move in range(1 if LAG == 1 else 2, n_z - 1):
            for back in range(steps):
                u = t - LAG * back - (LAG > 1)
                if 0 <= u < total:
                    for g in stages[u]:
                        g.advance(back, move)
        room = ROOM_A
        while work and work[0][0] <= t - LAG * steps and (room > 0 or t == ticks - 1):
            need, cost, piece = work.pop(0)
            room -= cost
            piece()
    for st in stages:
        for g in st:
            g.finish()


ROOM_A = 12
LAG = 2
FINE = 1
Z_DOWN = (1,)


def forward_plan(shards, model):
    def split(w, rows, first, widths, last):
        at, pieces = first, []
        for width, order in zip(widths, (ZYX, ZXY, last)):
            pieces.append((w, (0, rows), (at, width), order))
            at += width
        return pieces

    rows = shards[1].shape[0]
    stages, needs = [[(4, (0, rows), (0, 128), ZYX)]], {"tiny": 0}
    wide = model * 5 // 12, model * 5 // 12, model // 6
    for i, name in enumerate("qkv"):
        needs[name] = len(stages)
        stages.append(split(0, rows, i * model, wide, (XYZ, YXZ)[i % 2]))
    needs["out"] = len(stages)
    stages.append(split(1, rows, 0, wide, YXZ))
    needs["up"], needs["down"] = [], []
    for i in range(shards[2].shape[1] // model):
        needs["up"].append(len(stages))
        stages.append(split(2, rows, i * model, wide, (XYZ, YXZ)[i % 2]))
    groups = model // 256
    deep = shards[3].shape[0]
    for i in range(groups):
        if i >= groups - FINE:
            for half in range(2):
                cols = (i * 256 + half * 128, 128)
                stages.append([(3, (0, deep // 2), cols, ZYX), (3, (deep // 2, deep // 2), cols, ZXY)])
        else:
            pair = (XYZ, YXZ) if i in Z_DOWN else (ZYX, ZXY)
            stages.append([(3, (0, deep), (i * 256 + n * 128, 128), pair[n]) for n in range(2)])
        needs["down"].append(len(stages) - 1)
    return stages, needs


def forward_all(shards, lat, media, cot, hot, bias, n_z):
    model, hidden_n = lat.shape[1], shards[2].shape[1]
    stages, needs = forward_plan(shards, model)
    plan, count = number(stages)
    queries_n, media_rows = lat.shape[0], media.shape[0]
    key_rows = queries_n + media_rows
    bf, f32 = jnp.bfloat16, jnp.float32
    rows = shards[1].shape[0]
    part = (2, 2, 2 * n_z, 48)
    made = [((queries_n, model), bf), ((key_rows, model), bf), ((key_rows, model), bf), ((queries_n, hidden_n), bf), ((queries_n, model), f32), ((queries_n, model), bf), ((HEADS, queries_n), f32),
            (part + (key_rows,), bf), (part + (queries_n,), bf), (part + (queries_n,), bf), (part + (queries_n,), bf), ((2, 2, 2 * n_z * hidden_n // model, 48, queries_n), bf), ((2, queries_n, model), bf)]
    vm = [((key_rows, model), bf), ((queries_n, model), bf), ((key_rows, model), bf), ((key_rows, model), bf), ((queries_n, model), bf), ((queries_n, model), bf), ((queries_n, hidden_n), bf),
          ((queries_n, hidden_n), f32), ((queries_n, hidden_n), f32), ((queries_n, model), f32), ((queries_n, model), bf),
                     ((2, 2, n_z, 2, rows, 128), bf), ((128, model), f32), ((HEADS, queries_n), f32), ((2, 2, n_z, 2, rows, model), bf), ((2, 2, n_z, 2, shards[3].shape[0], 256), bf),
                     ((12, 8, 48, queries_n), bf), ((2, 8, 48, key_rows), bf)]
    sem = pltpu.SemaphoreType.DMA
    in_vmem, in_any = pl.BlockSpec(memory_space=pltpu.VMEM), pl.BlockSpec(memory_space=ANY)
    out = pl.pallas_call(
        functools.partial(forward_kernel, n_z, plan, needs),
        out_shape=[jax.ShapeDtypeStruct((2, 2, n_z, 2) + s.shape, s.dtype) for s in shards] + [jax.ShapeDtypeStruct(*m) for m in made],
        in_specs=[in_vmem] * 10,
        out_specs=[in_any] * (5 + len(made)),
        scratch_shapes=[pltpu.VMEM(*m) for m in vm] + [sem((count * n_sems(n_z),)), sem((count * n_sems(n_z),)), sem((5,)), sem((16,)), sem((1,)), sem((48,)), sem((48,)), sem((48,))],
        name="gather_and_forward",
        compiler_params=pltpu.CompilerParams(collective_id=0, has_side_effects=True, vmem_limit_bytes=60 * 2**20),
    )(*shards, lat, media, cot, hot, bias)
    return out[:5], out[5:]


def layer_norm(values_in, gain):
    mean_row = jnp.mean(values_in, axis=-1, keepdims=True)
    centered = values_in - mean_row
    var_row = jnp.mean(centered * centered, axis=-1, keepdims=True)
    return centered * lax.rsqrt(var_row + norm_eps) * gain


def exact_gelu(values_in):
    return jax.nn.gelu(values_in, approximate=False)


def frame_tables(counts, frame_slots, time_len):
    slot_total = counts.shape[0]
    order = jnp.arange(slot_total, dtype=jnp.int32)
    slot_ends = jnp.sum(jnp.where(order[None, :] <= order[:, None], counts[None, :], 0), axis=1)
    slot_starts = slot_ends - counts
    frame_ids = jnp.arange(frame_slots, dtype=jnp.int32)
    frame_owner = jnp.sum((frame_ids[:, None] >= slot_ends[None, :]).astype(jnp.int32), axis=1)
    slot_ids = jnp.arange(slot_total, dtype=jnp.int32)
    start_of = jnp.sum(
        jnp.where(frame_owner[:, None] == slot_ids[None, :], slot_starts[None, :], 0), axis=1
    )
    time_index = frame_ids - start_of
    live_frame = frame_owner < slot_total
    time_ids = jnp.arange(time_len, dtype=jnp.int32)
    time_hot = ((time_index[:, None] == time_ids[None, :]) & live_frame[:, None]).astype(
        jnp.float32
    )
    return (frame_owner, time_hot)


def gather_params(part_qkv, part_out, part_up, part_down, part_time, part_gains):
    inner_part = (
        lax.all_gather(part_qkv, FSDP, axis=0, tiled=True),
        lax.all_gather(part_out, FSDP, axis=0, tiled=True),
        lax.all_gather(part_up, FSDP, axis=0, tiled=True),
        lax.all_gather(part_down, FSDP, axis=0, tiled=True),
        lax.all_gather(part_time, FSDP, axis=0, tiled=True),
        lax.all_gather(part_gains, FSDP, axis=0, tiled=True),
    )
    return (
        lax.all_gather(inner_part[0], DP, axis=0, tiled=True),
        lax.all_gather(inner_part[1], DP, axis=0, tiled=True),
        lax.all_gather(inner_part[2], DP, axis=0, tiled=True),
        lax.all_gather(inner_part[3], DP, axis=0, tiled=True),
        lax.all_gather(inner_part[4], DP, axis=0, tiled=True),
        lax.all_gather(inner_part[5], DP, axis=0, tiled=True),
    )


def reduce_grads(grad_qkv, grad_out, grad_up, grad_down, grad_time, grad_gains):
    outer_part = (
        lax.psum_scatter(
            grad_qkv.astype(jnp.bfloat16), DP, scatter_dimension=0, tiled=True
        ).astype(jnp.float32),
        lax.psum_scatter(
            grad_out.astype(jnp.bfloat16), DP, scatter_dimension=0, tiled=True
        ).astype(jnp.float32),
        lax.psum_scatter(
            grad_up.astype(jnp.bfloat16), DP, scatter_dimension=0, tiled=True
        ).astype(jnp.float32),
        lax.psum_scatter(
            grad_down.astype(jnp.bfloat16), DP, scatter_dimension=0, tiled=True
        ).astype(jnp.float32),
        lax.psum_scatter(
            grad_time.astype(jnp.bfloat16), DP, scatter_dimension=0, tiled=True
        ).astype(jnp.float32),
        lax.psum_scatter(
            grad_gains.astype(jnp.bfloat16), DP, scatter_dimension=0, tiled=True
        ).astype(jnp.float32),
    )
    return (
        lax.psum_scatter(
            outer_part[0].astype(jnp.bfloat16), FSDP, scatter_dimension=0, tiled=True
        ).astype(jnp.float32),
        lax.psum_scatter(
            outer_part[1].astype(jnp.bfloat16), FSDP, scatter_dimension=0, tiled=True
        ).astype(jnp.float32),
        lax.psum_scatter(
            outer_part[2].astype(jnp.bfloat16), FSDP, scatter_dimension=0, tiled=True
        ).astype(jnp.float32),
        lax.psum_scatter(
            outer_part[3].astype(jnp.bfloat16), FSDP, scatter_dimension=0, tiled=True
        ).astype(jnp.float32),
        lax.psum_scatter(
            outer_part[4].astype(jnp.bfloat16), FSDP, scatter_dimension=0, tiled=True
        ).astype(jnp.float32),
        lax.psum_scatter(
            outer_part[5].astype(jnp.bfloat16), FSDP, scatter_dimension=0, tiled=True
        ).astype(jnp.float32),
    )


def masked_scores(q_heads, k_heads, allowed, score_scale):
    scores = (
        jnp.einsum("qhe,khe->hqk", q_heads, k_heads, preferred_element_type=jnp.float32)
        * score_scale
    )
    return jnp.where(allowed[None, :, :], scores, -1e30)


def adamw_step(weight, first, second, grad, factor, rate):
    clipped = grad * factor
    first_new = beta_one * first + (1.0 - beta_one) * clipped
    second_new = beta_two * second + (1.0 - beta_two) * clipped * clipped
    first_hat = first_new / (1.0 - beta_one**STEP)
    second_hat = second_new / (1.0 - beta_two**STEP)
    weight_new = weight - rate * (
        first_hat / (jnp.sqrt(second_hat) + adam_eps) + decay_rate * weight
    )
    return (weight_new, first_new, second_new)


def on_device(
    latents,
    media,
    frame_counts,
    cotangent,
    w_qkv,
    m_qkv,
    v_qkv,
    w_out,
    m_out,
    v_out,
    w_up,
    m_up,
    v_up,
    w_down,
    m_down,
    v_down,
    time_table,
    m_time,
    v_time,
    gains,
    m_gains,
    v_gains,
):
    low_qkv = w_qkv.astype(jnp.bfloat16)
    low_out = w_out.astype(jnp.bfloat16)
    low_up = w_up.astype(jnp.bfloat16)
    low_down = w_down.astype(jnp.bfloat16)
    low_time = time_table.astype(jnp.bfloat16)
    low_gains = gains.astype(jnp.bfloat16)
    n_dp, n_fsdp = lax.axis_size(DP), lax.axis_size(FSDP)
    own_rows = w_qkv.shape[0]
    item_slots, lat_count, model_width = latents.shape
    frame_slots, patch_rows, _ = media.shape
    queries_n, media_rows = item_slots * lat_count, frame_slots * patch_rows
    frame_owner, time_hot = frame_tables(frame_counts, frame_slots, time_table.shape[1])
    query_owner = jnp.arange(queries_n, dtype=jnp.int32) // lat_count
    key_owner = jnp.concatenate([jnp.repeat(frame_owner, patch_rows), query_owner], axis=0)
    allowed = query_owner[:, None] == key_owner[None, :]
    lows = (low_qkv, low_out, low_up, low_down, low_time, low_gains)
    if fits_kernels(n_dp, n_fsdp, w_qkv, w_up, w_down, queries_n, frame_slots, patch_rows):
        new_latents, d_latents, grad_norm, reduced = by_kernels(lows, latents, media, cotangent, time_hot, allowed, n_fsdp // 2)
    else:
        new_latents, d_latents, grad_norm, reduced = by_collectives(lows, latents, media, cotangent, time_hot, allowed)
    factor = jnp.minimum(1.0, clip_limit / (grad_norm + 1e-06))
    masters = (w_qkv, w_out, w_up, w_down, time_table, gains)
    firsts = (m_qkv, m_out, m_up, m_down, m_time, m_gains)
    seconds = (v_qkv, v_out, v_up, v_down, v_time, v_gains)
    rates = (0.02, 0.1, 0.02, 0.01, 0.2, 0.5)
    updated = []
    for index in range(6):
        updated.extend(adamw_step(masters[index], firsts[index], seconds[index], reduced[index], factor, rates[index]))
    return (new_latents, d_latents, grad_norm, *updated)


def fits_kernels(n_dp, n_fsdp, w_qkv, w_up, w_down, queries_n, frame_slots, patch_rows):
    rows, _, model = w_qkv.shape
    return (
        n_dp == 4 and n_fsdp == 8 and rows == 48 and model == 1536 and w_up.shape[1] == 4 * model and w_down.shape[0] == 192
        and queries_n == 256 and patch_rows == 48 and frame_slots % 3 == 0
    )


def by_kernels(lows, latents, media, cotangent, time_hot, allowed, n_z):
    low_qkv, low_out, low_up, low_down, low_time, low_gains = lows
    own_rows, _, model = low_qkv.shape
    time_len = low_time.shape[1]
    queries_n = allowed.shape[0]
    frame_slots, patch_rows, _ = media.shape
    tiny = jnp.concatenate([low_time, low_gains], axis=1)
    shards = [low_qkv.reshape(own_rows, -1), low_out, low_up, low_down, jnp.pad(tiny, ((0, 0), (0, 128 - tiny.shape[1])))]
    hot = jnp.pad(jnp.repeat(time_hot, patch_rows, axis=0), ((0, 0), (0, 128 - time_len))).astype(jnp.bfloat16)
    hotc = jnp.broadcast_to(time_hot[:, :, None], time_hot.shape + (128,))
    bias = jnp.where(allowed.T, 0.0, -1e30).astype(jnp.float32)
    lat = latents.reshape(queries_n, model)
    med = media.reshape(frame_slots * patch_rows, model)
    full, made = forward_all(shards, lat, med, cotangent.reshape(queries_n, model), hot, bias, n_z)
    own = backward_all(full, made, lat, med, hot, hotc, bias, shards, n_z)
    small = own.g_tiny
    reduced = (
        own.g_qkv.reshape(low_qkv.shape), own.g_out, own.g_up, own.g_down, small[:, :time_len], small[:, time_len : time_len + 3]
    )
    return made[5].reshape(latents.shape), own.d_lat.reshape(latents.shape), jnp.sqrt(jnp.sum(own.norm)), reduced


def by_collectives(lows, latents, media, cotangent, time_hot, allowed):
    full_qkv, full_out, full_up, full_down, full_time, full_gains = gather_params(*lows)
    item_slots, lat_count, model_width = latents.shape
    frame_slots, patch_rows, unused_width = media.shape
    queries_n = item_slots * lat_count
    media_rows = frame_slots * patch_rows
    head_size = model_width // HEADS
    score_scale = 1.0 / head_size**0.5
    time_f32 = full_time.astype(jnp.float32)
    gains_f32 = full_gains.astype(jnp.float32)
    frame_time = jnp.dot(time_hot, time_f32.T, precision=highest)
    mixed = media.astype(jnp.float32) + frame_time[:, None, :]
    media_norm, media_back = jax.vjp(layer_norm, mixed, gains_f32[:, 0])
    media_low = media_norm.astype(jnp.bfloat16).reshape(media_rows, model_width)
    lat_rows = latents.reshape(queries_n, model_width).astype(jnp.float32)
    lat_norm, lat_back = jax.vjp(layer_norm, lat_rows, gains_f32[:, 1])
    lat_low = lat_norm.astype(jnp.bfloat16)
    keys_in = jnp.concatenate([media_low, lat_low], axis=0)
    key_rows = keys_in.shape[0]
    qkv_flat = full_qkv.reshape(model_width, 3 * model_width)
    queries = jnp.dot(
        lat_low, qkv_flat[:, :model_width], preferred_element_type=jnp.float32
    ).astype(jnp.bfloat16)
    key_value = jnp.dot(
        keys_in, qkv_flat[:, model_width:], preferred_element_type=jnp.float32
    ).astype(jnp.bfloat16)
    q_heads = queries.reshape(queries_n, HEADS, head_size)
    k_heads = key_value[:, :model_width].reshape(key_rows, HEADS, head_size)
    v_heads = key_value[:, model_width:].reshape(key_rows, HEADS, head_size)
    scores = masked_scores(q_heads, k_heads, allowed, score_scale)
    row_top = jnp.max(scores, axis=-1, keepdims=True)
    row_total = jnp.sum(jnp.exp(scores - row_top), axis=-1, keepdims=True)
    log_total = row_top + jnp.log(row_total)
    probs_low = jnp.exp(scores - log_total).astype(jnp.bfloat16)
    attended = jnp.einsum("hqk,khe->qhe", probs_low, v_heads, preferred_element_type=jnp.float32)
    attended = attended.reshape(queries_n, model_width).astype(jnp.bfloat16)
    middle = lat_rows + jnp.dot(attended, full_out, preferred_element_type=jnp.float32)
    hidden, ffn_back = jax.vjp(layer_norm, middle, gains_f32[:, 2])
    hidden_low = hidden.astype(jnp.bfloat16)
    pre_act = jnp.dot(hidden_low, full_up, preferred_element_type=jnp.float32)
    activated, gelu_back = jax.vjp(exact_gelu, pre_act)
    act_low = activated.astype(jnp.bfloat16)
    result = middle + jnp.dot(act_low, full_down, preferred_element_type=jnp.float32)
    new_latents = result.astype(jnp.bfloat16).reshape(item_slots, lat_count, model_width)
    d_result = cotangent.reshape(queries_n, model_width)
    g_down = jnp.einsum("qf,qd->fd", act_low, d_result, preferred_element_type=jnp.float32)
    d_act = jnp.einsum("qd,fd->qf", d_result, full_down, preferred_element_type=jnp.float32)
    d_pre = gelu_back(d_act)[0].astype(jnp.bfloat16)
    g_up = jnp.einsum("qd,qf->df", hidden_low, d_pre, preferred_element_type=jnp.float32)
    d_hidden = jnp.einsum("qf,df->qd", d_pre, full_up, preferred_element_type=jnp.float32)
    d_middle_ln, g_gain_ffn = ffn_back(d_hidden)
    d_middle = d_result.astype(jnp.float32) + d_middle_ln
    d_branch = d_middle.astype(jnp.bfloat16)
    g_out = jnp.einsum("qe,qd->ed", attended, d_branch, preferred_element_type=jnp.float32)
    d_attended = jnp.einsum(
        "qd,ed->qe", d_branch, full_out, preferred_element_type=jnp.float32
    ).astype(jnp.bfloat16)
    scores_again = masked_scores(q_heads, k_heads, allowed, score_scale)
    probs = jnp.exp(scores_again - log_total)
    probs_again = probs.astype(jnp.bfloat16)
    d_att_heads = d_attended.reshape(queries_n, HEADS, head_size)
    d_probs = jnp.einsum("qhe,khe->hqk", d_att_heads, v_heads, preferred_element_type=jnp.float32)
    row_dot = jnp.sum(probs * d_probs, axis=-1, keepdims=True)
    d_scores = (probs * (d_probs - row_dot)).astype(jnp.bfloat16)
    d_queries = (
        (
            jnp.einsum("hqk,khe->qhe", d_scores, k_heads, preferred_element_type=jnp.float32)
            * score_scale
        )
        .reshape(queries_n, model_width)
        .astype(jnp.bfloat16)
    )
    d_keys = (
        (
            jnp.einsum("hqk,qhe->khe", d_scores, q_heads, preferred_element_type=jnp.float32)
            * score_scale
        )
        .reshape(key_rows, model_width)
        .astype(jnp.bfloat16)
    )
    d_values = (
        jnp.einsum("hqk,qhe->khe", probs_again, d_att_heads, preferred_element_type=jnp.float32)
        .reshape(key_rows, model_width)
        .astype(jnp.bfloat16)
    )
    g_query = jnp.einsum("qd,qe->de", lat_low, d_queries, preferred_element_type=jnp.float32)
    d_key_value = jnp.concatenate([d_keys, d_values], axis=1)
    g_key_value = jnp.einsum("kd,kx->dx", keys_in, d_key_value, preferred_element_type=jnp.float32)
    g_qkv = jnp.concatenate([g_query, g_key_value], axis=1).reshape(model_width, 3, model_width)
    back_flat = full_qkv.reshape(model_width, 3 * model_width)
    d_keys_in = jnp.einsum(
        "kx,dx->kd", d_key_value, back_flat[:, model_width:], preferred_element_type=jnp.float32
    )
    d_lat_norm = (
        jnp.einsum(
            "qe,de->qd", d_queries, back_flat[:, :model_width], preferred_element_type=jnp.float32
        )
        + d_keys_in[media_rows:]
    )
    d_lat_ln, g_gain_lat = lat_back(d_lat_norm)
    d_latents = (d_middle + d_lat_ln).reshape(item_slots, lat_count, model_width)
    d_mixed, g_gain_media = media_back(
        d_keys_in[:media_rows].reshape(frame_slots, patch_rows, model_width)
    )
    frame_grad = jnp.sum(d_mixed, axis=1)
    g_time = jnp.einsum("fd,ft->dt", frame_grad, time_hot, precision=highest)
    g_gains = jnp.stack([g_gain_media, g_gain_lat, g_gain_ffn], axis=1)
    reduced = reduce_grads(g_qkv, g_out, g_up, g_down, g_time, g_gains)
    local_sq = jnp.zeros((), jnp.float32)
    for grad in reduced:
        local_sq = local_sq + jnp.sum(grad * grad)
    grad_norm = jnp.sqrt(lax.psum(local_sq, (DP, FSDP)))
    return new_latents, d_latents, grad_norm, reduced


def solution(mesh):
    both = (DP, FSDP)
    one, two, three = P(both), P(both, None), P(both, None, None)
    updated = (three,) * 3 + (two,) * 15
    placed = (three, three, one, three, *updated)
    return jax.shard_map(
        on_device,
        mesh=mesh,
        in_specs=placed,
        out_specs=(three, three, P(), *updated),
        check_vma=False,
    )
```

```python
import functools
import math
import types

import jax
import jax.numpy as jnp
from jax import lax
from jax.experimental import pallas as pl
from jax.experimental.pallas import tpu as pltpu
from jax.sharding import PartitionSpec as P

DP, FSDP = "dp", "fsdp"
HEADS = 16
STEP = 10


highest = lax.Precision.HIGHEST
norm_eps = 1e-05
clip_limit = 1.0
beta_one = 0.9
beta_two = 0.999
adam_eps = 1e-08
decay_rate = 0.1

MESH=pl.DeviceIdType.MESH
ANY=pl.ANY

class Place:
    def __init__(self, n_z):
        dp = lax.axis_index(DP); fs = lax.axis_index(FSDP)
        self.n_z = n_z
        self.at = {"x": dp // 2, "c": dp % 2, "z": fs // 2, "y": fs % 2}
    def dev(self, **new):
        p = {**self.at, **new}
        return (p["x"] * 2 + p["c"], p["z"] * 2 + p["y"])
    def other(self, ax):
        return self.dev(**{ax: 1 - self.at[ax]})
    def along_z(self, k):
        return self.dev(z=(self.at["z"] + k) % self.n_z)
    def level(self):
        flip = lambda ax, by: 1 - self.at[ax] if by else self.at[ax]
        return [self.dev(x=flip("x", n & 4), c=flip("c", n & 2), y=flip("y", n & 1)) for n in range(1, 8)]
    def partners(self):
        return [self.other(a) for a in "cxy"] + [self.along_z(k) for k in range(1, self.n_z)]

def greet(place, wide=False):
    bar = pltpu.get_barrier_semaphore()
    others = place.level() + place.partners()[3:] if wide else place.partners()
    for d in others:
        pl.semaphore_signal(bar, inc=1, device_id=d, device_id_type=MESH)
    pl.semaphore_wait(bar, len(others))

def block_index(place, held, **at):
    where = {**place.at, **at}
    return tuple(slice(None) if ax in held else where[ax] for ax in "xczy")

class Gather:
    def __init__(self, place, src, dst, rows, cols, order, sems, base):
        self.place, self.src, self.dst = place, src, dst
        self.sl = (pl.ds(*rows), pl.ds(*cols))
        self.order, self.sems, self.base = order, sems, base
        self.copies = {}

    def region(self, held, **at):
        return self.dst.at[block_index(self.place, held, **at) + self.sl]

    def copy(self, src, dst, n, to):
        ss, rs = self.sems
        n += self.base
        return pltpu.make_async_remote_copy(src_ref=src, dst_ref=dst, send_sem=ss.at[n], recv_sem=rs.at[n], device_id=to, device_id_type=MESH)

    def start(self, step):
        ax, held, p = self.order[step], self.order[:step], self.place
        if ax == "z":
            self.line(step, 1)
            return
        d = self.copy(self.src.at[self.sl] if step == 0 else self.region(held), self.region(held), "xyc".index(ax), p.other(ax))
        d.start()
        self.copies[step] = d

    def line(self, step, k):
        p, held = self.place, self.order[:step]
        z, last = p.at["z"], p.n_z - 1
        for side, from_z, to_z in ((0, z - (k - 1), z + 1), (1, z + (k - 1), z - 1)):
            ok = (from_z >= 0) & (to_z <= last) if side == 0 else (from_z <= last) & (to_z >= 0)
            at = jnp.clip(from_z, 0, last)
            dst = self.region(held, z=at)
            src = self.src.at[self.sl] if step == 0 and k == 1 else dst
            d = self.copy(src, dst, 3 + 2 * (k - 1) + side, p.dev(z=jnp.clip(to_z, 0, last)))
            pl.when(ok)(d.start)
            came = z >= k if side == 0 else z + k <= last
            self.copies[step, k, side] = (d, ok, came)

    def came(self, step, k):
        for side in range(2):
            d, _, came = self.copies[step, k, side]
            pl.when(came)(d.wait_recv)

    def advance(self, step, k):
        if self.order[step] == "z":
            self.came(step, k)
            self.line(step, k + 1)

    def arrive(self, step):
        if self.order[step] == "z":
            self.came(step, self.place.n_z - 1)
        else:
            self.copies[step].wait_recv()

    def finish(self):
        for key, d in self.copies.items():
            if isinstance(key, tuple):
                pl.when(d[1])(d[0].wait_send)
            else:
                d.wait_send()


def n_sems(n_z):
    return 3 + 2 * (n_z - 1)


def number(plan):
    j, out = 0, []
    for stage in plan:
        new = []
        for piece in stage:
            new.append((j,) + piece); j += 1
        out.append(new)
    return out, j

ZYX, ZXY, XYZ, YXZ = ("z", "y", "x", "c"), ("z", "x", "y", "c"), ("x", "y", "z", "c"), ("y", "x", "z", "c")

BACK_LAG, SEND_SLOTS, LAND_SLOTS = 2, 3, 6
ROOM_B = 4
FINE_B = 0


class Scatter:
    def __init__(self, place, out, rows, cols, order, piece, turn, sems, bufs, total_sq):
        self.p, self.order, self.piece, self.width = place, order, piece, cols[1]
        model = out.shape[-1]
        self.out = out.at[cols[0] // model, pl.ds(*rows), pl.ds(cols[0] % model, cols[1])] if len(out.shape) == 3 else out.at[pl.ds(*rows), pl.ds(*cols)]
        self.ss, self.rs, self.ls = sems
        self.b, self.sq = bufs, total_sq
        self.turn, self.h, self.n = turn, turn % SEND_SLOTS, turn % LAND_SLOTS
        self.sent, self.moves = {}, {}

    def v(self, ref, *lead):
        return ref.at[lead + (slice(None), pl.ds(0, self.width))]

    def copy(self, src, dst, to, n):
        n += self.piece * n_sems(self.p.n_z)
        return pltpu.make_async_remote_copy(src_ref=src, dst_ref=dst, send_sem=self.ss.at[n], recv_sem=self.rs.at[n], device_id=to, device_id_type=MESH)

    def send(self, step, src, dst, ax):
        d = self.copy(src, dst, self.p.other(ax), "xyc".index(ax))
        d.start()
        self.sent[step] = d

    def add(self, count, dst, a, b):
        w = slice(0, self.width)

        def one(i, carry):
            (da, di), (aa, ai), (ba, bi) = dst(i), a(i), b(i)
            da[di + (slice(None), w)] = aa[ai + (slice(None), w)] + ba[bi + (slice(None), w)]
            return carry

        if count == 1:
            one(0, 0)
        else:
            lax.fori_loop(0, count, one, 0)

    def row(self, d):
        if self.order[0] == "z":
            return self.v(self.b.s0, self.h, slice(None), d, slice(None))
        return self.v(self.b.s2, self.h, d)

    def land(self, side, k):
        if self.order[0] == "z":
            return self.v(self.b.rz, self.n, side, k - 1, slice(None), slice(None))
        return self.v(self.b.rz, self.n, side, k - 1)

    def add_landed(self, d, side, k):
        b, h, n = self.b, self.h, self.n
        if self.order[0] == "z":
            mine = lambda i: (b.s0, (h, i // 2, d, i % 2))
            self.add(4, mine, mine, lambda i: (b.rz, (n, side, k - 1, i // 2, i % 2)))
        else:
            mine = lambda i: (b.s2, (h, d))
            self.add(1, mine, mine, lambda i: (b.rz, (n, side, k - 1)))

    def line(self, step, k):
        p = self.p
        z, last = p.at["z"], p.n_z - 1
        for side, d, to in ((0, p.n_z - k + z, z + 1), (1, z - (p.n_z - k), z - 1)):
            ok = d <= last if side == 0 else d >= 0
            at = jnp.clip(d, 0, last)
            if k > 1:
                got, _, came = self.moves[step, k - 1, side]

                def forward(got=got, at=at, side=side):
                    got.wait_recv()
                    self.add_landed(at, side, k - 1)

                pl.when(came)(forward)
            c = self.copy(self.row(at), self.land(side, k), p.dev(z=jnp.clip(to, 0, last)), 3 + 2 * (k - 1) + side)
            pl.when(ok)(c.start)
            came = z <= k if side == 0 else z >= last - k
            came = came & (z > 0 if side == 0 else z < last)
            self.moves[step, k, side] = (c, ok, came)

    def last_move(self, step):
        p = self.p
        z, k = p.at["z"], p.n_z - 1
        for side in range(2):
            c, _, came = self.moves[step, k, side]

            def end(c=c, side=side):
                c.wait_recv()
                self.add_landed(z, side, k)

            pl.when(came)(end)

    def advance(self, step, k):
        if self.order[step] == "z":
            self.line(step, k + 1)

    def free(self, step):
        if step == 3:
            self.sent.pop(3).wait()
        elif self.order[step] == "z":
            for k in range(1, self.p.n_z):
                for side in range(2):
                    c, ok, _ = self.moves.pop((step, k, side))
                    pl.when(ok)(c.wait_send)
        else:
            self.sent.pop(step).wait_send()

    def start(self, step):
        p, b, A, h, n, nz = self.p, self.b, slice(None), self.h, self.n, self.p.n_z
        at = p.at
        if step < 3 and self.order[step] == "z":
            if step == 2:
                first, nxt = self.order[:2]
                mine = (lambda i: (b.s1, (h, i, at[nxt]))) if first == "x" else (lambda i: (b.s1, (h, at[nxt], i)))
                self.sent[1].wait_recv()
                self.add(nz, lambda i: (b.s2, (h, i)), mine, lambda i: (b.r2, (n, i)))
            self.line(step, 1)
            return
        first = self.order[0]
        if step == 0:
            o = 1 - at[first]
            src = self.v(b.s0, h, o, A, A) if first == "x" else self.v(b.s0, h, A, A, o)
            self.send(0, src, self.v(b.r1, n, A, A), first)
        elif step == 1 and first == "z":
            self.last_move(0)
            for x in range(2):
                b.s1[h, x] = b.s0[h, x, at["z"]]
            self.send(1, self.v(b.s1, h, 1 - at["x"], A), self.v(b.r1, n, A), "x")
        elif step == 1:
            self.sent[0].wait_recv()
            o = 1 - at[self.order[1]]
            i0, i1 = (lambda i: i // 2), (lambda i: i % 2)
            if first == "y":
                i0, i1 = (lambda i: i // nz), (lambda i: i % nz)
                mine = lambda i: (b.s0, (h, i0(i), i1(i), at["y"]))
            else:
                mine = lambda i: (b.s0, (h, at["x"], i0(i), i1(i)))
            self.add(2 * nz, lambda i: (b.s1, (h, i0(i), i1(i))), mine, lambda i: (b.r1, (n, i0(i), i1(i))))
            src = self.v(b.s1, h, A, o) if first == "x" else self.v(b.s1, h, o, A)
            self.send(1, src, self.v(b.r2, n, A), self.order[1])
        elif step == 2:
            self.sent[1].wait_recv()
            self.add(2, lambda i: (b.s2, (h, i)), lambda i: (b.s1, (h, at["x"], i)), lambda i: (b.r1, (n, i)))
            self.send(2, self.v(b.s2, h, 1 - at["y"]), self.v(b.r2, n), "y")
        else:
            w = slice(0, self.width)
            if first == "z":
                self.sent[2].wait_recv()
                total = b.s2[h, at["y"], :, w].astype(jnp.float32) + b.r2[n, :, w].astype(jnp.float32)
            else:
                p_last = nz - 1
                for side in range(2):
                    c, _, came = self.moves[2, p_last, side]
                    pl.when(came)(c.wait_recv)
                total = b.s2[h, at["z"], :, w].astype(jnp.float32)
                for side in range(2):
                    came = self.moves[2, p_last, side][2]
                    landed = b.rz[n, side, p_last - 1, :, w].astype(jnp.float32)
                    total = total + jnp.where(came, landed, 0.0)
            b.o[h, :, w] = total
            self.sq[:, w] += total * total
            d = pltpu.make_async_copy(self.v(b.o, h), self.out, self.ls.at[self.piece])
            d.start()
            self.sent[3] = d


def sum_squares(place, n_z, bufs, sems, out):
    ns, nr = sems
    sq, part, zs = bufs.sq, bufs.n, bufs.nz
    acc = jnp.zeros((8, 128), jnp.float32)
    for i in range(sq.shape[0] // 8):
        for j in range(sq.shape[1] // 128):
            acc = acc + sq[i * 8 : (i + 1) * 8, j * 128 : (j + 1) * 128]
    at = place.at
    me = at["x"] * 4 + at["c"] * 2 + at["y"]
    part[me] = acc
    made = []
    for n, d in enumerate(place.level()):
        made.append(pltpu.make_async_remote_copy(src_ref=part.at[me], dst_ref=part.at[me], send_sem=ns.at[n], recv_sem=nr.at[n], device_id=d, device_id_type=MESH))
    for d in made:
        d.start()
    for d in made:
        d.wait()
    acc = part[0]
    for n in range(1, 8):
        acc = acc + part[n]
    z = at["z"]
    zs[z] = acc
    made = []
    for k in range(1, n_z):
        d = pltpu.make_async_remote_copy(src_ref=zs.at[z], dst_ref=zs.at[z], send_sem=ns.at[6 + k], recv_sem=nr.at[6 + k], device_id=place.along_z(k), device_id_type=MESH)
        d.start()
        made.append(d)
    for d in made:
        d.wait()
    total = zs[0]
    for k in range(1, n_z):
        total = total + zs[k]
    out[...] = jnp.broadcast_to(jnp.sqrt(jnp.sum(total, keepdims=True)), out.shape)


def backward_kernel(n_z, plan, names, *refs):
    b = types.SimpleNamespace(**dict(zip(names, refs)))
    ss, rs, ls, ns, nr, ws, ps, pr, lt_sem, rhs_sem, out_sem = refs[len(names) :]
    own_grads = (b.g_qkv, b.g_out, b.g_up, b.g_down, b.g_tiny)
    place = Place(n_z)
    greet(place, True)
    core, A = place.at["c"], slice(None)
    queries_n, model = b.q.shape
    key_rows = b.keys.shape[0]
    media_rows = key_rows - queries_n
    hidden_n = b.dpre.shape[1]
    head = model // HEADS
    windows, group_width = head_windows(head)
    scale = 1.0 / head**0.5
    f32, bf = jnp.float32, jnp.bfloat16
    b.sq[...] = jnp.zeros_like(b.sq)
    given = {}

    def give(src, dst):
        n = len(given)
        d = pltpu.make_async_remote_copy(src_ref=src, dst_ref=dst, send_sem=ps.at[n], recv_sem=pr.at[n], device_id=place.other("c"), device_id_type=MESH)
        d.start()
        given[id(dst)] = [d, False]

    def got(dst):
        held_copy = given[id(dst)]
        if not held_copy[1]:
            held_copy[0].wait_recv()
            held_copy[1] = True

    give(b.dpre, b.x_dpre)
    keys_in = pltpu.make_async_copy(b.keys, b.k, out_sem.at[1])
    keys_in.start()

    wbuf = b.wbuf

    def fetch(src, slot):
        d = pltpu.make_async_copy(src, wbuf.at[slot], ws.at[slot])
        d.start()
        return d

    def tiles_of(jobs, use):
        ahead = fetch(jobs[0], 0)
        for i in range(len(jobs)):
            now = ahead
            if i + 1 < len(jobs):
                ahead = fetch(jobs[i + 1], (i + 1) % 2)
            now.wait()
            use(i, wbuf[i % 2].reshape(384, model))

    def hidden_part(i):
        d = pltpu.make_async_copy(b.dpre.at[:, pl.ds(i * model, model)], b.datt, ws.at[4])
        d.start()
        d.wait()

        def use(n, w):
            got_ = dot(b.datt[...], w, ((1,), (1,)))
            cols = slice(n * 384, (n + 1) * 384)
            if i == 0:
                b.dmid[:, cols] = got_
            else:
                b.dmid[:, cols] += got_

        tiles_of([b.f_up.at[x, c, :, :, :, pl.ds(i * model, model)] for x in range(2) for c in range(2)], use)

    def norm_back(rows_in, grad, gain):
        centered = rows_in - jnp.mean(rows_in, axis=-1, keepdims=True)
        inv = lax.rsqrt(jnp.mean(centered * centered, axis=-1, keepdims=True) + norm_eps)
        hat = centered * inv
        scaled = grad * gain
        back = inv * (scaled - jnp.mean(scaled, axis=-1, keepdims=True) - hat * jnp.mean(scaled * hat, axis=-1, keepdims=True))
        return back, jnp.sum(grad * hat, axis=0, keepdims=True)

    def ffn_norm():
        d = pltpu.make_async_copy(b.f_tiny, b.tiny, ws.at[3])
        d.start()
        e = pltpu.make_async_copy(b.p_cot.at[core], b.dbranch, ws.at[4])
        e.start()
        d.wait()
        e.wait()
        b.tiny_t[...] = b.tiny[...].reshape(model, 128).astype(f32).T
        b.gsmall[...] = jnp.zeros_like(b.gsmall)

        def rows(i, carry):
            at = pl.ds(pl.multiple_of(i * 64, 64), 64)
            back, gain = norm_back(b.mid[at, :], b.dmid[at, :], b.tiny_t[10:11, :])
            total = b.dbranch[at, :].astype(f32) + back
            b.dmid[at, :] = total
            b.dbranch[at, :] = total.astype(bf)
            b.gsmall[10:11, :] += gain
            return carry

        lax.fori_loop(0, queries_n // 64, rows, 0)
        give(b.dbranch, b.x_branch)

    def attended_back():
        def use(n, w):
            b.datt[:, n * 384 : (n + 1) * 384] = dot(b.dbranch[...], w, ((1,), (1,))).astype(bf)

        tiles_of([b.f_out.at[x, c] for x in range(2) for c in range(2)], use)

    def attend_back(g):
        if g == 0:
            keys_in.wait()
            b.bias[...] = own_keys(b.counts, media_rows, queries_n, 48)
        base = g * group_width
        n_tiles = group_width // 128
        last = {t: max(j for j, (t0, t1, _) in enumerate(windows) if t0 <= t < t1) for t in range(n_tiles)}
        sums = {}
        for j, (t0, t1, start) in enumerate(windows):
            cols = slice(base + t0 * 128, base + t1 * 128)
            q_in, k_in = lanes_of(queries_n, t1 - t0, start, head), lanes_of(key_rows, t1 - t0, start, head)
            qh = b.q[:, cols]
            qh = jnp.where(q_in, qh, jnp.zeros_like(qh))
            dah = b.datt[:, cols]
            dah = jnp.where(q_in, dah, jnp.zeros_like(dah))
            kw = b.k[:, cols]
            h = g * len(windows) + j
            p = jnp.exp(dot(kw, qh, ((1,), (1,))) * scale + b.bias[...] - b.lse[h : h + 1, :])
            dp = dot(b.v[:, cols], dah, ((1,), (1,)))
            row_dot = jnp.sum(p * dp, axis=0, keepdims=True)
            ds = (p * (dp - row_dot)).astype(bf)
            kh = jnp.where(k_in, kw, jnp.zeros_like(kw))
            parts = ((b.dv, dot(p.astype(bf), dah)), (b.dk, dot(ds, qh) * scale), (b.dq, dot(ds, kh, ((0,), (0,))) * scale))
            for n, (into, part) in enumerate(parts):
                for t in range(t0, t1):
                    new = part[:, (t - t0) * 128 : (t - t0 + 1) * 128]
                    sums[n, t] = sums[n, t] + new if (n, t) in sums else new
                    if last[t] == j:
                        into[:, base + t * 128 : base + (t + 1) * 128] = sums.pop((n, t)).astype(bf)
        if g == model // group_width - 1:
            give(b.dq, b.x_dq)
            give(b.dk, b.x_dk)
            give(b.dv, b.x_dv)

    def keys_back(n):
        x, c = n // 2, n % 2
        made = [fetch(b.f_qkv.at[x, c, :, :, :, pl.ds(i * model, model)], i) for i in range(3)]
        for d in made:
            d.wait()
        w = [wbuf[i].reshape(384, model) for i in range(3)]
        cols = slice(n * 384, (n + 1) * 384)
        lat_rows = slice(media_rows, key_rows)
        tail = dot(b.dq[...], w[0], ((1,), (1,))) + dot(b.dk[lat_rows, :], w[1], ((1,), (1,))) + dot(b.dv[lat_rows, :], w[2], ((1,), (1,)))
        b.k[lat_rows, cols] = tail.astype(bf)
        step = media_rows // 3
        for i in range(3):
            rows = slice(i * step, (i + 1) * step)
            b.k[rows, cols] = (dot(b.dk[rows, :], w[1], ((1,), (1,))) + dot(b.dv[rows, :], w[2], ((1,), (1,)))).astype(bf)

    def latents_back():
        def rows(i, carry):
            at = pl.ds(pl.multiple_of(i * 64, 64), 64)
            grad = b.k[pl.ds(pl.multiple_of(media_rows + i * 64, 16), 64), :].astype(f32)
            back, gain = norm_back(b.lat[at, :].astype(f32), grad, b.tiny_t[9:10, :])
            b.dmid[at, :] = b.dmid[at, :] + back
            b.gsmall[9:10, :] += gain
            return carry

        lax.fori_loop(0, queries_n // 64, rows, 0)
        d = pltpu.make_async_copy(b.dmid, b.d_lat, out_sem.at[0])
        d.start()
        late.append(d)

    late = []

    def media_back(part):
        step = media_rows // parts
        frames = step // 48
        d = pltpu.make_async_copy(b.media.at[pl.ds(part * step, step)], b.mrows, ws.at[3])
        d.start()
        if part == 0:
            b.hot[...] = time_table_rows(b.counts, media_rows, 48, 128, 8)
        d.wait()

        def frame(i, carry):
            at = pl.ds(pl.multiple_of(i * 48, 48), 48)
            whole = pl.ds(pl.multiple_of(part * step + i * 48, 48), 48)
            mixed = b.mrows[at, :].astype(f32) + dot(b.hot[whole, :], b.tiny_t[...].astype(bf))
            back, gain = norm_back(mixed, b.k[whole, :].astype(f32), b.tiny_t[8:9, :])
            b.gsmall[8:9, :] += gain
            f = part * frames + i
            ends = frame_ends(b.counts)
            time = f
            for s, end in enumerate(ends):
                time = time - jnp.where(f >= end, b.counts[s], 0)
            time = jnp.where(f < ends[-1], time, -1)
            at_time = jnp.where(lax.broadcasted_iota(jnp.int32, (8, 1), 0) == time, 1.0, 0.0)
            b.gsmall[0:8, :] += at_time * jnp.sum(back, axis=0, keepdims=True)
            return carry

        lax.fori_loop(0, frames, frame, 0)

    def small():
        b.tiny[...] = b.gsmall[...].T.astype(bf).reshape(b.tiny.shape)
        give(b.tiny.at[:, 1 - core], b.x_tiny)

    held = [None]

    def left(src):
        if held[0] is src:
            return
        held[0] = src
        if src is b.p_keys:
            into = b.ltk
        elif src is b.p_act:
            into = b.lt
        else:
            into = b.lt.at[:, :, pl.ds(0, 2 * n_z)]
        d = pltpu.make_async_copy(src, into, lt_sem.at[0])
        d.start()
        d.wait()

    coming = {}

    def sources(w, first):
        if w == 3:
            return b.p_cot.at[core], b.p_cot.at[1 - core], first
        if w == 2:
            return b.dpre, b.x_dpre, first
        if w == 1:
            return b.dbranch, b.x_branch, first
        return (b.dq, b.dk, b.dv)[first // model], (b.x_dq, b.x_dk, b.x_dv)[first // model], first % model

    def right(t):
        w, first, width = plan_of[t]
        if w == 4 or t in coming:
            return
        mine, theirs, at = sources(w, first)
        if w != 3:
            if id(theirs) not in given:
                return
            got(theirs)
        cols = pl.ds(at, width)
        made = []
        if w in (2, 3):
            made.append(pltpu.make_async_copy(mine.at[:, cols], b.rhs.at[t % 2, 0, :, pl.ds(0, width)], rhs_sem.at[t % 2, 0]))
        into = b.rhsk.at[:, pl.ds(0, width)] if w == 0 and first >= model else b.rhs.at[t % 2, 1, :, pl.ds(0, width)]
        made.append(pltpu.make_async_copy(theirs.at[:, cols], into, rhs_sem.at[t % 2, 1]))
        for d in made:
            d.start()
        coming[t] = made

    def blocks(x, k, group):
        if group == 1:
            return [b.lt[s, x, 0 : 2 * n_z].reshape(96 * n_z, queries_n) for s in (core, 1 - core)]
        return [jnp.concatenate([b.lt[s, x, i * group + k] for i in range(2 * n_z)], axis=0) for s in (core, 1 - core)]

    def fill(t, pieces):
        w, first, width = plan_of[t]
        h = pieces[0].h
        if w == 4:
            got(b.x_tiny)
            d = pltpu.make_async_copy(b.x_tiny, b.tiny2, ws.at[3])
            d.start()
            d.wait()

            def one(i, carry):
                x, z, y = i // (2 * n_z), (i // 2) % n_z, i % 2
                pieces[0].b.s0[h, x, z, y, :, 0:128] = b.tiny[x, core, z, y] + b.tiny2[x, z, y]
                return carry

            lax.fori_loop(0, 4 * n_z, one, 0)
            return
        right(t)
        for d in coming.pop(t):
            d.wait()
        mine, _, at = sources(w, first)
        keyed = w == 0 and first >= model
        left((b.p_keys if keyed else b.p_lat, b.p_att, b.p_hid, b.p_act)[w])
        r = [b.rhs[t % 2, 0, :, 0:width] if w in (2, 3) else mine[:, pl.ds(at, width)], b.rhsk[:, 0:width] if keyed else b.rhs[t % 2, 1, :, 0:width]]
        for x in range(2):
            if keyed:
                l = [b.ltk[s, x].reshape(96 * n_z, key_rows) for s in (core, 1 - core)]
            else:
                l = blocks(x, rows_of[t] // 48, 4 if w == 3 else 1)
            sums = (dot(l[0], r[0]) + dot(l[1], r[1])).astype(bf)
            start = 0
            for g in pieces:
                g.b.s0[h, x, :, :, :, 0 : g.width] = sums[:, start : start + g.width].reshape(n_z, 2, 48, g.width)
                start += g.width
        if t + 1 < total_stages:
            right(t + 1)

    parts = 6
    work = [(3, 5, functools.partial(hidden_part, i)) for i in range(hidden_n // model)] + [(0, 3, ffn_norm), (0, 4, attended_back)]
    work += [(0, 9, functools.partial(attend_back, g)) for g in range(model // group_width)]
    work += [(0, 5, functools.partial(keys_back, n)) for n in range(4)] + [(0, 3, latents_back)]
    work += [(0, 2, functools.partial(media_back, i)) for i in range(parts)] + [(0, 2, small)]

    def run_until(dst):
        while id(dst) not in given:
            work.pop(0)[2]()

    kinds = [types.SimpleNamespace(**{n: getattr(b, n + k) for n in NAMES}) for k in SETS]
    plan_of = [(st[0][1], st[0][3][0], sum(p[3][1] for p in st)) for st in plan]
    rows_of = [st[0][2][0] for st in plan]
    total_stages = len(plan)
    stages = [
        [Scatter(place, own_grads[w], rows, cols, order, j, t, (ss, rs, ls), kinds[part], b.sq) for part, (j, w, rows, cols, order) in enumerate(stage)]
        for t, stage in enumerate(plan)
    ]
    ticks = total_stages + 3 * BACK_LAG

    def moves(t, k):
        for back in range(3):
            u = t - BACK_LAG * back - 1
            if 0 <= u < total_stages:
                for g in stages[u]:
                    g.advance(back, k)

    for t in range(ticks):
        moves(t, 1)
        for back in range(4):
            u = t - BACK_LAG * back
            if not 0 <= u < total_stages:
                continue
            if u >= SEND_SLOTS:
                for g in stages[u - SEND_SLOTS]:
                    if back == 3 or g.order[back] == "z" or back in g.sent:
                        g.free(back)
            if back == 0:
                w = plan_of[u][0]
                run_until((b.x_dv, b.x_branch, b.x_dpre, b.x_dpre, b.x_tiny)[w])
                fill(u, stages[u])
            for g in stages[u]:
                g.start(back)
        for k in range(2, n_z - 1):
            moves(t, k)
        room = ROOM_B
        while work and room > 0:
            _, cost, piece = work.pop(0)
            room -= cost
            piece()
    for st in stages[-SEND_SLOTS:]:
        for g in st:
            for back in range(4):
                g.free(back)
    for d, done in given.values():
        d.wait_send()
    for d in late:
        d.wait()
    sum_squares(place, n_z, b, (ns, nr), b.norm)


SETS = "abc"
NAMES = ("s0", "r1", "s1", "r2", "s2", "rz", "o")


def backward_plan(shards, model):
    tile = 128
    stages = []

    def split(w, row, first, widths=None):
        widths = widths or ((3, 2, 1), (2, 3, 1))[len(stages) % 2]
        at, pieces = first, []
        for width, order in zip(widths, (("x", "y", "z"), ("y", "x", "z"), ("z", "x", "y"))):
            pieces.append((w, (row, 48), (at, width * tile), order))
            at += width * tile
        stages.append(pieces)

    for row in range(0, shards[3].shape[0], 48):
        for first in range(0, model, 768):
            split(3, row, first)
    for w, cols in ((2, shards[2].shape[1]), (1, model), (0, 3 * model)):
        for first in range(0, cols - FINE_B * 768 * (w == 0), 768):
            split(w, 0, first)
    for first in range(3 * model - FINE_B * 768, 3 * model, 384):
        split(0, 0, first, (1, 1, 1))
    return stages + [[(4, (0, 48), (0, 128), ("x", "y", "z"))]]


def backward_all(full, made, lat, media, counts, n_z):
    queries_n, model = lat.shape
    media_rows = media.shape[0]
    key_rows = queries_n + media_rows
    shards = [jax.ShapeDtypeStruct(f.shape[4:], f.dtype) for f in full]
    hidden_n = shards[2].shape[1]
    plan, count = number(backward_plan(shards, model))
    q, k, v, dpre, mid, new, lse, p_keys, p_lat, p_att, p_hid, p_act, p_cot = made
    given = dict(f_qkv=full[0], f_out=full[1], f_up=full[2], f_tiny=full[4], dpre=dpre, p_keys=p_keys, p_lat=p_lat, p_att=p_att, p_hid=p_hid, p_act=p_act, p_cot=p_cot,
                 media=media, q=q, keys=k, v=v, mid=mid, lse=lse, lat=lat, counts=counts)
    bf, f32 = jnp.bfloat16, jnp.float32
    grads = [(s.shape, f32) for s in shards]
    grads[0] = ((3, shards[1].shape[0], model), f32)
    outs = dict(g_qkv=grads[0], g_out=grads[1], g_up=grads[2], g_down=grads[3], g_tiny=grads[4], d_lat=((queries_n, model), f32), norm=((8, 128), f32),
                x_dpre=((queries_n, hidden_n), bf), x_branch=((queries_n, model), bf), x_dq=((queries_n, model), bf), x_dk=((key_rows, model), bf), x_dv=((key_rows, model), bf),
                x_tiny=((2, n_z, 2, 48, 128), bf))
    W, S, L = 384, SEND_SLOTS, LAND_SLOTS
    vm = dict(s0a=((S, 2, n_z, 2, 48, W), bf), r1a=((L, n_z, 2, 48, W), bf), s1a=((S, n_z, 2, 48, W), bf), r2a=((L, n_z, 48, W), bf), s2a=((S, n_z, 48, W), bf), rza=((L, 2, n_z - 1, 48, W), bf), oa=((S, 48, W), f32),
              s0b=((S, 2, n_z, 2, 48, W), bf), r1b=((L, 2, n_z, 48, W), bf), s1b=((S, 2, n_z, 48, W), bf), r2b=((L, n_z, 48, W), bf), s2b=((S, n_z, 48, W), bf), rzb=((L, 2, n_z - 1, 48, W), bf), ob=((S, 48, W), f32),
              s0c=((S, 2, n_z, 2, 48, 128), bf), rzc=((L, 2, n_z - 1, 2, 2, 48, 128), bf), r1c=((L, 2, 48, 128), bf), s1c=((S, 2, 2, 48, 128), bf), s2c=((S, 2, 48, 128), bf), r2c=((L, 48, 128), bf), oc=((S, 48, 128), f32),
          sq=((48, W), f32), n=((8, 8, 128), f32), nz=((n_z, 8, 128), f32),
          wbuf=((3, n_z, 2, 48, model), bf), dmid=((queries_n, model), f32), dbranch=((queries_n, model), bf), datt=((queries_n, model), bf),
          bias=((key_rows, queries_n), f32), hot=((media_rows, 128), bf), dq=((queries_n, model), bf), k=((key_rows, model), bf), dk=((key_rows, model), bf), dv=((key_rows, model), bf), tiny=((2, 2, n_z, 2, 48, 128), bf), tiny_t=((128, model), f32),
          gsmall=((128, model), f32), tiny2=((2, n_z, 2, 48, 128), bf), mrows=((media_rows // 6, model), bf),
          lt=(p_act.shape, bf), ltk=(p_keys.shape, bf), rhs=((2, 2, queries_n, 768), bf), rhsk=((key_rows, 768), bf))
    sem = pltpu.SemaphoreType.DMA
    in_vmem, in_any = pl.BlockSpec(memory_space=pltpu.VMEM), pl.BlockSpec(memory_space=ANY)
    resident = tuple(id(a) for a in (q, v, mid, lse, lat))
    n_copies = count * n_sems(n_z)
    res = pl.pallas_call(
        functools.partial(backward_kernel, n_z, plan, (*given, *outs, *vm)),
        out_shape=[jax.ShapeDtypeStruct(*o) for o in outs.values()],
        in_specs=[pl.BlockSpec(memory_space=pltpu.SMEM) if a is counts else in_vmem if id(a) in resident else in_any for a in given.values()],
        out_specs=[in_vmem if o is outs["norm"] else in_any for o in outs.values()],
        scratch_shapes=[pltpu.VMEM(*m) for m in vm.values()] + [sem((n_copies,)), sem((n_copies,)), sem((count,)), sem((n_z + 6,)), sem((n_z + 6,)), sem((5,)), sem((8,)), sem((8,)), sem((1,)), sem((2, 2)), sem((2,))],
        name="backward_and_scatter",
        compiler_params=pltpu.CompilerParams(collective_id=1, has_side_effects=True, vmem_limit_bytes=62 * 2**20),
    )(*given.values())
    return types.SimpleNamespace(**dict(zip(outs, res)))


def update_kernel(rates, norm, *refs):
    factor = jnp.minimum(1.0, clip_limit / (norm[0:1, 0:1] + 1e-06))
    n = len(rates)
    ws, ms, vs, gs, rows, outs = refs[:n], refs[n : 2 * n], refs[2 * n : 3 * n], refs[3 * n : 4 * n - 1], refs[4 * n - 1 : 4 * n + 1], refs[4 * n + 1 :]
    for row, o in zip(rows, outs[3 * n :]):
        o[...] = row[...]
    outs[-1][...] = norm[0:1, 0:1]
    small = gs[4][...].T
    steps = ws[4].shape[0]
    grads = [g[...] for g in gs[:4]] + [small[0:steps, :], small[steps : steps + 3, :]]
    for i, g in enumerate(grads):
        new = adamw_step(ws[i][...], ms[i][...], vs[i][...], g, factor if g.ndim == 2 else factor[None], rates[i])
        for o, value in zip(outs[3 * i : 3 * i + 3], new):
            o[...] = value


def update_all(norm, masters, firsts, seconds, grads, rows, rates):
    steps = masters[1].shape[0] // 8

    def spec(a):
        if a.ndim == 3:
            return pl.BlockSpec((3, 8, a.shape[2]), lambda i: (0, i, 0))
        if any(a is r for r in rows):
            return pl.BlockSpec((64, a.shape[1]), lambda i: (jnp.minimum(i, a.shape[0] // 64 - 1), 0))
        if a.shape[1] > 128:
            return pl.BlockSpec((a.shape[0] // steps, a.shape[1]), lambda i: (i, 0))
        return pl.BlockSpec(a.shape, lambda i: (0, 0))

    args = [norm, *masters, *firsts, *seconds, *grads, *rows]
    outs = [a for w in masters for a in (w, w, w)] + list(rows) + [jax.ShapeDtypeStruct((1, 1), jnp.float32)]
    return pl.pallas_call(
        functools.partial(update_kernel, rates),
        grid=(steps,),
        out_shape=[jax.ShapeDtypeStruct(a.shape, a.dtype) for a in outs],
        in_specs=[spec(a) for a in args],
        out_specs=[spec(a) for a in outs],
        name="adamw",
        compiler_params=pltpu.CompilerParams(vmem_limit_bytes=62 * 2**20),
    )(*args)


def out_copies(pairs, sems, at, running):
    for src, dst in pairs:
        d = pltpu.make_async_copy(src, dst, sems.at[len(running)])
        d.start()
        running.append(d)


def dot(a, b, contract=((1,), (0,))):
    return lax.dot_general(a, b, (contract, ((), ())), preferred_element_type=jnp.float32)


def head_windows(head):
    group = 128 // math.gcd(head, 128)
    out = []
    for j in range(group):
        first, last = j * head // 128, ((j + 1) * head - 1) // 128
        out.append((first, last + 1, j * head - first * 128))
    return out, group * head


def lanes_of(rows, tiles, start, head):
    lane = lax.broadcasted_iota(jnp.int32, (rows, tiles * 128), 1)
    return (lane >= start) & (lane < start + head)


def normed(rows_in, gain):
    centered = rows_in - jnp.mean(rows_in, axis=-1, keepdims=True)
    var_row = jnp.mean(centered * centered, axis=-1, keepdims=True)
    return centered * lax.rsqrt(var_row + norm_eps) * gain


def frame_ends(counts):
    ends, total = [], 0
    for s in range(counts.shape[0]):
        total = total + counts[s]
        ends.append(total)
    return ends


def time_table_rows(counts, rows, patch, lanes, time_len):
    row = lax.broadcasted_iota(jnp.int32, (rows, lanes), 0)
    lane = lax.broadcasted_iota(jnp.int32, (rows, lanes), 1)
    ends = frame_ends(counts)
    start = jnp.zeros((rows, lanes), jnp.int32)
    for s, end in enumerate(ends):
        start = start + jnp.where(row >= end * patch, counts[s] * patch, 0)
    off = row - start - lane * patch
    live = (off >= 0) & (off < patch) & (row < ends[-1] * patch) & (lane < time_len)
    return jnp.where(live, 1.0, 0.0).astype(jnp.bfloat16)


def own_keys(counts, media_rows, queries_n, patch):
    slots = counts.shape[0]
    each = queries_n // slots
    shape = (media_rows + queries_n, queries_n)
    row = lax.broadcasted_iota(jnp.int32, shape, 0)
    lane = lax.broadcasted_iota(jnp.int32, shape, 1)
    owner, asks = jnp.zeros(shape, jnp.int32), jnp.zeros(shape, jnp.int32)
    for s, end in enumerate(frame_ends(counts)):
        owner = owner + jnp.where(row >= end * patch, 1, 0)
        if s + 1 < slots:
            asks = asks + jnp.where(lane >= (s + 1) * each, 1, 0)
    mine = jnp.zeros(shape, jnp.int32)
    for s in range(1, slots):
        mine = mine + jnp.where(row >= media_rows + s * each, 1, 0)
    owner = jnp.where(row >= media_rows, mine, owner)
    return jnp.where(owner == asks, 0.0, -1e30)


def forward_kernel(n_z, plan, needs, *refs):
    (w_qkv, w_out, w_up, w_down, w_time, w_gains, lat, media, cot, counts), full, outs, scratch = refs[:10], refs[10:15], refs[15:27], refs[27:]
    o_q, o_k, o_v, o_dpre, o_mid, o_new, o_lse, p_keys, p_lat, p_att, p_hid, p_act = outs[:12]
    p_cot, *scratch = scratch
    *sh, small, hot, bias = scratch[:8]
    keys, q, k, v, att, hid, act, slope, dact, mid, new, tiny, tiny_t, lse, wbuf, wdown, flip, flip_keys, ss, rs, ls, os_, ws, ps, pr, pl_ = scratch[8:]
    f_qkv, f_out, f_up, f_down, f_tiny = full
    place = Place(n_z)
    queries_n, model = lat.shape
    for i in range(3):
        sh[0][:, i * model : (i + 1) * model] = w_qkv[i].astype(jnp.bfloat16)
    for low, w in zip(sh[1:4], (w_out, w_up, w_down)):
        low[...] = w[...].astype(jnp.bfloat16)
    time_len = w_time.shape[0]
    small[...] = jnp.zeros_like(small)
    small[0:time_len, :] = w_time[...]
    small[time_len : time_len + 3, :] = w_gains[...]
    sh[4][...] = small[...].T.astype(jnp.bfloat16)
    greet(place)
    media_rows = media.shape[0]
    key_rows = media_rows + queries_n
    hidden_n = act.shape[1]
    head = model // HEADS
    windows, group_width = head_windows(head)
    scale = 1.0 / head**0.5
    written = []
    given = []
    core = place.at["c"]

    def give(src, dst, theirs):
        n = len(given)
        if theirs:
            d = pltpu.make_async_remote_copy(src_ref=src, dst_ref=dst, send_sem=ps.at[n], recv_sem=pr.at[n], device_id=place.other("c"), device_id_type=MESH)
        else:
            d = pltpu.make_async_copy(src, dst, pl_.at[n])
        d.start()
        given.append([d, theirs, False])
        return n

    def gone(n):
        d, theirs, done = given[n]
        if not done:
            d.wait_send() if theirs else d.wait()
            given[n][2] = True

    def turn(a, dst, slot, x, wide, before=()):
        made = []
        for n in before:
            gone(n)
        for theirs in (False, True):
            who = 1 - core if theirs else core
            for m in range(wide // 384):
                cols = pl.ds(pl.multiple_of((x * 2 + who) * wide + m * 384, 128), 384)
                flip[slot] = a[:, cols].T.reshape(8, 48, queries_n)
                made.append(give(flip.at[slot], dst.at[core, x, pl.ds(m * 8, 8)], theirs))
                slot += 1
        return made

    def load(src, dst):
        d = pltpu.make_async_copy(src, dst, ws.at[0])
        d.start()
        d.wait()

    def write(*pairs):
        out_copies(pairs, os_, 0, written)

    def norms():
        hot[...] = time_table_rows(counts, media_rows, 48, hot.shape[1], time_len)
        load(f_tiny, tiny)
        tiny_t[...] = tiny[...].reshape(model, 128).astype(jnp.float32).T
        give(cot, p_cot.at[core], False)
        give(cot, p_cot.at[core], True)
        hid[...] = normed(lat[...].astype(jnp.float32), tiny_t[9:10, :]).astype(jnp.bfloat16)
        keys[media_rows:key_rows, :] = hid[...]
        for x in range(2):
            turn(hid, p_lat, 2 * x, x, 384)

        def frame(i, carry):
            rows = pl.ds(pl.multiple_of(i * 48, 48), 48)
            mixed = media[rows, :].astype(jnp.float32) + dot(hot[rows, :], tiny_t[...].astype(jnp.bfloat16))
            keys[rows, :] = normed(mixed, tiny_t[8:9, :]).astype(jnp.bfloat16)
            return carry

        lax.fori_loop(0, media_rows // 48, frame, 0)

    key_turns = []

    def turn_keys(x):
        for n in key_turns:
            gone(n)
        for theirs in (False, True):
            who = 1 - core if theirs else core
            cols = pl.ds(pl.multiple_of((x * 2 + who) * 384, 128), 384)
            flip_keys[int(theirs)] = keys[:, cols].T.reshape(8, 48, key_rows)
            key_turns.append(give(flip_keys.at[int(theirs)], p_keys.at[core, x], theirs))

    def project(i, dst, first):
        load(f_qkv.at[:, :, :, :, :, pl.ds(i * model, model)], wbuf)

        def tile(n, carry):
            cols = pl.ds(pl.multiple_of(n * 256, 256), 256)
            w = wbuf[:, :, :, :, :, cols].reshape(model, 256)
            dst[:, cols] = dot(keys[first:key_rows, :], w).astype(jnp.bfloat16)
            return carry

        lax.fori_loop(0, model // 256, tile, 0)

    def project_q():
        project(0, q, media_rows)
        write((q, o_q))

    def project_k():
        project(1, k, 0)
        write((k, o_k))

    def project_v():
        project(2, v, 0)
        write((v, o_v))

    def attend(g):
        if g == 0:
            bias[...] = own_keys(counts, media_rows, queries_n, 48)
        base = g * group_width
        tiles = [jnp.zeros((queries_n, 128), jnp.float32) for _ in range(group_width // 128)]
        for j, (t0, t1, start) in enumerate(windows):
            cols = slice(base + t0 * 128, base + t1 * 128)
            qh = q[:, cols]
            qh = jnp.where(lanes_of(queries_n, t1 - t0, start, head), qh, jnp.zeros_like(qh))
            s = dot(k[:, cols], qh, ((1,), (1,))) * scale + bias[...]
            top = jnp.max(s, axis=0, keepdims=True)
            e = jnp.exp(s - top)
            total = jnp.sum(e, axis=0, keepdims=True)
            p = (e * (1.0 / total)).astype(jnp.bfloat16)
            lse[g * len(windows) + j : g * len(windows) + j + 1, :] = top + jnp.log(total)
            vh = v[:, cols]
            vh = jnp.where(lanes_of(key_rows, t1 - t0, start, head), vh, jnp.zeros_like(vh))
            got = dot(p, vh, ((0,), (0,)))
            for t in range(t0, t1):
                tiles[t] = tiles[t] + got[:, (t - t0) * 128 : (t - t0 + 1) * 128]
        for t, tile in enumerate(tiles):
            att[:, base + t * 128 : base + (t + 1) * 128] = tile.astype(jnp.bfloat16)

    def project_out():
        write((lse, o_lse))
        for x in range(2):
            turn(att, p_att, 4 + 2 * x, x, 384)
        load(f_out, wbuf)

        def tile(n, carry):
            cols = pl.ds(pl.multiple_of(n * 256, 256), 256)
            w = wbuf[:, :, :, :, :, cols].reshape(model, 256)
            mid[:, cols] = lat[:, cols].astype(jnp.float32) + dot(att[...], w)
            return carry

        lax.fori_loop(0, model // 256, tile, 0)
        hid[...] = normed(mid[...], tiny_t[10:11, :]).astype(jnp.bfloat16)
        write((mid, o_mid))
        for x in range(2):
            hid_turns.extend(turn(hid, p_hid, 8 + 2 * x, x, 384))

    hid_turns = []
    act_turns = []

    def up(i):
        load(f_up.at[:, :, :, :, :, pl.ds(i * model, model)], wbuf)

        def tile(n, carry):
            cols = pl.ds(pl.multiple_of(n * 256, 256), 256)
            into = pl.ds(pl.multiple_of(i * model + n * 256, 256), 256)
            w = wbuf[:, :, :, :, :, cols].reshape(model, 256)
            x = dot(hid[...], w)
            cdf = 0.5 + 0.5 * lax.erf(x * 0.7071067811865476)
            act[:, into] = (x * cdf).astype(jnp.bfloat16)
            slope[:, into] = cdf + x * (jnp.exp(-0.5 * x * x) * 0.3989422804014327)
            return carry

        lax.fori_loop(0, model // 256, tile, 0)
        if i % 2 == 1:
            before = list(range(len(given))) if i == 1 else act_turns
            act_turns.extend(turn(act, p_act, 0, i // 2, model, before))

    def down(i, width):
        cols = slice(i * width, (i + 1) * width)
        load(f_down.at[:, :, :, :, :, pl.ds(i * width, width)], wdown)
        per = hidden_n // 4
        got = jnp.zeros((queries_n, width), jnp.float32)
        for b in range(4):
            w = wdown[b // 2, b % 2].reshape(per, width)
            got = got + dot(act[:, b * per : (b + 1) * per], w)
            back = dot(cot[:, cols], w, ((1,), (1,)))
            if i == 0:
                dact[:, b * per : (b + 1) * per] = back
            else:
                dact[:, b * per : (b + 1) * per] += back
        new[:, cols] = (mid[:, cols] + got).astype(jnp.bfloat16)

    def finish():
        def tile(n, carry):
            cols = pl.ds(pl.multiple_of(n * 512, 512), 512)
            act[:, cols] = (dact[:, cols] * slope[:, cols]).astype(jnp.bfloat16)
            return carry

        lax.fori_loop(0, hidden_n // 512, tile, 0)
        write((act, o_dpre), (new, o_new))
        for d in written:
            d.wait()
        for n, (d, theirs, done) in enumerate(given):
            gone(n)
            if theirs:
                d.wait_recv()

    work = [(needs["tiny"], 8, norms), (needs["q"], 4, project_q), (needs["k"], 8, project_k), (needs["v"], 8, project_v)]
    work[2:2] = [(needs["q"], 3, functools.partial(turn_keys, x)) for x in range(2)]
    work += [(needs["v"], 7, functools.partial(attend, g)) for g in range(model // group_width)]
    work += [(needs["out"], 5, project_out)]
    work += [(s, 6, functools.partial(up, i)) for i, s in enumerate(needs["up"])]
    work += [(s, 5, functools.partial(down, i, model // len(needs["down"]))) for i, s in enumerate(needs["down"])]
    work += [(needs["down"][-1], 5, finish)]
    locals_ = []
    for i in range(5):
        d = pltpu.make_async_copy(sh[i], full[i].at[block_index(place, ())], ls.at[i])
        d.start()
        locals_.append(d)
    stages = [[Gather(place, sh[w], full[w], rows, cols, order, (ss, rs), j * n_sems(n_z)) for (j, w, rows, cols, order) in stage] for stage in plan]
    waited = set()
    total, steps = len(stages), 4
    ticks = total + LAG * steps
    for t in range(ticks):
        for back in range(steps):
            u = t - LAG * back - 1
            if LAG > 1 and 0 <= u < total:
                for g in stages[u]:
                    g.advance(back, 1)
        for back in range(steps + 1):
            u = t - LAG * back
            if not 0 <= u < total:
                continue
            for g, (j, w, *_) in zip(stages[u], plan[u]):
                if back == 1 and w not in waited:
                    locals_[w].wait()
                    waited.add(w)
                if back > 0:
                    g.arrive(back - 1)
                if back < steps:
                    g.start(back)
        for move in range(1 if LAG == 1 else 2, n_z - 1):
            for back in range(steps):
                u = t - LAG * back - (LAG > 1)
                if 0 <= u < total:
                    for g in stages[u]:
                        g.advance(back, move)
        room = ROOM_A
        while work and work[0][0] <= t - LAG * steps and (room > 0 or t == ticks - 1):
            need, cost, piece = work.pop(0)
            room -= cost
            piece()
    for st in stages:
        for g in st:
            g.finish()


ROOM_A = 12
LAG = 2
FINE = 1
Z_DOWN = (1,)


def forward_plan(shards, model):
    def split(w, rows, first, widths, last):
        at, pieces = first, []
        for width, order in zip(widths, (ZYX, ZXY, last)):
            pieces.append((w, (0, rows), (at, width), order))
            at += width
        return pieces

    rows = shards[1].shape[0]
    stages, needs = [[(4, (0, rows), (0, 128), ZYX)]], {"tiny": 0}
    wide = model * 5 // 12, model * 5 // 12, model // 6
    for i, name in enumerate("qkv"):
        needs[name] = len(stages)
        stages.append(split(0, rows, i * model, wide, (XYZ, YXZ)[i % 2]))
    needs["out"] = len(stages)
    stages.append(split(1, rows, 0, wide, YXZ))
    needs["up"], needs["down"] = [], []
    for i in range(shards[2].shape[1] // model):
        needs["up"].append(len(stages))
        stages.append(split(2, rows, i * model, wide, (XYZ, YXZ)[i % 2]))
    groups = model // 256
    deep = shards[3].shape[0]
    for i in range(groups):
        if i >= groups - FINE:
            for half in range(2):
                cols = (i * 256 + half * 128, 128)
                stages.append([(3, (0, deep // 2), cols, ZYX), (3, (deep // 2, deep // 2), cols, ZXY)])
        else:
            pair = (XYZ, YXZ) if i in Z_DOWN else (ZYX, ZXY)
            stages.append([(3, (0, deep), (i * 256 + n * 128, 128), pair[n]) for n in range(2)])
        needs["down"].append(len(stages) - 1)
    return stages, needs


def forward_all(weights, lat, media, cot, counts, n_z):
    bf, f32 = jnp.bfloat16, jnp.float32
    rows, model = weights[1].shape
    hidden_n = weights[2].shape[1]
    shards = [jax.ShapeDtypeStruct(s, bf) for s in ((rows, 3 * model), weights[1].shape, weights[2].shape, weights[3].shape, (rows, 128))]
    stages, needs = forward_plan(shards, model)
    plan, count = number(stages)
    queries_n, media_rows = lat.shape[0], media.shape[0]
    key_rows = queries_n + media_rows
    part = (2, 2, 2 * n_z, 48)
    made = [((queries_n, model), bf), ((key_rows, model), bf), ((key_rows, model), bf), ((queries_n, hidden_n), bf), ((queries_n, model), f32), ((queries_n, model), bf), ((HEADS, queries_n), f32),
            (part + (key_rows,), bf), (part + (queries_n,), bf), (part + (queries_n,), bf), (part + (queries_n,), bf), ((2, 2, 2 * n_z * hidden_n // model, 48, queries_n), bf), ((2, queries_n, model), bf)]
    vm = [(s.shape, bf) for s in shards] + [((128, rows), f32), ((media_rows, 128), bf), ((key_rows, queries_n), f32)]
    vm += [((key_rows, model), bf), ((queries_n, model), bf), ((key_rows, model), bf), ((key_rows, model), bf), ((queries_n, model), bf), ((queries_n, model), bf), ((queries_n, hidden_n), bf),
          ((queries_n, hidden_n), f32), ((queries_n, hidden_n), f32), ((queries_n, model), f32), ((queries_n, model), bf),
                     ((2, 2, n_z, 2, rows, 128), bf), ((128, model), f32), ((HEADS, queries_n), f32), ((2, 2, n_z, 2, rows, model), bf), ((2, 2, n_z, 2, shards[3].shape[0], 256), bf),
                     ((12, 8, 48, queries_n), bf), ((2, 8, 48, key_rows), bf)]
    sem = pltpu.SemaphoreType.DMA
    in_vmem, in_any = pl.BlockSpec(memory_space=pltpu.VMEM), pl.BlockSpec(memory_space=ANY)
    out = pl.pallas_call(
        functools.partial(forward_kernel, n_z, plan, needs),
        out_shape=[jax.ShapeDtypeStruct((2, 2, n_z, 2) + s.shape, s.dtype) for s in shards] + [jax.ShapeDtypeStruct(*m) for m in made],
        in_specs=[in_vmem] * 9 + [pl.BlockSpec(memory_space=pltpu.SMEM)],
        out_specs=[in_any] * (5 + len(made)),
        scratch_shapes=[pltpu.VMEM(*m) for m in vm] + [sem((count * n_sems(n_z),)), sem((count * n_sems(n_z),)), sem((5,)), sem((16,)), sem((1,)), sem((48,)), sem((48,)), sem((48,))],
        name="gather_and_forward",
        compiler_params=pltpu.CompilerParams(collective_id=0, has_side_effects=True, vmem_limit_bytes=60 * 2**20),
    )(*weights, lat, media, cot, counts)
    return out[:5], out[5:]


def layer_norm(values_in, gain):
    mean_row = jnp.mean(values_in, axis=-1, keepdims=True)
    centered = values_in - mean_row
    var_row = jnp.mean(centered * centered, axis=-1, keepdims=True)
    return centered * lax.rsqrt(var_row + norm_eps) * gain


def exact_gelu(values_in):
    return jax.nn.gelu(values_in, approximate=False)


def frame_tables(counts, frame_slots, time_len):
    slot_total = counts.shape[0]
    order = jnp.arange(slot_total, dtype=jnp.int32)
    slot_ends = jnp.sum(jnp.where(order[None, :] <= order[:, None], counts[None, :], 0), axis=1)
    slot_starts = slot_ends - counts
    frame_ids = jnp.arange(frame_slots, dtype=jnp.int32)
    frame_owner = jnp.sum((frame_ids[:, None] >= slot_ends[None, :]).astype(jnp.int32), axis=1)
    slot_ids = jnp.arange(slot_total, dtype=jnp.int32)
    start_of = jnp.sum(
        jnp.where(frame_owner[:, None] == slot_ids[None, :], slot_starts[None, :], 0), axis=1
    )
    time_index = frame_ids - start_of
    live_frame = frame_owner < slot_total
    time_ids = jnp.arange(time_len, dtype=jnp.int32)
    time_hot = ((time_index[:, None] == time_ids[None, :]) & live_frame[:, None]).astype(
        jnp.float32
    )
    return (frame_owner, time_hot)


def gather_params(part_qkv, part_out, part_up, part_down, part_time, part_gains):
    inner_part = (
        lax.all_gather(part_qkv, FSDP, axis=0, tiled=True),
        lax.all_gather(part_out, FSDP, axis=0, tiled=True),
        lax.all_gather(part_up, FSDP, axis=0, tiled=True),
        lax.all_gather(part_down, FSDP, axis=0, tiled=True),
        lax.all_gather(part_time, FSDP, axis=0, tiled=True),
        lax.all_gather(part_gains, FSDP, axis=0, tiled=True),
    )
    return (
        lax.all_gather(inner_part[0], DP, axis=0, tiled=True),
        lax.all_gather(inner_part[1], DP, axis=0, tiled=True),
        lax.all_gather(inner_part[2], DP, axis=0, tiled=True),
        lax.all_gather(inner_part[3], DP, axis=0, tiled=True),
        lax.all_gather(inner_part[4], DP, axis=0, tiled=True),
        lax.all_gather(inner_part[5], DP, axis=0, tiled=True),
    )


def reduce_grads(grad_qkv, grad_out, grad_up, grad_down, grad_time, grad_gains):
    outer_part = (
        lax.psum_scatter(
            grad_qkv.astype(jnp.bfloat16), DP, scatter_dimension=0, tiled=True
        ).astype(jnp.float32),
        lax.psum_scatter(
            grad_out.astype(jnp.bfloat16), DP, scatter_dimension=0, tiled=True
        ).astype(jnp.float32),
        lax.psum_scatter(
            grad_up.astype(jnp.bfloat16), DP, scatter_dimension=0, tiled=True
        ).astype(jnp.float32),
        lax.psum_scatter(
            grad_down.astype(jnp.bfloat16), DP, scatter_dimension=0, tiled=True
        ).astype(jnp.float32),
        lax.psum_scatter(
            grad_time.astype(jnp.bfloat16), DP, scatter_dimension=0, tiled=True
        ).astype(jnp.float32),
        lax.psum_scatter(
            grad_gains.astype(jnp.bfloat16), DP, scatter_dimension=0, tiled=True
        ).astype(jnp.float32),
    )
    return (
        lax.psum_scatter(
            outer_part[0].astype(jnp.bfloat16), FSDP, scatter_dimension=0, tiled=True
        ).astype(jnp.float32),
        lax.psum_scatter(
            outer_part[1].astype(jnp.bfloat16), FSDP, scatter_dimension=0, tiled=True
        ).astype(jnp.float32),
        lax.psum_scatter(
            outer_part[2].astype(jnp.bfloat16), FSDP, scatter_dimension=0, tiled=True
        ).astype(jnp.float32),
        lax.psum_scatter(
            outer_part[3].astype(jnp.bfloat16), FSDP, scatter_dimension=0, tiled=True
        ).astype(jnp.float32),
        lax.psum_scatter(
            outer_part[4].astype(jnp.bfloat16), FSDP, scatter_dimension=0, tiled=True
        ).astype(jnp.float32),
        lax.psum_scatter(
            outer_part[5].astype(jnp.bfloat16), FSDP, scatter_dimension=0, tiled=True
        ).astype(jnp.float32),
    )


def masked_scores(q_heads, k_heads, allowed, score_scale):
    scores = (
        jnp.einsum("qhe,khe->hqk", q_heads, k_heads, preferred_element_type=jnp.float32)
        * score_scale
    )
    return jnp.where(allowed[None, :, :], scores, -1e30)


def adamw_step(weight, first, second, grad, factor, rate):
    clipped = grad * factor
    first_new = beta_one * first + (1.0 - beta_one) * clipped
    second_new = beta_two * second + (1.0 - beta_two) * clipped * clipped
    first_hat = first_new / (1.0 - beta_one**STEP)
    second_hat = second_new / (1.0 - beta_two**STEP)
    weight_new = weight - rate * (
        first_hat / (jnp.sqrt(second_hat) + adam_eps) + decay_rate * weight
    )
    return (weight_new, first_new, second_new)


def on_device(
    latents,
    media,
    frame_counts,
    cotangent,
    w_qkv,
    m_qkv,
    v_qkv,
    w_out,
    m_out,
    v_out,
    w_up,
    m_up,
    v_up,
    w_down,
    m_down,
    v_down,
    time_table,
    m_time,
    v_time,
    gains,
    m_gains,
    v_gains,
):
    n_dp, n_fsdp = lax.axis_size(DP), lax.axis_size(FSDP)
    masters = (w_qkv, w_out, w_up, w_down, time_table, gains)
    firsts = (m_qkv, m_out, m_up, m_down, m_time, m_gains)
    seconds = (v_qkv, v_out, v_up, v_down, v_time, v_gains)
    rates = (0.02, 0.1, 0.02, 0.01, 0.2, 0.5)
    item_slots, lat_count, _ = latents.shape
    frame_slots, patch_rows, _ = media.shape
    queries_n = item_slots * lat_count
    if fits_kernels(n_dp, n_fsdp, w_qkv, w_up, w_down, queries_n, frame_slots, patch_rows):
        new_latents, d_latents, grad_norm, updated = by_kernels(
            turned(masters), turned(firsts), turned(seconds), rates, latents, media, cotangent, frame_counts, n_fsdp // 2
        )
    else:
        frame_owner, time_hot = frame_tables(frame_counts, frame_slots, time_table.shape[1])
        query_owner = jnp.arange(queries_n, dtype=jnp.int32) // lat_count
        key_owner = jnp.concatenate([jnp.repeat(frame_owner, patch_rows), query_owner], axis=0)
        allowed = query_owner[:, None] == key_owner[None, :]
        lows = tuple(w.astype(jnp.bfloat16) for w in masters)
        new_latents, d_latents, grad_norm, reduced = by_collectives(lows, latents, media, cotangent, time_hot, allowed)
        factor = jnp.minimum(1.0, clip_limit / (grad_norm + 1e-06))
        updated = []
        for index in range(6):
            updated.extend(adamw_step(masters[index], firsts[index], seconds[index], reduced[index], factor, rates[index]))
    return (new_latents, d_latents, grad_norm, *updated)


def turned(arrays):
    qkv, out, up, down, time, gain = arrays
    return qkv.transpose(1, 0, 2), out, up, down, time.T, gain.T


def fits_kernels(n_dp, n_fsdp, w_qkv, w_up, w_down, queries_n, frame_slots, patch_rows):
    rows, _, model = w_qkv.shape
    return (
        n_dp == 4 and n_fsdp == 8 and rows == 48 and model == 1536 and w_up.shape[1] == 4 * model and w_down.shape[0] == 192
        and queries_n == 256 and patch_rows == 48 and frame_slots % 3 == 0
    )


def by_kernels(masters, firsts, seconds, rates, latents, media, cotangent, counts, n_z):
    model = latents.shape[2]
    lat, med, cot = (a.reshape(-1, model) for a in (latents, media, cotangent))
    full, made = forward_all(masters, lat, med, cot, counts, n_z)
    own = backward_all(full, made, lat, med, counts, n_z)
    grads = [own.g_qkv, own.g_out, own.g_up, own.g_down, own.g_tiny]
    *new, new_rows, d_rows, norm = update_all(own.norm, masters, firsts, seconds, grads, (made[5], own.d_lat), rates)
    kinds = [turned(new[n::3]) for n in range(3)]
    updated = [kinds[n][i] for i in range(6) for n in range(3)]
    return new_rows.reshape(latents.shape), d_rows.reshape(latents.shape), norm.reshape(()), updated


def by_collectives(lows, latents, media, cotangent, time_hot, allowed):
    full_qkv, full_out, full_up, full_down, full_time, full_gains = gather_params(*lows)
    item_slots, lat_count, model_width = latents.shape
    frame_slots, patch_rows, unused_width = media.shape
    queries_n = item_slots * lat_count
    media_rows = frame_slots * patch_rows
    head_size = model_width // HEADS
    score_scale = 1.0 / head_size**0.5
    time_f32 = full_time.astype(jnp.float32)
    gains_f32 = full_gains.astype(jnp.float32)
    frame_time = jnp.dot(time_hot, time_f32.T, precision=highest)
    mixed = media.astype(jnp.float32) + frame_time[:, None, :]
    media_norm, media_back = jax.vjp(layer_norm, mixed, gains_f32[:, 0])
    media_low = media_norm.astype(jnp.bfloat16).reshape(media_rows, model_width)
    lat_rows = latents.reshape(queries_n, model_width).astype(jnp.float32)
    lat_norm, lat_back = jax.vjp(layer_norm, lat_rows, gains_f32[:, 1])
    lat_low = lat_norm.astype(jnp.bfloat16)
    keys_in = jnp.concatenate([media_low, lat_low], axis=0)
    key_rows = keys_in.shape[0]
    qkv_flat = full_qkv.reshape(model_width, 3 * model_width)
    queries = jnp.dot(
        lat_low, qkv_flat[:, :model_width], preferred_element_type=jnp.float32
    ).astype(jnp.bfloat16)
    key_value = jnp.dot(
        keys_in, qkv_flat[:, model_width:], preferred_element_type=jnp.float32
    ).astype(jnp.bfloat16)
    q_heads = queries.reshape(queries_n, HEADS, head_size)
    k_heads = key_value[:, :model_width].reshape(key_rows, HEADS, head_size)
    v_heads = key_value[:, model_width:].reshape(key_rows, HEADS, head_size)
    scores = masked_scores(q_heads, k_heads, allowed, score_scale)
    row_top = jnp.max(scores, axis=-1, keepdims=True)
    row_total = jnp.sum(jnp.exp(scores - row_top), axis=-1, keepdims=True)
    log_total = row_top + jnp.log(row_total)
    probs_low = jnp.exp(scores - log_total).astype(jnp.bfloat16)
    attended = jnp.einsum("hqk,khe->qhe", probs_low, v_heads, preferred_element_type=jnp.float32)
    attended = attended.reshape(queries_n, model_width).astype(jnp.bfloat16)
    middle = lat_rows + jnp.dot(attended, full_out, preferred_element_type=jnp.float32)
    hidden, ffn_back = jax.vjp(layer_norm, middle, gains_f32[:, 2])
    hidden_low = hidden.astype(jnp.bfloat16)
    pre_act = jnp.dot(hidden_low, full_up, preferred_element_type=jnp.float32)
    activated, gelu_back = jax.vjp(exact_gelu, pre_act)
    act_low = activated.astype(jnp.bfloat16)
    result = middle + jnp.dot(act_low, full_down, preferred_element_type=jnp.float32)
    new_latents = result.astype(jnp.bfloat16).reshape(item_slots, lat_count, model_width)
    d_result = cotangent.reshape(queries_n, model_width)
    g_down = jnp.einsum("qf,qd->fd", act_low, d_result, preferred_element_type=jnp.float32)
    d_act = jnp.einsum("qd,fd->qf", d_result, full_down, preferred_element_type=jnp.float32)
    d_pre = gelu_back(d_act)[0].astype(jnp.bfloat16)
    g_up = jnp.einsum("qd,qf->df", hidden_low, d_pre, preferred_element_type=jnp.float32)
    d_hidden = jnp.einsum("qf,df->qd", d_pre, full_up, preferred_element_type=jnp.float32)
    d_middle_ln, g_gain_ffn = ffn_back(d_hidden)
    d_middle = d_result.astype(jnp.float32) + d_middle_ln
    d_branch = d_middle.astype(jnp.bfloat16)
    g_out = jnp.einsum("qe,qd->ed", attended, d_branch, preferred_element_type=jnp.float32)
    d_attended = jnp.einsum(
        "qd,ed->qe", d_branch, full_out, preferred_element_type=jnp.float32
    ).astype(jnp.bfloat16)
    scores_again = masked_scores(q_heads, k_heads, allowed, score_scale)
    probs = jnp.exp(scores_again - log_total)
    probs_again = probs.astype(jnp.bfloat16)
    d_att_heads = d_attended.reshape(queries_n, HEADS, head_size)
    d_probs = jnp.einsum("qhe,khe->hqk", d_att_heads, v_heads, preferred_element_type=jnp.float32)
    row_dot = jnp.sum(probs * d_probs, axis=-1, keepdims=True)
    d_scores = (probs * (d_probs - row_dot)).astype(jnp.bfloat16)
    d_queries = (
        (
            jnp.einsum("hqk,khe->qhe", d_scores, k_heads, preferred_element_type=jnp.float32)
            * score_scale
        )
        .reshape(queries_n, model_width)
        .astype(jnp.bfloat16)
    )
    d_keys = (
        (
            jnp.einsum("hqk,qhe->khe", d_scores, q_heads, preferred_element_type=jnp.float32)
            * score_scale
        )
        .reshape(key_rows, model_width)
        .astype(jnp.bfloat16)
    )
    d_values = (
        jnp.einsum("hqk,qhe->khe", probs_again, d_att_heads, preferred_element_type=jnp.float32)
        .reshape(key_rows, model_width)
        .astype(jnp.bfloat16)
    )
    g_query = jnp.einsum("qd,qe->de", lat_low, d_queries, preferred_element_type=jnp.float32)
    d_key_value = jnp.concatenate([d_keys, d_values], axis=1)
    g_key_value = jnp.einsum("kd,kx->dx", keys_in, d_key_value, preferred_element_type=jnp.float32)
    g_qkv = jnp.concatenate([g_query, g_key_value], axis=1).reshape(model_width, 3, model_width)
    back_flat = full_qkv.reshape(model_width, 3 * model_width)
    d_keys_in = jnp.einsum(
        "kx,dx->kd", d_key_value, back_flat[:, model_width:], preferred_element_type=jnp.float32
    )
    d_lat_norm = (
        jnp.einsum(
            "qe,de->qd", d_queries, back_flat[:, :model_width], preferred_element_type=jnp.float32
        )
        + d_keys_in[media_rows:]
    )
    d_lat_ln, g_gain_lat = lat_back(d_lat_norm)
    d_latents = (d_middle + d_lat_ln).reshape(item_slots, lat_count, model_width)
    d_mixed, g_gain_media = media_back(
        d_keys_in[:media_rows].reshape(frame_slots, patch_rows, model_width)
    )
    frame_grad = jnp.sum(d_mixed, axis=1)
    g_time = jnp.einsum("fd,ft->dt", frame_grad, time_hot, precision=highest)
    g_gains = jnp.stack([g_gain_media, g_gain_lat, g_gain_ffn], axis=1)
    reduced = reduce_grads(g_qkv, g_out, g_up, g_down, g_time, g_gains)
    local_sq = jnp.zeros((), jnp.float32)
    for grad in reduced:
        local_sq = local_sq + jnp.sum(grad * grad)
    grad_norm = jnp.sqrt(lax.psum(local_sq, (DP, FSDP)))
    return new_latents, d_latents, grad_norm, reduced


def solution(mesh):
    both = (DP, FSDP)
    one, two, three = P(both), P(both, None), P(both, None, None)
    updated = (three,) * 3 + (two,) * 15
    placed = (three, three, one, three, *updated)
    return jax.shard_map(
        on_device,
        mesh=mesh,
        in_specs=placed,
        out_specs=(three, three, P(), *updated),
        check_vma=False,
    )
```

```python
import functools
import math
import types

import jax
import jax.numpy as jnp
from jax import lax
from jax.experimental import pallas as pl
from jax.experimental.pallas import tpu as pltpu
from jax.sharding import PartitionSpec as P

DP, FSDP = "dp", "fsdp"
HEADS = 16
STEP = 10


highest = lax.Precision.HIGHEST
norm_eps = 1e-05
clip_limit = 1.0
beta_one = 0.9
beta_two = 0.999
adam_eps = 1e-08
decay_rate = 0.1

MESH=pl.DeviceIdType.MESH
ANY=pl.ANY

class Place:
    def __init__(self, n_z):
        dp = lax.axis_index(DP); fs = lax.axis_index(FSDP)
        self.n_z = n_z
        self.at = {"x": dp // 2, "c": dp % 2, "z": fs // 2, "y": fs % 2}
    def dev(self, **new):
        p = {**self.at, **new}
        return (p["x"] * 2 + p["c"], p["z"] * 2 + p["y"])
    def other(self, ax):
        return self.dev(**{ax: 1 - self.at[ax]})
    def along_z(self, k):
        return self.dev(z=(self.at["z"] + k) % self.n_z)
    def level(self):
        flip = lambda ax, by: 1 - self.at[ax] if by else self.at[ax]
        return [self.dev(x=flip("x", n & 4), c=flip("c", n & 2), y=flip("y", n & 1)) for n in range(1, 8)]
    def partners(self):
        return [self.other(a) for a in "cxy"] + [self.along_z(k) for k in range(1, self.n_z)]

def greet(place, wide=False):
    bar = pltpu.get_barrier_semaphore()
    others = place.level() + place.partners()[3:] if wide else place.partners()
    for d in others:
        pl.semaphore_signal(bar, inc=1, device_id=d, device_id_type=MESH)
    pl.semaphore_wait(bar, len(others))

def block_index(place, held, **at):
    where = {**place.at, **at}
    return tuple(slice(None) if ax in held else where[ax] for ax in "xczy")

class Gather:
    def __init__(self, place, src, dst, rows, cols, order, sems, base):
        self.place, self.src, self.dst = place, src, dst
        self.sl = (pl.ds(*rows), pl.ds(*cols))
        self.order, self.sems, self.base = order, sems, base
        self.copies = {}

    def region(self, held, **at):
        return self.dst.at[block_index(self.place, held, **at) + self.sl]

    def copy(self, src, dst, n, to):
        ss, rs = self.sems
        n += self.base
        return pltpu.make_async_remote_copy(src_ref=src, dst_ref=dst, send_sem=ss.at[n], recv_sem=rs.at[n], device_id=to, device_id_type=MESH)

    def start(self, step):
        ax, held, p = self.order[step], self.order[:step], self.place
        if ax == "z":
            self.line(step, 1)
            return
        d = self.copy(self.src.at[self.sl] if step == 0 else self.region(held), self.region(held), "xyc".index(ax), p.other(ax))
        d.start()
        self.copies[step] = d

    def line(self, step, k):
        p, held = self.place, self.order[:step]
        z, last = p.at["z"], p.n_z - 1
        for side, from_z, to_z in ((0, z - (k - 1), z + 1), (1, z + (k - 1), z - 1)):
            ok = (from_z >= 0) & (to_z <= last) if side == 0 else (from_z <= last) & (to_z >= 0)
            at = jnp.clip(from_z, 0, last)
            dst = self.region(held, z=at)
            src = self.src.at[self.sl] if step == 0 and k == 1 else dst
            d = self.copy(src, dst, 3 + 2 * (k - 1) + side, p.dev(z=jnp.clip(to_z, 0, last)))
            pl.when(ok)(d.start)
            came = z >= k if side == 0 else z + k <= last
            self.copies[step, k, side] = (d, ok, came)

    def came(self, step, k):
        for side in range(2):
            d, _, came = self.copies[step, k, side]
            pl.when(came)(d.wait_recv)

    def advance(self, step, k):
        if self.order[step] == "z":
            self.came(step, k)
            self.line(step, k + 1)

    def arrive(self, step):
        if self.order[step] == "z":
            self.came(step, self.place.n_z - 1)
        else:
            self.copies[step].wait_recv()

    def finish(self):
        for key, d in self.copies.items():
            if isinstance(key, tuple):
                pl.when(d[1])(d[0].wait_send)
            else:
                d.wait_send()


def n_sems(n_z):
    return 3 + 2 * (n_z - 1)


def number(plan):
    j, out = 0, []
    for stage in plan:
        new = []
        for piece in stage:
            new.append((j,) + piece); j += 1
        out.append(new)
    return out, j

ZYX, ZXY, XYZ, YXZ = ("z", "y", "x", "c"), ("z", "x", "y", "c"), ("x", "y", "z", "c"), ("y", "x", "z", "c")

BACK_LAG, SEND_SLOTS, LAND_SLOTS = 2, 3, 6
ROOM_B = 3
FINE_B = 0
WIDE_B = ((3, 2, 1), (2, 3, 1), (2, 2, 2))


class Scatter:
    def __init__(self, place, out, rows, cols, order, piece, turn, sems, bufs, total_sq):
        self.p, self.order, self.piece, self.width = place, order, piece, cols[1]
        model = out.shape[-1]
        self.out = out.at[cols[0] // model, pl.ds(*rows), pl.ds(cols[0] % model, cols[1])] if len(out.shape) == 3 else out.at[pl.ds(*rows), pl.ds(*cols)]
        self.ss, self.rs, self.ls = sems
        self.b, self.sq = bufs, total_sq
        self.turn, self.h, self.n = turn, turn % SEND_SLOTS, turn % LAND_SLOTS
        self.sent, self.moves = {}, {}

    def v(self, ref, *lead):
        return ref.at[lead + (slice(None), pl.ds(0, self.width))]

    def copy(self, src, dst, to, n):
        n += self.piece * n_sems(self.p.n_z)
        return pltpu.make_async_remote_copy(src_ref=src, dst_ref=dst, send_sem=self.ss.at[n], recv_sem=self.rs.at[n], device_id=to, device_id_type=MESH)

    def send(self, step, src, dst, ax):
        d = self.copy(src, dst, self.p.other(ax), "xyc".index(ax))
        d.start()
        self.sent[step] = d

    def add(self, count, dst, a, b):
        w = slice(0, self.width)

        def one(i, carry):
            (da, di), (aa, ai), (ba, bi) = dst(i), a(i), b(i)
            da[di + (slice(None), w)] = aa[ai + (slice(None), w)] + ba[bi + (slice(None), w)]
            return carry

        if count == 1:
            one(0, 0)
        else:
            lax.fori_loop(0, count, one, 0)

    def row(self, d):
        if self.order[0] == "z":
            return self.v(self.b.s0, self.h, slice(None), d, slice(None))
        return self.v(self.b.s2, self.h, d)

    def land(self, side, k):
        if self.order[0] == "z":
            return self.v(self.b.rz, self.n, side, k - 1, slice(None), slice(None))
        return self.v(self.b.rz, self.n, side, k - 1)

    def add_landed(self, d, side, k):
        b, h, n = self.b, self.h, self.n
        if self.order[0] == "z":
            mine = lambda i: (b.s0, (h, i // 2, d, i % 2))
            self.add(4, mine, mine, lambda i: (b.rz, (n, side, k - 1, i // 2, i % 2)))
        else:
            mine = lambda i: (b.s2, (h, d))
            self.add(1, mine, mine, lambda i: (b.rz, (n, side, k - 1)))

    def line(self, step, k):
        p = self.p
        z, last = p.at["z"], p.n_z - 1
        for side, d, to in ((0, p.n_z - k + z, z + 1), (1, z - (p.n_z - k), z - 1)):
            ok = d <= last if side == 0 else d >= 0
            at = jnp.clip(d, 0, last)
            if k > 1:
                got, _, came = self.moves[step, k - 1, side]

                def forward(got=got, at=at, side=side):
                    got.wait_recv()
                    self.add_landed(at, side, k - 1)

                pl.when(came)(forward)
            c = self.copy(self.row(at), self.land(side, k), p.dev(z=jnp.clip(to, 0, last)), 3 + 2 * (k - 1) + side)
            pl.when(ok)(c.start)
            came = z <= k if side == 0 else z >= last - k
            came = came & (z > 0 if side == 0 else z < last)
            self.moves[step, k, side] = (c, ok, came)

    def last_move(self, step):
        p = self.p
        z, k = p.at["z"], p.n_z - 1
        for side in range(2):
            c, _, came = self.moves[step, k, side]

            def end(c=c, side=side):
                c.wait_recv()
                self.add_landed(z, side, k)

            pl.when(came)(end)

    def advance(self, step, k):
        if self.order[step] == "z":
            self.line(step, k + 1)

    def free(self, step):
        if step == 3:
            self.sent.pop(3).wait()
        elif self.order[step] == "z":
            for k in range(1, self.p.n_z):
                for side in range(2):
                    c, ok, _ = self.moves.pop((step, k, side))
                    pl.when(ok)(c.wait_send)
        else:
            self.sent.pop(step).wait_send()

    def start(self, step):
        p, b, A, h, n, nz = self.p, self.b, slice(None), self.h, self.n, self.p.n_z
        at = p.at
        if step < 3 and self.order[step] == "z":
            if step == 2:
                first, nxt = self.order[:2]
                mine = (lambda i: (b.s1, (h, i, at[nxt]))) if first == "x" else (lambda i: (b.s1, (h, at[nxt], i)))
                self.sent[1].wait_recv()
                self.add(nz, lambda i: (b.s2, (h, i)), mine, lambda i: (b.r2, (n, i)))
            self.line(step, 1)
            return
        first = self.order[0]
        if step == 0:
            o = 1 - at[first]
            src = self.v(b.s0, h, o, A, A) if first == "x" else self.v(b.s0, h, A, A, o)
            self.send(0, src, self.v(b.r1, n, A, A), first)
        elif step == 1 and first == "z":
            self.last_move(0)
            for x in range(2):
                b.s1[h, x, :, :, 0 : self.width] = b.s0[h, x, at["z"], :, :, 0 : self.width]
            self.send(1, self.v(b.s1, h, 1 - at["x"], A), self.v(b.r1, n, A), "x")
        elif step == 1:
            self.sent[0].wait_recv()
            o = 1 - at[self.order[1]]
            i0, i1 = (lambda i: i // 2), (lambda i: i % 2)
            if first == "y":
                i0, i1 = (lambda i: i // nz), (lambda i: i % nz)
                mine = lambda i: (b.s0, (h, i0(i), i1(i), at["y"]))
            else:
                mine = lambda i: (b.s0, (h, at["x"], i0(i), i1(i)))
            self.add(2 * nz, lambda i: (b.s1, (h, i0(i), i1(i))), mine, lambda i: (b.r1, (n, i0(i), i1(i))))
            src = self.v(b.s1, h, A, o) if first == "x" else self.v(b.s1, h, o, A)
            self.send(1, src, self.v(b.r2, n, A), self.order[1])
        elif step == 2:
            self.sent[1].wait_recv()
            self.add(2, lambda i: (b.s2, (h, i)), lambda i: (b.s1, (h, at["x"], i)), lambda i: (b.r1, (n, i)))
            self.send(2, self.v(b.s2, h, 1 - at["y"]), self.v(b.r2, n), "y")
        else:
            w = slice(0, self.width)
            if first == "z":
                self.sent[2].wait_recv()
                total = b.s2[h, at["y"], :, w].astype(jnp.float32) + b.r2[n, :, w].astype(jnp.float32)
            else:
                p_last = nz - 1
                for side in range(2):
                    c, _, came = self.moves[2, p_last, side]
                    pl.when(came)(c.wait_recv)
                total = b.s2[h, at["z"], :, w].astype(jnp.float32)
                for side in range(2):
                    came = self.moves[2, p_last, side][2]
                    landed = b.rz[n, side, p_last - 1, :, w].astype(jnp.float32)
                    total = total + jnp.where(came, landed, 0.0)
            b.o[h, :, w] = total
            self.sq[:, w] += total * total
            d = pltpu.make_async_copy(self.v(b.o, h), self.out, self.ls.at[self.piece])
            d.start()
            self.sent[3] = d


def sum_squares(place, n_z, bufs, sems, out):
    ns, nr = sems
    sq, part, zs = bufs.sq, bufs.n, bufs.nz
    acc = jnp.zeros((8, 128), jnp.float32)
    for i in range(sq.shape[0] // 8):
        for j in range(sq.shape[1] // 128):
            acc = acc + sq[i * 8 : (i + 1) * 8, j * 128 : (j + 1) * 128]
    at = place.at
    me = at["x"] * 4 + at["c"] * 2 + at["y"]
    part[me] = acc
    made = []
    for n, d in enumerate(place.level()):
        made.append(pltpu.make_async_remote_copy(src_ref=part.at[me], dst_ref=part.at[me], send_sem=ns.at[n], recv_sem=nr.at[n], device_id=d, device_id_type=MESH))
    for d in made:
        d.start()
    for d in made:
        d.wait()
    acc = part[0]
    for n in range(1, 8):
        acc = acc + part[n]
    z = at["z"]
    zs[z] = acc
    made = []
    for k in range(1, n_z):
        d = pltpu.make_async_remote_copy(src_ref=zs.at[z], dst_ref=zs.at[z], send_sem=ns.at[6 + k], recv_sem=nr.at[6 + k], device_id=place.along_z(k), device_id_type=MESH)
        d.start()
        made.append(d)
    for d in made:
        d.wait()
    total = zs[0]
    for k in range(1, n_z):
        total = total + zs[k]
    out[...] = jnp.broadcast_to(jnp.sqrt(jnp.sum(total, keepdims=True)), out.shape)


def backward_kernel(n_z, plan, names, *refs):
    b = types.SimpleNamespace(**dict(zip(names, refs)))
    ss, rs, ls, ns, nr, ws, ps, pr, lt_sem, rhs_sem, out_sem = refs[len(names) :]
    own_grads = (b.g_qkv, b.g_out, b.g_up, b.g_down, b.g_tiny)
    early = [
        pltpu.make_async_copy(src, dst, out_sem.at[1 + n])
        for n, (src, dst) in enumerate(((b.p_act, b.lt), (b.mid_in, b.mid), (b.q_in, b.q), (b.keys, b.k), (b.v_in, b.v), (b.lat_in, b.lat)))
    ]
    for d in early:
        d.start()

    def here(*which):
        for n in which:
            early[n].wait()

    place = Place(n_z)
    greet(place, True)
    core, A = place.at["c"], slice(None)
    queries_n, model = b.q_in.shape
    key_rows = b.keys.shape[0]
    media_rows = key_rows - queries_n
    hidden_n = b.dpre.shape[1]
    head = model // HEADS
    windows, group_width = head_windows(head)
    scale = 1.0 / head**0.5
    f32, bf = jnp.float32, jnp.bfloat16
    b.sq[...] = jnp.zeros_like(b.sq)
    given = {}

    def give(src, dst):
        n = len(given)
        d = pltpu.make_async_remote_copy(src_ref=src, dst_ref=dst, send_sem=ps.at[n], recv_sem=pr.at[n], device_id=place.other("c"), device_id_type=MESH)
        d.start()
        given[id(dst)] = [d, False]

    def got(dst):
        held_copy = given[id(dst)]
        if not held_copy[1]:
            held_copy[0].wait_recv()
            held_copy[1] = True

    give(b.dpre, b.x_dpre)

    wbuf = b.wbuf

    def fetch(src, slot):
        d = pltpu.make_async_copy(src, wbuf.at[slot], ws.at[slot])
        d.start()
        return d

    def tiles_of(jobs, use):
        ahead = fetch(jobs[0], 0)
        for i in range(len(jobs)):
            now = ahead
            if i + 1 < len(jobs):
                ahead = fetch(jobs[i + 1], (i + 1) % 2)
            now.wait()
            use(i, wbuf[i % 2].reshape(384, model))

    def hidden_part(i):
        d = pltpu.make_async_copy(b.dpre.at[:, pl.ds(i * model, model)], b.datt, ws.at[4])
        d.start()
        d.wait()

        def use(n, w):
            got_ = dot(b.datt[...], w, ((1,), (1,)))
            cols = slice(n * 384, (n + 1) * 384)
            if i == 0:
                b.dmid[:, cols] = got_
            else:
                b.dmid[:, cols] += got_

        tiles_of([b.f_up.at[x, c, :, :, :, pl.ds(i * model, model)] for x in range(2) for c in range(2)], use)

    def norm_back(rows_in, grad, gain):
        centered = rows_in - jnp.mean(rows_in, axis=-1, keepdims=True)
        inv = lax.rsqrt(jnp.mean(centered * centered, axis=-1, keepdims=True) + norm_eps)
        hat = centered * inv
        scaled = grad * gain
        back = inv * (scaled - jnp.mean(scaled, axis=-1, keepdims=True) - hat * jnp.mean(scaled * hat, axis=-1, keepdims=True))
        return back, jnp.sum(grad * hat, axis=0, keepdims=True)

    def ffn_norm():
        d = pltpu.make_async_copy(b.f_tiny, b.tiny, ws.at[3])
        d.start()
        e = pltpu.make_async_copy(b.p_cot.at[core], b.dbranch, ws.at[4])
        e.start()
        d.wait()
        e.wait()
        here(1)
        b.tiny_t[...] = b.tiny[...].reshape(model, 128).astype(f32).T
        b.gsmall[...] = jnp.zeros_like(b.gsmall)

        def rows(i, carry):
            at = pl.ds(pl.multiple_of(i * 64, 64), 64)
            back, gain = norm_back(b.mid[at, :], b.dmid[at, :], b.tiny_t[10:11, :])
            total = b.dbranch[at, :].astype(f32) + back
            b.dmid[at, :] = total
            b.dbranch[at, :] = total.astype(bf)
            b.gsmall[10:11, :] += gain
            return carry

        lax.fori_loop(0, queries_n // 64, rows, 0)
        give(b.dbranch, b.x_branch)

    def attended_back():
        def use(n, w):
            b.datt[:, n * 384 : (n + 1) * 384] = dot(b.dbranch[...], w, ((1,), (1,))).astype(bf)

        tiles_of([b.f_out.at[x, c] for x in range(2) for c in range(2)], use)

    def attend_back(g):
        if g == 0:
            here(2, 3, 4)
            b.bias[...] = own_keys(b.counts, media_rows, queries_n, 48)
        base = g * group_width
        n_tiles = group_width // 128
        last = {t: max(j for j, (t0, t1, _) in enumerate(windows) if t0 <= t < t1) for t in range(n_tiles)}
        sums = {}
        for j, (t0, t1, start) in enumerate(windows):
            cols = slice(base + t0 * 128, base + t1 * 128)
            q_in, k_in = lanes_of(queries_n, t1 - t0, start, head), lanes_of(key_rows, t1 - t0, start, head)
            qh = b.q[:, cols]
            qh = jnp.where(q_in, qh, jnp.zeros_like(qh))
            dah = b.datt[:, cols]
            dah = jnp.where(q_in, dah, jnp.zeros_like(dah))
            kw = b.k[:, cols]
            h = g * len(windows) + j
            p = jnp.exp(dot(kw, qh, ((1,), (1,))) * scale + b.bias[...] - b.lse[h : h + 1, :])
            dp = dot(b.v[:, cols], dah, ((1,), (1,)))
            row_dot = jnp.sum(p * dp, axis=0, keepdims=True)
            ds = (p * (dp - row_dot)).astype(bf)
            kh = jnp.where(k_in, kw, jnp.zeros_like(kw))
            parts = ((b.dv, dot(p.astype(bf), dah)), (b.dk, dot(ds, qh) * scale), (b.dq, dot(ds, kh, ((0,), (0,))) * scale))
            for n, (into, part) in enumerate(parts):
                for t in range(t0, t1):
                    new = part[:, (t - t0) * 128 : (t - t0 + 1) * 128]
                    sums[n, t] = sums[n, t] + new if (n, t) in sums else new
                    if last[t] == j:
                        into[:, base + t * 128 : base + (t + 1) * 128] = sums.pop((n, t)).astype(bf)
        if g == model // group_width - 1:
            give(b.dq, b.x_dq)
            give(b.dk, b.x_dk)
            give(b.dv, b.x_dv)

    def keys_back(n):
        x, c = n // 2, n % 2
        made = [fetch(b.f_qkv.at[x, c, :, :, :, pl.ds(i * model, model)], i) for i in range(3)]
        for d in made:
            d.wait()
        w = [wbuf[i].reshape(384, model) for i in range(3)]
        cols = slice(n * 384, (n + 1) * 384)
        lat_rows = slice(media_rows, key_rows)
        tail = dot(b.dq[...], w[0], ((1,), (1,))) + dot(b.dk[lat_rows, :], w[1], ((1,), (1,))) + dot(b.dv[lat_rows, :], w[2], ((1,), (1,)))
        b.k[lat_rows, cols] = tail.astype(bf)
        step = media_rows // 3
        for i in range(3):
            rows = slice(i * step, (i + 1) * step)
            b.k[rows, cols] = (dot(b.dk[rows, :], w[1], ((1,), (1,))) + dot(b.dv[rows, :], w[2], ((1,), (1,)))).astype(bf)

    def latents_back():
        here(5)

        def rows(i, carry):
            at = pl.ds(pl.multiple_of(i * 64, 64), 64)
            grad = b.k[pl.ds(pl.multiple_of(media_rows + i * 64, 16), 64), :].astype(f32)
            back, gain = norm_back(b.lat[at, :].astype(f32), grad, b.tiny_t[9:10, :])
            b.dmid[at, :] = b.dmid[at, :] + back
            b.gsmall[9:10, :] += gain
            return carry

        lax.fori_loop(0, queries_n // 64, rows, 0)
        d = pltpu.make_async_copy(b.dmid, b.d_lat, out_sem.at[0])
        d.start()
        late.append(d)

    late = []

    def media_back(part):
        step = media_rows // parts
        frames = step // 48
        d = pltpu.make_async_copy(b.media.at[pl.ds(part * step, step)], b.mrows, ws.at[3])
        d.start()
        if part == 0:
            b.hot[...] = time_table_rows(b.counts, media_rows, 48, 128, 8)
        d.wait()

        def frame(i, carry):
            at = pl.ds(pl.multiple_of(i * 48, 48), 48)
            whole = pl.ds(pl.multiple_of(part * step + i * 48, 48), 48)
            mixed = b.mrows[at, :].astype(f32) + dot(b.hot[whole, :], b.tiny_t[...].astype(bf))
            back, gain = norm_back(mixed, b.k[whole, :].astype(f32), b.tiny_t[8:9, :])
            b.gsmall[8:9, :] += gain
            f = part * frames + i
            ends = frame_ends(b.counts)
            time = f
            for s, end in enumerate(ends):
                time = time - jnp.where(f >= end, b.counts[s], 0)
            time = jnp.where(f < ends[-1], time, -1)
            at_time = jnp.where(lax.broadcasted_iota(jnp.int32, (8, 1), 0) == time, 1.0, 0.0)
            b.gsmall[0:8, :] += at_time * jnp.sum(back, axis=0, keepdims=True)
            return carry

        lax.fori_loop(0, frames, frame, 0)

    def small():
        b.tiny[...] = b.gsmall[...].T.astype(bf).reshape(b.tiny.shape)
        give(b.tiny.at[:, 1 - core], b.x_tiny)

    held = [None]

    def left(src):
        if held[0] is src:
            return
        if held[0] is None:
            here(0)
            held[0] = src
            return
        held[0] = src
        if src is b.p_keys:
            into = b.ltk
        elif src is b.p_act:
            into = b.lt
        else:
            into = b.lt.at[:, :, pl.ds(0, 2 * n_z)]
        d = pltpu.make_async_copy(src, into, lt_sem.at[0])
        d.start()
        d.wait()

    coming = {}

    def sources(w, first):
        if w == 3:
            return b.p_cot.at[core], b.p_cot.at[1 - core], first
        if w == 2:
            return b.dpre, b.x_dpre, first
        if w == 1:
            return b.dbranch, b.x_branch, first
        return (b.dq, b.dk, b.dv)[first // model], (b.x_dq, b.x_dk, b.x_dv)[first // model], first % model

    def right(t):
        w, first, width = plan_of[t]
        if w == 4 or t in coming:
            return
        mine, theirs, at = sources(w, first)
        if w != 3:
            if id(theirs) not in given:
                return
            got(theirs)
        cols = pl.ds(at, width)
        made = []
        if w in (2, 3):
            made.append(pltpu.make_async_copy(mine.at[:, cols], b.rhs.at[t % 2, 0, :, pl.ds(0, width)], rhs_sem.at[t % 2, 0]))
        into = b.rhsk.at[:, pl.ds(0, width)] if w == 0 and first >= model else b.rhs.at[t % 2, 1, :, pl.ds(0, width)]
        made.append(pltpu.make_async_copy(theirs.at[:, cols], into, rhs_sem.at[t % 2, 1]))
        for d in made:
            d.start()
        coming[t] = made

    def blocks(x, k, group):
        if group == 1:
            return [b.lt[s, x, 0 : 2 * n_z].reshape(96 * n_z, queries_n) for s in (core, 1 - core)]
        return [jnp.concatenate([b.lt[s, x, i * group + k] for i in range(2 * n_z)], axis=0) for s in (core, 1 - core)]

    def fill(t, pieces):
        w, first, width = plan_of[t]
        h = pieces[0].h
        if w == 4:
            got(b.x_tiny)
            d = pltpu.make_async_copy(b.x_tiny, b.tiny2, ws.at[3])
            d.start()
            d.wait()

            def one(i, carry):
                x, z, y = i // (2 * n_z), (i // 2) % n_z, i % 2
                pieces[0].b.s0[h, x, z, y, :, 0:128] = b.tiny[x, core, z, y] + b.tiny2[x, z, y]
                return carry

            lax.fori_loop(0, 4 * n_z, one, 0)
            return
        right(t)
        for d in coming.pop(t):
            d.wait()
        mine, _, at = sources(w, first)
        keyed = w == 0 and first >= model
        left((b.p_keys if keyed else b.p_lat, b.p_att, b.p_hid, b.p_act)[w])
        r = [b.rhs[t % 2, 0, :, 0:width] if w in (2, 3) else mine[:, pl.ds(at, width)], b.rhsk[:, 0:width] if keyed else b.rhs[t % 2, 1, :, 0:width]]
        for x in range(2):
            if keyed:
                l = [b.ltk[s, x].reshape(96 * n_z, key_rows) for s in (core, 1 - core)]
            else:
                l = blocks(x, rows_of[t] // 48, 4 if w == 3 else 1)
            sums = (dot(l[0], r[0]) + dot(l[1], r[1])).astype(bf)
            start = 0
            for g in pieces:
                g.b.s0[h, x, :, :, :, 0 : g.width] = sums[:, start : start + g.width].reshape(n_z, 2, 48, g.width)
                start += g.width
        if t + 1 < total_stages:
            right(t + 1)

    parts = 6
    work = [(3, 5, functools.partial(hidden_part, i)) for i in range(hidden_n // model)] + [(0, 3, ffn_norm), (0, 4, attended_back)]
    work += [(0, 9, functools.partial(attend_back, g)) for g in range(model // group_width)]
    work += [(0, 5, functools.partial(keys_back, n)) for n in range(4)] + [(0, 3, latents_back)]
    work += [(0, 2, functools.partial(media_back, i)) for i in range(parts)] + [(0, 2, small)]

    def run_until(dst):
        while id(dst) not in given:
            work.pop(0)[2]()

    kinds = [types.SimpleNamespace(**{n: getattr(b, n + k) for n in NAMES}) for k in SETS]
    plan_of = [(st[0][1], st[0][3][0], sum(p[3][1] for p in st)) for st in plan]
    rows_of = [st[0][2][0] for st in plan]
    total_stages = len(plan)
    stages = [
        [Scatter(place, own_grads[w], rows, cols, order, j, t, (ss, rs, ls), kinds[part], b.sq) for part, (j, w, rows, cols, order) in enumerate(stage)]
        for t, stage in enumerate(plan)
    ]
    ticks = total_stages + 3 * BACK_LAG

    def moves(t, k):
        for back in range(3):
            u = t - BACK_LAG * back - 1
            if 0 <= u < total_stages:
                for g in stages[u]:
                    g.advance(back, k)

    for t in range(ticks):
        moves(t, 1)
        for back in range(4):
            u = t - BACK_LAG * back
            if not 0 <= u < total_stages:
                continue
            if u >= SEND_SLOTS:
                for g in stages[u - SEND_SLOTS]:
                    if back == 3 or g.order[back] == "z" or back in g.sent:
                        g.free(back)
            if back == 0:
                w = plan_of[u][0]
                run_until((b.x_dv, b.x_branch, b.x_dpre, b.x_dpre, b.x_tiny)[w])
                fill(u, stages[u])
            for g in stages[u]:
                g.start(back)
        for k in range(2, n_z - 1):
            moves(t, k)
        room = ROOM_B
        while work and room > 0:
            _, cost, piece = work.pop(0)
            room -= cost
            piece()
    for st in stages[-SEND_SLOTS:]:
        for g in st:
            for back in range(4):
                g.free(back)
    for d, done in given.values():
        d.wait_send()
    for d in late:
        d.wait()
    sum_squares(place, n_z, b, (ns, nr), b.norm)


SETS = "abc"
NAMES = ("s0", "r1", "s1", "r2", "s2", "rz", "o")


def backward_plan(shards, model):
    tile = 128
    stages = []

    def split(w, row, first, widths=None):
        widths = widths or WIDE_B[len(stages) % len(WIDE_B)]
        at, pieces = first, []
        for width, order in zip(widths, (("x", "y", "z"), ("y", "x", "z"), ("z", "x", "y"))):
            pieces.append((w, (row, 48), (at, width * tile), order))
            at += width * tile
        stages.append(pieces)

    for row in range(0, shards[3].shape[0], 48):
        for first in range(0, model, 768):
            split(3, row, first)
    for w, cols in ((2, shards[2].shape[1]), (1, model), (0, 3 * model)):
        for first in range(0, cols - FINE_B * 768 * (w == 0), 768):
            split(w, 0, first)
    for first in range(3 * model - FINE_B * 768, 3 * model, 384):
        split(0, 0, first, (1, 1, 1))
    return stages + [[(4, (0, 48), (0, 128), ("x", "y", "z"))]]


def backward_all(full, made, lat, media, counts, n_z):
    queries_n, model = lat.shape
    media_rows = media.shape[0]
    key_rows = queries_n + media_rows
    shards = [jax.ShapeDtypeStruct(f.shape[4:], f.dtype) for f in full]
    hidden_n = shards[2].shape[1]
    plan, count = number(backward_plan(shards, model))
    q, k, v, dpre, mid, new, lse, p_keys, p_lat, p_att, p_hid, p_act, p_cot = made
    given = dict(f_qkv=full[0], f_out=full[1], f_up=full[2], f_tiny=full[4], dpre=dpre, p_keys=p_keys, p_lat=p_lat, p_att=p_att, p_hid=p_hid, p_act=p_act, p_cot=p_cot,
                 media=media, q_in=q, keys=k, v_in=v, mid_in=mid, lse=lse, lat_in=lat, counts=counts)
    bf, f32 = jnp.bfloat16, jnp.float32
    grads = [(s.shape, f32) for s in shards]
    grads[0] = ((3, shards[1].shape[0], model), f32)
    outs = dict(g_qkv=grads[0], g_out=grads[1], g_up=grads[2], g_down=grads[3], g_tiny=grads[4], d_lat=((queries_n, model), f32), norm=((8, 128), f32),
                x_dpre=((queries_n, hidden_n), bf), x_branch=((queries_n, model), bf), x_dq=((queries_n, model), bf), x_dk=((key_rows, model), bf), x_dv=((key_rows, model), bf),
                x_tiny=((2, n_z, 2, 48, 128), bf))
    W, S, L = 384, SEND_SLOTS, LAND_SLOTS
    N = max(w[2] for w in WIDE_B) * 128
    vm = dict(s0a=((S, 2, n_z, 2, 48, W), bf), r1a=((L, n_z, 2, 48, W), bf), s1a=((S, n_z, 2, 48, W), bf), r2a=((L, n_z, 48, W), bf), s2a=((S, n_z, 48, W), bf), rza=((L, 2, n_z - 1, 48, W), bf), oa=((S, 48, W), f32),
              s0b=((S, 2, n_z, 2, 48, W), bf), r1b=((L, 2, n_z, 48, W), bf), s1b=((S, 2, n_z, 48, W), bf), r2b=((L, n_z, 48, W), bf), s2b=((S, n_z, 48, W), bf), rzb=((L, 2, n_z - 1, 48, W), bf), ob=((S, 48, W), f32),
              s0c=((S, 2, n_z, 2, 48, N), bf), rzc=((L, 2, n_z - 1, 2, 2, 48, N), bf), r1c=((L, 2, 48, N), bf), s1c=((S, 2, 2, 48, N), bf), s2c=((S, 2, 48, N), bf), r2c=((L, 48, N), bf), oc=((S, 48, N), f32),
          sq=((48, W), f32), n=((8, 8, 128), f32), nz=((n_z, 8, 128), f32),
          wbuf=((3, n_z, 2, 48, model), bf), dmid=((queries_n, model), f32), dbranch=((queries_n, model), bf), datt=((queries_n, model), bf),
          q=(q.shape, bf), v=(v.shape, bf), mid=(mid.shape, f32), lat=(lat.shape, bf), bias=((key_rows, queries_n), f32), hot=((media_rows, 128), bf), dq=((queries_n, model), bf), k=((key_rows, model), bf), dk=((key_rows, model), bf), dv=((key_rows, model), bf), tiny=((2, 2, n_z, 2, 48, 128), bf), tiny_t=((128, model), f32),
          gsmall=((128, model), f32), tiny2=((2, n_z, 2, 48, 128), bf), mrows=((media_rows // 6, model), bf),
          lt=(p_act.shape, bf), ltk=(p_keys.shape, bf), rhs=((2, 2, queries_n, 768), bf), rhsk=((key_rows, 768), bf))
    sem = pltpu.SemaphoreType.DMA
    in_vmem, in_any = pl.BlockSpec(memory_space=pltpu.VMEM), pl.BlockSpec(memory_space=ANY)
    resident = tuple(id(a) for a in (lse,))
    n_copies = count * n_sems(n_z)
    res = pl.pallas_call(
        functools.partial(backward_kernel, n_z, plan, (*given, *outs, *vm)),
        out_shape=[jax.ShapeDtypeStruct(*o) for o in outs.values()],
        in_specs=[pl.BlockSpec(memory_space=pltpu.SMEM) if a is counts else in_vmem if id(a) in resident else in_any for a in given.values()],
        out_specs=[in_vmem if o is outs["norm"] else in_any for o in outs.values()],
        scratch_shapes=[pltpu.VMEM(*m) for m in vm.values()] + [sem((n_copies,)), sem((n_copies,)), sem((count,)), sem((n_z + 6,)), sem((n_z + 6,)), sem((5,)), sem((8,)), sem((8,)), sem((1,)), sem((2, 2)), sem((7,))],
        name="backward_and_scatter",
        compiler_params=pltpu.CompilerParams(collective_id=1, has_side_effects=True, vmem_limit_bytes=62 * 2**20),
    )(*given.values())
    return types.SimpleNamespace(**dict(zip(outs, res)))


def update_kernel(rates, norm, *refs):
    factor = jnp.minimum(1.0, clip_limit / (norm[0:1, 0:1] + 1e-06))
    n = len(rates)
    ws, ms, vs, gs, rows, outs = refs[:n], refs[n : 2 * n], refs[2 * n : 3 * n], refs[3 * n : 4 * n - 1], refs[4 * n - 1 : 4 * n + 1], refs[4 * n + 1 :]
    for row, o in zip(rows, outs[3 * n :]):
        o[...] = row[...]
    outs[-1][...] = norm[0:1, 0:1]
    small = gs[4][...].T
    steps = ws[4].shape[0]
    grads = [g[...] for g in gs[:4]] + [small[0:steps, :], small[steps : steps + 3, :]]
    for i, g in enumerate(grads):
        new = adamw_step(ws[i][...], ms[i][...], vs[i][...], g, factor if g.ndim == 2 else factor[None], rates[i])
        for o, value in zip(outs[3 * i : 3 * i + 3], new):
            o[...] = value


def update_all(norm, masters, firsts, seconds, grads, rows, rates):
    steps = masters[1].shape[0] // 8

    def spec(a):
        if a.ndim == 3:
            return pl.BlockSpec((3, 8, a.shape[2]), lambda i: (0, i, 0))
        if any(a is r for r in rows):
            return pl.BlockSpec((64, a.shape[1]), lambda i: (jnp.minimum(i, a.shape[0] // 64 - 1), 0))
        if a.shape[1] > 128:
            return pl.BlockSpec((a.shape[0] // steps, a.shape[1]), lambda i: (i, 0))
        return pl.BlockSpec(a.shape, lambda i: (0, 0))

    args = [norm, *masters, *firsts, *seconds, *grads, *rows]
    outs = [a for w in masters for a in (w, w, w)] + list(rows) + [jax.ShapeDtypeStruct((1, 1), jnp.float32)]
    return pl.pallas_call(
        functools.partial(update_kernel, rates),
        grid=(steps,),
        out_shape=[jax.ShapeDtypeStruct(a.shape, a.dtype) for a in outs],
        in_specs=[spec(a) for a in args],
        out_specs=[spec(a) for a in outs],
        name="adamw",
        compiler_params=pltpu.CompilerParams(vmem_limit_bytes=62 * 2**20),
    )(*args)


def out_copies(pairs, sems, at, running):
    for src, dst in pairs:
        d = pltpu.make_async_copy(src, dst, sems.at[len(running)])
        d.start()
        running.append(d)


def dot(a, b, contract=((1,), (0,))):
    return lax.dot_general(a, b, (contract, ((), ())), preferred_element_type=jnp.float32)


def head_windows(head):
    group = 128 // math.gcd(head, 128)
    out = []
    for j in range(group):
        first, last = j * head // 128, ((j + 1) * head - 1) // 128
        out.append((first, last + 1, j * head - first * 128))
    return out, group * head


def lanes_of(rows, tiles, start, head):
    lane = lax.broadcasted_iota(jnp.int32, (rows, tiles * 128), 1)
    return (lane >= start) & (lane < start + head)


def normed(rows_in, gain):
    centered = rows_in - jnp.mean(rows_in, axis=-1, keepdims=True)
    var_row = jnp.mean(centered * centered, axis=-1, keepdims=True)
    return centered * lax.rsqrt(var_row + norm_eps) * gain


def frame_ends(counts):
    ends, total = [], 0
    for s in range(counts.shape[0]):
        total = total + counts[s]
        ends.append(total)
    return ends


def time_table_rows(counts, rows, patch, lanes, time_len):
    row = lax.broadcasted_iota(jnp.int32, (rows, lanes), 0)
    lane = lax.broadcasted_iota(jnp.int32, (rows, lanes), 1)
    ends = frame_ends(counts)
    start = jnp.zeros((rows, lanes), jnp.int32)
    for s, end in enumerate(ends):
        start = start + jnp.where(row >= end * patch, counts[s] * patch, 0)
    off = row - start - lane * patch
    live = (off >= 0) & (off < patch) & (row < ends[-1] * patch) & (lane < time_len)
    return jnp.where(live, 1.0, 0.0).astype(jnp.bfloat16)


def own_keys(counts, media_rows, queries_n, patch):
    slots = counts.shape[0]
    each = queries_n // slots
    shape = (media_rows + queries_n, queries_n)
    row = lax.broadcasted_iota(jnp.int32, shape, 0)
    lane = lax.broadcasted_iota(jnp.int32, shape, 1)
    owner, asks = jnp.zeros(shape, jnp.int32), jnp.zeros(shape, jnp.int32)
    for s, end in enumerate(frame_ends(counts)):
        owner = owner + jnp.where(row >= end * patch, 1, 0)
        if s + 1 < slots:
            asks = asks + jnp.where(lane >= (s + 1) * each, 1, 0)
    mine = jnp.zeros(shape, jnp.int32)
    for s in range(1, slots):
        mine = mine + jnp.where(row >= media_rows + s * each, 1, 0)
    owner = jnp.where(row >= media_rows, mine, owner)
    return jnp.where(owner == asks, 0.0, -1e30)


def forward_kernel(n_z, plan, needs, *refs):
    (w_qkv, w_out, w_up, w_down, w_time, w_gains, lat_in, media_in, cot_in, counts), full, outs, scratch = refs[:10], refs[10:15], refs[15:27], refs[27:]
    o_q, o_k, o_v, o_dpre, o_mid, o_new, o_lse, p_keys, p_lat, p_att, p_hid, p_act = outs[:12]
    p_cot, *scratch = scratch
    *sh, small, hot, bias, lat, media, cot = scratch[:11]
    keys, q, k, v, att, hid, act, slope, dact, mid, new, tiny, tiny_t, lse, wbuf, wdown, flip, flip_keys, ss, rs, ls, os_, ws, ps, pr, pl_, ins = scratch[11:]
    f_qkv, f_out, f_up, f_down, f_tiny = full
    place = Place(n_z)
    queries_n, model = lat.shape
    coming = [pltpu.make_async_copy(src, dst, ins.at[n]) for n, (src, dst) in enumerate(((lat_in, lat), (cot_in, cot), (media_in, media)))]
    for d in coming:
        d.start()
    for i in range(3):
        sh[0][:, i * model : (i + 1) * model] = w_qkv[i].astype(jnp.bfloat16)
    for low, w in zip(sh[1:4], (w_out, w_up, w_down)):
        low[...] = w[...].astype(jnp.bfloat16)
    time_len = w_time.shape[0]
    small[...] = jnp.zeros_like(small)
    small[0:time_len, :] = w_time[...]
    small[time_len : time_len + 3, :] = w_gains[...]
    sh[4][...] = small[...].T.astype(jnp.bfloat16)
    greet(place)
    media_rows = media.shape[0]
    key_rows = media_rows + queries_n
    hidden_n = act.shape[1]
    head = model // HEADS
    windows, group_width = head_windows(head)
    scale = 1.0 / head**0.5
    written = []
    given = []
    core = place.at["c"]

    def give(src, dst, theirs):
        n = len(given)
        if theirs:
            d = pltpu.make_async_remote_copy(src_ref=src, dst_ref=dst, send_sem=ps.at[n], recv_sem=pr.at[n], device_id=place.other("c"), device_id_type=MESH)
        else:
            d = pltpu.make_async_copy(src, dst, pl_.at[n])
        d.start()
        given.append([d, theirs, False])
        return n

    def gone(n):
        d, theirs, done = given[n]
        if not done:
            d.wait_send() if theirs else d.wait()
            given[n][2] = True

    def turn(a, dst, slot, x, wide, before=()):
        made = []
        for n in before:
            gone(n)
        for theirs in (False, True):
            who = 1 - core if theirs else core
            for m in range(wide // 384):
                cols = pl.ds(pl.multiple_of((x * 2 + who) * wide + m * 384, 128), 384)
                flip[slot] = a[:, cols].T.reshape(8, 48, queries_n)
                made.append(give(flip.at[slot], dst.at[core, x, pl.ds(m * 8, 8)], theirs))
                slot += 1
        return made

    def load(src, dst):
        d = pltpu.make_async_copy(src, dst, ws.at[0])
        d.start()
        d.wait()

    def write(*pairs):
        out_copies(pairs, os_, 0, written)

    def norms():
        for d in coming:
            d.wait()
        hot[...] = time_table_rows(counts, media_rows, 48, hot.shape[1], time_len)
        load(f_tiny, tiny)
        tiny_t[...] = tiny[...].reshape(model, 128).astype(jnp.float32).T
        give(cot, p_cot.at[core], False)
        give(cot, p_cot.at[core], True)
        hid[...] = normed(lat[...].astype(jnp.float32), tiny_t[9:10, :]).astype(jnp.bfloat16)
        keys[media_rows:key_rows, :] = hid[...]
        for x in range(2):
            turn(hid, p_lat, 2 * x, x, 384)

        def frame(i, carry):
            rows = pl.ds(pl.multiple_of(i * 48, 48), 48)
            mixed = media[rows, :].astype(jnp.float32) + dot(hot[rows, :], tiny_t[...].astype(jnp.bfloat16))
            keys[rows, :] = normed(mixed, tiny_t[8:9, :]).astype(jnp.bfloat16)
            return carry

        lax.fori_loop(0, media_rows // 48, frame, 0)

    key_turns = []

    def turn_keys(x):
        for n in key_turns:
            gone(n)
        for theirs in (False, True):
            who = 1 - core if theirs else core
            cols = pl.ds(pl.multiple_of((x * 2 + who) * 384, 128), 384)
            flip_keys[int(theirs)] = keys[:, cols].T.reshape(8, 48, key_rows)
            key_turns.append(give(flip_keys.at[int(theirs)], p_keys.at[core, x], theirs))

    def project(i, dst, first):
        load(f_qkv.at[:, :, :, :, :, pl.ds(i * model, model)], wbuf)

        def tile(n, carry):
            cols = pl.ds(pl.multiple_of(n * 256, 256), 256)
            w = wbuf[:, :, :, :, :, cols].reshape(model, 256)
            dst[:, cols] = dot(keys[first:key_rows, :], w).astype(jnp.bfloat16)
            return carry

        lax.fori_loop(0, model // 256, tile, 0)

    def project_q():
        project(0, q, media_rows)
        write((q, o_q))

    def project_k():
        project(1, k, 0)
        write((k, o_k))

    def project_v():
        project(2, v, 0)
        write((v, o_v))

    def attend(g):
        if g == 0:
            bias[...] = own_keys(counts, media_rows, queries_n, 48)
        base = g * group_width
        tiles = [jnp.zeros((queries_n, 128), jnp.float32) for _ in range(group_width // 128)]
        for j, (t0, t1, start) in enumerate(windows):
            cols = slice(base + t0 * 128, base + t1 * 128)
            qh = q[:, cols]
            qh = jnp.where(lanes_of(queries_n, t1 - t0, start, head), qh, jnp.zeros_like(qh))
            s = dot(k[:, cols], qh, ((1,), (1,))) * scale + bias[...]
            top = jnp.max(s, axis=0, keepdims=True)
            e = jnp.exp(s - top)
            total = jnp.sum(e, axis=0, keepdims=True)
            p = (e * (1.0 / total)).astype(jnp.bfloat16)
            lse[g * len(windows) + j : g * len(windows) + j + 1, :] = top + jnp.log(total)
            vh = v[:, cols]
            vh = jnp.where(lanes_of(key_rows, t1 - t0, start, head), vh, jnp.zeros_like(vh))
            got = dot(p, vh, ((0,), (0,)))
            for t in range(t0, t1):
                tiles[t] = tiles[t] + got[:, (t - t0) * 128 : (t - t0 + 1) * 128]
        for t, tile in enumerate(tiles):
            att[:, base + t * 128 : base + (t + 1) * 128] = tile.astype(jnp.bfloat16)

    def project_out():
        write((lse, o_lse))
        for x in range(2):
            turn(att, p_att, 4 + 2 * x, x, 384)
        load(f_out, wbuf)

        def tile(n, carry):
            cols = pl.ds(pl.multiple_of(n * 256, 256), 256)
            w = wbuf[:, :, :, :, :, cols].reshape(model, 256)
            mid[:, cols] = lat[:, cols].astype(jnp.float32) + dot(att[...], w)
            return carry

        lax.fori_loop(0, model // 256, tile, 0)
        hid[...] = normed(mid[...], tiny_t[10:11, :]).astype(jnp.bfloat16)
        write((mid, o_mid))
        for x in range(2):
            hid_turns.extend(turn(hid, p_hid, 8 + 2 * x, x, 384))

    hid_turns = []
    act_turns = []

    def up(i):
        load(f_up.at[:, :, :, :, :, pl.ds(i * model, model)], wbuf)

        def tile(n, carry):
            cols = pl.ds(pl.multiple_of(n * 256, 256), 256)
            into = pl.ds(pl.multiple_of(i * model + n * 256, 256), 256)
            w = wbuf[:, :, :, :, :, cols].reshape(model, 256)
            x = dot(hid[...], w)
            cdf = 0.5 + 0.5 * lax.erf(x * 0.7071067811865476)
            act[:, into] = (x * cdf).astype(jnp.bfloat16)
            slope[:, into] = cdf + x * (jnp.exp(-0.5 * x * x) * 0.3989422804014327)
            return carry

        lax.fori_loop(0, model // 256, tile, 0)
        if i % 2 == 1:
            before = list(range(len(given))) if i == 1 else act_turns
            act_turns.extend(turn(act, p_act, 0, i // 2, model, before))

    def down(i, width):
        cols = slice(i * width, (i + 1) * width)
        load(f_down.at[:, :, :, :, :, pl.ds(i * width, width)], wdown)
        per = hidden_n // 4
        got = jnp.zeros((queries_n, width), jnp.float32)
        for b in range(4):
            w = wdown[b // 2, b % 2].reshape(per, width)
            got = got + dot(act[:, b * per : (b + 1) * per], w)
            back = dot(cot[:, cols], w, ((1,), (1,)))
            if i == 0:
                dact[:, b * per : (b + 1) * per] = back
            else:
                dact[:, b * per : (b + 1) * per] += back
        new[:, cols] = (mid[:, cols] + got).astype(jnp.bfloat16)

    def finish():
        def tile(n, carry):
            cols = pl.ds(pl.multiple_of(n * 512, 512), 512)
            act[:, cols] = (dact[:, cols] * slope[:, cols]).astype(jnp.bfloat16)
            return carry

        lax.fori_loop(0, hidden_n // 512, tile, 0)
        write((act, o_dpre), (new, o_new))
        for d in written:
            d.wait()
        for n, (d, theirs, done) in enumerate(given):
            gone(n)
            if theirs:
                d.wait_recv()

    work = [(needs["tiny"], 8, norms), (needs["q"], 4, project_q), (needs["k"], 8, project_k), (needs["v"], 8, project_v)]
    work[2:2] = [(needs["q"], 3, functools.partial(turn_keys, x)) for x in range(2)]
    work += [(needs["v"], 7, functools.partial(attend, g)) for g in range(model // group_width)]
    work += [(needs["out"], 5, project_out)]
    work += [(s, 6, functools.partial(up, i)) for i, s in enumerate(needs["up"])]
    work += [(s, 5, functools.partial(down, i, model // len(needs["down"]))) for i, s in enumerate(needs["down"])]
    work += [(needs["down"][-1], 5, finish)]
    locals_ = []
    for i in range(5):
        d = pltpu.make_async_copy(sh[i], full[i].at[block_index(place, ())], ls.at[i])
        d.start()
        locals_.append(d)
    stages = [[Gather(place, sh[w], full[w], rows, cols, order, (ss, rs), j * n_sems(n_z)) for (j, w, rows, cols, order) in stage] for stage in plan]
    waited = set()
    total, steps = len(stages), 4
    ticks = total + LAG * steps
    for t in range(ticks):
        for back in range(steps):
            u = t - LAG * back - 1
            if LAG > 1 and 0 <= u < total:
                for g in stages[u]:
                    g.advance(back, 1)
        for back in range(steps + 1):
            u = t - LAG * back
            if not 0 <= u < total:
                continue
            for g, (j, w, *_) in zip(stages[u], plan[u]):
                if back == 1 and w not in waited:
                    locals_[w].wait()
                    waited.add(w)
                if back > 0:
                    g.arrive(back - 1)
                if back < steps:
                    g.start(back)
        for move in range(1 if LAG == 1 else 2, n_z - 1):
            for back in range(steps):
                u = t - LAG * back - (LAG > 1)
                if 0 <= u < total:
                    for g in stages[u]:
                        g.advance(back, move)
        room = ROOM_A
        while work and work[0][0] <= t - LAG * steps and (room > 0 or t == ticks - 1):
            need, cost, piece = work.pop(0)
            room -= cost
            piece()
    for st in stages:
        for g in st:
            g.finish()


ROOM_A = 12
LAG = 2
FINE = 2
WIDE_A = ((5, 5, 2), (5, 4, 3), (5, 5, 2), (4, 5, 3))
Z_DOWN = (1,)


def forward_plan(shards, model):
    def split(w, rows, first, widths, last):
        at, pieces = first, []
        for width, order in zip(widths, (ZYX, ZXY, last)):
            pieces.append((w, (0, rows), (at, width), order))
            at += width
        return pieces

    rows = shards[1].shape[0]
    stages, needs = [[(4, (0, rows), (0, 128), ZYX)]], {"tiny": 0}
    twelfth = model // 12
    widths = [tuple(n * twelfth for n in WIDE_A[i % len(WIDE_A)]) for i in range(4 + shards[2].shape[1] // model)]
    for i, name in enumerate("qkv"):
        needs[name] = len(stages)
        stages.append(split(0, rows, i * model, widths[i], (XYZ, YXZ)[i % 2]))
    needs["out"] = len(stages)
    stages.append(split(1, rows, 0, widths[3], YXZ))
    needs["up"], needs["down"] = [], []
    for i in range(shards[2].shape[1] // model):
        needs["up"].append(len(stages))
        stages.append(split(2, rows, i * model, widths[4 + i], (XYZ, YXZ)[i % 2]))
    groups = model // 256
    deep = shards[3].shape[0]
    for i in range(groups):
        if i >= groups - FINE:
            for half in range(2):
                cols = (i * 256 + half * 128, 128)
                stages.append([(3, (0, deep // 2), cols, ZYX), (3, (deep // 2, deep // 2), cols, ZXY)])
        else:
            pair = (XYZ, YXZ) if i in Z_DOWN else (ZYX, ZXY)
            stages.append([(3, (0, deep), (i * 256 + n * 128, 128), pair[n]) for n in range(2)])
        needs["down"].append(len(stages) - 1)
    return stages, needs


def forward_all(weights, lat, media, cot, counts, n_z):
    bf, f32 = jnp.bfloat16, jnp.float32
    rows, model = weights[1].shape
    hidden_n = weights[2].shape[1]
    shards = [jax.ShapeDtypeStruct(s, bf) for s in ((rows, 3 * model), weights[1].shape, weights[2].shape, weights[3].shape, (rows, 128))]
    stages, needs = forward_plan(shards, model)
    plan, count = number(stages)
    queries_n, media_rows = lat.shape[0], media.shape[0]
    key_rows = queries_n + media_rows
    part = (2, 2, 2 * n_z, 48)
    made = [((queries_n, model), bf), ((key_rows, model), bf), ((key_rows, model), bf), ((queries_n, hidden_n), bf), ((queries_n, model), f32), ((queries_n, model), bf), ((HEADS, queries_n), f32),
            (part + (key_rows,), bf), (part + (queries_n,), bf), (part + (queries_n,), bf), (part + (queries_n,), bf), ((2, 2, 2 * n_z * hidden_n // model, 48, queries_n), bf), ((2, queries_n, model), bf)]
    vm = [(s.shape, bf) for s in shards] + [((128, rows), f32), ((media_rows, 128), bf), ((key_rows, queries_n), f32), (lat.shape, bf), (media.shape, bf), (cot.shape, bf)]
    vm += [((key_rows, model), bf), ((queries_n, model), bf), ((key_rows, model), bf), ((key_rows, model), bf), ((queries_n, model), bf), ((queries_n, model), bf), ((queries_n, hidden_n), bf),
          ((queries_n, hidden_n), f32), ((queries_n, hidden_n), f32), ((queries_n, model), f32), ((queries_n, model), bf),
                     ((2, 2, n_z, 2, rows, 128), bf), ((128, model), f32), ((HEADS, queries_n), f32), ((2, 2, n_z, 2, rows, model), bf), ((2, 2, n_z, 2, shards[3].shape[0], 256), bf),
                     ((12, 8, 48, queries_n), bf), ((2, 8, 48, key_rows), bf)]
    sem = pltpu.SemaphoreType.DMA
    in_vmem, in_any = pl.BlockSpec(memory_space=pltpu.VMEM), pl.BlockSpec(memory_space=ANY)
    out = pl.pallas_call(
        functools.partial(forward_kernel, n_z, plan, needs),
        out_shape=[jax.ShapeDtypeStruct((2, 2, n_z, 2) + s.shape, s.dtype) for s in shards] + [jax.ShapeDtypeStruct(*m) for m in made],
        in_specs=[in_vmem] * 6 + [in_any] * 3 + [pl.BlockSpec(memory_space=pltpu.SMEM)],
        out_specs=[in_any] * (5 + len(made)),
        scratch_shapes=[pltpu.VMEM(*m) for m in vm] + [sem((count * n_sems(n_z),)), sem((count * n_sems(n_z),)), sem((5,)), sem((16,)), sem((1,)), sem((48,)), sem((48,)), sem((48,)), sem((3,))],
        name="gather_and_forward",
        compiler_params=pltpu.CompilerParams(collective_id=0, has_side_effects=True, vmem_limit_bytes=60 * 2**20),
    )(*weights, lat, media, cot, counts)
    return out[:5], out[5:]


def layer_norm(values_in, gain):
    mean_row = jnp.mean(values_in, axis=-1, keepdims=True)
    centered = values_in - mean_row
    var_row = jnp.mean(centered * centered, axis=-1, keepdims=True)
    return centered * lax.rsqrt(var_row + norm_eps) * gain


def exact_gelu(values_in):
    return jax.nn.gelu(values_in, approximate=False)


def frame_tables(counts, frame_slots, time_len):
    slot_total = counts.shape[0]
    order = jnp.arange(slot_total, dtype=jnp.int32)
    slot_ends = jnp.sum(jnp.where(order[None, :] <= order[:, None], counts[None, :], 0), axis=1)
    slot_starts = slot_ends - counts
    frame_ids = jnp.arange(frame_slots, dtype=jnp.int32)
    frame_owner = jnp.sum((frame_ids[:, None] >= slot_ends[None, :]).astype(jnp.int32), axis=1)
    slot_ids = jnp.arange(slot_total, dtype=jnp.int32)
    start_of = jnp.sum(
        jnp.where(frame_owner[:, None] == slot_ids[None, :], slot_starts[None, :], 0), axis=1
    )
    time_index = frame_ids - start_of
    live_frame = frame_owner < slot_total
    time_ids = jnp.arange(time_len, dtype=jnp.int32)
    time_hot = ((time_index[:, None] == time_ids[None, :]) & live_frame[:, None]).astype(
        jnp.float32
    )
    return (frame_owner, time_hot)


def gather_params(part_qkv, part_out, part_up, part_down, part_time, part_gains):
    inner_part = (
        lax.all_gather(part_qkv, FSDP, axis=0, tiled=True),
        lax.all_gather(part_out, FSDP, axis=0, tiled=True),
        lax.all_gather(part_up, FSDP, axis=0, tiled=True),
        lax.all_gather(part_down, FSDP, axis=0, tiled=True),
        lax.all_gather(part_time, FSDP, axis=0, tiled=True),
        lax.all_gather(part_gains, FSDP, axis=0, tiled=True),
    )
    return (
        lax.all_gather(inner_part[0], DP, axis=0, tiled=True),
        lax.all_gather(inner_part[1], DP, axis=0, tiled=True),
        lax.all_gather(inner_part[2], DP, axis=0, tiled=True),
        lax.all_gather(inner_part[3], DP, axis=0, tiled=True),
        lax.all_gather(inner_part[4], DP, axis=0, tiled=True),
        lax.all_gather(inner_part[5], DP, axis=0, tiled=True),
    )


def reduce_grads(grad_qkv, grad_out, grad_up, grad_down, grad_time, grad_gains):
    outer_part = (
        lax.psum_scatter(
            grad_qkv.astype(jnp.bfloat16), DP, scatter_dimension=0, tiled=True
        ).astype(jnp.float32),
        lax.psum_scatter(
            grad_out.astype(jnp.bfloat16), DP, scatter_dimension=0, tiled=True
        ).astype(jnp.float32),
        lax.psum_scatter(
            grad_up.astype(jnp.bfloat16), DP, scatter_dimension=0, tiled=True
        ).astype(jnp.float32),
        lax.psum_scatter(
            grad_down.astype(jnp.bfloat16), DP, scatter_dimension=0, tiled=True
        ).astype(jnp.float32),
        lax.psum_scatter(
            grad_time.astype(jnp.bfloat16), DP, scatter_dimension=0, tiled=True
        ).astype(jnp.float32),
        lax.psum_scatter(
            grad_gains.astype(jnp.bfloat16), DP, scatter_dimension=0, tiled=True
        ).astype(jnp.float32),
    )
    return (
        lax.psum_scatter(
            outer_part[0].astype(jnp.bfloat16), FSDP, scatter_dimension=0, tiled=True
        ).astype(jnp.float32),
        lax.psum_scatter(
            outer_part[1].astype(jnp.bfloat16), FSDP, scatter_dimension=0, tiled=True
        ).astype(jnp.float32),
        lax.psum_scatter(
            outer_part[2].astype(jnp.bfloat16), FSDP, scatter_dimension=0, tiled=True
        ).astype(jnp.float32),
        lax.psum_scatter(
            outer_part[3].astype(jnp.bfloat16), FSDP, scatter_dimension=0, tiled=True
        ).astype(jnp.float32),
        lax.psum_scatter(
            outer_part[4].astype(jnp.bfloat16), FSDP, scatter_dimension=0, tiled=True
        ).astype(jnp.float32),
        lax.psum_scatter(
            outer_part[5].astype(jnp.bfloat16), FSDP, scatter_dimension=0, tiled=True
        ).astype(jnp.float32),
    )


def masked_scores(q_heads, k_heads, allowed, score_scale):
    scores = (
        jnp.einsum("qhe,khe->hqk", q_heads, k_heads, preferred_element_type=jnp.float32)
        * score_scale
    )
    return jnp.where(allowed[None, :, :], scores, -1e30)


def adamw_step(weight, first, second, grad, factor, rate):
    clipped = grad * factor
    first_new = beta_one * first + (1.0 - beta_one) * clipped
    second_new = beta_two * second + (1.0 - beta_two) * clipped * clipped
    first_hat = first_new / (1.0 - beta_one**STEP)
    second_hat = second_new / (1.0 - beta_two**STEP)
    weight_new = weight - rate * (
        first_hat / (jnp.sqrt(second_hat) + adam_eps) + decay_rate * weight
    )
    return (weight_new, first_new, second_new)


def on_device(
    latents,
    media,
    frame_counts,
    cotangent,
    w_qkv,
    m_qkv,
    v_qkv,
    w_out,
    m_out,
    v_out,
    w_up,
    m_up,
    v_up,
    w_down,
    m_down,
    v_down,
    time_table,
    m_time,
    v_time,
    gains,
    m_gains,
    v_gains,
):
    n_dp, n_fsdp = lax.axis_size(DP), lax.axis_size(FSDP)
    masters = (w_qkv, w_out, w_up, w_down, time_table, gains)
    firsts = (m_qkv, m_out, m_up, m_down, m_time, m_gains)
    seconds = (v_qkv, v_out, v_up, v_down, v_time, v_gains)
    rates = (0.02, 0.1, 0.02, 0.01, 0.2, 0.5)
    item_slots, lat_count, _ = latents.shape
    frame_slots, patch_rows, _ = media.shape
    queries_n = item_slots * lat_count
    if fits_kernels(n_dp, n_fsdp, w_qkv, w_up, w_down, queries_n, frame_slots, patch_rows):
        new_latents, d_latents, grad_norm, updated = by_kernels(
            turned(masters), turned(firsts), turned(seconds), rates, latents, media, cotangent, frame_counts, n_fsdp // 2
        )
    else:
        frame_owner, time_hot = frame_tables(frame_counts, frame_slots, time_table.shape[1])
        query_owner = jnp.arange(queries_n, dtype=jnp.int32) // lat_count
        key_owner = jnp.concatenate([jnp.repeat(frame_owner, patch_rows), query_owner], axis=0)
        allowed = query_owner[:, None] == key_owner[None, :]
        lows = tuple(w.astype(jnp.bfloat16) for w in masters)
        new_latents, d_latents, grad_norm, reduced = by_collectives(lows, latents, media, cotangent, time_hot, allowed)
        factor = jnp.minimum(1.0, clip_limit / (grad_norm + 1e-06))
        updated = []
        for index in range(6):
            updated.extend(adamw_step(masters[index], firsts[index], seconds[index], reduced[index], factor, rates[index]))
    return (new_latents, d_latents, grad_norm, *updated)


def turned(arrays):
    qkv, out, up, down, time, gain = arrays
    return qkv.transpose(1, 0, 2), out, up, down, time.T, gain.T


def fits_kernels(n_dp, n_fsdp, w_qkv, w_up, w_down, queries_n, frame_slots, patch_rows):
    rows, _, model = w_qkv.shape
    return (
        n_dp == 4 and n_fsdp == 8 and rows == 48 and model == 1536 and w_up.shape[1] == 4 * model and w_down.shape[0] == 192
        and queries_n == 256 and patch_rows == 48 and frame_slots % 3 == 0
    )


def by_kernels(masters, firsts, seconds, rates, latents, media, cotangent, counts, n_z):
    model = latents.shape[2]
    lat, med, cot = (a.reshape(-1, model) for a in (latents, media, cotangent))
    full, made = forward_all(masters, lat, med, cot, counts, n_z)
    own = backward_all(full, made, lat, med, counts, n_z)
    grads = [own.g_qkv, own.g_out, own.g_up, own.g_down, own.g_tiny]
    *new, new_rows, d_rows, norm = update_all(own.norm, masters, firsts, seconds, grads, (made[5], own.d_lat), rates)
    kinds = [turned(new[n::3]) for n in range(3)]
    updated = [kinds[n][i] for i in range(6) for n in range(3)]
    return new_rows.reshape(latents.shape), d_rows.reshape(latents.shape), norm.reshape(()), updated


def by_collectives(lows, latents, media, cotangent, time_hot, allowed):
    full_qkv, full_out, full_up, full_down, full_time, full_gains = gather_params(*lows)
    item_slots, lat_count, model_width = latents.shape
    frame_slots, patch_rows, unused_width = media.shape
    queries_n = item_slots * lat_count
    media_rows = frame_slots * patch_rows
    head_size = model_width // HEADS
    score_scale = 1.0 / head_size**0.5
    time_f32 = full_time.astype(jnp.float32)
    gains_f32 = full_gains.astype(jnp.float32)
    frame_time = jnp.dot(time_hot, time_f32.T, precision=highest)
    mixed = media.astype(jnp.float32) + frame_time[:, None, :]
    media_norm, media_back = jax.vjp(layer_norm, mixed, gains_f32[:, 0])
    media_low = media_norm.astype(jnp.bfloat16).reshape(media_rows, model_width)
    lat_rows = latents.reshape(queries_n, model_width).astype(jnp.float32)
    lat_norm, lat_back = jax.vjp(layer_norm, lat_rows, gains_f32[:, 1])
    lat_low = lat_norm.astype(jnp.bfloat16)
    keys_in = jnp.concatenate([media_low, lat_low], axis=0)
    key_rows = keys_in.shape[0]
    qkv_flat = full_qkv.reshape(model_width, 3 * model_width)
    queries = jnp.dot(
        lat_low, qkv_flat[:, :model_width], preferred_element_type=jnp.float32
    ).astype(jnp.bfloat16)
    key_value = jnp.dot(
        keys_in, qkv_flat[:, model_width:], preferred_element_type=jnp.float32
    ).astype(jnp.bfloat16)
    q_heads = queries.reshape(queries_n, HEADS, head_size)
    k_heads = key_value[:, :model_width].reshape(key_rows, HEADS, head_size)
    v_heads = key_value[:, model_width:].reshape(key_rows, HEADS, head_size)
    scores = masked_scores(q_heads, k_heads, allowed, score_scale)
    row_top = jnp.max(scores, axis=-1, keepdims=True)
    row_total = jnp.sum(jnp.exp(scores - row_top), axis=-1, keepdims=True)
    log_total = row_top + jnp.log(row_total)
    probs_low = jnp.exp(scores - log_total).astype(jnp.bfloat16)
    attended = jnp.einsum("hqk,khe->qhe", probs_low, v_heads, preferred_element_type=jnp.float32)
    attended = attended.reshape(queries_n, model_width).astype(jnp.bfloat16)
    middle = lat_rows + jnp.dot(attended, full_out, preferred_element_type=jnp.float32)
    hidden, ffn_back = jax.vjp(layer_norm, middle, gains_f32[:, 2])
    hidden_low = hidden.astype(jnp.bfloat16)
    pre_act = jnp.dot(hidden_low, full_up, preferred_element_type=jnp.float32)
    activated, gelu_back = jax.vjp(exact_gelu, pre_act)
    act_low = activated.astype(jnp.bfloat16)
    result = middle + jnp.dot(act_low, full_down, preferred_element_type=jnp.float32)
    new_latents = result.astype(jnp.bfloat16).reshape(item_slots, lat_count, model_width)
    d_result = cotangent.reshape(queries_n, model_width)
    g_down = jnp.einsum("qf,qd->fd", act_low, d_result, preferred_element_type=jnp.float32)
    d_act = jnp.einsum("qd,fd->qf", d_result, full_down, preferred_element_type=jnp.float32)
    d_pre = gelu_back(d_act)[0].astype(jnp.bfloat16)
    g_up = jnp.einsum("qd,qf->df", hidden_low, d_pre, preferred_element_type=jnp.float32)
    d_hidden = jnp.einsum("qf,df->qd", d_pre, full_up, preferred_element_type=jnp.float32)
    d_middle_ln, g_gain_ffn = ffn_back(d_hidden)
    d_middle = d_result.astype(jnp.float32) + d_middle_ln
    d_branch = d_middle.astype(jnp.bfloat16)
    g_out = jnp.einsum("qe,qd->ed", attended, d_branch, preferred_element_type=jnp.float32)
    d_attended = jnp.einsum(
        "qd,ed->qe", d_branch, full_out, preferred_element_type=jnp.float32
    ).astype(jnp.bfloat16)
    scores_again = masked_scores(q_heads, k_heads, allowed, score_scale)
    probs = jnp.exp(scores_again - log_total)
    probs_again = probs.astype(jnp.bfloat16)
    d_att_heads = d_attended.reshape(queries_n, HEADS, head_size)
    d_probs = jnp.einsum("qhe,khe->hqk", d_att_heads, v_heads, preferred_element_type=jnp.float32)
    row_dot = jnp.sum(probs * d_probs, axis=-1, keepdims=True)
    d_scores = (probs * (d_probs - row_dot)).astype(jnp.bfloat16)
    d_queries = (
        (
            jnp.einsum("hqk,khe->qhe", d_scores, k_heads, preferred_element_type=jnp.float32)
            * score_scale
        )
        .reshape(queries_n, model_width)
        .astype(jnp.bfloat16)
    )
    d_keys = (
        (
            jnp.einsum("hqk,qhe->khe", d_scores, q_heads, preferred_element_type=jnp.float32)
            * score_scale
        )
        .reshape(key_rows, model_width)
        .astype(jnp.bfloat16)
    )
    d_values = (
        jnp.einsum("hqk,qhe->khe", probs_again, d_att_heads, preferred_element_type=jnp.float32)
        .reshape(key_rows, model_width)
        .astype(jnp.bfloat16)
    )
    g_query = jnp.einsum("qd,qe->de", lat_low, d_queries, preferred_element_type=jnp.float32)
    d_key_value = jnp.concatenate([d_keys, d_values], axis=1)
    g_key_value = jnp.einsum("kd,kx->dx", keys_in, d_key_value, preferred_element_type=jnp.float32)
    g_qkv = jnp.concatenate([g_query, g_key_value], axis=1).reshape(model_width, 3, model_width)
    back_flat = full_qkv.reshape(model_width, 3 * model_width)
    d_keys_in = jnp.einsum(
        "kx,dx->kd", d_key_value, back_flat[:, model_width:], preferred_element_type=jnp.float32
    )
    d_lat_norm = (
        jnp.einsum(
            "qe,de->qd", d_queries, back_flat[:, :model_width], preferred_element_type=jnp.float32
        )
        + d_keys_in[media_rows:]
    )
    d_lat_ln, g_gain_lat = lat_back(d_lat_norm)
    d_latents = (d_middle + d_lat_ln).reshape(item_slots, lat_count, model_width)
    d_mixed, g_gain_media = media_back(
        d_keys_in[:media_rows].reshape(frame_slots, patch_rows, model_width)
    )
    frame_grad = jnp.sum(d_mixed, axis=1)
    g_time = jnp.einsum("fd,ft->dt", frame_grad, time_hot, precision=highest)
    g_gains = jnp.stack([g_gain_media, g_gain_lat, g_gain_ffn], axis=1)
    reduced = reduce_grads(g_qkv, g_out, g_up, g_down, g_time, g_gains)
    local_sq = jnp.zeros((), jnp.float32)
    for grad in reduced:
        local_sq = local_sq + jnp.sum(grad * grad)
    grad_norm = jnp.sqrt(lax.psum(local_sq, (DP, FSDP)))
    return new_latents, d_latents, grad_norm, reduced


def solution(mesh):
    both = (DP, FSDP)
    one, two, three = P(both), P(both, None), P(both, None, None)
    updated = (three,) * 3 + (two,) * 15
    placed = (three, three, one, three, *updated)
    return jax.shard_map(
        on_device,
        mesh=mesh,
        in_specs=placed,
        out_specs=(three, three, P(), *updated),
        check_vma=False,
    )
```

```python
import functools
import math
import types

import jax
import jax.numpy as jnp
from jax import lax
from jax.experimental import pallas as pl
from jax.experimental.pallas import tpu as pltpu
from jax.sharding import PartitionSpec as P

DP, FSDP = "dp", "fsdp"
HEADS = 16
STEP = 10


highest = lax.Precision.HIGHEST
norm_eps = 1e-05
clip_limit = 1.0
beta_one = 0.9
beta_two = 0.999
adam_eps = 1e-08
decay_rate = 0.1

MESH=pl.DeviceIdType.MESH
ANY=pl.ANY

class Place:
    def __init__(self, n_z):
        dp = lax.axis_index(DP); fs = lax.axis_index(FSDP)
        self.n_z = n_z
        self.at = {"x": dp // 2, "c": dp % 2, "z": fs // 2, "y": fs % 2}
    def dev(self, **new):
        p = {**self.at, **new}
        return (p["x"] * 2 + p["c"], p["z"] * 2 + p["y"])
    def other(self, ax):
        return self.dev(**{ax: 1 - self.at[ax]})
    def along_z(self, k):
        return self.dev(z=(self.at["z"] + k) % self.n_z)
    def level(self):
        flip = lambda ax, by: 1 - self.at[ax] if by else self.at[ax]
        return [self.dev(x=flip("x", n & 4), c=flip("c", n & 2), y=flip("y", n & 1)) for n in range(1, 8)]
    def partners(self):
        return [self.other(a) for a in "cxy"] + [self.along_z(k) for k in range(1, self.n_z)]

def greet(place, wide=False):
    bar = pltpu.get_barrier_semaphore()
    others = place.level() + place.partners()[3:] if wide else place.partners()
    for d in others:
        pl.semaphore_signal(bar, inc=1, device_id=d, device_id_type=MESH)
    pl.semaphore_wait(bar, len(others))

def block_index(place, held, **at):
    where = {**place.at, **at}
    return tuple(slice(None) if ax in held else where[ax] for ax in "xczy")

class Gather:
    def __init__(self, place, src, dst, rows, cols, order, sems, base):
        self.place, self.src, self.dst = place, src, dst
        self.sl = (pl.ds(*rows), pl.ds(*cols))
        self.order, self.sems, self.base = order, sems, base
        self.copies = {}

    def region(self, held, **at):
        return self.dst.at[block_index(self.place, held, **at) + self.sl]

    def copy(self, src, dst, n, to):
        ss, rs = self.sems
        n += self.base
        return pltpu.make_async_remote_copy(src_ref=src, dst_ref=dst, send_sem=ss.at[n], recv_sem=rs.at[n], device_id=to, device_id_type=MESH)

    def start(self, step):
        ax, held, p = self.order[step], self.order[:step], self.place
        if ax == "z":
            self.line(step, 1)
            return
        d = self.copy(self.src.at[self.sl] if step == 0 else self.region(held), self.region(held), "xyc".index(ax), p.other(ax))
        d.start()
        self.copies[step] = d

    def line(self, step, k):
        p, held = self.place, self.order[:step]
        z, last = p.at["z"], p.n_z - 1
        for side, from_z, to_z in ((0, z - (k - 1), z + 1), (1, z + (k - 1), z - 1)):
            ok = (from_z >= 0) & (to_z <= last) if side == 0 else (from_z <= last) & (to_z >= 0)
            at = jnp.clip(from_z, 0, last)
            dst = self.region(held, z=at)
            src = self.src.at[self.sl] if step == 0 and k == 1 else dst
            d = self.copy(src, dst, 3 + 2 * (k - 1) + side, p.dev(z=jnp.clip(to_z, 0, last)))
            pl.when(ok)(d.start)
            came = z >= k if side == 0 else z + k <= last
            self.copies[step, k, side] = (d, ok, came)

    def came(self, step, k):
        for side in range(2):
            d, _, came = self.copies[step, k, side]
            pl.when(came)(d.wait_recv)

    def advance(self, step, k):
        if self.order[step] == "z":
            self.came(step, k)
            self.line(step, k + 1)

    def arrive(self, step):
        if self.order[step] == "z":
            self.came(step, self.place.n_z - 1)
        else:
            self.copies[step].wait_recv()

    def finish(self):
        for key, d in self.copies.items():
            if isinstance(key, tuple):
                pl.when(d[1])(d[0].wait_send)
            else:
                d.wait_send()


def n_sems(n_z):
    return 3 + 2 * (n_z - 1)


def number(plan):
    j, out = 0, []
    for stage in plan:
        new = []
        for piece in stage:
            new.append((j,) + piece); j += 1
        out.append(new)
    return out, j

ZYX, ZXY, XYZ, YXZ = ("z", "y", "x", "c"), ("z", "x", "y", "c"), ("x", "y", "z", "c"), ("y", "x", "z", "c")

BACK_LAG, SEND_SLOTS, LAND_SLOTS = 2, 3, 6
ROOM_B = 3
FINE_B = 0
WIDE_B = ((3, 2, 1), (2, 3, 1), (2, 2, 2))


class Scatter:
    def __init__(self, place, out, rows, cols, order, piece, turn, sems, bufs, total_sq):
        self.p, self.order, self.piece, self.width = place, order, piece, cols[1]
        model = out.shape[-1]
        self.out = out.at[cols[0] // model, pl.ds(*rows), pl.ds(cols[0] % model, cols[1])] if len(out.shape) == 3 else out.at[pl.ds(*rows), pl.ds(*cols)]
        self.ss, self.rs, self.ls = sems
        self.b, self.sq = bufs, total_sq
        self.turn, self.h, self.n = turn, turn % SEND_SLOTS, turn % LAND_SLOTS
        self.sent, self.moves = {}, {}

    def v(self, ref, *lead):
        return ref.at[lead + (slice(None), pl.ds(0, self.width))]

    def copy(self, src, dst, to, n):
        n += self.piece * n_sems(self.p.n_z)
        return pltpu.make_async_remote_copy(src_ref=src, dst_ref=dst, send_sem=self.ss.at[n], recv_sem=self.rs.at[n], device_id=to, device_id_type=MESH)

    def send(self, step, src, dst, ax):
        d = self.copy(src, dst, self.p.other(ax), "xyc".index(ax))
        d.start()
        self.sent[step] = d

    def add(self, count, dst, a, b):
        w = slice(0, self.width)

        def one(i, carry):
            (da, di), (aa, ai), (ba, bi) = dst(i), a(i), b(i)
            da[di + (slice(None), w)] = aa[ai + (slice(None), w)] + ba[bi + (slice(None), w)]
            return carry

        if count == 1:
            one(0, 0)
        else:
            lax.fori_loop(0, count, one, 0)

    def row(self, d):
        if self.order[0] == "z":
            return self.v(self.b.s0, self.h, slice(None), d, slice(None))
        return self.v(self.b.s2, self.h, d)

    def land(self, side, k):
        if self.order[0] == "z":
            return self.v(self.b.rz, self.n, side, k - 1, slice(None), slice(None))
        return self.v(self.b.rz, self.n, side, k - 1)

    def add_landed(self, d, side, k):
        b, h, n = self.b, self.h, self.n
        if self.order[0] == "z":
            mine = lambda i: (b.s0, (h, i // 2, d, i % 2))
            self.add(4, mine, mine, lambda i: (b.rz, (n, side, k - 1, i // 2, i % 2)))
        else:
            mine = lambda i: (b.s2, (h, d))
            self.add(1, mine, mine, lambda i: (b.rz, (n, side, k - 1)))

    def line(self, step, k):
        p = self.p
        z, last = p.at["z"], p.n_z - 1
        for side, d, to in ((0, p.n_z - k + z, z + 1), (1, z - (p.n_z - k), z - 1)):
            ok = d <= last if side == 0 else d >= 0
            at = jnp.clip(d, 0, last)
            if k > 1:
                got, _, came = self.moves[step, k - 1, side]

                def forward(got=got, at=at, side=side):
                    got.wait_recv()
                    self.add_landed(at, side, k - 1)

                pl.when(came)(forward)
            c = self.copy(self.row(at), self.land(side, k), p.dev(z=jnp.clip(to, 0, last)), 3 + 2 * (k - 1) + side)
            pl.when(ok)(c.start)
            came = z <= k if side == 0 else z >= last - k
            came = came & (z > 0 if side == 0 else z < last)
            self.moves[step, k, side] = (c, ok, came)

    def last_move(self, step):
        p = self.p
        z, k = p.at["z"], p.n_z - 1
        for side in range(2):
            c, _, came = self.moves[step, k, side]

            def end(c=c, side=side):
                c.wait_recv()
                self.add_landed(z, side, k)

            pl.when(came)(end)

    def advance(self, step, k):
        if self.order[step] == "z":
            self.line(step, k + 1)

    def free(self, step):
        if step == 3:
            self.sent.pop(3).wait()
        elif self.order[step] == "z":
            for k in range(1, self.p.n_z):
                for side in range(2):
                    c, ok, _ = self.moves.pop((step, k, side))
                    pl.when(ok)(c.wait_send)
        else:
            self.sent.pop(step).wait_send()

    def start(self, step):
        p, b, A, h, n, nz = self.p, self.b, slice(None), self.h, self.n, self.p.n_z
        at = p.at
        if step < 3 and self.order[step] == "z":
            if step == 2:
                first, nxt = self.order[:2]
                mine = (lambda i: (b.s1, (h, i, at[nxt]))) if first == "x" else (lambda i: (b.s1, (h, at[nxt], i)))
                self.sent[1].wait_recv()
                self.add(nz, lambda i: (b.s2, (h, i)), mine, lambda i: (b.r2, (n, i)))
            self.line(step, 1)
            return
        first = self.order[0]
        if step == 0:
            o = 1 - at[first]
            src = self.v(b.s0, h, o, A, A) if first == "x" else self.v(b.s0, h, A, A, o)
            self.send(0, src, self.v(b.r1, n, A, A), first)
        elif step == 1 and first == "z":
            self.last_move(0)
            for x in range(2):
                b.s1[h, x, :, :, 0 : self.width] = b.s0[h, x, at["z"], :, :, 0 : self.width]
            self.send(1, self.v(b.s1, h, 1 - at["x"], A), self.v(b.r1, n, A), "x")
        elif step == 1:
            self.sent[0].wait_recv()
            o = 1 - at[self.order[1]]
            i0, i1 = (lambda i: i // 2), (lambda i: i % 2)
            if first == "y":
                i0, i1 = (lambda i: i // nz), (lambda i: i % nz)
                mine = lambda i: (b.s0, (h, i0(i), i1(i), at["y"]))
            else:
                mine = lambda i: (b.s0, (h, at["x"], i0(i), i1(i)))
            self.add(2 * nz, lambda i: (b.s1, (h, i0(i), i1(i))), mine, lambda i: (b.r1, (n, i0(i), i1(i))))
            src = self.v(b.s1, h, A, o) if first == "x" else self.v(b.s1, h, o, A)
            self.send(1, src, self.v(b.r2, n, A), self.order[1])
        elif step == 2:
            self.sent[1].wait_recv()
            self.add(2, lambda i: (b.s2, (h, i)), lambda i: (b.s1, (h, at["x"], i)), lambda i: (b.r1, (n, i)))
            self.send(2, self.v(b.s2, h, 1 - at["y"]), self.v(b.r2, n), "y")
        else:
            w = slice(0, self.width)
            if first == "z":
                self.sent[2].wait_recv()
                total = b.s2[h, at["y"], :, w].astype(jnp.float32) + b.r2[n, :, w].astype(jnp.float32)
            else:
                p_last = nz - 1
                for side in range(2):
                    c, _, came = self.moves[2, p_last, side]
                    pl.when(came)(c.wait_recv)
                total = b.s2[h, at["z"], :, w].astype(jnp.float32)
                for side in range(2):
                    came = self.moves[2, p_last, side][2]
                    landed = b.rz[n, side, p_last - 1, :, w].astype(jnp.float32)
                    total = total + jnp.where(came, landed, 0.0)
            b.o[h, :, w] = total
            self.sq[:, w] += total * total
            d = pltpu.make_async_copy(self.v(b.o, h), self.out, self.ls.at[self.piece])
            d.start()
            self.sent[3] = d


def sum_squares(place, n_z, bufs, sems, out):
    ns, nr = sems
    sq, part, zs = bufs.sq, bufs.n, bufs.nz
    acc = jnp.zeros((8, 128), jnp.float32)
    for i in range(sq.shape[0] // 8):
        for j in range(sq.shape[1] // 128):
            acc = acc + sq[i * 8 : (i + 1) * 8, j * 128 : (j + 1) * 128]
    at = place.at
    me = at["x"] * 4 + at["c"] * 2 + at["y"]
    part[me] = acc
    made = []
    for n, d in enumerate(place.level()):
        made.append(pltpu.make_async_remote_copy(src_ref=part.at[me], dst_ref=part.at[me], send_sem=ns.at[n], recv_sem=nr.at[n], device_id=d, device_id_type=MESH))
    for d in made:
        d.start()
    for d in made:
        d.wait()
    acc = part[0]
    for n in range(1, 8):
        acc = acc + part[n]
    z = at["z"]
    zs[z] = acc
    made = []
    for k in range(1, n_z):
        d = pltpu.make_async_remote_copy(src_ref=zs.at[z], dst_ref=zs.at[z], send_sem=ns.at[6 + k], recv_sem=nr.at[6 + k], device_id=place.along_z(k), device_id_type=MESH)
        d.start()
        made.append(d)
    for d in made:
        d.wait()
    total = zs[0]
    for k in range(1, n_z):
        total = total + zs[k]
    out[...] = jnp.broadcast_to(jnp.sqrt(jnp.sum(total, keepdims=True)), out.shape)


def backward_kernel(n_z, plan, names, *refs):
    b = types.SimpleNamespace(**dict(zip(names, refs)))
    ss, rs, ls, ns, nr, ws, ps, pr, lt_sem, rhs_sem, out_sem = refs[len(names) :]
    own_grads = (b.g_qkv, b.g_out, b.g_up, b.g_down, b.g_tiny)
    early = [
        pltpu.make_async_copy(src, dst, out_sem.at[1 + n])
        for n, (src, dst) in enumerate(((b.p_act, b.lt), (b.mid_in, b.mid), (b.q_in, b.q), (b.keys, b.k), (b.v_in, b.v), (b.lat_in, b.lat)))
    ]
    for d in early:
        d.start()

    def here(*which):
        for n in which:
            early[n].wait()

    place = Place(n_z)
    greet(place, True)
    core, A = place.at["c"], slice(None)
    queries_n, model = b.q_in.shape
    key_rows = b.keys.shape[0]
    media_rows = key_rows - queries_n
    hidden_n = b.dpre.shape[1]
    head = model // HEADS
    windows, group_width = head_windows(head)
    scale = 1.0 / head**0.5
    f32, bf = jnp.float32, jnp.bfloat16
    b.sq[...] = jnp.zeros_like(b.sq)
    given = {}

    def give(src, dst):
        n = len(given)
        d = pltpu.make_async_remote_copy(src_ref=src, dst_ref=dst, send_sem=ps.at[n], recv_sem=pr.at[n], device_id=place.other("c"), device_id_type=MESH)
        d.start()
        given[id(dst)] = [d, False]

    def got(dst):
        held_copy = given[id(dst)]
        if not held_copy[1]:
            held_copy[0].wait_recv()
            held_copy[1] = True

    give(b.dpre, b.x_dpre)

    wbuf = b.wbuf

    def fetch(src, slot):
        d = pltpu.make_async_copy(src, wbuf.at[slot], ws.at[slot])
        d.start()
        return d

    def tiles_of(jobs, use):
        ahead = fetch(jobs[0], 0)
        for i in range(len(jobs)):
            now = ahead
            if i + 1 < len(jobs):
                ahead = fetch(jobs[i + 1], (i + 1) % 2)
            now.wait()
            use(i, wbuf[i % 2].reshape(384, model))

    def hidden_part(i):
        d = pltpu.make_async_copy(b.dpre.at[:, pl.ds(i * model, model)], b.datt, ws.at[4])
        d.start()
        d.wait()

        def use(n, w):
            got_ = dot(b.datt[...], w, ((1,), (1,)))
            cols = slice(n * 384, (n + 1) * 384)
            if i == 0:
                b.dmid[:, cols] = got_
            else:
                b.dmid[:, cols] += got_

        tiles_of([b.f_up.at[x, c, :, :, :, pl.ds(i * model, model)] for x in range(2) for c in range(2)], use)

    def norm_back(rows_in, grad, gain):
        centered = rows_in - jnp.mean(rows_in, axis=-1, keepdims=True)
        inv = lax.rsqrt(jnp.mean(centered * centered, axis=-1, keepdims=True) + norm_eps)
        hat = centered * inv
        scaled = grad * gain
        back = inv * (scaled - jnp.mean(scaled, axis=-1, keepdims=True) - hat * jnp.mean(scaled * hat, axis=-1, keepdims=True))
        return back, jnp.sum(grad * hat, axis=0, keepdims=True)

    def ffn_norm():
        d = pltpu.make_async_copy(b.f_tiny, b.tiny, ws.at[3])
        d.start()
        e = pltpu.make_async_copy(b.p_cot.at[core], b.dbranch, ws.at[4])
        e.start()
        d.wait()
        e.wait()
        here(1)
        b.tiny_t[...] = b.tiny[...].reshape(model, 128).astype(f32).T
        b.gsmall[...] = jnp.zeros_like(b.gsmall)

        def rows(i, carry):
            at = pl.ds(pl.multiple_of(i * 64, 64), 64)
            back, gain = norm_back(b.mid[at, :], b.dmid[at, :], b.tiny_t[10:11, :])
            total = b.dbranch[at, :].astype(f32) + back
            b.dmid[at, :] = total
            b.dbranch[at, :] = total.astype(bf)
            b.gsmall[10:11, :] += gain
            return carry

        lax.fori_loop(0, queries_n // 64, rows, 0)
        give(b.dbranch, b.x_branch)

    def attended_back():
        def use(n, w):
            b.datt[:, n * 384 : (n + 1) * 384] = dot(b.dbranch[...], w, ((1,), (1,))).astype(bf)

        tiles_of([b.f_out.at[x, c] for x in range(2) for c in range(2)], use)

    def attend_back(g):
        if g == 0:
            here(2, 3, 4)
            b.bias[...] = own_keys(b.counts, media_rows, queries_n, 48)
        base = g * group_width
        n_tiles = group_width // 128
        last = {t: max(j for j, (t0, t1, _) in enumerate(windows) if t0 <= t < t1) for t in range(n_tiles)}
        sums = {}
        for j, (t0, t1, start) in enumerate(windows):
            cols = slice(base + t0 * 128, base + t1 * 128)
            q_in, k_in = lanes_of(queries_n, t1 - t0, start, head), lanes_of(key_rows, t1 - t0, start, head)
            qh = b.q[:, cols]
            qh = jnp.where(q_in, qh, jnp.zeros_like(qh))
            dah = b.datt[:, cols]
            dah = jnp.where(q_in, dah, jnp.zeros_like(dah))
            kw = b.k[:, cols]
            h = g * len(windows) + j
            p = jnp.exp(dot(kw, qh, ((1,), (1,))) * scale + b.bias[...] - b.lse[h : h + 1, :])
            dp = dot(b.v[:, cols], dah, ((1,), (1,)))
            row_dot = jnp.sum(p * dp, axis=0, keepdims=True)
            ds = (p * (dp - row_dot)).astype(bf)
            kh = jnp.where(k_in, kw, jnp.zeros_like(kw))
            parts = ((b.dv, dot(p.astype(bf), dah)), (b.dk, dot(ds, qh) * scale), (b.dq, dot(ds, kh, ((0,), (0,))) * scale))
            for n, (into, part) in enumerate(parts):
                for t in range(t0, t1):
                    new = part[:, (t - t0) * 128 : (t - t0 + 1) * 128]
                    sums[n, t] = sums[n, t] + new if (n, t) in sums else new
                    if last[t] == j:
                        into[:, base + t * 128 : base + (t + 1) * 128] = sums.pop((n, t)).astype(bf)
        if g == model // group_width - 1:
            give(b.dq, b.x_dq)
            give(b.dk, b.x_dk)
            give(b.dv, b.x_dv)

    def keys_back(n):
        x, c = n // 2, n % 2
        made = [fetch(b.f_qkv.at[x, c, :, :, :, pl.ds(i * model, model)], i) for i in range(3)]
        for d in made:
            d.wait()
        w = [wbuf[i].reshape(384, model) for i in range(3)]
        cols = slice(n * 384, (n + 1) * 384)
        lat_rows = slice(media_rows, key_rows)
        tail = dot(b.dq[...], w[0], ((1,), (1,))) + dot(b.dk[lat_rows, :], w[1], ((1,), (1,))) + dot(b.dv[lat_rows, :], w[2], ((1,), (1,)))
        b.k[lat_rows, cols] = tail.astype(bf)
        step = media_rows // 3
        for i in range(3):
            rows = slice(i * step, (i + 1) * step)
            b.k[rows, cols] = (dot(b.dk[rows, :], w[1], ((1,), (1,))) + dot(b.dv[rows, :], w[2], ((1,), (1,)))).astype(bf)

    def latents_back():
        here(5)

        def rows(i, carry):
            at = pl.ds(pl.multiple_of(i * 64, 64), 64)
            grad = b.k[pl.ds(pl.multiple_of(media_rows + i * 64, 16), 64), :].astype(f32)
            back, gain = norm_back(b.lat[at, :].astype(f32), grad, b.tiny_t[9:10, :])
            b.dmid[at, :] = b.dmid[at, :] + back
            b.gsmall[9:10, :] += gain
            return carry

        lax.fori_loop(0, queries_n // 64, rows, 0)
        d = pltpu.make_async_copy(b.dmid, b.d_lat, out_sem.at[0])
        d.start()
        late.append(d)

    late = []

    def media_back(part):
        step = media_rows // parts
        frames = step // 48
        d = pltpu.make_async_copy(b.media.at[pl.ds(part * step, step)], b.mrows, ws.at[3])
        d.start()
        if part == 0:
            b.hot[...] = time_table_rows(b.counts, media_rows, 48, 128, 8)
        d.wait()

        def frame(i, carry):
            at = pl.ds(pl.multiple_of(i * 48, 48), 48)
            whole = pl.ds(pl.multiple_of(part * step + i * 48, 48), 48)
            mixed = b.mrows[at, :].astype(f32) + dot(b.hot[whole, :], b.tiny_t[...].astype(bf))
            back, gain = norm_back(mixed, b.k[whole, :].astype(f32), b.tiny_t[8:9, :])
            b.gsmall[8:9, :] += gain
            f = part * frames + i
            ends = frame_ends(b.counts)
            time = f
            for s, end in enumerate(ends):
                time = time - jnp.where(f >= end, b.counts[s], 0)
            time = jnp.where(f < ends[-1], time, -1)
            at_time = jnp.where(lax.broadcasted_iota(jnp.int32, (8, 1), 0) == time, 1.0, 0.0)
            b.gsmall[0:8, :] += at_time * jnp.sum(back, axis=0, keepdims=True)
            return carry

        lax.fori_loop(0, frames, frame, 0)

    def small():
        b.tiny[...] = b.gsmall[...].T.astype(bf).reshape(b.tiny.shape)
        give(b.tiny.at[:, 1 - core], b.x_tiny)

    held = [None]

    def left(src):
        if held[0] is src:
            return
        if held[0] is None:
            here(0)
            held[0] = src
            return
        held[0] = src
        if src is b.p_keys:
            into = b.ltk
        elif src is b.p_act:
            into = b.lt
        else:
            into = b.lt.at[:, :, pl.ds(0, 2 * n_z)]
        d = pltpu.make_async_copy(src, into, lt_sem.at[0])
        d.start()
        d.wait()

    coming = {}

    def sources(w, first):
        if w == 3:
            return b.p_cot.at[core], b.p_cot.at[1 - core], first
        if w == 2:
            return b.dpre, b.x_dpre, first
        if w == 1:
            return b.dbranch, b.x_branch, first
        return (b.dq, b.dk, b.dv)[first // model], (b.x_dq, b.x_dk, b.x_dv)[first // model], first % model

    def right(t):
        w, first, width = plan_of[t]
        if w == 4 or t in coming:
            return
        mine, theirs, at = sources(w, first)
        if w != 3:
            if id(theirs) not in given:
                return
            got(theirs)
        cols = pl.ds(at, width)
        made = []
        if w in (2, 3):
            made.append(pltpu.make_async_copy(mine.at[:, cols], b.rhs.at[t % 2, 0, :, pl.ds(0, width)], rhs_sem.at[t % 2, 0]))
        into = b.rhsk.at[:, pl.ds(0, width)] if w == 0 and first >= model else b.rhs.at[t % 2, 1, :, pl.ds(0, width)]
        made.append(pltpu.make_async_copy(theirs.at[:, cols], into, rhs_sem.at[t % 2, 1]))
        for d in made:
            d.start()
        coming[t] = made

    def blocks(x, k, group):
        if group == 1:
            return [b.lt[s, x, 0 : 2 * n_z].reshape(96 * n_z, queries_n) for s in (core, 1 - core)]
        return [jnp.concatenate([b.lt[s, x, i * group + k] for i in range(2 * n_z)], axis=0) for s in (core, 1 - core)]

    def fill(t, pieces):
        w, first, width = plan_of[t]
        h = pieces[0].h
        if w == 4:
            got(b.x_tiny)
            d = pltpu.make_async_copy(b.x_tiny, b.tiny2, ws.at[3])
            d.start()
            d.wait()

            def one(i, carry):
                x, z, y = i // (2 * n_z), (i // 2) % n_z, i % 2
                pieces[0].b.s0[h, x, z, y, :, 0:128] = b.tiny[x, core, z, y] + b.tiny2[x, z, y]
                return carry

            lax.fori_loop(0, 4 * n_z, one, 0)
            return
        right(t)
        for d in coming.pop(t):
            d.wait()
        mine, _, at = sources(w, first)
        keyed = w == 0 and first >= model
        left((b.p_keys if keyed else b.p_lat, b.p_att, b.p_hid, b.p_act)[w])
        r = [b.rhs[t % 2, 0, :, 0:width] if w in (2, 3) else mine[:, pl.ds(at, width)], b.rhsk[:, 0:width] if keyed else b.rhs[t % 2, 1, :, 0:width]]
        for x in range(2):
            if keyed:
                l = [b.ltk[s, x].reshape(96 * n_z, key_rows) for s in (core, 1 - core)]
            else:
                l = blocks(x, rows_of[t] // 48, 4 if w == 3 else 1)
            sums = (dot(l[0], r[0]) + dot(l[1], r[1])).astype(bf)
            start = 0
            for g in pieces:
                g.b.s0[h, x, :, :, :, 0 : g.width] = sums[:, start : start + g.width].reshape(n_z, 2, 48, g.width)
                start += g.width
        if t + 1 < total_stages:
            right(t + 1)

    parts = 6
    work = [(3, 5, functools.partial(hidden_part, i)) for i in range(hidden_n // model)] + [(0, 3, ffn_norm), (0, 4, attended_back)]
    work += [(0, 9, functools.partial(attend_back, g)) for g in range(model // group_width)]
    work += [(0, 5, functools.partial(keys_back, n)) for n in range(4)] + [(0, 3, latents_back)]
    work += [(0, 2, functools.partial(media_back, i)) for i in range(parts)] + [(0, 2, small)]

    def run_until(dst):
        while id(dst) not in given:
            work.pop(0)[2]()

    kinds = [types.SimpleNamespace(**{n: getattr(b, n + k) for n in NAMES}) for k in SETS]
    plan_of = [(st[0][1], st[0][3][0], sum(p[3][1] for p in st)) for st in plan]
    rows_of = [st[0][2][0] for st in plan]
    total_stages = len(plan)
    stages = [
        [Scatter(place, own_grads[w], rows, cols, order, j, t, (ss, rs, ls), kinds[part], b.sq) for part, (j, w, rows, cols, order) in enumerate(stage)]
        for t, stage in enumerate(plan)
    ]
    ticks = total_stages + 3 * BACK_LAG

    def moves(t, k):
        for back in range(3):
            u = t - BACK_LAG * back - 1
            if 0 <= u < total_stages:
                for g in stages[u]:
                    g.advance(back, k)

    for t in range(ticks):
        moves(t, 1)
        for back in range(4):
            u = t - BACK_LAG * back
            if not 0 <= u < total_stages:
                continue
            if u >= SEND_SLOTS:
                for g in stages[u - SEND_SLOTS]:
                    if back == 3 or g.order[back] == "z" or back in g.sent:
                        g.free(back)
            if back == 0:
                w = plan_of[u][0]
                run_until((b.x_dv, b.x_branch, b.x_dpre, b.x_dpre, b.x_tiny)[w])
                fill(u, stages[u])
            for g in stages[u]:
                g.start(back)
        for k in range(2, n_z - 1):
            moves(t, k)
        room = ROOM_B
        while work and room > 0:
            _, cost, piece = work.pop(0)
            room -= cost
            piece()
    for st in stages[-SEND_SLOTS:]:
        for g in st:
            for back in range(4):
                g.free(back)
    for d, done in given.values():
        d.wait_send()
    for d in late:
        d.wait()
    sum_squares(place, n_z, b, (ns, nr), b.norm)


SETS = "abc"
NAMES = ("s0", "r1", "s1", "r2", "s2", "rz", "o")


def backward_plan(shards, model):
    tile = 128
    stages = []

    def split(w, row, first, widths=None):
        widths = widths or WIDE_B[len(stages) % len(WIDE_B)]
        at, pieces = first, []
        for width, order in zip(widths, (("x", "y", "z"), ("y", "x", "z"), ("z", "x", "y"))):
            pieces.append((w, (row, 48), (at, width * tile), order))
            at += width * tile
        stages.append(pieces)

    for row in range(0, shards[3].shape[0], 48):
        for first in range(0, model, 768):
            split(3, row, first)
    for w, cols in ((2, shards[2].shape[1]), (1, model), (0, 3 * model)):
        for first in range(0, cols - FINE_B * 768 * (w == 0), 768):
            split(w, 0, first)
    for first in range(3 * model - FINE_B * 768, 3 * model, 384):
        split(0, 0, first, (1, 1, 1))
    return stages + [[(4, (0, 48), (0, 128), ("x", "y", "z"))]]


def backward_all(full, made, lat, media, counts, n_z):
    queries_n, model = lat.shape
    media_rows = media.shape[0]
    key_rows = queries_n + media_rows
    shards = [jax.ShapeDtypeStruct(f.shape[4:], f.dtype) for f in full]
    hidden_n = shards[2].shape[1]
    plan, count = number(backward_plan(shards, model))
    q, k, v, dpre, mid, new, lse, p_keys, p_lat, p_att, p_hid, p_act, p_cot = made
    given = dict(f_qkv=full[0], f_out=full[1], f_up=full[2], f_tiny=full[4], dpre=dpre, p_keys=p_keys, p_lat=p_lat, p_att=p_att, p_hid=p_hid, p_act=p_act, p_cot=p_cot,
                 media=media, q_in=q, keys=k, v_in=v, mid_in=mid, lse=lse, lat_in=lat, counts=counts)
    bf, f32 = jnp.bfloat16, jnp.float32
    grads = [(s.shape, f32) for s in shards]
    grads[0] = ((3, shards[1].shape[0], model), f32)
    outs = dict(g_qkv=grads[0], g_out=grads[1], g_up=grads[2], g_down=grads[3], g_tiny=grads[4], d_lat=((queries_n, model), f32), norm=((8, 128), f32),
                x_dpre=((queries_n, hidden_n), bf), x_branch=((queries_n, model), bf), x_dq=((queries_n, model), bf), x_dk=((key_rows, model), bf), x_dv=((key_rows, model), bf),
                x_tiny=((2, n_z, 2, 48, 128), bf))
    W, S, L = 384, SEND_SLOTS, LAND_SLOTS
    N = max(w[2] for w in WIDE_B) * 128
    vm = dict(s0a=((S, 2, n_z, 2, 48, W), bf), r1a=((L, n_z, 2, 48, W), bf), s1a=((S, n_z, 2, 48, W), bf), r2a=((L, n_z, 48, W), bf), s2a=((S, n_z, 48, W), bf), rza=((L, 2, n_z - 1, 48, W), bf), oa=((S, 48, W), f32),
              s0b=((S, 2, n_z, 2, 48, W), bf), r1b=((L, 2, n_z, 48, W), bf), s1b=((S, 2, n_z, 48, W), bf), r2b=((L, n_z, 48, W), bf), s2b=((S, n_z, 48, W), bf), rzb=((L, 2, n_z - 1, 48, W), bf), ob=((S, 48, W), f32),
              s0c=((S, 2, n_z, 2, 48, N), bf), rzc=((L, 2, n_z - 1, 2, 2, 48, N), bf), r1c=((L, 2, 48, N), bf), s1c=((S, 2, 2, 48, N), bf), s2c=((S, 2, 48, N), bf), r2c=((L, 48, N), bf), oc=((S, 48, N), f32),
          sq=((48, W), f32), n=((8, 8, 128), f32), nz=((n_z, 8, 128), f32),
          wbuf=((3, n_z, 2, 48, model), bf), dmid=((queries_n, model), f32), dbranch=((queries_n, model), bf), datt=((queries_n, model), bf),
          q=(q.shape, bf), v=(v.shape, bf), mid=(mid.shape, f32), lat=(lat.shape, bf), bias=((key_rows, queries_n), f32), hot=((media_rows, 128), bf), dq=((queries_n, model), bf), k=((key_rows, model), bf), dk=((key_rows, model), bf), dv=((key_rows, model), bf), tiny=((2, 2, n_z, 2, 48, 128), bf), tiny_t=((128, model), f32),
          gsmall=((128, model), f32), tiny2=((2, n_z, 2, 48, 128), bf), mrows=((media_rows // 6, model), bf),
          lt=(p_act.shape, bf), ltk=(p_keys.shape, bf), rhs=((2, 2, queries_n, 768), bf), rhsk=((key_rows, 768), bf))
    sem = pltpu.SemaphoreType.DMA
    in_vmem, in_any = pl.BlockSpec(memory_space=pltpu.VMEM), pl.BlockSpec(memory_space=ANY)
    resident = tuple(id(a) for a in (lse,))
    n_copies = count * n_sems(n_z)
    res = pl.pallas_call(
        functools.partial(backward_kernel, n_z, plan, (*given, *outs, *vm)),
        out_shape=[jax.ShapeDtypeStruct(*o) for o in outs.values()],
        in_specs=[pl.BlockSpec(memory_space=pltpu.SMEM) if a is counts else in_vmem if id(a) in resident else in_any for a in given.values()],
        out_specs=[in_vmem if o is outs["norm"] else in_any for o in outs.values()],
        scratch_shapes=[pltpu.VMEM(*m) for m in vm.values()] + [sem((n_copies,)), sem((n_copies,)), sem((count,)), sem((n_z + 6,)), sem((n_z + 6,)), sem((5,)), sem((8,)), sem((8,)), sem((1,)), sem((2, 2)), sem((7,))],
        name="backward_and_scatter",
        compiler_params=pltpu.CompilerParams(collective_id=1, has_side_effects=True, vmem_limit_bytes=62 * 2**20),
    )(*given.values())
    return types.SimpleNamespace(**dict(zip(outs, res)))


def update_kernel(rates, norm, *refs):
    factor = jnp.minimum(1.0, clip_limit / (norm[0:1, 0:1] + 1e-06))
    n = len(rates)
    ws, ms, vs, gs, rows, outs = refs[:n], refs[n : 2 * n], refs[2 * n : 3 * n], refs[3 * n : 4 * n - 1], refs[4 * n - 1 : 4 * n + 1], refs[4 * n + 1 :]
    for row, o in zip(rows, outs[3 * n :]):
        o[...] = row[...]
    outs[-1][...] = norm[0:1, 0:1]
    small = gs[4][...].T
    steps = ws[4].shape[0]
    grads = [g[...] for g in gs[:4]] + [small[0:steps, :], small[steps : steps + 3, :]]
    for i, g in enumerate(grads):
        new = adamw_step(ws[i][...], ms[i][...], vs[i][...], g, factor if g.ndim == 2 else factor[None], rates[i])
        for o, value in zip(outs[3 * i : 3 * i + 3], new):
            o[...] = value


def update_all(norm, masters, firsts, seconds, grads, rows, rates):
    steps = masters[1].shape[0] // 8

    def spec(a):
        if a.ndim == 3:
            return pl.BlockSpec((3, 8, a.shape[2]), lambda i: (0, i, 0))
        if any(a is r for r in rows):
            return pl.BlockSpec((64, a.shape[1]), lambda i: (jnp.minimum(i, a.shape[0] // 64 - 1), 0))
        if a.shape[1] > 128:
            return pl.BlockSpec((a.shape[0] // steps, a.shape[1]), lambda i: (i, 0))
        return pl.BlockSpec(a.shape, lambda i: (0, 0))

    args = [norm, *masters, *firsts, *seconds, *grads, *rows]
    outs = [a for w in masters for a in (w, w, w)] + list(rows) + [jax.ShapeDtypeStruct((1, 1), jnp.float32)]
    return pl.pallas_call(
        functools.partial(update_kernel, rates),
        grid=(steps,),
        out_shape=[jax.ShapeDtypeStruct(a.shape, a.dtype) for a in outs],
        in_specs=[spec(a) for a in args],
        out_specs=[spec(a) for a in outs],
        name="adamw",
        compiler_params=pltpu.CompilerParams(vmem_limit_bytes=62 * 2**20),
    )(*args)


def out_copies(pairs, sems, at, running):
    for src, dst in pairs:
        d = pltpu.make_async_copy(src, dst, sems.at[len(running)])
        d.start()
        running.append(d)


def dot(a, b, contract=((1,), (0,))):
    return lax.dot_general(a, b, (contract, ((), ())), preferred_element_type=jnp.float32)


def head_windows(head):
    group = 128 // math.gcd(head, 128)
    out = []
    for j in range(group):
        first, last = j * head // 128, ((j + 1) * head - 1) // 128
        out.append((first, last + 1, j * head - first * 128))
    return out, group * head


def lanes_of(rows, tiles, start, head):
    lane = lax.broadcasted_iota(jnp.int32, (rows, tiles * 128), 1)
    return (lane >= start) & (lane < start + head)


def normed(rows_in, gain):
    centered = rows_in - jnp.mean(rows_in, axis=-1, keepdims=True)
    var_row = jnp.mean(centered * centered, axis=-1, keepdims=True)
    return centered * lax.rsqrt(var_row + norm_eps) * gain


def frame_ends(counts):
    ends, total = [], 0
    for s in range(counts.shape[0]):
        total = total + counts[s]
        ends.append(total)
    return ends


def time_table_rows(counts, rows, patch, lanes, time_len):
    row = lax.broadcasted_iota(jnp.int32, (rows, lanes), 0)
    lane = lax.broadcasted_iota(jnp.int32, (rows, lanes), 1)
    ends = frame_ends(counts)
    start = jnp.zeros((rows, lanes), jnp.int32)
    for s, end in enumerate(ends):
        start = start + jnp.where(row >= end * patch, counts[s] * patch, 0)
    off = row - start - lane * patch
    live = (off >= 0) & (off < patch) & (row < ends[-1] * patch) & (lane < time_len)
    return jnp.where(live, 1.0, 0.0).astype(jnp.bfloat16)


def own_keys(counts, media_rows, queries_n, patch):
    slots = counts.shape[0]
    each = queries_n // slots
    shape = (media_rows + queries_n, queries_n)
    row = lax.broadcasted_iota(jnp.int32, shape, 0)
    lane = lax.broadcasted_iota(jnp.int32, shape, 1)
    owner, asks = jnp.zeros(shape, jnp.int32), jnp.zeros(shape, jnp.int32)
    for s, end in enumerate(frame_ends(counts)):
        owner = owner + jnp.where(row >= end * patch, 1, 0)
        if s + 1 < slots:
            asks = asks + jnp.where(lane >= (s + 1) * each, 1, 0)
    mine = jnp.zeros(shape, jnp.int32)
    for s in range(1, slots):
        mine = mine + jnp.where(row >= media_rows + s * each, 1, 0)
    owner = jnp.where(row >= media_rows, mine, owner)
    return jnp.where(owner == asks, 0.0, -1e30)


def forward_kernel(n_z, plan, needs, *refs):
    (w_qkv, w_out, w_up, w_down, w_time, w_gains, lat_in, media_in, cot_in, counts), full, outs, scratch = refs[:10], refs[10:15], refs[15:27], refs[27:]
    o_q, o_k, o_v, o_dpre, o_mid, o_new, o_lse, p_keys, p_lat, p_att, p_hid, p_act = outs[:12]
    p_cot, *scratch = scratch
    *sh, small, hot, bias, lat, media, cot = scratch[:11]
    keys, q, k, v, att, hid, act, slope, dact, mid, new, tiny, tiny_t, lse, wbuf, wdown, flip, flip_keys, ss, rs, ls, os_, ws, ps, pr, pl_, ins = scratch[11:]
    f_qkv, f_out, f_up, f_down, f_tiny = full
    place = Place(n_z)
    queries_n, model = lat.shape
    coming = [pltpu.make_async_copy(src, dst, ins.at[n]) for n, (src, dst) in enumerate(((lat_in, lat), (cot_in, cot), (media_in, media)))]
    for d in coming:
        d.start()
    for i in range(3):
        sh[0][:, i * model : (i + 1) * model] = w_qkv[i].astype(jnp.bfloat16)
    for low, w in zip(sh[1:4], (w_out, w_up, w_down)):
        low[...] = w[...].astype(jnp.bfloat16)
    time_len = w_time.shape[0]
    small[...] = jnp.zeros_like(small)
    small[0:time_len, :] = w_time[...]
    small[time_len : time_len + 3, :] = w_gains[...]
    sh[4][...] = small[...].T.astype(jnp.bfloat16)
    greet(place)
    media_rows = media.shape[0]
    key_rows = media_rows + queries_n
    hidden_n = act.shape[1]
    head = model // HEADS
    windows, group_width = head_windows(head)
    scale = 1.0 / head**0.5
    written = []
    given = []
    core = place.at["c"]

    def give(src, dst, theirs):
        n = len(given)
        if theirs:
            d = pltpu.make_async_remote_copy(src_ref=src, dst_ref=dst, send_sem=ps.at[n], recv_sem=pr.at[n], device_id=place.other("c"), device_id_type=MESH)
        else:
            d = pltpu.make_async_copy(src, dst, pl_.at[n])
        d.start()
        given.append([d, theirs, False])
        return n

    def gone(n):
        d, theirs, done = given[n]
        if not done:
            d.wait_send() if theirs else d.wait()
            given[n][2] = True

    def turn(a, dst, slot, x, wide, before=()):
        made = []
        for n in before:
            gone(n)
        for theirs in (False, True):
            who = 1 - core if theirs else core
            for m in range(wide // 384):
                cols = pl.ds(pl.multiple_of((x * 2 + who) * wide + m * 384, 128), 384)
                flip[slot] = a[:, cols].T.reshape(8, 48, queries_n)
                made.append(give(flip.at[slot], dst.at[core, x, pl.ds(m * 8, 8)], theirs))
                slot += 1
        return made

    def load(src, dst):
        d = pltpu.make_async_copy(src, dst, ws.at[0])
        d.start()
        d.wait()

    def write(*pairs):
        out_copies(pairs, os_, 0, written)

    def norms():
        for d in coming:
            d.wait()
        hot[...] = time_table_rows(counts, media_rows, 48, hot.shape[1], time_len)
        load(f_tiny, tiny)
        tiny_t[...] = tiny[...].reshape(model, 128).astype(jnp.float32).T
        give(cot, p_cot.at[core], False)
        give(cot, p_cot.at[core], True)
        hid[...] = normed(lat[...].astype(jnp.float32), tiny_t[9:10, :]).astype(jnp.bfloat16)
        keys[media_rows:key_rows, :] = hid[...]
        for x in range(2):
            turn(hid, p_lat, 2 * x, x, 384)

        def frame(i, carry):
            rows = pl.ds(pl.multiple_of(i * 48, 48), 48)
            mixed = media[rows, :].astype(jnp.float32) + dot(hot[rows, :], tiny_t[...].astype(jnp.bfloat16))
            keys[rows, :] = normed(mixed, tiny_t[8:9, :]).astype(jnp.bfloat16)
            return carry

        lax.fori_loop(0, media_rows // 48, frame, 0)

    key_turns = []

    def turn_keys(x):
        for n in key_turns:
            gone(n)
        for theirs in (False, True):
            who = 1 - core if theirs else core
            cols = pl.ds(pl.multiple_of((x * 2 + who) * 384, 128), 384)
            flip_keys[int(theirs)] = keys[:, cols].T.reshape(8, 48, key_rows)
            key_turns.append(give(flip_keys.at[int(theirs)], p_keys.at[core, x], theirs))

    def project(i, dst, first):
        load(f_qkv.at[:, :, :, :, :, pl.ds(i * model, model)], wbuf)

        def tile(n, carry):
            cols = pl.ds(pl.multiple_of(n * 256, 256), 256)
            w = wbuf[:, :, :, :, :, cols].reshape(model, 256)
            dst[:, cols] = dot(keys[first:key_rows, :], w).astype(jnp.bfloat16)
            return carry

        lax.fori_loop(0, model // 256, tile, 0)

    def project_q():
        project(0, q, media_rows)
        write((q, o_q))

    def project_k():
        project(1, k, 0)
        write((k, o_k))

    def project_v():
        project(2, v, 0)
        write((v, o_v))

    def attend(g):
        if g == 0:
            bias[...] = own_keys(counts, media_rows, queries_n, 48)
        base = g * group_width
        tiles = [jnp.zeros((queries_n, 128), jnp.float32) for _ in range(group_width // 128)]
        for j, (t0, t1, start) in enumerate(windows):
            cols = slice(base + t0 * 128, base + t1 * 128)
            qh = q[:, cols]
            qh = jnp.where(lanes_of(queries_n, t1 - t0, start, head), qh, jnp.zeros_like(qh))
            s = dot(k[:, cols], qh, ((1,), (1,))) * scale + bias[...]
            top = jnp.max(s, axis=0, keepdims=True)
            e = jnp.exp(s - top)
            total = jnp.sum(e, axis=0, keepdims=True)
            p = (e * (1.0 / total)).astype(jnp.bfloat16)
            lse[g * len(windows) + j : g * len(windows) + j + 1, :] = top + jnp.log(total)
            vh = v[:, cols]
            vh = jnp.where(lanes_of(key_rows, t1 - t0, start, head), vh, jnp.zeros_like(vh))
            got = dot(p, vh, ((0,), (0,)))
            for t in range(t0, t1):
                tiles[t] = tiles[t] + got[:, (t - t0) * 128 : (t - t0 + 1) * 128]
        for t, tile in enumerate(tiles):
            att[:, base + t * 128 : base + (t + 1) * 128] = tile.astype(jnp.bfloat16)

    def project_out():
        write((lse, o_lse))
        for x in range(2):
            turn(att, p_att, 4 + 2 * x, x, 384)
        load(f_out, wbuf)

        def tile(n, carry):
            cols = pl.ds(pl.multiple_of(n * 256, 256), 256)
            w = wbuf[:, :, :, :, :, cols].reshape(model, 256)
            mid[:, cols] = lat[:, cols].astype(jnp.float32) + dot(att[...], w)
            return carry

        lax.fori_loop(0, model // 256, tile, 0)
        hid[...] = normed(mid[...], tiny_t[10:11, :]).astype(jnp.bfloat16)
        write((mid, o_mid))
        for x in range(2):
            hid_turns.extend(turn(hid, p_hid, 8 + 2 * x, x, 384))

    hid_turns = []
    act_turns = []

    def up(i):
        load(f_up.at[:, :, :, :, :, pl.ds(i * model, model)], wbuf)

        def tile(n, carry):
            cols = pl.ds(pl.multiple_of(n * 256, 256), 256)
            into = pl.ds(pl.multiple_of(i * model + n * 256, 256), 256)
            w = wbuf[:, :, :, :, :, cols].reshape(model, 256)
            x = dot(hid[...], w)
            cdf = 0.5 + 0.5 * lax.erf(x * 0.7071067811865476)
            act[:, into] = (x * cdf).astype(jnp.bfloat16)
            slope[:, into] = cdf + x * (jnp.exp(-0.5 * x * x) * 0.3989422804014327)
            return carry

        lax.fori_loop(0, model // 256, tile, 0)
        if i % 2 == 1:
            before = list(range(len(given))) if i == 1 else act_turns
            act_turns.extend(turn(act, p_act, 0, i // 2, model, before))

    def down(i, width):
        cols = slice(i * width, (i + 1) * width)
        load(f_down.at[:, :, :, :, :, pl.ds(i * width, width)], wdown)
        per = hidden_n // 4
        got = jnp.zeros((queries_n, width), jnp.float32)
        for b in range(4):
            w = wdown[b // 2, b % 2].reshape(per, width)
            got = got + dot(act[:, b * per : (b + 1) * per], w)
            back = dot(cot[:, cols], w, ((1,), (1,)))
            part = slice(b * per, (b + 1) * per)
            if (i + 1) * width == model:
                act[:, part] = ((dact[:, part] + back) * slope[:, part]).astype(jnp.bfloat16)
                write((act.at[:, part], o_dpre.at[:, part]))
            elif i == 0:
                dact[:, b * per : (b + 1) * per] = back
            else:
                dact[:, b * per : (b + 1) * per] += back
        new[:, cols] = (mid[:, cols] + got).astype(jnp.bfloat16)

    def finish():
        write((new, o_new))
        for d in written:
            d.wait()
        for n, (d, theirs, done) in enumerate(given):
            gone(n)
            if theirs:
                d.wait_recv()

    work = [(needs["tiny"], 8, norms), (needs["q"], 4, project_q), (needs["k"], 8, project_k), (needs["v"], 8, project_v)]
    work[2:2] = [(needs["q"], 3, functools.partial(turn_keys, x)) for x in range(2)]
    work += [(needs["v"], 7, functools.partial(attend, g)) for g in range(model // group_width)]
    work += [(needs["out"], 5, project_out)]
    work += [(s, 6, functools.partial(up, i)) for i, s in enumerate(needs["up"])]
    work += [(s, 5, functools.partial(down, i, model // len(needs["down"]))) for i, s in enumerate(needs["down"])]
    work += [(needs["down"][-1], 5, finish)]
    locals_ = []
    for i in range(5):
        d = pltpu.make_async_copy(sh[i], full[i].at[block_index(place, ())], ls.at[i])
        d.start()
        locals_.append(d)
    stages = [[Gather(place, sh[w], full[w], rows, cols, order, (ss, rs), j * n_sems(n_z)) for (j, w, rows, cols, order) in stage] for stage in plan]
    waited = set()
    total, steps = len(stages), 4
    ticks = total + LAG * steps
    for t in range(ticks):
        for back in range(steps):
            u = t - LAG * back - 1
            if LAG > 1 and 0 <= u < total:
                for g in stages[u]:
                    g.advance(back, 1)
        for back in range(steps + 1):
            u = t - LAG * back
            if not 0 <= u < total:
                continue
            for g, (j, w, *_) in zip(stages[u], plan[u]):
                if back == 1 and w not in waited:
                    locals_[w].wait()
                    waited.add(w)
                if back > 0:
                    g.arrive(back - 1)
                if back < steps:
                    g.start(back)
        for move in range(1 if LAG == 1 else 2, n_z - 1):
            for back in range(steps):
                u = t - LAG * back - (LAG > 1)
                if 0 <= u < total:
                    for g in stages[u]:
                        g.advance(back, move)
        room = ROOM_A
        while work and work[0][0] <= t - LAG * steps and (room > 0 or t == ticks - 1):
            need, cost, piece = work.pop(0)
            room -= cost
            piece()
    for st in stages:
        for g in st:
            g.finish()


ROOM_A = 12
LAG = 2
FINE = 2
WIDE_A = ((5, 5, 2), (5, 4, 3), (5, 5, 2), (4, 5, 3))
Z_DOWN = (1,)


def forward_plan(shards, model):
    def split(w, rows, first, widths, last):
        at, pieces = first, []
        for width, order in zip(widths, (ZYX, ZXY, last)):
            pieces.append((w, (0, rows), (at, width), order))
            at += width
        return pieces

    rows = shards[1].shape[0]
    stages, needs = [[(4, (0, rows), (0, 128), ZYX)]], {"tiny": 0}
    twelfth = model // 12
    widths = [tuple(n * twelfth for n in WIDE_A[i % len(WIDE_A)]) for i in range(4 + shards[2].shape[1] // model)]
    for i, name in enumerate("qkv"):
        needs[name] = len(stages)
        stages.append(split(0, rows, i * model, widths[i], (XYZ, YXZ)[i % 2]))
    needs["out"] = len(stages)
    stages.append(split(1, rows, 0, widths[3], YXZ))
    needs["up"], needs["down"] = [], []
    for i in range(shards[2].shape[1] // model):
        needs["up"].append(len(stages))
        stages.append(split(2, rows, i * model, widths[4 + i], (XYZ, YXZ)[i % 2]))
    groups = model // 256
    deep = shards[3].shape[0]
    for i in range(groups):
        if i >= groups - FINE:
            for half in range(2):
                cols = (i * 256 + half * 128, 128)
                stages.append([(3, (0, deep // 2), cols, ZYX), (3, (deep // 2, deep // 2), cols, ZXY)])
        else:
            pair = (XYZ, YXZ) if i in Z_DOWN else (ZYX, ZXY)
            stages.append([(3, (0, deep), (i * 256 + n * 128, 128), pair[n]) for n in range(2)])
        needs["down"].append(len(stages) - 1)
    return stages, needs


def forward_all(weights, lat, media, cot, counts, n_z):
    bf, f32 = jnp.bfloat16, jnp.float32
    rows, model = weights[1].shape
    hidden_n = weights[2].shape[1]
    shards = [jax.ShapeDtypeStruct(s, bf) for s in ((rows, 3 * model), weights[1].shape, weights[2].shape, weights[3].shape, (rows, 128))]
    stages, needs = forward_plan(shards, model)
    plan, count = number(stages)
    queries_n, media_rows = lat.shape[0], media.shape[0]
    key_rows = queries_n + media_rows
    part = (2, 2, 2 * n_z, 48)
    made = [((queries_n, model), bf), ((key_rows, model), bf), ((key_rows, model), bf), ((queries_n, hidden_n), bf), ((queries_n, model), f32), ((queries_n, model), bf), ((HEADS, queries_n), f32),
            (part + (key_rows,), bf), (part + (queries_n,), bf), (part + (queries_n,), bf), (part + (queries_n,), bf), ((2, 2, 2 * n_z * hidden_n // model, 48, queries_n), bf), ((2, queries_n, model), bf)]
    vm = [(s.shape, bf) for s in shards] + [((128, rows), f32), ((media_rows, 128), bf), ((key_rows, queries_n), f32), (lat.shape, bf), (media.shape, bf), (cot.shape, bf)]
    vm += [((key_rows, model), bf), ((queries_n, model), bf), ((key_rows, model), bf), ((key_rows, model), bf), ((queries_n, model), bf), ((queries_n, model), bf), ((queries_n, hidden_n), bf),
          ((queries_n, hidden_n), f32), ((queries_n, hidden_n), f32), ((queries_n, model), f32), ((queries_n, model), bf),
                     ((2, 2, n_z, 2, rows, 128), bf), ((128, model), f32), ((HEADS, queries_n), f32), ((2, 2, n_z, 2, rows, model), bf), ((2, 2, n_z, 2, shards[3].shape[0], 256), bf),
                     ((12, 8, 48, queries_n), bf), ((2, 8, 48, key_rows), bf)]
    sem = pltpu.SemaphoreType.DMA
    in_vmem, in_any = pl.BlockSpec(memory_space=pltpu.VMEM), pl.BlockSpec(memory_space=ANY)
    out = pl.pallas_call(
        functools.partial(forward_kernel, n_z, plan, needs),
        out_shape=[jax.ShapeDtypeStruct((2, 2, n_z, 2) + s.shape, s.dtype) for s in shards] + [jax.ShapeDtypeStruct(*m) for m in made],
        in_specs=[in_vmem] * 6 + [in_any] * 3 + [pl.BlockSpec(memory_space=pltpu.SMEM)],
        out_specs=[in_any] * (5 + len(made)),
        scratch_shapes=[pltpu.VMEM(*m) for m in vm] + [sem((count * n_sems(n_z),)), sem((count * n_sems(n_z),)), sem((5,)), sem((16,)), sem((1,)), sem((48,)), sem((48,)), sem((48,)), sem((3,))],
        name="gather_and_forward",
        compiler_params=pltpu.CompilerParams(collective_id=0, has_side_effects=True, vmem_limit_bytes=60 * 2**20),
    )(*weights, lat, media, cot, counts)
    return out[:5], out[5:]


def layer_norm(values_in, gain):
    mean_row = jnp.mean(values_in, axis=-1, keepdims=True)
    centered = values_in - mean_row
    var_row = jnp.mean(centered * centered, axis=-1, keepdims=True)
    return centered * lax.rsqrt(var_row + norm_eps) * gain


def exact_gelu(values_in):
    return jax.nn.gelu(values_in, approximate=False)


def frame_tables(counts, frame_slots, time_len):
    slot_total = counts.shape[0]
    order = jnp.arange(slot_total, dtype=jnp.int32)
    slot_ends = jnp.sum(jnp.where(order[None, :] <= order[:, None], counts[None, :], 0), axis=1)
    slot_starts = slot_ends - counts
    frame_ids = jnp.arange(frame_slots, dtype=jnp.int32)
    frame_owner = jnp.sum((frame_ids[:, None] >= slot_ends[None, :]).astype(jnp.int32), axis=1)
    slot_ids = jnp.arange(slot_total, dtype=jnp.int32)
    start_of = jnp.sum(
        jnp.where(frame_owner[:, None] == slot_ids[None, :], slot_starts[None, :], 0), axis=1
    )
    time_index = frame_ids - start_of
    live_frame = frame_owner < slot_total
    time_ids = jnp.arange(time_len, dtype=jnp.int32)
    time_hot = ((time_index[:, None] == time_ids[None, :]) & live_frame[:, None]).astype(
        jnp.float32
    )
    return (frame_owner, time_hot)


def gather_params(part_qkv, part_out, part_up, part_down, part_time, part_gains):
    inner_part = (
        lax.all_gather(part_qkv, FSDP, axis=0, tiled=True),
        lax.all_gather(part_out, FSDP, axis=0, tiled=True),
        lax.all_gather(part_up, FSDP, axis=0, tiled=True),
        lax.all_gather(part_down, FSDP, axis=0, tiled=True),
        lax.all_gather(part_time, FSDP, axis=0, tiled=True),
        lax.all_gather(part_gains, FSDP, axis=0, tiled=True),
    )
    return (
        lax.all_gather(inner_part[0], DP, axis=0, tiled=True),
        lax.all_gather(inner_part[1], DP, axis=0, tiled=True),
        lax.all_gather(inner_part[2], DP, axis=0, tiled=True),
        lax.all_gather(inner_part[3], DP, axis=0, tiled=True),
        lax.all_gather(inner_part[4], DP, axis=0, tiled=True),
        lax.all_gather(inner_part[5], DP, axis=0, tiled=True),
    )


def reduce_grads(grad_qkv, grad_out, grad_up, grad_down, grad_time, grad_gains):
    outer_part = (
        lax.psum_scatter(
            grad_qkv.astype(jnp.bfloat16), DP, scatter_dimension=0, tiled=True
        ).astype(jnp.float32),
        lax.psum_scatter(
            grad_out.astype(jnp.bfloat16), DP, scatter_dimension=0, tiled=True
        ).astype(jnp.float32),
        lax.psum_scatter(
            grad_up.astype(jnp.bfloat16), DP, scatter_dimension=0, tiled=True
        ).astype(jnp.float32),
        lax.psum_scatter(
            grad_down.astype(jnp.bfloat16), DP, scatter_dimension=0, tiled=True
        ).astype(jnp.float32),
        lax.psum_scatter(
            grad_time.astype(jnp.bfloat16), DP, scatter_dimension=0, tiled=True
        ).astype(jnp.float32),
        lax.psum_scatter(
            grad_gains.astype(jnp.bfloat16), DP, scatter_dimension=0, tiled=True
        ).astype(jnp.float32),
    )
    return (
        lax.psum_scatter(
            outer_part[0].astype(jnp.bfloat16), FSDP, scatter_dimension=0, tiled=True
        ).astype(jnp.float32),
        lax.psum_scatter(
            outer_part[1].astype(jnp.bfloat16), FSDP, scatter_dimension=0, tiled=True
        ).astype(jnp.float32),
        lax.psum_scatter(
            outer_part[2].astype(jnp.bfloat16), FSDP, scatter_dimension=0, tiled=True
        ).astype(jnp.float32),
        lax.psum_scatter(
            outer_part[3].astype(jnp.bfloat16), FSDP, scatter_dimension=0, tiled=True
        ).astype(jnp.float32),
        lax.psum_scatter(
            outer_part[4].astype(jnp.bfloat16), FSDP, scatter_dimension=0, tiled=True
        ).astype(jnp.float32),
        lax.psum_scatter(
            outer_part[5].astype(jnp.bfloat16), FSDP, scatter_dimension=0, tiled=True
        ).astype(jnp.float32),
    )


def masked_scores(q_heads, k_heads, allowed, score_scale):
    scores = (
        jnp.einsum("qhe,khe->hqk", q_heads, k_heads, preferred_element_type=jnp.float32)
        * score_scale
    )
    return jnp.where(allowed[None, :, :], scores, -1e30)


def adamw_step(weight, first, second, grad, factor, rate):
    clipped = grad * factor
    first_new = beta_one * first + (1.0 - beta_one) * clipped
    second_new = beta_two * second + (1.0 - beta_two) * clipped * clipped
    first_hat = first_new / (1.0 - beta_one**STEP)
    second_hat = second_new / (1.0 - beta_two**STEP)
    weight_new = weight - rate * (
        first_hat / (jnp.sqrt(second_hat) + adam_eps) + decay_rate * weight
    )
    return (weight_new, first_new, second_new)


def on_device(
    latents,
    media,
    frame_counts,
    cotangent,
    w_qkv,
    m_qkv,
    v_qkv,
    w_out,
    m_out,
    v_out,
    w_up,
    m_up,
    v_up,
    w_down,
    m_down,
    v_down,
    time_table,
    m_time,
    v_time,
    gains,
    m_gains,
    v_gains,
):
    n_dp, n_fsdp = lax.axis_size(DP), lax.axis_size(FSDP)
    masters = (w_qkv, w_out, w_up, w_down, time_table, gains)
    firsts = (m_qkv, m_out, m_up, m_down, m_time, m_gains)
    seconds = (v_qkv, v_out, v_up, v_down, v_time, v_gains)
    rates = (0.02, 0.1, 0.02, 0.01, 0.2, 0.5)
    item_slots, lat_count, _ = latents.shape
    frame_slots, patch_rows, _ = media.shape
    queries_n = item_slots * lat_count
    if fits_kernels(n_dp, n_fsdp, w_qkv, w_up, w_down, queries_n, frame_slots, patch_rows):
        new_latents, d_latents, grad_norm, updated = by_kernels(
            turned(masters), turned(firsts), turned(seconds), rates, latents, media, cotangent, frame_counts, n_fsdp // 2
        )
    else:
        frame_owner, time_hot = frame_tables(frame_counts, frame_slots, time_table.shape[1])
        query_owner = jnp.arange(queries_n, dtype=jnp.int32) // lat_count
        key_owner = jnp.concatenate([jnp.repeat(frame_owner, patch_rows), query_owner], axis=0)
        allowed = query_owner[:, None] == key_owner[None, :]
        lows = tuple(w.astype(jnp.bfloat16) for w in masters)
        new_latents, d_latents, grad_norm, reduced = by_collectives(lows, latents, media, cotangent, time_hot, allowed)
        factor = jnp.minimum(1.0, clip_limit / (grad_norm + 1e-06))
        updated = []
        for index in range(6):
            updated.extend(adamw_step(masters[index], firsts[index], seconds[index], reduced[index], factor, rates[index]))
    return (new_latents, d_latents, grad_norm, *updated)


def turned(arrays):
    qkv, out, up, down, time, gain = arrays
    return qkv.transpose(1, 0, 2), out, up, down, time.T, gain.T


def fits_kernels(n_dp, n_fsdp, w_qkv, w_up, w_down, queries_n, frame_slots, patch_rows):
    rows, _, model = w_qkv.shape
    return (
        n_dp == 4 and n_fsdp == 8 and rows == 48 and model == 1536 and w_up.shape[1] == 4 * model and w_down.shape[0] == 192
        and queries_n == 256 and patch_rows == 48 and frame_slots % 3 == 0
    )


def by_kernels(masters, firsts, seconds, rates, latents, media, cotangent, counts, n_z):
    model = latents.shape[2]
    lat, med, cot = (a.reshape(-1, model) for a in (latents, media, cotangent))
    full, made = forward_all(masters, lat, med, cot, counts, n_z)
    own = backward_all(full, made, lat, med, counts, n_z)
    grads = [own.g_qkv, own.g_out, own.g_up, own.g_down, own.g_tiny]
    *new, new_rows, d_rows, norm = update_all(own.norm, masters, firsts, seconds, grads, (made[5], own.d_lat), rates)
    kinds = [turned(new[n::3]) for n in range(3)]
    updated = [kinds[n][i] for i in range(6) for n in range(3)]
    return new_rows.reshape(latents.shape), d_rows.reshape(latents.shape), norm.reshape(()), updated


def by_collectives(lows, latents, media, cotangent, time_hot, allowed):
    full_qkv, full_out, full_up, full_down, full_time, full_gains = gather_params(*lows)
    item_slots, lat_count, model_width = latents.shape
    frame_slots, patch_rows, unused_width = media.shape
    queries_n = item_slots * lat_count
    media_rows = frame_slots * patch_rows
    head_size = model_width // HEADS
    score_scale = 1.0 / head_size**0.5
    time_f32 = full_time.astype(jnp.float32)
    gains_f32 = full_gains.astype(jnp.float32)
    frame_time = jnp.dot(time_hot, time_f32.T, precision=highest)
    mixed = media.astype(jnp.float32) + frame_time[:, None, :]
    media_norm, media_back = jax.vjp(layer_norm, mixed, gains_f32[:, 0])
    media_low = media_norm.astype(jnp.bfloat16).reshape(media_rows, model_width)
    lat_rows = latents.reshape(queries_n, model_width).astype(jnp.float32)
    lat_norm, lat_back = jax.vjp(layer_norm, lat_rows, gains_f32[:, 1])
    lat_low = lat_norm.astype(jnp.bfloat16)
    keys_in = jnp.concatenate([media_low, lat_low], axis=0)
    key_rows = keys_in.shape[0]
    qkv_flat = full_qkv.reshape(model_width, 3 * model_width)
    queries = jnp.dot(
        lat_low, qkv_flat[:, :model_width], preferred_element_type=jnp.float32
    ).astype(jnp.bfloat16)
    key_value = jnp.dot(
        keys_in, qkv_flat[:, model_width:], preferred_element_type=jnp.float32
    ).astype(jnp.bfloat16)
    q_heads = queries.reshape(queries_n, HEADS, head_size)
    k_heads = key_value[:, :model_width].reshape(key_rows, HEADS, head_size)
    v_heads = key_value[:, model_width:].reshape(key_rows, HEADS, head_size)
    scores = masked_scores(q_heads, k_heads, allowed, score_scale)
    row_top = jnp.max(scores, axis=-1, keepdims=True)
    row_total = jnp.sum(jnp.exp(scores - row_top), axis=-1, keepdims=True)
    log_total = row_top + jnp.log(row_total)
    probs_low = jnp.exp(scores - log_total).astype(jnp.bfloat16)
    attended = jnp.einsum("hqk,khe->qhe", probs_low, v_heads, preferred_element_type=jnp.float32)
    attended = attended.reshape(queries_n, model_width).astype(jnp.bfloat16)
    middle = lat_rows + jnp.dot(attended, full_out, preferred_element_type=jnp.float32)
    hidden, ffn_back = jax.vjp(layer_norm, middle, gains_f32[:, 2])
    hidden_low = hidden.astype(jnp.bfloat16)
    pre_act = jnp.dot(hidden_low, full_up, preferred_element_type=jnp.float32)
    activated, gelu_back = jax.vjp(exact_gelu, pre_act)
    act_low = activated.astype(jnp.bfloat16)
    result = middle + jnp.dot(act_low, full_down, preferred_element_type=jnp.float32)
    new_latents = result.astype(jnp.bfloat16).reshape(item_slots, lat_count, model_width)
    d_result = cotangent.reshape(queries_n, model_width)
    g_down = jnp.einsum("qf,qd->fd", act_low, d_result, preferred_element_type=jnp.float32)
    d_act = jnp.einsum("qd,fd->qf", d_result, full_down, preferred_element_type=jnp.float32)
    d_pre = gelu_back(d_act)[0].astype(jnp.bfloat16)
    g_up = jnp.einsum("qd,qf->df", hidden_low, d_pre, preferred_element_type=jnp.float32)
    d_hidden = jnp.einsum("qf,df->qd", d_pre, full_up, preferred_element_type=jnp.float32)
    d_middle_ln, g_gain_ffn = ffn_back(d_hidden)
    d_middle = d_result.astype(jnp.float32) + d_middle_ln
    d_branch = d_middle.astype(jnp.bfloat16)
    g_out = jnp.einsum("qe,qd->ed", attended, d_branch, preferred_element_type=jnp.float32)
    d_attended = jnp.einsum(
        "qd,ed->qe", d_branch, full_out, preferred_element_type=jnp.float32
    ).astype(jnp.bfloat16)
    scores_again = masked_scores(q_heads, k_heads, allowed, score_scale)
    probs = jnp.exp(scores_again - log_total)
    probs_again = probs.astype(jnp.bfloat16)
    d_att_heads = d_attended.reshape(queries_n, HEADS, head_size)
    d_probs = jnp.einsum("qhe,khe->hqk", d_att_heads, v_heads, preferred_element_type=jnp.float32)
    row_dot = jnp.sum(probs * d_probs, axis=-1, keepdims=True)
    d_scores = (probs * (d_probs - row_dot)).astype(jnp.bfloat16)
    d_queries = (
        (
            jnp.einsum("hqk,khe->qhe", d_scores, k_heads, preferred_element_type=jnp.float32)
            * score_scale
        )
        .reshape(queries_n, model_width)
        .astype(jnp.bfloat16)
    )
    d_keys = (
        (
            jnp.einsum("hqk,qhe->khe", d_scores, q_heads, preferred_element_type=jnp.float32)
            * score_scale
        )
        .reshape(key_rows, model_width)
        .astype(jnp.bfloat16)
    )
    d_values = (
        jnp.einsum("hqk,qhe->khe", probs_again, d_att_heads, preferred_element_type=jnp.float32)
        .reshape(key_rows, model_width)
        .astype(jnp.bfloat16)
    )
    g_query = jnp.einsum("qd,qe->de", lat_low, d_queries, preferred_element_type=jnp.float32)
    d_key_value = jnp.concatenate([d_keys, d_values], axis=1)
    g_key_value = jnp.einsum("kd,kx->dx", keys_in, d_key_value, preferred_element_type=jnp.float32)
    g_qkv = jnp.concatenate([g_query, g_key_value], axis=1).reshape(model_width, 3, model_width)
    back_flat = full_qkv.reshape(model_width, 3 * model_width)
    d_keys_in = jnp.einsum(
        "kx,dx->kd", d_key_value, back_flat[:, model_width:], preferred_element_type=jnp.float32
    )
    d_lat_norm = (
        jnp.einsum(
            "qe,de->qd", d_queries, back_flat[:, :model_width], preferred_element_type=jnp.float32
        )
        + d_keys_in[media_rows:]
    )
    d_lat_ln, g_gain_lat = lat_back(d_lat_norm)
    d_latents = (d_middle + d_lat_ln).reshape(item_slots, lat_count, model_width)
    d_mixed, g_gain_media = media_back(
        d_keys_in[:media_rows].reshape(frame_slots, patch_rows, model_width)
    )
    frame_grad = jnp.sum(d_mixed, axis=1)
    g_time = jnp.einsum("fd,ft->dt", frame_grad, time_hot, precision=highest)
    g_gains = jnp.stack([g_gain_media, g_gain_lat, g_gain_ffn], axis=1)
    reduced = reduce_grads(g_qkv, g_out, g_up, g_down, g_time, g_gains)
    local_sq = jnp.zeros((), jnp.float32)
    for grad in reduced:
        local_sq = local_sq + jnp.sum(grad * grad)
    grad_norm = jnp.sqrt(lax.psum(local_sq, (DP, FSDP)))
    return new_latents, d_latents, grad_norm, reduced


def solution(mesh):
    both = (DP, FSDP)
    one, two, three = P(both), P(both, None), P(both, None, None)
    updated = (three,) * 3 + (two,) * 15
    placed = (three, three, one, three, *updated)
    return jax.shard_map(
        on_device,
        mesh=mesh,
        in_specs=placed,
        out_specs=(three, three, P(), *updated),
        check_vma=False,
    )
```
